128 devices in a mesh: dp: 8 (over x, core), rows: 4 (over y), chan: 4 (over z).
Axes of the slice: x: 4, y: 4, z: 4, core: 2. Of those that a mesh axis runs over, the one named last changes fastest.
Arguments:
- features: bfloat16 [256, 24, 24, 1024], P(('dp', 'chan'), 'rows'), may hold values from -6 to 6
- counts: int32 [64], P(('dp', 'rows')), may hold values from 0 to 4, as said below
- pre_reduce: bfloat16 [1024, 1024], replicated, may hold values from -0.1875 to 0.1875
- pre_conv: bfloat16 [3, 3, 1024], replicated, may hold values from -2 to 2
- pre_expand: bfloat16 [1024, 1024], replicated, may hold values from -0.1875 to 0.1875
- pre_gain: float32 [1024], replicated, may hold values from 0.5 to 1.5
- post_reduce: bfloat16 [1024, 1024], P('chan'), may hold values from -0.1875 to 0.1875
- post_conv: bfloat16 [3, 3, 1024], replicated, may hold values from -2 to 2
- post_expand: bfloat16 [1024, 1024], P(None, 'chan'), may hold values from -0.1875 to 0.1875
- post_gain: float32 [1024], P('chan'), may hold values from 0.5 to 1.5
- readout: bfloat16 [1024, 4096], replicated, may hold values from -0.1875 to 0.1875
- cotangent: bfloat16 [256, 12, 12, 4096], P(('dp', 'rows'), None, None, 'chan'), may hold values from -6 to 6
Outputs:
- tokens: bfloat16 [256, 12, 12, 4096], P(('dp', 'rows'), None, None, 'chan')
- feature_grad: float32 [256, 24, 24, 1024], P(('dp', 'chan'), 'rows')
- pre_reduce_grad: float32 [1024, 1024], replicated
- pre_conv_grad: float32 [3, 3, 1024], replicated
- pre_expand_grad: float32 [1024, 1024], replicated
- pre_gain_grad: float32 [1024], replicated
- post_reduce_grad: float32 [1024, 1024], P('chan')
- post_conv_grad: float32 [3, 3, 1024], replicated
- post_expand_grad: float32 [1024, 1024], P(None, 'chan')
- post_gain_grad: float32 [1024], P('chan')
- readout_grad: float32 [1024, 4096], P('chan')
The draws below stay inside these ranges and needn't reach their ends.
Inputs may be any that keep to these rules, and one draw needn't show every extreme that they name: Sample k owns slots 4 k to 4 k + 3 and uses the first counts[k] of them; some sample has 4 images and some has none.
All inputs are finite; a program needn't handle non-finite values.
Results may differ from the reference program's by a relative error of at most 0.02.
Values may be sent and summed in bfloat16 or wider, within the bound.
No kernel may reach another device: no remote copies, remote signals or barrier semaphores. Data moves between devices by JAX's collectives and lax.ppermute only.
A program may use at most 256 MiB of HBM per device.

```python
import jax
import jax.numpy as jnp
from jax import lax

CH = 1024
OUT = 4096
GRID = 24
POOL = 12
MID = 1024
SLOT = 4
SAMPLES = 64
SLOTS = 256


def draw_counts(key, part):
    key = jax.random.fold_in(key, 7)
    first_key, second_key, third_key = jax.random.split(key, 3)
    values = jax.random.randint(first_key, (SAMPLES,), 0, SLOT + 1)
    full_at = jax.random.randint(second_key, (), 0, SAMPLES)
    offset = jax.random.randint(third_key, (), 1, SAMPLES)
    empty_at = (full_at + offset) % SAMPLES
    values = values.at[empty_at].set(0)
    values = values.at[full_at].set(SLOT)
    return values.astype(jnp.int32)


def levels(rng, dims, cuts, low, top_value):
    level = 1.0
    for dim, parts in cuts:
        draws = jax.random.uniform(jax.random.fold_in(jax.random.fold_in(rng, 6), dim), (parts,), jnp.float32, low / len(cuts), top_value / len(cuts))
        level = level * jnp.repeat(jnp.exp(draws), dims[dim] // parts).reshape((-1,) + (1,) * (len(dims) - 1 - dim))
    return level


def noise(key, dims, deviation, bound, pieces=(), dtype=jnp.bfloat16):
    gain = levels(key, dims, pieces, -0.22, 0.18) if pieces else 1.0
    drawn = jax.random.normal(key, dims, jnp.float32) * deviation * gain
    return jnp.minimum(jnp.maximum(drawn, -bound), bound).astype(dtype)


def setup_inputs(seed: int = 0) -> dict:
    arg_keys = jax.random.split(jax.random.key(seed), 13)
    features = noise(arg_keys[0], (SLOTS, GRID, GRID, CH), 1.0, 6.0, ((0, 32), (1, 4)))
    counts = draw_counts(jax.random.fold_in(arg_keys[12], 71), 0)
    pre_reduce = noise(arg_keys[2], (CH, MID), CH ** -0.5, 0.1875)
    pre_conv = noise(arg_keys[3], (3, 3, MID), 9 ** -0.5, 2.0)
    pre_expand = noise(arg_keys[4], (MID, CH), MID ** -0.5, 0.1875)
    pre_gain = jnp.clip(1.0 + 0.1 * jax.random.normal(arg_keys[5], (CH,), jnp.float32), 0.5, 1.5)
    post_reduce = noise(arg_keys[6], (CH, MID), CH ** -0.5, 0.1875, ((0, 4),))
    post_conv = noise(arg_keys[7], (3, 3, MID), 9 ** -0.5, 2.0)
    post_expand = noise(arg_keys[8], (MID, CH), MID ** -0.5, 0.1875, ((1, 4),))
    post_gain = jnp.clip(1.0 + 0.1 * jax.random.normal(arg_keys[9], (CH,), jnp.float32), 0.5, 1.5)
    readout = noise(arg_keys[10], (CH, OUT), CH ** -0.5, 0.1875)
    cotangent = noise(arg_keys[11], (SLOTS, POOL, POOL, OUT), 1.0, 6.0, ((0, 32), (3, 4)))
    return {"features": features, "counts": counts, "pre_reduce": pre_reduce, "pre_conv": pre_conv, "pre_expand": pre_expand, "pre_gain": pre_gain, "post_reduce": post_reduce, "post_conv": post_conv, "post_expand": post_expand, "post_gain": post_gain, "readout": readout, "cotangent": cotangent}


EPS = 1e-06
HIGH = lax.Precision.HIGHEST

@jax.custom_vjp
def low(v):
    return lax.optimization_barrier(v.astype(jnp.bfloat16)).astype(jnp.float32)

@jax.custom_vjp
def low_back(v):
    return v

def low_keep(v):
    return (low(v), None)

def low_pass(kept, grad):
    return (grad,)

def back_keep(v):
    return (v, None)

def back_low(kept, grad):
    return (low(grad),)
low.defvjp(low_keep, low_pass)
low_back.defvjp(back_keep, back_low)

def conv_grid(values, kernel):
    height = values.shape[1]
    breadth = values.shape[2]
    padded = jnp.pad(values, ((0, 0), (1, 1), (1, 1), (0, 0)))
    total = padded[:, 0:height, 0:breadth, :] * kernel[0, 0]
    for shift_row in range(3):
        for shift_col in range(3):
            if shift_row + shift_col > 0:
                total = total + padded[:, shift_row:shift_row + height, shift_col:shift_col + breadth, :] * kernel[shift_row, shift_col]
    return total

def layer_norm(values, norm_gain):
    mean_value = lax.optimization_barrier(jnp.mean(values, -1, keepdims=True))
    mean_square = lax.optimization_barrier(jnp.mean(values * values, -1, keepdims=True))
    inverse_std = lax.rsqrt(mean_square - mean_value * mean_value + EPS)
    return (values - mean_value) * inverse_std * norm_gain

def bottleneck(inputs, reduce_w, conv_w, expand_w, norm_gain):
    reduced = low_back(jnp.einsum('abcd,de->abce', inputs, reduce_w, precision=HIGH))
    reduced_act = low(jax.nn.silu(reduced))
    convolved = low_back(conv_grid(reduced_act, conv_w))
    convolved_act = low(jax.nn.silu(convolved))
    expanded = low_back(jnp.einsum('abce,ed->abcd', convolved_act, expand_w, precision=HIGH))
    return inputs + jax.nn.silu(layer_norm(expanded, norm_gain))

def abstractor(images, pre_reduce, pre_conv, pre_expand, pre_gain, post_reduce, post_conv, post_expand, post_gain, readout):
    blended = bottleneck(images, pre_reduce, pre_conv, pre_expand, pre_gain)
    slot_count, grid_rows, grid_cols, channels = blended.shape
    pooled = lax.optimization_barrier(jnp.mean(blended.reshape(slot_count, grid_rows // 2, 2, grid_cols // 2, 2, channels), axis=(2, 4)))
    pooled = low(low_back(pooled))
    refined = bottleneck(pooled, post_reduce, post_conv, post_expand, post_gain)
    logits = low_back(jnp.einsum('abcd,de->abce', low(refined), readout, precision=HIGH))
    return jax.nn.gelu(logits)

def reference(features, counts, pre_reduce, pre_conv, pre_expand, pre_gain, post_reduce, post_conv, post_expand, post_gain, readout, cotangent):
    weights = (pre_reduce.astype(jnp.float32), pre_conv.astype(jnp.float32), pre_expand.astype(jnp.float32), pre_gain.astype(jnp.float32), post_reduce.astype(jnp.float32), post_conv.astype(jnp.float32), post_expand.astype(jnp.float32), post_gain.astype(jnp.float32), readout.astype(jnp.float32))
    live = (jnp.arange(SLOT)[None, :] < counts[:, None]).astype(jnp.float32)
    inputs = (features.reshape(SAMPLES, SLOT, GRID, GRID, CH), cotangent.reshape(SAMPLES, SLOT, POOL, POOL, OUT), live)

    def step(totals, blocks):
        image_block, grad_block, alive = blocks
        images = image_block.astype(jnp.float32)
        outputs, pullback = jax.vjp(abstractor, images, *weights)
        grads = pullback(grad_block.astype(jnp.float32) * alive[:, None, None, None])
        totals = jax.tree.map(jnp.add, totals, tuple(grads[1:]))
        return (totals, (outputs.astype(jnp.bfloat16), grads[0]))
    initial = tuple((jnp.zeros(weight.shape, jnp.float32) for weight in weights))
    totals, (token_blocks, image_grads) = lax.scan(step, initial, inputs)
    tokens = token_blocks.reshape(SLOTS, POOL, POOL, OUT)
    feature_grad = image_grads.reshape(SLOTS, GRID, GRID, CH)
    return (tokens, feature_grad, totals[0], totals[1], totals[2], totals[3], totals[4], totals[5], totals[6], totals[7], totals[8])
```

```python
import jax
import jax.numpy as jnp
from jax import lax
from jax.sharding import Mesh, PartitionSpec as P

SLOT = 4
EPS = 1e-06
BF = jnp.bfloat16
F32 = jnp.float32
DP = ("x", "core")


def dot(a, b, dims):
    return lax.dot_general(a, b, (dims, ((), ())), preferred_element_type=F32)


def silu_slope(values):
    sigma = jax.nn.sigmoid(values)
    return sigma * (1.0 + values * (1.0 - sigma))


def conv(padded, kernel):
    rows, cols = padded.shape[1] - 2, padded.shape[2] - 2
    wide = kernel.astype(F32)
    total = 0.0
    for a in range(3):
        for b in range(3):
            total = total + padded[:, a : a + rows, b : b + cols, :].astype(F32) * wide[a, b]
    return total


def conv_grad(padded, grads):
    rows, cols = grads.shape[1], grads.shape[2]
    wide = grads.astype(F32)
    return jnp.stack(
        [
            jnp.stack(
                [
                    jnp.sum(padded[:, a : a + rows, b : b + cols, :].astype(F32) * wide, axis=(0, 1, 2))
                    for b in range(3)
                ]
            )
            for a in range(3)
        ]
    )


def pad_columns(values):
    return jnp.pad(values, ((0, 0), (0, 0), (1, 1), (0, 0)))


def pad_sides(values):
    return jnp.pad(values, ((0, 0), (1, 1), (1, 1), (0, 0)))


def halo(values):
    ends = lax.axis_size("rows") - 1
    above = lax.ppermute(values[:, -1:], "rows", [(i, i + 1) for i in range(ends)])
    below = lax.ppermute(values[:, :1], "rows", [(i + 1, i) for i in range(ends)])
    return above, below


def swap(blocks, axis):
    n = lax.axis_size(axis)
    me = lax.axis_index(axis)
    got = [lax.dynamic_index_in_dim(blocks, me, 0, keepdims=False)]
    for k in range(1, n):
        send = lax.dynamic_index_in_dim(blocks, (me + k) % n, 0, keepdims=False)
        got.append(lax.ppermute(send, axis, [(i, (i + k) % n) for i in range(n)]))
    stacked = jnp.stack(got)
    return [lax.dynamic_index_in_dim(stacked, (me - j) % n, 0, keepdims=False) for j in range(n)]


def cross(n, k):
    return [(a * n + b, ((b + k) % n) * n + a) for a in range(n) for b in range(n)]


def spread(n, k):
    return [(a * n + b, b * n + (a + k) % n) for a in range(n) for b in range(n)]


def scatter_sum(blocks, axis):
    got = lax.all_to_all(blocks, axis, 0, 0, tiled=False)
    return jnp.sum(got.astype(F32), axis=0).astype(BF)


def core_sum(blocks):
    me = lax.axis_index("core")
    keep = lax.dynamic_index_in_dim(blocks, me, 0, keepdims=False)
    send = lax.dynamic_index_in_dim(blocks, 1 - me, 0, keepdims=False)
    got = lax.ppermute(send, "core", [(0, 1), (1, 0)])
    return (keep.astype(F32) + got.astype(F32)).astype(BF)


def body(features, counts, pre_reduce, pre_conv, pre_expand, pre_gain, post_reduce, post_conv, post_expand, post_gain, readout, cotangent):
    n = lax.axis_size("chan")
    row = lax.axis_index("rows")
    chan = lax.axis_index("chan")
    ch = pre_reduce.shape[0]
    slots, high, wide = features.shape[0], features.shape[1], features.shape[2]
    part = slots // n
    cells = high * wide
    pool = wide // 2
    spots = pool * pool
    out_share = cotangent.shape[3]

    above, below = halo(features)
    shards = jnp.concatenate([post_reduce, post_expand.T], axis=1)
    full = lax.all_gather(shards, "chan", axis=0, tiled=True)
    post_reduce_all = full[:, :ch]
    post_expand_all = full[:, ch:]
    gain_all = lax.all_gather(post_gain, "chan", axis=0, tiled=True)
    live = (jnp.arange(SLOT)[None, :] < counts[:, None]).astype(F32).reshape(slots)
    masked = (cotangent.astype(F32) * live[:, None, None, None]).astype(BF).reshape(n, part * spots, out_share)
    cots = [
        lax.ppermute(lax.dynamic_index_in_dim(masked, (chan + k) % n, 0, keepdims=False), ("rows", "chan"), cross(n, k))
        for k in range(n)
    ]
    blocks_at = [(row - k) % n for k in range(n)]

    ext = jnp.concatenate([above, features, below], axis=1)
    reduced_ext = dot(ext.reshape(-1, ch), pre_reduce, ((1,), (0,))).reshape(slots, high + 2, wide, -1)
    reduced = reduced_ext[:, 1:-1]
    act_ext = jax.nn.silu(reduced_ext).astype(BF)
    rimmed = pad_columns(act_ext)
    convolved = conv(rimmed, pre_conv)
    convolved_act = jax.nn.silu(convolved).astype(BF)
    expanded = dot(convolved_act.reshape(-1, ch), pre_expand, ((1,), (0,)))
    mean_value = jnp.mean(expanded, -1, keepdims=True)
    mean_square = jnp.mean(expanded * expanded, -1, keepdims=True)
    pre_std = lax.rsqrt(mean_square - mean_value * mean_value + EPS)
    normal_pre = (expanded - mean_value) * pre_std
    normed = normal_pre * pre_gain
    blended = features.astype(F32).reshape(-1, ch) + jax.nn.silu(normed)
    pooled = jnp.mean(blended.reshape(slots, high // 2, 2, pool, 2, ch), axis=(2, 4)).astype(BF)

    moved = jnp.concatenate(swap(pooled.reshape(n, part, high // 2, pool, ch), "rows"), axis=1)
    flat = moved.reshape(part * spots, ch)

    post_reduced = dot(flat, post_reduce_all, ((1,), (0,)))
    post_act = jax.nn.silu(post_reduced).astype(BF)
    post_padded = pad_sides(post_act.reshape(part, pool, pool, ch))
    post_convolved = conv(post_padded, post_conv).reshape(-1, ch)
    post_convolved_act = jax.nn.silu(post_convolved).astype(BF)
    post_expanded = dot(post_convolved_act, post_expand_all, ((1,), (1,)))
    post_mean = jnp.mean(post_expanded, -1, keepdims=True)
    post_square = jnp.mean(post_expanded * post_expanded, -1, keepdims=True)
    post_std = lax.rsqrt(post_square - post_mean * post_mean + EPS)
    post_normal = (post_expanded - post_mean) * post_std
    post_normed = post_normal * gain_all
    refined = flat.astype(F32) + jax.nn.silu(post_normed)
    refined_low = refined.astype(BF)

    refined_grad = 0.0
    for k in range(n):
        rows_part = lax.dynamic_slice_in_dim(readout, blocks_at[k] * out_share, out_share, 1)
        logits = dot(refined_low, rows_part, ((1,), (0,)))
        pull = jax.vjp(jax.nn.gelu, logits)[1]
        piece = pull(cots[k].astype(F32))[0].astype(BF)
        refined_grad = refined_grad + dot(piece, rows_part, ((1,), (1,)))

    gathered = [lax.ppermute(refined_low, ("rows", "chan"), spread(n, k)) for k in range(n)]
    stacked = jnp.stack(gathered)
    order = [lax.dynamic_index_in_dim(stacked, (chan - j) % n, 0, keepdims=False) for j in range(n)]
    refined_here = jnp.concatenate(order, axis=0)
    columns = lax.dynamic_slice_in_dim(readout, chan * out_share, out_share, 1)
    logits_here = dot(refined_here, columns, ((1,), (0,)))
    token_values, pull_here = jax.vjp(jax.nn.gelu, logits_here)
    tokens = token_values.astype(BF).reshape(slots, pool, pool, out_share)
    piece_here = pull_here(masked.reshape(-1, out_share).astype(F32))[0].astype(BF)
    readout_grad = dot(refined_here, piece_here, ((0,), (0,)))

    post_normed_grad = refined_grad * silu_slope(post_normed)
    post_gain_grad = jnp.sum(post_normed_grad * post_normal, axis=0)
    post_scaled = post_normed_grad * gain_all
    post_expanded_grad = (
        post_std
        * (
            post_scaled
            - jnp.mean(post_scaled, -1, keepdims=True)
            - post_normal * jnp.mean(post_scaled * post_normal, -1, keepdims=True)
        )
    ).astype(BF)
    post_expand_grad_t = dot(post_expanded_grad, post_convolved_act, ((0,), (0,)))
    post_act_grad = dot(post_expanded_grad, post_expand_all, ((1,), (0,)))
    post_convolved_grad = (post_act_grad * silu_slope(post_convolved)).astype(BF).reshape(part, pool, pool, ch)
    post_conv_grad = conv_grad(post_padded, post_convolved_grad)
    post_reduced_act_grad = conv(pad_sides(post_convolved_grad), post_conv[::-1, ::-1]).reshape(-1, ch)
    post_reduced_grad = (post_reduced_act_grad * silu_slope(post_reduced)).astype(BF)
    post_reduce_grad = dot(flat, post_reduced_grad, ((0,), (0,)))
    pooled_grad = (refined_grad + dot(post_reduced_grad, post_reduce_all, ((1,), (1,)))).astype(BF)

    back = pooled_grad.reshape(part, n, high // 2, pool, ch).transpose(1, 0, 2, 3, 4)
    returned = jnp.concatenate(swap(back, "rows"), axis=0)

    share = ch // n
    eight = share // 32
    extra = jnp.zeros((n, share, 128), F32)
    extra = extra.at[:, : share // 128].set(post_gain_grad.reshape(n, share // 128, 128))
    taps = post_conv_grad.reshape(-1, 128)
    extra = extra.at[:, share // 128 : share // 128 + taps.shape[0]].set(taps[None])
    load = jnp.concatenate(
        [
            post_reduce_grad.reshape(n, share, ch),
            post_expand_grad_t.reshape(n, share, ch),
            readout_grad.reshape(n, share, out_share),
            extra,
        ],
        axis=2,
    ).astype(BF)
    load = load.reshape(n, 2, 4, 4, eight, -1).transpose(1, 2, 3, 0, 4, 5)
    load = scatter_sum(scatter_sum(core_sum(load), "x"), "rows")
    load = lax.all_to_all(load, "chan", 0, 0, tiled=False)
    summed = jnp.sum(load.astype(F32), axis=0).astype(BF)
    mine = jnp.concatenate([summed[:, : 2 * ch], summed[:, 2 * ch + out_share :]] + [load[j, :, 2 * ch : 2 * ch + out_share] for j in range(n)], axis=1)
    post_all = lax.all_gather(mine, ("core", "x", "rows"), axis=0, tiled=True).astype(F32)
    post_reduce_out = post_all[:, :ch]
    post_expand_out = post_all[:, ch : 2 * ch].T
    extra_out = post_all[:, 2 * ch : 2 * ch + 128]
    post_gain_out = extra_out[: share // 128].reshape(share)
    post_conv_out = extra_out[share // 128 : share // 128 + taps.shape[0]].reshape(3, 3, ch)
    readout_out = post_all[:, 2 * ch + 128 :]

    blended_grad = jnp.repeat(jnp.repeat(returned.astype(F32) * 0.25, 2, axis=1), 2, axis=2).reshape(-1, ch)
    normed_grad = blended_grad * silu_slope(normed)
    pre_gain_grad = jnp.sum(normed_grad * normal_pre, axis=0)
    pre_scaled = normed_grad * pre_gain
    expanded_grad = (
        pre_std
        * (
            pre_scaled
            - jnp.mean(pre_scaled, -1, keepdims=True)
            - normal_pre * jnp.mean(pre_scaled * normal_pre, -1, keepdims=True)
        )
    ).astype(BF)
    convolved_act_grad = dot(expanded_grad, pre_expand, ((1,), (1,)))
    convolved_grad = (convolved_act_grad.reshape(convolved.shape) * silu_slope(convolved)).astype(BF)
    grad_above, grad_below = halo(convolved_grad)
    pre_expand_grad = dot(convolved_act.reshape(-1, ch), expanded_grad, ((0,), (0,)))
    pre_conv_grad = conv_grad(rimmed, convolved_grad)
    grad_padded = pad_columns(jnp.concatenate([grad_above, convolved_grad, grad_below], axis=1))
    reduced_act_grad = conv(grad_padded, pre_conv[::-1, ::-1])
    reduced_grad = (reduced_act_grad * silu_slope(reduced)).astype(BF).reshape(-1, ch)
    pre_reduce_grad = dot(features.reshape(-1, ch), reduced_grad, ((0,), (0,)))
    feature_grad = (blended_grad + dot(reduced_grad, pre_reduce, ((1,), (1,)))).reshape(features.shape)

    tail = jnp.concatenate([pre_conv_grad.reshape(-1, 128), pre_gain_grad.reshape(-1, 128)], axis=0)
    tail = jnp.pad(tail, ((0, ch - tail.shape[0]), (0, 0)))
    load = jnp.concatenate([pre_reduce_grad, pre_expand_grad, tail], axis=1).astype(BF).reshape(2, 4, 4, 4, ch // 128, -1)
    load = scatter_sum(scatter_sum(scatter_sum(core_sum(load), "x"), "rows"), "chan")
    pre_all = lax.all_gather(load, ("core", "x", "rows", "chan"), axis=0, tiled=True).astype(F32)
    taps = 9 * ch // 128
    return (
        tokens,
        feature_grad,
        pre_all[:, :ch],
        pre_all[:taps, 2 * ch :].reshape(3, 3, ch),
        pre_all[:, ch : 2 * ch],
        pre_all[taps : taps + ch // 128, 2 * ch :].reshape(ch),
        post_reduce_out,
        post_conv_out,
        post_expand_out,
        post_gain_out,
        readout_out,
    )


def solution(mesh):
    grid = Mesh(mesh.devices.reshape(4, 2, 4, 4), ("x", "core", "rows", "chan"))
    images = P(("x", "core", "chan"), "rows", None, None)
    grids = P(("x", "core", "rows"), None, None, "chan")
    return jax.shard_map(
        body,
        mesh=grid,
        in_specs=(
            images,
            P(("x", "core", "rows")),
            P(),
            P(),
            P(),
            P(),
            P("chan", None),
            P(),
            P(None, "chan"),
            P("chan"),
            P(),
            grids,
        ),
        out_specs=(grids, images, P(), P(), P(), P(), P("chan", None), P(), P(None, "chan"), P("chan"), P("chan", None)),
        check_vma=False,
    )
```

```python
import functools

import jax
import jax.numpy as jnp
import numpy as np
from jax import lax
from jax.experimental import pallas as pl
from jax.experimental.pallas import tpu as pltpu
from jax.sharding import Mesh, PartitionSpec as P

SLOT = 4
EPS = 1e-06
BF = jnp.bfloat16
F32 = jnp.float32
LANES = 128
VMEM_LIMIT = 56 * 1024 * 1024
NN = ((1,), (0,))
NT = ((1,), (1,))
TN = ((0,), (0,))


def dot(a, b, dims=NN):
    return lax.dot_general(a, b, (dims, ((), ())), preferred_element_type=F32)


def sigmoid(v):
    return 0.5 * jnp.tanh(0.5 * v) + 0.5


def silu(v):
    return v * sigmoid(v)


def silu_slope(v):
    s = sigmoid(v)
    return s * (1.0 + v * (1.0 - s))


def gelu_parts(v):
    c = 0.7978845608028654
    square = v * v
    t = jnp.tanh(v * (c + (c * 0.044715) * square))
    half = 0.5 * (1.0 + t)
    slope = half + 0.5 * v * (1.0 - t * t) * (c + (3.0 * c * 0.044715) * square)
    return v * half, slope


def chunks(count, body, width=LANES):
    def step(i, carry):
        body(pl.ds(pl.multiple_of(i * width, width), width))
        return carry

    lax.fori_loop(0, count, step, 0)


def call(kernel, *, grid, ins, outs, scratch=(), prefetch=0, flops=0, name):
    def spec(shape, block, index):
        if block is None:
            block, index = shape, lambda *_: (0,) * len(shape)
        return pl.BlockSpec(block, index)

    arrays = [i[0] for i in ins]
    in_specs = [spec(a.shape, b, m) for a, b, m in ins]
    out_specs = [spec(s.shape, b, m) for s, b, m in outs]
    moved = sum(a.size * a.dtype.itemsize for a in arrays) + sum(s[0].size * s[0].dtype.itemsize for s in outs)

    def run(*scalars):
        return pl.pallas_call(
            kernel,
            grid_spec=pltpu.PrefetchScalarGridSpec(
                num_scalar_prefetch=prefetch,
                grid=grid,
                in_specs=in_specs,
                out_specs=out_specs,
                scratch_shapes=list(scratch),
            ),
            out_shape=[s[0] for s in outs],
            compiler_params=pltpu.CompilerParams(
                dimension_semantics=("arbitrary",) * len(grid), vmem_limit_bytes=VMEM_LIMIT
            ),
            cost_estimate=pl.CostEstimate(flops=flops, bytes_accessed=int(moved), transcendentals=0),
            name=name,
        )(*scalars, *arrays)

    return run


def shape(dims, dtype):
    return jax.ShapeDtypeStruct(dims, dtype)


def columns_moved(t, by, first, last):
    rows = t.shape[0]
    return pltpu.roll(t, by % rows, 0) * (first if by > 0 else last)


def edge_masks(rows, width, depth):
    at = lax.broadcasted_iota(jnp.int32, (rows, LANES), 0) % (width * depth)
    return (at >= depth).astype(F32), (at < (width - 1) * depth).astype(F32)


def pre_forward(order, reduced, above, below, features, pre_reduce, taps, pre_expand, gain, pool):
    slots, cells, ch = reduced.shape
    high, wide = features.shape[1], features.shape[2]
    n = order.shape[0]
    part = slots // n

    def kernel(order_ref, red, up_ref, down_ref, feat, wr, tap, we, gn, pool_ref, conv_out, act_out, norm_out, std_out, pooled_out, halo, exp, sums):
        k = pl.program_id(0)

        @pl.when(k == 0)
        def _():
            for side, ref in enumerate((up_ref, down_ref)):
                halo[side] = dot(ref[...].reshape(slots * wide, ch), wr[...]).reshape(slots, wide, ch)

        first, last = edge_masks(wide, wide, 1)
        at = order_ref[k] * part
        for u in range(part):

            def conv(lanes):
                w = [tap[pl.ds(i, 1), lanes] for i in range(9)]
                rows = [halo[0, at + u, :, lanes]]
                rows += [red[u, pl.ds(i * wide, wide), lanes] for i in range(high)]
                rows += [halo[1, at + u, :, lanes]]
                rows = [silu(r).astype(BF).astype(F32) for r in rows]
                acts = []
                for i in range(high):
                    t = [sum(rows[i + a] * w[3 * a + b] for a in range(3)) for b in range(3)]
                    c = t[1] + columns_moved(t[0], 1, first, last) + columns_moved(t[2], -1, first, last)
                    conv_out[u, pl.ds(i * wide, wide), lanes] = c
                    acts.append(silu(c))
                act_out[u, :, lanes] = jnp.concatenate(acts, 0).astype(BF)

            chunks(ch // LANES, conv)

        exp[...] = dot(act_out[...].reshape(part * cells, ch), we[...])

        def norm(p, carry):
            u, i = p // (high // 2), p % (high // 2)
            total = [0.0] * (wide // 8)
            for half in range(2):
                f = feat[u, 2 * i + half].astype(F32)
                for t in range(wide // 8):
                    row = (2 * i + half) * wide + 8 * t
                    e = exp[pl.ds(pl.multiple_of(u * cells + row, 8), 8), :]
                    mean = jnp.mean(e, -1, keepdims=True)
                    square = jnp.mean(e * e, -1, keepdims=True)
                    std = lax.rsqrt(square - mean * mean + EPS)
                    nrm = (e - mean) * std
                    norm_out[u, pl.ds(pl.multiple_of(row, 8), 8), :] = nrm
                    std_out[u, pl.ds(pl.multiple_of(row, 8), 8), :] = std
                    total[t] = total[t] + f[8 * t : 8 * t + 8] + silu(nrm * gn[...])
            for t in range(wide // 8):
                sums[pl.ds(pl.multiple_of(p * wide + 8 * t, 8), 8), :] = total[t]
            return carry

        lax.fori_loop(0, part * high // 2, norm, 0)
        s = sums[...]
        hi = s.astype(BF)
        lo = (s - hi.astype(F32)).astype(BF)
        pooled_out[0] = (dot(pool_ref[...], hi) + dot(pool_ref[...], lo)).astype(BF)

    def by_order(rest):
        return lambda k, order: (order[k],) + (0,) * rest

    pooled_rows = pool.shape[0]
    return call(
        kernel,
        grid=(n,),
        prefetch=1,
        ins=[
            (reduced, (part, cells, ch), by_order(2)),
            (above, None, None),
            (below, None, None),
            (features, (part, high, wide, ch), by_order(3)),
            (pre_reduce, None, None),
            (taps, None, None),
            (pre_expand, None, None),
            (gain, None, None),
            (pool, None, None),
        ],
        outs=[
            (shape((slots, cells, ch), F32), (part, cells, ch), by_order(2)),
            (shape((slots, cells, ch), BF), (part, cells, ch), by_order(2)),
            (shape((slots, cells, ch), F32), (part, cells, ch), by_order(2)),
            (shape((slots, cells, 1), F32), (part, cells, 1), by_order(2)),
            (shape((n, pooled_rows, ch), BF), (1, pooled_rows, ch), lambda k, order: (k, 0, 0)),
        ],
        scratch=[
            pltpu.VMEM((2, slots, wide, ch), F32),
            pltpu.VMEM((part * cells, ch), F32),
            pltpu.VMEM((part * cells // 2, ch), F32),
        ],
        flops=2 * slots * cells * ch * ch,
        name="pre_forward",
    )(order)


def post_forward(source, moved, weights, gain, taps, pool):
    n, rows, ch = moved.shape
    total = n * rows
    depth = total // (pool * pool)
    share = ch // n

    def kernel(src, got, w, gn, tap, flat_out, red_out, act_out, conv_out, cact_out, norm_out, std_out, low_out, wide_ref):
        for r in range(n):
            wide_ref[pl.ds(r * rows, rows), :] = got[src[r]].astype(F32)
        flat_out[...] = wide_ref[...].astype(BF)
        red = 0.0
        for c in range(n):
            red = red + dot(flat_out[:, c * share : (c + 1) * share], w[c, 0])
        red_out[...] = red
        first, last = edge_masks(total, pool, depth)
        step = pool * depth

        def conv(lanes):
            x = silu(red_out[:, lanes]).astype(BF)
            act_out[:, lanes] = x
            x = x.astype(F32)
            moves = [columns_moved(x, depth, first, last), x, columns_moved(x, -depth, first, last)]
            t = [sum(moves[b] * tap[pl.ds(3 * a + b, 1), lanes] for b in range(3)) for a in range(3)]
            none = jnp.zeros((step, LANES), F32)
            c = t[1] + jnp.concatenate([none, t[0][:-step]], 0) + jnp.concatenate([t[2][step:], none], 0)
            conv_out[:, lanes] = c
            cact_out[:, lanes] = silu(c).astype(BF)

        chunks(ch // LANES, conv)
        for c in range(n):
            wide2 = dot(cact_out[...], w[c, 1], NT)
            norm_out[:, c * share : (c + 1) * share] = wide2

        def norm(i, carry):
            at = pl.ds(pl.multiple_of(i * 16, 16), 16)
            e = norm_out[at, :]
            mean = jnp.mean(e, -1, keepdims=True)
            square = jnp.mean(e * e, -1, keepdims=True)
            std = lax.rsqrt(square - mean * mean + EPS)
            nrm = (e - mean) * std
            norm_out[at, :] = nrm
            std_out[at, :] = std
            low_out[at, :] = (wide_ref[at, :] + silu(nrm * gn[...])).astype(BF)
            return carry

        lax.fori_loop(0, total // 16, norm, 0)

    wide = shape((total, ch), F32)
    narrow = shape((total, ch), BF)
    return call(
        kernel,
        grid=(1,),
        prefetch=1,
        ins=[(a, None, None) for a in (moved, weights, gain, taps)],
        outs=[(s, None, None) for s in (narrow, wide, narrow, wide, narrow, wide, shape((total, 1), F32), narrow)],
        scratch=[pltpu.VMEM((total, ch), F32)],
        flops=4 * total * ch * ch,
        name="post_forward",
    )(source)


def post_backward(source, low, readout, cots, weights, gain, taps, act, red, conv, nrm, std, pool):
    total, ch = low.shape
    n = cots.shape[0]
    share = ch // n
    out_share = cots.shape[2]
    rows = total // n
    depth = total // (pool * pool)

    def kernel(src, low_ref, ro, cot, w, gn, tap, act_ref, red_ref, conv_ref, norm_ref, std_ref, exp_out, redg_out, back_out, taps_out, gain_out, grad, cgrad):
        k = pl.program_id(0)
        logits = dot(low_ref[...], ro[...])
        piece = (cot[0].astype(F32) * gelu_parts(logits)[1]).astype(BF)
        term = dot(piece, ro[...], NT)

        @pl.when(k == 0)
        def _():
            grad[...] = term

        @pl.when(k > 0)
        def _():
            grad[...] += term

        @pl.when(k == n - 1)
        def _():
            def norm(i, total_gain):
                at = pl.ds(pl.multiple_of(i * 16, 16), 16)
                nm = norm_ref[at, :]
                ng = grad[at, :] * silu_slope(nm * gn[...])
                sc = ng * gn[...]
                one = jnp.mean(sc, -1, keepdims=True)
                two = jnp.mean(sc * nm, -1, keepdims=True)
                exp_out[at, :] = (std_ref[at, :] * (sc - one - nm * two)).astype(BF)
                g = ng * nm
                return total_gain + g[:8] + g[8:]

            gain_out[...] = lax.fori_loop(0, total // 16, norm, jnp.zeros((8, ch), F32))
            cg = 0.0
            for c in range(n):
                cg = cg + dot(exp_out[:, c * share : (c + 1) * share], w[c, 1])
            cgrad[...] = cg
            first, last = edge_masks(total, pool, depth)
            step = pool * depth

            def back(lanes):
                g = (cgrad[:, lanes] * silu_slope(conv_ref[:, lanes])).astype(BF).astype(F32)
                x = act_ref[:, lanes].astype(F32)
                moves = [columns_moved(g, -depth, first, last), g, columns_moved(g, depth, first, last)]
                none = jnp.zeros((step, LANES), F32)
                xs = [
                    jnp.concatenate([none, x[:-step]], 0),
                    x,
                    jnp.concatenate([x[step:], none], 0),
                ]
                for a in range(3):
                    for b in range(3):
                        prod = xs[a] * moves[b]
                        taps_out[3 * a + b, :, lanes] = jnp.sum(prod.reshape(total // 8, 8, LANES), 0)
                t = [sum(moves[b] * tap[pl.ds(3 * a + b, 1), lanes] for b in range(3)) for a in range(3)]
                d = t[1] + jnp.concatenate([t[0][step:], none], 0) + jnp.concatenate([none, t[2][:-step]], 0)
                redg_out[:, lanes] = (d * silu_slope(red_ref[:, lanes])).astype(BF)

            chunks(ch // LANES, back)
            for c in range(n):
                cut = slice(c * share, (c + 1) * share)
                grad[:, cut] += dot(redg_out[...], w[c, 0], NT)
            for r in range(n):
                at = pl.ds(pl.multiple_of(src[r] * rows, 8), rows)
                back_out[r] = grad[at, :].astype(BF)

    return call(
        kernel,
        grid=(n,),
        prefetch=1,
        ins=[
            (low, None, None),
            (readout, (ch, out_share), lambda k, s: (0, k)),
            (cots, (1, total, out_share), lambda k, s: (k, 0, 0)),
        ]
        + [(a, None, None) for a in (weights, gain, taps, act, red, conv, nrm, std)],
        outs=[
            (s, None, None)
            for s in (
                shape((total, ch), BF),
                shape((total, ch), BF),
                shape((n, rows, ch), BF),
                shape((9, 8, ch), F32),
                shape((8, ch), F32),
            )
        ],
        scratch=[pltpu.VMEM((total, ch), F32), pltpu.VMEM((total, ch), F32)],
        flops=2 * total * ch * (2 * out_share * n + 2 * ch),
        name="post_backward",
    )(source)


def cotangent_by_image(cotangent, select):
    rows, width = cotangent.shape
    size = select.shape[0]
    pairs = SLOT
    each = size // pairs
    per = 3

    def kernel(x, sel, out):
        for q in range(per):
            y = dot(sel[...], x[pl.ds(q * size, size), :]).astype(BF)
            for s in range(pairs):
                out[s, pl.ds(q * each, each), :] = y[s * each : (s + 1) * each]

    return call(
        kernel,
        grid=(rows // (per * size),),
        ins=[(cotangent, (per * size, width), lambda i: (i, 0)), (select, None, None)],
        outs=[(shape((pairs, rows // pairs, width), BF), (pairs, per * each, width), lambda i: (0, i, 0))],
        flops=2 * rows * size * width,
        name="cotangent_by_image",
    )()[0]


def token_block(chan, low, place, readout, cotangent, live):
    pairs, each_all, ch = low.shape
    rows, width = cotangent.shape
    size = place.shape[0]
    each = size // pairs
    per = 3

    def kernel(chan_ref, low_ref, place_ref, ro, cot, alive, tok_out, piece_out, low_out):
        for q in range(per):
            at = pl.ds(q * size, size)
            x = jnp.concatenate([low_ref[s, pl.ds(q * each, each), :] for s in range(pairs)], 0)
            low_out[at, :] = dot(place_ref[...], x).astype(BF)
        logits = dot(low_out[...], ro[...])
        value, slope = gelu_parts(logits)
        tok_out[...] = value.astype(BF)
        piece_out[...] = (cot[...].astype(F32) * alive[...] * slope).astype(BF)

    block = per * size
    row_block = lambda i, c: (i, 0)
    return call(
        kernel,
        grid=(rows // block,),
        prefetch=1,
        ins=[
            (low, (pairs, per * each, ch), lambda i, c: (0, i, 0)),
            (place, None, None),
            (readout, (ch, width), lambda i, c: (0, c[0])),
            (cotangent, (block, width), row_block),
            (live, None, None),
        ],
        outs=[
            (shape((rows, width), BF), (block, width), row_block),
            (shape((rows, width), BF), (block, width), row_block),
            (shape((rows, ch), BF), (block, ch), row_block),
        ],
        flops=2 * rows * ch * width,
        name="token_block",
    )(chan)


def pre_backward(order, returned, spread_up, nrm, std, gain, conv, pre_expand):
    slots, cells, ch = nrm.shape
    n = order.shape[0]
    part = slots // n
    wide = 24
    rows = part * cells

    def kernel(order_ref, ret, up, norm_ref, std_ref, gn, conv_ref, we, exp_out, conv_grad_out, top_out, bottom_out, gain_out, grad, cgrad):
        k = pl.program_id(0)
        grad[...] = dot(up[...], ret[0])

        def norm(i, total_gain):
            u, j = i // (cells // 16), i % (cells // 16)
            at = pl.ds(pl.multiple_of(j * 16, 16), 16)
            nm = norm_ref[u, at, :]
            ng = grad[pl.ds(pl.multiple_of(i * 16, 16), 16), :] * silu_slope(nm * gn[...])
            sc = ng * gn[...]
            one = jnp.mean(sc, -1, keepdims=True)
            two = jnp.mean(sc * nm, -1, keepdims=True)
            exp_out[u, at, :] = (std_ref[u, at, :] * (sc - one - nm * two)).astype(BF)
            g = ng * nm
            return total_gain + g[:8] + g[8:]

        gains = lax.fori_loop(0, rows // 16, norm, jnp.zeros((8, ch), F32))

        @pl.when(k == 0)
        def _():
            gain_out[...] = gains

        @pl.when(k > 0)
        def _():
            gain_out[...] += gains

        cgrad[...] = dot(exp_out[...].reshape(rows, ch), we[...], NT)
        for u in range(part):

            def slope(lanes):
                g = cgrad[pl.ds(u * cells, cells), lanes] * silu_slope(conv_ref[u, :, lanes])
                conv_grad_out[u, :, lanes] = g.astype(BF)
                top_out[u, :, lanes] = g[:wide].astype(BF)
                bottom_out[u, :, lanes] = g[cells - wide :].astype(BF)

            chunks(ch // LANES, slope)

    by_order = lambda k, order: (order[k], 0, 0)
    whole = (part, cells, ch)
    edge = (part, wide, ch)
    return call(
        kernel,
        grid=(n,),
        prefetch=1,
        ins=[
            (returned, (1,) + returned.shape[1:], lambda k, order: (k, 0, 0)),
            (spread_up, None, None),
            (nrm, whole, by_order),
            (std, (part, cells, 1), by_order),
            (gain, None, None),
            (conv, whole, by_order),
            (pre_expand, None, None),
        ],
        outs=[
            (shape((slots, cells, ch), BF), whole, by_order),
            (shape((slots, cells, ch), BF), whole, by_order),
            (shape((slots, wide, ch), BF), edge, by_order),
            (shape((slots, wide, ch), BF), edge, by_order),
            (shape((8, ch), F32), None, None),
        ],
        scratch=[pltpu.VMEM((rows, ch), F32), pltpu.VMEM((rows, ch), F32)],
        flops=2 * slots * cells * ch * ch,
        name="pre_backward",
    )(order)


def pre_conv_backward(conv_grad, above, below, reduced, taps):
    slots, cells, ch = reduced.shape
    wide = above.shape[1]
    high = cells // wide

    def kernel(cg, up, down, red, tap, redg_out, taps_out):
        step = pl.program_id(0)
        first, last = edge_masks(wide, wide, 1)

        @pl.when(step == 0)
        def _():
            taps_out[...] = jnp.zeros_like(taps_out)

        def back(lanes):
            w = [tap[pl.ds(i, 1), lanes] for i in range(9)]
            mid = cg[0, :, lanes].astype(F32)
            rows = [up[0, :, lanes].astype(F32)]
            rows += [mid[i * wide : (i + 1) * wide] for i in range(high)]
            rows += [down[0, :, lanes].astype(F32)]
            v = [red[0, pl.ds(i * wide, wide), lanes] for i in range(high)]
            s = [sigmoid(t) for t in v]
            x = [(a * b).astype(BF).astype(F32) for a, b in zip(v, s)]
            d = [0.0] * high
            sums = [0.0] * 9
            for p in range(high + 2):
                g = rows[p]
                moves = [columns_moved(g, -1, first, last), g, columns_moved(g, 1, first, last)]
                for a in range(3):
                    i = p - 1 + a - 1
                    if 0 <= i < high:
                        for b in range(3):
                            d[i] = d[i] + moves[b] * w[3 * a + b]
                            prod = x[i] * moves[b]
                            sums[3 * a + b] = sums[3 * a + b] + (prod[:8] + prod[8:16] + prod[16:])
            out = [d[i] * (s[i] * (1.0 + v[i] * (1.0 - s[i]))) for i in range(high)]
            redg_out[0, :, lanes] = jnp.concatenate(out, 0).astype(BF)
            for i in range(9):
                taps_out[i, :, lanes] += sums[i]

        chunks(ch // LANES, back)

    image = lambda i: (i, 0, 0)
    return call(
        kernel,
        grid=(slots,),
        ins=[
            (conv_grad, (1, cells, ch), image),
            (above, (1, wide, ch), image),
            (below, (1, wide, ch), image),
            (reduced, (1, cells, ch), image),
            (taps, None, None),
        ],
        outs=[
            (shape((slots, cells, ch), BF), (1, cells, ch), image),
            (shape((9, 8, ch), F32), None, None),
        ],
        flops=0,
        name="pre_conv_backward",
    )()


def feature_backward(order, reduced_grad, pre_reduce, returned, spread_up):
    slots, cells, ch = reduced_grad.shape
    n = order.shape[0]
    part = slots // n

    def kernel(order_ref, rg, wr, ret, up, out):
        g = dot(rg[...].reshape(part * cells, ch), wr[...], NT) + dot(up[...], ret[0])
        out[...] = g.reshape(part, cells, ch)

    by_order = lambda k, order: (order[k], 0, 0)
    whole = (part, cells, ch)
    return call(
        kernel,
        grid=(n,),
        prefetch=1,
        ins=[
            (reduced_grad, whole, by_order),
            (pre_reduce, None, None),
            (returned, (1,) + returned.shape[1:], lambda k, order: (k, 0, 0)),
            (spread_up, None, None),
        ],
        outs=[(shape((slots, cells, ch), F32), whole, by_order)],
        flops=2 * slots * cells * ch * ch,
        name="feature_backward",
    )(order)[0]


def spread(n, k):
    return [(a * n + b, b * n + (a + k) % n) for a in range(n) for b in range(n)]


def scatter_sum(blocks, axis):
    got = lax.all_to_all(blocks, axis, 0, 0, tiled=False)
    return jnp.sum(got.astype(F32), axis=0).astype(BF)


def core_sum(blocks):
    me = lax.axis_index("core")
    keep = lax.dynamic_index_in_dim(blocks, me, 0, keepdims=False)
    send = lax.dynamic_index_in_dim(blocks, 1 - me, 0, keepdims=False)
    got = lax.ppermute(send, "core", [(0, 1), (1, 0)])
    return (keep.astype(F32) + got.astype(F32)).astype(BF)


def pool_matrix(part, high, wide):
    half = wide // 2
    m = np.zeros((high // 2 * half * part, part * (high // 2) * wide), np.float32)
    for u in range(part):
        for i in range(high // 2):
            for j in range(wide):
                m[(i * half + j // 2) * part + u, (u * (high // 2) + i) * wide + j] = 0.25
    return m


def spread_matrix(part, high, wide):
    half = wide // 2
    m = np.zeros((part * high * wide, high // 2 * half * part), np.float32)
    for u in range(part):
        for i in range(high):
            for j in range(wide):
                m[(u * high + i) * wide + j, ((i // 2) * half + j // 2) * part + u] = 0.25
    return m


def place_matrix(cells, slots, pairs):
    per = slots // pairs
    m = np.zeros((cells * slots, cells * slots), np.float32)
    for c in range(cells):
        for s in range(slots):
            m[c * slots + s, (s // per) * cells * per + c * per + s % per] = 1.0
    return m


def body(features, counts, pre_reduce, pre_conv, pre_expand, pre_gain, post_reduce, post_conv, post_expand, post_gain, readout, cotangent):
    n = lax.axis_size("chan")
    row = lax.axis_index("rows").astype(jnp.int32)
    chan = lax.axis_index("chan").astype(jnp.int32)
    ch = pre_reduce.shape[0]
    slots, high, wide = features.shape[0], features.shape[1], features.shape[2]
    part = slots // n
    cells = high * wide
    pool = wide // 2
    share = ch // n
    out_share = cotangent.shape[3]
    steps = jnp.arange(n, dtype=jnp.int32)
    order = (row + steps) % n
    source = (chan - steps) % n
    rank = jnp.full((1,), chan, jnp.int32)
    pre_taps = pre_conv.astype(F32).reshape(9, ch)
    post_taps = post_conv.astype(F32).reshape(9, ch)
    pre_gain_row = pre_gain.reshape(1, ch)
    pool_m = jnp.asarray(pool_matrix(part, high, wide), BF)
    up_m = jnp.asarray(spread_matrix(part, high, wide), BF)
    place = jnp.asarray(place_matrix(16, slots, n), BF)

    ends = n - 1
    down_pairs = [(i, i + 1) for i in range(ends)]
    up_pairs = [(i + 1, i) for i in range(ends)]
    above = lax.ppermute(features[:, -1], "rows", down_pairs)
    below = lax.ppermute(features[:, 0], "rows", up_pairs)
    gain_hi = post_gain.astype(BF)
    gain_lo = (post_gain - gain_hi.astype(F32)).astype(BF)
    extra = jnp.zeros((16, ch), BF).at[0, :share].set(gain_hi).at[0, share : 2 * share].set(gain_lo)
    shards = jnp.concatenate([post_reduce, post_expand.T, extra], axis=0)
    full = lax.all_gather(shards, "chan", axis=0, tiled=False)
    weights = full[:, : 2 * share].reshape(n, 2, share, ch)
    gain_parts = full[:, 2 * share].astype(F32)
    post_gain_row = (gain_parts[:, :share] + gain_parts[:, share : 2 * share]).reshape(1, ch)
    live = (jnp.arange(SLOT)[None, :] < counts[:, None]).astype(F32).reshape(slots)
    select = place.T * jnp.tile(live.astype(BF), 16)[None, :]
    cot_rows = cotangent.transpose(1, 2, 0, 3).reshape(-1, out_share)
    cots = lax.all_to_all(cotangent_by_image(cot_rows, select), "chan", 0, 0, tiled=False)

    flat_features = features.reshape(slots * cells, ch)
    reduced = dot(flat_features, pre_reduce).reshape(slots, cells, ch)
    convolved, convolved_act, normal_pre, pre_std, pooled = pre_forward(
        order, reduced, above, below, features, pre_reduce, pre_taps, pre_expand, pre_gain_row, pool_m
    )

    moved = jnp.stack([lax.ppermute(pooled[k], ("rows", "chan"), spread(n, k)) for k in range(n)])
    flat, post_reduced, post_act, post_convolved, post_cact, post_normal, post_std, low = post_forward(
        source, moved, weights, post_gain_row, post_taps, pool
    )
    low_all = lax.all_gather(low, "chan", axis=0, tiled=False)
    post_expanded_grad, post_reduced_grad, back, post_taps_grad, post_gain_grad = post_backward(
        source, low, readout, cots, weights, post_gain_row, post_taps, post_act, post_reduced, post_convolved, post_normal, post_std, pool
    )

    returned = jnp.stack(
        [lax.ppermute(back[k], ("rows", "chan"), [(d, s) for s, d in spread(n, k)]) for k in range(n)]
    )
    post_reduce_grad = dot(flat, post_reduced_grad, TN).astype(BF)
    post_expand_grad_t = dot(post_expanded_grad, post_cact, TN).astype(BF)

    expanded_grad, convolved_grad, top, bottom, pre_gain_grad = pre_backward(
        order, returned, up_m, normal_pre, pre_std, pre_gain_row, convolved, pre_expand
    )
    grad_above = lax.ppermute(bottom, "rows", down_pairs)
    grad_below = lax.ppermute(top, "rows", up_pairs)
    pre_expand_grad = dot(convolved_act.reshape(-1, ch), expanded_grad.reshape(-1, ch), TN).astype(BF)
    reduced_grad, pre_taps_grad = pre_conv_backward(convolved_grad, grad_above, grad_below, reduced, pre_taps)
    pre_reduce_grad = dot(flat_features, reduced_grad.reshape(-1, ch), TN).astype(BF)
    feature_grad = feature_backward(order, reduced_grad, pre_reduce, returned, up_m).reshape(features.shape)

    alive = jnp.broadcast_to(jnp.tile(live, 48)[:, None], (48 * slots, 1))
    tokens, piece, low_here = token_block(rank, low_all, place, readout, cot_rows, alive)
    readout_grad = dot(low_here, piece, TN).astype(BF)
    tokens = tokens.reshape(pool, pool, slots, out_share).transpose(2, 0, 1, 3)

    eight = share // 32
    tail = jnp.zeros((n, share, LANES), F32)
    tail = tail.at[:, : share // LANES].set(jnp.sum(post_gain_grad, 0).reshape(n, share // LANES, LANES))
    taps_rows = jnp.sum(post_taps_grad, 1).reshape(-1, LANES)
    tail = tail.at[:, share // LANES : share // LANES + taps_rows.shape[0]].set(taps_rows[None])
    load = jnp.concatenate(
        [
            post_reduce_grad.reshape(n, share, ch),
            post_expand_grad_t.reshape(n, share, ch),
            tail.astype(BF),
            readout_grad.reshape(n, share, out_share),
        ],
        axis=2,
    )
    load = load.reshape(n, 2, 4, 4, eight, -1).transpose(1, 2, 3, 0, 4, 5)
    load = scatter_sum(scatter_sum(core_sum(load), "x"), "rows")
    load = lax.all_to_all(load, "chan", 0, 0, tiled=False)
    cut = 2 * ch + LANES
    summed = jnp.sum(load[:, :, :cut].astype(F32), axis=0).astype(BF)
    mine = jnp.concatenate([summed] + [load[j, :, cut:] for j in range(n)], axis=1)
    post_all = lax.all_gather(mine, ("core", "x", "rows"), axis=0, tiled=True).astype(F32)
    post_reduce_out = post_all[:, :ch]
    post_expand_out = post_all[:, ch : 2 * ch].T
    tail_out = post_all[:, 2 * ch : cut]
    post_gain_out = tail_out[: share // LANES].reshape(share)
    post_conv_out = tail_out[share // LANES : share // LANES + taps_rows.shape[0]].reshape(3, 3, ch)
    readout_out = post_all[:, cut:]

    tail = jnp.concatenate([jnp.sum(pre_taps_grad, 1).reshape(-1, LANES), jnp.sum(pre_gain_grad, 0).reshape(-1, LANES)], axis=0)
    tail = jnp.pad(tail, ((0, ch - tail.shape[0]), (0, 0))).astype(BF)
    load = jnp.concatenate([pre_reduce_grad, pre_expand_grad, tail], axis=1).reshape(2, 4, 4, 4, ch // 128, -1)
    load = scatter_sum(scatter_sum(scatter_sum(core_sum(load), "x"), "rows"), "chan")
    pre_all = lax.all_gather(load, ("core", "x", "rows", "chan"), axis=0, tiled=True).astype(F32)
    taps = 9 * ch // LANES
    return (
        tokens,
        feature_grad,
        pre_all[:, :ch],
        pre_all[:taps, 2 * ch :].reshape(3, 3, ch),
        pre_all[:, ch : 2 * ch],
        pre_all[taps : taps + ch // LANES, 2 * ch :].reshape(ch),
        post_reduce_out,
        post_conv_out,
        post_expand_out,
        post_gain_out,
        readout_out,
    )


def solution(mesh):
    grid = Mesh(mesh.devices.reshape(4, 2, 4, 4), ("x", "core", "rows", "chan"))
    images = P(("x", "core", "chan"), "rows", None, None)
    grids = P(("x", "core", "rows"), None, None, "chan")
    return jax.shard_map(
        body,
        mesh=grid,
        in_specs=(
            images,
            P(("x", "core", "rows")),
            P(),
            P(),
            P(),
            P(),
            P("chan", None),
            P(),
            P(None, "chan"),
            P("chan"),
            P(),
            grids,
        ),
        out_specs=(grids, images, P(), P(), P(), P(), P("chan", None), P(), P(None, "chan"), P("chan"), P("chan", None)),
        check_vma=False,
    )
```

```python
import functools

import jax
import jax.numpy as jnp
import numpy as np
from jax import lax
from jax.experimental import pallas as pl
from jax.experimental.pallas import tpu as pltpu
from jax.sharding import Mesh, PartitionSpec as P

SLOT = 4
EPS = 1e-06
BF = jnp.bfloat16
F32 = jnp.float32
LANES = 128
VMEM_LIMIT = 56 * 1024 * 1024
NN = ((1,), (0,))
NT = ((1,), (1,))
TN = ((0,), (0,))


def dot(a, b, dims=NN):
    return lax.dot_general(a, b, (dims, ((), ())), preferred_element_type=F32)


def sigmoid(v):
    return 0.5 * jnp.tanh(0.5 * v) + 0.5


def silu(v):
    return v * sigmoid(v)


def silu_slope(v):
    s = sigmoid(v)
    return s * (1.0 + v * (1.0 - s))


def gelu_parts(v):
    c = 0.7978845608028654
    square = v * v
    t = jnp.tanh(v * (c + (c * 0.044715) * square))
    half = 0.5 * (1.0 + t)
    slope = half + 0.5 * v * (1.0 - t * t) * (c + (3.0 * c * 0.044715) * square)
    return v * half, slope


def chunks(count, body, width=LANES):
    def step(i, carry):
        body(pl.ds(pl.multiple_of(i * width, width), width))
        return carry

    lax.fori_loop(0, count, step, 0)


def call(kernel, *, grid, ins, outs, scratch=(), prefetch=0, flops=0, name):
    def spec(shape, block, index):
        if block is None:
            block, index = shape, lambda *_: (0,) * len(shape)
        return pl.BlockSpec(block, index)

    arrays = [i[0] for i in ins]
    in_specs = [spec(a.shape, b, m) for a, b, m in ins]
    out_specs = [spec(s.shape, b, m) for s, b, m in outs]
    moved = sum(a.size * a.dtype.itemsize for a in arrays) + sum(s[0].size * s[0].dtype.itemsize for s in outs)

    def run(*scalars):
        return pl.pallas_call(
            kernel,
            grid_spec=pltpu.PrefetchScalarGridSpec(
                num_scalar_prefetch=prefetch,
                grid=grid,
                in_specs=in_specs,
                out_specs=out_specs,
                scratch_shapes=list(scratch),
            ),
            out_shape=[s[0] for s in outs],
            compiler_params=pltpu.CompilerParams(
                dimension_semantics=("arbitrary",) * len(grid), vmem_limit_bytes=VMEM_LIMIT
            ),
            cost_estimate=pl.CostEstimate(flops=flops, bytes_accessed=int(moved), transcendentals=0),
            name=name,
        )(*scalars, *arrays)

    return run


def shape(dims, dtype):
    return jax.ShapeDtypeStruct(dims, dtype)


def columns_moved(t, by, first, last):
    rows = t.shape[0]
    return pltpu.roll(t, by % rows, 0) * (first if by > 0 else last)


def edge_masks(rows, width, depth):
    at = lax.broadcasted_iota(jnp.int32, (rows, LANES), 0) % (width * depth)
    return (at >= depth).astype(F32), (at < (width - 1) * depth).astype(F32)


def pre_forward(order, reduced, above, below, features, pre_reduce, taps, pre_expand, gain, pool):
    slots, cells, ch = reduced.shape
    high, wide = features.shape[1], features.shape[2]
    n = order.shape[0]
    part = slots // n

    def kernel(order_ref, red, up_ref, down_ref, feat, wr, tap, we, gn, pool_ref, conv_out, act_out, norm_out, std_out, pooled_out, halo, exp, sums):
        k = pl.program_id(0)

        @pl.when(k == 0)
        def _():
            for side, ref in enumerate((up_ref, down_ref)):
                halo[side] = dot(ref[...].reshape(slots * wide, ch), wr[...]).reshape(slots, wide, ch)

        first, last = edge_masks(wide, wide, 1)
        at = order_ref[k] * part
        for u in range(part):

            def conv(lanes):
                w = [tap[pl.ds(i, 1), lanes] for i in range(9)]
                rows = [halo[0, at + u, :, lanes]]
                rows += [red[u, pl.ds(i * wide, wide), lanes] for i in range(high)]
                rows += [halo[1, at + u, :, lanes]]
                rows = [silu(r).astype(BF).astype(F32) for r in rows]
                acts = []
                for i in range(high):
                    t = [sum(rows[i + a] * w[3 * a + b] for a in range(3)) for b in range(3)]
                    c = t[1] + columns_moved(t[0], 1, first, last) + columns_moved(t[2], -1, first, last)
                    conv_out[u, pl.ds(i * wide, wide), lanes] = c
                    acts.append(silu(c))
                act_out[u, :, lanes] = jnp.concatenate(acts, 0).astype(BF)

            chunks(ch // LANES, conv)

        exp[...] = dot(act_out[...].reshape(part * cells, ch), we[...])

        def norm(p, carry):
            u, i = p // (high // 2), p % (high // 2)
            total = [0.0] * (wide // 8)
            for half in range(2):
                f = feat[u, 2 * i + half].astype(F32)
                for t in range(wide // 8):
                    row = (2 * i + half) * wide + 8 * t
                    e = exp[pl.ds(pl.multiple_of(u * cells + row, 8), 8), :]
                    mean = jnp.mean(e, -1, keepdims=True)
                    square = jnp.mean(e * e, -1, keepdims=True)
                    std = lax.rsqrt(square - mean * mean + EPS)
                    nrm = (e - mean) * std
                    norm_out[u, pl.ds(pl.multiple_of(row, 8), 8), :] = nrm
                    std_out[u, pl.ds(pl.multiple_of(row, 8), 8), :] = std
                    total[t] = total[t] + f[8 * t : 8 * t + 8] + silu(nrm * gn[...])
            for t in range(wide // 8):
                sums[pl.ds(pl.multiple_of(p * wide + 8 * t, 8), 8), :] = total[t]
            return carry

        lax.fori_loop(0, part * high // 2, norm, 0)
        s = sums[...]
        hi = s.astype(BF)
        lo = (s - hi.astype(F32)).astype(BF)
        pooled_out[0] = (dot(pool_ref[...], hi) + dot(pool_ref[...], lo)).astype(BF)

    def by_order(rest):
        return lambda k, order: (order[k],) + (0,) * rest

    pooled_rows = pool.shape[0]
    return call(
        kernel,
        grid=(n,),
        prefetch=1,
        ins=[
            (reduced, (part, cells, ch), by_order(2)),
            (above, None, None),
            (below, None, None),
            (features, (part, high, wide, ch), by_order(3)),
            (pre_reduce, None, None),
            (taps, None, None),
            (pre_expand, None, None),
            (gain, None, None),
            (pool, None, None),
        ],
        outs=[
            (shape((slots, cells, ch), F32), (part, cells, ch), by_order(2)),
            (shape((slots, cells, ch), BF), (part, cells, ch), by_order(2)),
            (shape((slots, cells, ch), F32), (part, cells, ch), by_order(2)),
            (shape((slots, cells, 1), F32), (part, cells, 1), by_order(2)),
            (shape((n, pooled_rows, ch), BF), (1, pooled_rows, ch), lambda k, order: (k, 0, 0)),
        ],
        scratch=[
            pltpu.VMEM((2, slots, wide, ch), F32),
            pltpu.VMEM((part * cells, ch), F32),
            pltpu.VMEM((part * cells // 2, ch), F32),
        ],
        flops=2 * slots * cells * ch * ch,
        name="pre_forward",
    )(order)


def post_forward(source, moved, weights, gain, taps, pool):
    n, rows, ch = moved.shape
    total = n * rows
    depth = total // (pool * pool)
    share = ch // n

    def kernel(src, got, w, gn, tap, flat_out, red_out, act_out, conv_out, cact_out, norm_out, std_out, low_out, wide_ref):
        for r in range(n):
            wide_ref[pl.ds(r * rows, rows), :] = got[src[r]].astype(F32)
        flat_out[...] = wide_ref[...].astype(BF)
        red = 0.0
        for c in range(n):
            red = red + dot(flat_out[:, c * share : (c + 1) * share], w[c, 0])
        red_out[...] = red
        first, last = edge_masks(total, pool, depth)
        step = pool * depth

        def conv(lanes):
            x = silu(red_out[:, lanes]).astype(BF)
            act_out[:, lanes] = x
            x = x.astype(F32)
            moves = [columns_moved(x, depth, first, last), x, columns_moved(x, -depth, first, last)]
            t = [sum(moves[b] * tap[pl.ds(3 * a + b, 1), lanes] for b in range(3)) for a in range(3)]
            none = jnp.zeros((step, LANES), F32)
            c = t[1] + jnp.concatenate([none, t[0][:-step]], 0) + jnp.concatenate([t[2][step:], none], 0)
            conv_out[:, lanes] = c
            cact_out[:, lanes] = silu(c).astype(BF)

        chunks(ch // LANES, conv)
        for c in range(n):
            e = 0.0
            for q in range(n):
                cut = slice(q * share, (q + 1) * share)
                e = e + dot(cact_out[:, cut], w[c, 1, :, cut])
            norm_out[:, c * share : (c + 1) * share] = e

        def norm(i, carry):
            at = pl.ds(pl.multiple_of(i * 16, 16), 16)
            e = norm_out[at, :]
            mean = jnp.mean(e, -1, keepdims=True)
            square = jnp.mean(e * e, -1, keepdims=True)
            std = lax.rsqrt(square - mean * mean + EPS)
            nrm = (e - mean) * std
            norm_out[at, :] = nrm
            std_out[at, :] = std
            low_out[at, :] = (wide_ref[at, :] + silu(nrm * gn[...])).astype(BF)
            return carry

        lax.fori_loop(0, total // 16, norm, 0)

    wide = shape((total, ch), F32)
    narrow = shape((total, ch), BF)
    return call(
        kernel,
        grid=(1,),
        prefetch=1,
        ins=[(a, None, None) for a in (moved, weights, gain, taps)],
        outs=[(s, None, None) for s in (narrow, wide, narrow, wide, narrow, wide, shape((total, 1), F32), narrow)],
        scratch=[pltpu.VMEM((total, ch), F32)],
        flops=4 * total * ch * ch,
        name="post_forward",
    )(source)


def post_backward(source, low, readout, cots, weights, gain, taps, act, red, conv, nrm, std, pool):
    total, ch = low.shape
    n = cots.shape[0]
    share = ch // n
    out_share = cots.shape[2]
    rows = total // n
    depth = total // (pool * pool)

    def kernel(src, low_ref, ro, cot, w, gn, tap, act_ref, red_ref, conv_ref, norm_ref, std_ref, exp_out, redg_out, back_out, taps_out, gain_out, grad, cgrad):
        k = pl.program_id(0)
        logits = dot(low_ref[...], ro[...])
        piece = (cot[0].astype(F32) * gelu_parts(logits)[1]).astype(BF)
        term = dot(piece, ro[...], NT)

        @pl.when(k == 0)
        def _():
            grad[...] = term

        @pl.when(k > 0)
        def _():
            grad[...] += term

        @pl.when(k == n - 1)
        def _():
            def norm(i, total_gain):
                at = pl.ds(pl.multiple_of(i * 16, 16), 16)
                nm = norm_ref[at, :]
                ng = grad[at, :] * silu_slope(nm * gn[...])
                sc = ng * gn[...]
                one = jnp.mean(sc, -1, keepdims=True)
                two = jnp.mean(sc * nm, -1, keepdims=True)
                exp_out[at, :] = (std_ref[at, :] * (sc - one - nm * two)).astype(BF)
                g = ng * nm
                return total_gain + g[:8] + g[8:]

            gain_out[...] = lax.fori_loop(0, total // 16, norm, jnp.zeros((8, ch), F32))
            for q in range(n):
                cut = slice(q * share, (q + 1) * share)
                cg = 0.0
                for c in range(n):
                    cg = cg + dot(exp_out[:, c * share : (c + 1) * share], w[c, 1, :, cut], NT)
                cgrad[:, cut] = cg
            first, last = edge_masks(total, pool, depth)
            step = pool * depth

            def back(lanes):
                g = (cgrad[:, lanes] * silu_slope(conv_ref[:, lanes])).astype(BF).astype(F32)
                x = act_ref[:, lanes].astype(F32)
                moves = [columns_moved(g, -depth, first, last), g, columns_moved(g, depth, first, last)]
                none = jnp.zeros((step, LANES), F32)
                xs = [
                    jnp.concatenate([none, x[:-step]], 0),
                    x,
                    jnp.concatenate([x[step:], none], 0),
                ]
                for a in range(3):
                    for b in range(3):
                        prod = xs[a] * moves[b]
                        taps_out[3 * a + b, :, lanes] = jnp.sum(prod.reshape(total // 8, 8, LANES), 0)
                t = [sum(moves[b] * tap[pl.ds(3 * a + b, 1), lanes] for b in range(3)) for a in range(3)]
                d = t[1] + jnp.concatenate([t[0][step:], none], 0) + jnp.concatenate([none, t[2][:-step]], 0)
                redg_out[:, lanes] = (d * silu_slope(red_ref[:, lanes])).astype(BF)

            chunks(ch // LANES, back)
            for c in range(n):
                cut = slice(c * share, (c + 1) * share)
                grad[:, cut] += dot(redg_out[...], w[c, 0], NT)
            for r in range(n):
                at = pl.ds(pl.multiple_of(src[r] * rows, 8), rows)
                back_out[r] = grad[at, :].astype(BF)

    return call(
        kernel,
        grid=(n,),
        prefetch=1,
        ins=[
            (low, None, None),
            (readout, (ch, out_share), lambda k, s: (0, k)),
            (cots, (1, total, out_share), lambda k, s: (k, 0, 0)),
        ]
        + [(a, None, None) for a in (weights, gain, taps, act, red, conv, nrm, std)],
        outs=[
            (s, None, None)
            for s in (
                shape((total, ch), BF),
                shape((total, ch), BF),
                shape((n, rows, ch), BF),
                shape((9, 8, ch), F32),
                shape((8, ch), F32),
            )
        ],
        scratch=[pltpu.VMEM((total, ch), F32), pltpu.VMEM((total, ch), F32)],
        flops=2 * total * ch * (2 * out_share * n + 2 * ch),
        name="post_backward",
    )(source)


def cotangent_by_image(cotangent, select):
    rows, width = cotangent.shape
    size = select.shape[0]
    pairs = SLOT
    each = size // pairs
    per = 3

    def kernel(x, sel, out):
        for q in range(per):
            y = dot(sel[...], x[pl.ds(q * size, size), :]).astype(BF)
            for s in range(pairs):
                out[s, pl.ds(q * each, each), :] = y[s * each : (s + 1) * each]

    return call(
        kernel,
        grid=(rows // (per * size),),
        ins=[(cotangent, (per * size, width), lambda i: (i, 0)), (select, None, None)],
        outs=[(shape((pairs, rows // pairs, width), BF), (pairs, per * each, width), lambda i: (0, i, 0))],
        flops=2 * rows * size * width,
        name="cotangent_by_image",
    )()[0]


def token_block(chan, source, low, place, readout, cotangent, live):
    pairs, each_all, ch = low.shape
    rows, width = cotangent.shape
    size = place.shape[0]
    each = size // pairs
    per = 3

    def kernel(chan_ref, src, low_ref, place_ref, ro, cot, alive, tok_out, piece_out, low_out):
        for q in range(per):
            at = pl.ds(q * size, size)
            x = jnp.concatenate([low_ref[src[s], pl.ds(q * each, each), :] for s in range(pairs)], 0)
            low_out[at, :] = dot(place_ref[...], x).astype(BF)
        logits = dot(low_out[...], ro[...])
        value, slope = gelu_parts(logits)
        tok_out[...] = value.astype(BF)
        piece_out[...] = (cot[...].astype(F32) * alive[...] * slope).astype(BF)

    block = per * size
    row_block = lambda i, c, s: (i, 0)
    return call(
        kernel,
        grid=(rows // block,),
        prefetch=2,
        ins=[
            (low, (pairs, per * each, ch), lambda i, c, s: (0, i, 0)),
            (place, None, None),
            (readout, (ch, width), lambda i, c, s: (0, c[0])),
            (cotangent, (block, width), row_block),
            (live, None, None),
        ],
        outs=[
            (shape((rows, width), BF), (block, width), row_block),
            (shape((rows, width), BF), (block, width), row_block),
            (shape((rows, ch), BF), (block, ch), row_block),
        ],
        flops=2 * rows * ch * width,
        name="token_block",
    )(chan, source)


def pre_backward(order, returned, spread_up, nrm, std, gain, conv, pre_expand):
    slots, cells, ch = nrm.shape
    n = order.shape[0]
    part = slots // n
    wide = 24
    rows = part * cells

    def kernel(order_ref, ret, up, norm_ref, std_ref, gn, conv_ref, we, exp_out, conv_grad_out, top_out, bottom_out, gain_out, grad, cgrad):
        k = pl.program_id(0)
        grad[...] = dot(up[...], ret[0])

        def norm(i, total_gain):
            u, j = i // (cells // 16), i % (cells // 16)
            at = pl.ds(pl.multiple_of(j * 16, 16), 16)
            nm = norm_ref[u, at, :]
            ng = grad[pl.ds(pl.multiple_of(i * 16, 16), 16), :] * silu_slope(nm * gn[...])
            sc = ng * gn[...]
            one = jnp.mean(sc, -1, keepdims=True)
            two = jnp.mean(sc * nm, -1, keepdims=True)
            exp_out[u, at, :] = (std_ref[u, at, :] * (sc - one - nm * two)).astype(BF)
            g = ng * nm
            return total_gain + g[:8] + g[8:]

        gains = lax.fori_loop(0, rows // 16, norm, jnp.zeros((8, ch), F32))

        @pl.when(k == 0)
        def _():
            gain_out[...] = gains

        @pl.when(k > 0)
        def _():
            gain_out[...] += gains

        cgrad[...] = dot(exp_out[...].reshape(rows, ch), we[...], NT)
        for u in range(part):

            def slope(lanes):
                g = cgrad[pl.ds(u * cells, cells), lanes] * silu_slope(conv_ref[u, :, lanes])
                conv_grad_out[u, :, lanes] = g.astype(BF)
                top_out[u, :, lanes] = g[:wide].astype(BF)
                bottom_out[u, :, lanes] = g[cells - wide :].astype(BF)

            chunks(ch // LANES, slope)

    by_order = lambda k, order: (order[k], 0, 0)
    whole = (part, cells, ch)
    edge = (part, wide, ch)
    return call(
        kernel,
        grid=(n,),
        prefetch=1,
        ins=[
            (returned, (1,) + returned.shape[1:], lambda k, order: (k, 0, 0)),
            (spread_up, None, None),
            (nrm, whole, by_order),
            (std, (part, cells, 1), by_order),
            (gain, None, None),
            (conv, whole, by_order),
            (pre_expand, None, None),
        ],
        outs=[
            (shape((slots, cells, ch), BF), whole, by_order),
            (shape((slots, cells, ch), BF), whole, by_order),
            (shape((slots, wide, ch), BF), edge, by_order),
            (shape((slots, wide, ch), BF), edge, by_order),
            (shape((8, ch), F32), None, None),
        ],
        scratch=[pltpu.VMEM((rows, ch), F32), pltpu.VMEM((rows, ch), F32)],
        flops=2 * slots * cells * ch * ch,
        name="pre_backward",
    )(order)


def pre_conv_backward(conv_grad, above, below, reduced, taps):
    slots, cells, ch = reduced.shape
    wide = above.shape[1]
    high = cells // wide

    def kernel(cg, up, down, red, tap, redg_out, taps_out):
        step = pl.program_id(0)
        first, last = edge_masks(wide, wide, 1)

        @pl.when(step == 0)
        def _():
            taps_out[...] = jnp.zeros_like(taps_out)

        def back(lanes):
            w = [tap[pl.ds(i, 1), lanes] for i in range(9)]
            mid = cg[0, :, lanes].astype(F32)
            rows = [up[0, :, lanes].astype(F32)]
            rows += [mid[i * wide : (i + 1) * wide] for i in range(high)]
            rows += [down[0, :, lanes].astype(F32)]
            v = [red[0, pl.ds(i * wide, wide), lanes] for i in range(high)]
            s = [sigmoid(t) for t in v]
            x = [(a * b).astype(BF).astype(F32) for a, b in zip(v, s)]
            d = [0.0] * high
            sums = [0.0] * 9
            for p in range(high + 2):
                g = rows[p]
                moves = [columns_moved(g, -1, first, last), g, columns_moved(g, 1, first, last)]
                for a in range(3):
                    i = p - 1 + a - 1
                    if 0 <= i < high:
                        for b in range(3):
                            d[i] = d[i] + moves[b] * w[3 * a + b]
                            prod = x[i] * moves[b]
                            sums[3 * a + b] = sums[3 * a + b] + (prod[:8] + prod[8:16] + prod[16:])
            out = [d[i] * (s[i] * (1.0 + v[i] * (1.0 - s[i]))) for i in range(high)]
            redg_out[0, :, lanes] = jnp.concatenate(out, 0).astype(BF)
            for i in range(9):
                taps_out[i, :, lanes] += sums[i]

        chunks(ch // LANES, back)

    image = lambda i: (i, 0, 0)
    return call(
        kernel,
        grid=(slots,),
        ins=[
            (conv_grad, (1, cells, ch), image),
            (above, (1, wide, ch), image),
            (below, (1, wide, ch), image),
            (reduced, (1, cells, ch), image),
            (taps, None, None),
        ],
        outs=[
            (shape((slots, cells, ch), BF), (1, cells, ch), image),
            (shape((9, 8, ch), F32), None, None),
        ],
        flops=0,
        name="pre_conv_backward",
    )()


def feature_backward(order, reduced_grad, pre_reduce, returned, spread_up):
    slots, cells, ch = reduced_grad.shape
    n = order.shape[0]
    part = slots // n

    def kernel(order_ref, rg, wr, ret, up, out):
        g = dot(rg[...].reshape(part * cells, ch), wr[...], NT) + dot(up[...], ret[0])
        out[...] = g.reshape(part, cells, ch)

    by_order = lambda k, order: (order[k], 0, 0)
    whole = (part, cells, ch)
    return call(
        kernel,
        grid=(n,),
        prefetch=1,
        ins=[
            (reduced_grad, whole, by_order),
            (pre_reduce, None, None),
            (returned, (1,) + returned.shape[1:], lambda k, order: (k, 0, 0)),
            (spread_up, None, None),
        ],
        outs=[(shape((slots, cells, ch), F32), whole, by_order)],
        flops=2 * slots * cells * ch * ch,
        name="feature_backward",
    )(order)[0]


def post_weight_grads(flat, reduced_grad, act, expanded_grad, n):
    total, ch = flat.shape
    share = ch // n

    def kernel(x, g, a, e, out):
        for c in range(n):
            cut = slice(c * share, (c + 1) * share)
            out[0, c] = dot(x[:, cut], g[...], TN).astype(BF)
            for q in range(n):
                rows = slice(q * share, (q + 1) * share)
                out[1, c, :, rows] = dot(a[:, rows], e[:, cut], TN).astype(BF)

    return call(
        kernel,
        grid=(1,),
        ins=[(v, None, None) for v in (flat, reduced_grad, act, expanded_grad)],
        outs=[(shape((2, n, share, ch), BF), None, None)],
        flops=4 * total * ch * ch,
        name="post_weight_grads",
    )()[0]


def spread(n, k):
    return [(a * n + b, b * n + (a + k) % n) for a in range(n) for b in range(n)]


def other_core(values):
    return lax.ppermute(values, "core", [(0, 1), (1, 0)])


def small_rows(*grads):
    ch = grads[0].shape[-1]
    counts = [g.shape[0] if g.ndim == 3 else 1 for g in grads]
    per = ch // LANES

    def kernel(*refs):
        out = refs[-1]
        at = 0
        for ref, count in zip(refs, counts):
            for i in range(count):
                v = jnp.sum(ref[i] if len(ref.shape) == 3 else ref[...], 0, keepdims=True)
                for q in range(per):
                    out[pl.ds(at, 1), :] = v[:, q * LANES : (q + 1) * LANES]
                    at += 1

    return call(
        kernel,
        grid=(1,),
        ins=[(g, None, None) for g in grads],
        outs=[(shape((sum(counts) * per, LANES), F32), None, None)],
        name="small_rows",
    )()[0]


def join_halves(core, mine, theirs, small, their_small, parts):
    rows, ch = mine[0].shape
    half = rows // 2
    width = len(mine) * ch + LANES
    count = small.shape[0]
    m = len(mine)

    def kernel(core_ref, *refs):
        own, got = refs[:m], refs[m : 2 * m]
        sm, got_sm, out = refs[2 * m :]
        for i in range(m):
            out[:, i * ch : (i + 1) * ch] = (own[i][...].astype(F32) + got[i][...].astype(F32)).astype(BF)
        first = (core_ref[0] == 0).astype(F32)
        total = (sm[...] + got_sm[...]) * first
        pad = jnp.zeros((half - count, LANES), F32)
        out[:, m * ch :] = jnp.concatenate([total, pad], 0).astype(BF)

    return call(
        kernel,
        grid=(1,),
        prefetch=1,
        ins=[(v, (half, ch), lambda i, c: (c[0], 0)) for v in mine]
        + [(v, None, None) for v in (*theirs, small, their_small)],
        outs=[(shape((half, width), BF), None, None)],
        name="join_halves",
    )(core)[0].reshape(parts, half // parts, width)


def sum_and_copy(blocks):
    parts, rows, width = blocks.shape

    def kernel(x, out):
        def cut(lanes):
            total = jnp.sum(x[:, :, lanes].astype(F32), 0).astype(BF)
            out[:, :, lanes] = jnp.broadcast_to(total[None], (parts, rows, LANES))

        chunks(width // LANES, cut)

    return call(
        kernel,
        grid=(1,),
        ins=[(blocks, None, None)],
        outs=[(shape(blocks.shape, BF), None, None)],
        name="sum_and_copy",
    )()[0]


def finish_pre(core, own, got, ch):
    half, width = own.shape
    m = (width - LANES) // ch

    def kernel(core_ref, a, b, *outs):
        h = pl.program_id(0)

        def write(ref):
            for i in range(m):
                outs[i][...] = ref[:, i * ch : (i + 1) * ch].astype(F32)

            @pl.when(h == 0)
            def _():
                outs[m][...] = ref[:, m * ch :].astype(F32)

        @pl.when(h == core_ref[0])
        def _():
            write(a)

        @pl.when(h != core_ref[0])
        def _():
            write(b)

    return call(
        kernel,
        grid=(2,),
        prefetch=1,
        ins=[(own, None, None), (got, None, None)],
        outs=[(shape((2 * half, ch), F32), (half, ch), lambda h, c: (h, 0)) for _ in range(m)]
        + [(shape((half, LANES), F32), None, None)],
        name="finish_pre",
    )(core)


def pool_matrix(part, high, wide):
    half = wide // 2
    m = np.zeros((high // 2 * half * part, part * (high // 2) * wide), np.float32)
    for u in range(part):
        for i in range(high // 2):
            for j in range(wide):
                m[(i * half + j // 2) * part + u, (u * (high // 2) + i) * wide + j] = 0.25
    return m


def spread_matrix(part, high, wide):
    half = wide // 2
    m = np.zeros((part * high * wide, high // 2 * half * part), np.float32)
    for u in range(part):
        for i in range(high):
            for j in range(wide):
                m[(u * high + i) * wide + j, ((i // 2) * half + j // 2) * part + u] = 0.25
    return m


def place_matrix(cells, slots, pairs):
    per = slots // pairs
    m = np.zeros((cells * slots, cells * slots), np.float32)
    for c in range(cells):
        for s in range(slots):
            m[c * slots + s, (s // per) * cells * per + c * per + s % per] = 1.0
    return m


def body(features, counts, pre_reduce, pre_conv, pre_expand, pre_gain, post_reduce, post_conv, post_expand, post_gain, readout, cotangent):
    n = lax.axis_size("chan")
    row = lax.axis_index("rows").astype(jnp.int32)
    chan = lax.axis_index("chan").astype(jnp.int32)
    core = lax.axis_index("core").astype(jnp.int32)
    eighth = lax.axis_index(("x", "core"))
    ch = pre_reduce.shape[0]
    slots, high, wide = features.shape[0], features.shape[1], features.shape[2]
    part = slots // n
    cells = high * wide
    pool = wide // 2
    share = ch // n
    out_share = cotangent.shape[3]
    steps = jnp.arange(n, dtype=jnp.int32)
    order = (row + steps) % n
    source = (chan - steps) % n
    rank = jnp.full((1,), chan, jnp.int32)
    core_at = jnp.full((1,), core, jnp.int32)
    pre_taps = pre_conv.astype(F32).reshape(9, ch)
    post_taps = post_conv.astype(F32).reshape(9, ch)
    pre_gain_row = pre_gain.reshape(1, ch)
    pool_m = jnp.asarray(pool_matrix(part, high, wide), BF)
    up_m = jnp.asarray(spread_matrix(part, high, wide), BF)
    place = jnp.asarray(place_matrix(16, slots, n), BF)

    ends = n - 1
    down_pairs = [(i, i + 1) for i in range(ends)]
    up_pairs = [(i + 1, i) for i in range(ends)]
    above = lax.ppermute(features[:, -1], "rows", down_pairs)
    below = lax.ppermute(features[:, 0], "rows", up_pairs)
    gain_hi = post_gain.astype(BF)
    gain_lo = (post_gain - gain_hi.astype(F32)).astype(BF)
    gain_row = jnp.concatenate([gain_hi, gain_lo, jnp.zeros((ch - 2 * share,), BF)])[None]
    square = post_expand.reshape(n, share, share)
    shards = jnp.concatenate(
        [post_reduce, jnp.concatenate([square[q] for q in range(n)], axis=1), jnp.pad(gain_row, ((0, 63), (0, 0)))], axis=0
    )
    eighths = shards.reshape(8, -1, ch)
    full = lax.all_gather(lax.dynamic_index_in_dim(eighths, eighth, 0, keepdims=False), ("chan", "x", "core"), axis=0, tiled=True)
    full = full.reshape(n, 2 * share + 64, ch)
    live = (jnp.arange(SLOT)[None, :] < counts[:, None]).astype(F32).reshape(slots)
    select = place.T * jnp.tile(live.astype(BF), 16)[None, :]
    cot_rows = cotangent.transpose(1, 2, 0, 3).reshape(-1, out_share)
    cots = lax.all_to_all(cotangent_by_image(cot_rows, select), "chan", 0, 0, tiled=False)

    flat_features = features.reshape(slots * cells, ch)
    reduced = dot(flat_features, pre_reduce).reshape(slots, cells, ch)
    convolved, convolved_act, normal_pre, pre_std, pooled = pre_forward(
        order, reduced, above, below, features, pre_reduce, pre_taps, pre_expand, pre_gain_row, pool_m
    )

    moved = jnp.stack([lax.ppermute(pooled[k], ("rows", "chan"), spread(n, k)) for k in range(n)])
    weights = full[:, : 2 * share].reshape(n, 2, share, ch)
    gain_parts = full[:, 2 * share].astype(F32)
    post_gain_row = (gain_parts[:, :share] + gain_parts[:, share : 2 * share]).reshape(1, ch)
    flat, post_reduced, post_act, post_convolved, post_cact, post_normal, post_std, low = post_forward(
        source, moved, weights, post_gain_row, post_taps, pool
    )
    lows = [low] + [lax.ppermute(low, "chan", [(i, (i + k) % n) for i in range(n)]) for k in range(1, n)]
    post_expanded_grad, post_reduced_grad, back, post_taps_grad, post_gain_grad = post_backward(
        source, low, readout, cots, weights, post_gain_row, post_taps, post_act, post_reduced, post_convolved, post_normal, post_std, pool
    )

    returned = jnp.stack(
        [lax.ppermute(back[k], ("rows", "chan"), [(d, s) for s, d in spread(n, k)]) for k in range(n)]
    )

    post_load = post_weight_grads(flat, post_reduced_grad, post_cact, post_expanded_grad, n)
    post_keep = lax.dynamic_index_in_dim(post_load, core, 0, keepdims=False)
    post_got = other_core(lax.dynamic_index_in_dim(post_load, 1 - core, 0, keepdims=False))
    post_sum = lax.psum_scatter((post_keep.astype(F32) + post_got.astype(F32)).astype(BF), "chan", scatter_dimension=0, tiled=False)

    alive = jnp.broadcast_to(jnp.tile(live, 48)[:, None], (48 * slots, 1))
    tokens, piece, low_here = token_block(rank, source, jnp.stack(lows), place, readout, cot_rows, alive)
    readout_grad = dot(low_here, piece, TN).astype(BF).reshape(n, 2, share // 2, out_share)
    tokens = tokens.reshape(pool, pool, slots, out_share).transpose(2, 0, 1, 3)
    read_keep = lax.dynamic_index_in_dim(readout_grad, core, 1, keepdims=False)
    read_got = other_core(lax.dynamic_index_in_dim(readout_grad, 1 - core, 1, keepdims=False))
    read_sum = (read_keep.astype(F32) + read_got.astype(F32)).astype(BF)
    eight = share // 32
    load = jnp.concatenate(
        [
            post_sum.reshape(4, 4, 2 * eight, ch),
            read_sum.reshape(n, 4, 4, eight, out_share).transpose(1, 2, 0, 3, 4).reshape(4, 4, n * eight, out_share),
        ],
        axis=2,
    )
    load = lax.psum_scatter(load, "x", scatter_dimension=0, tiled=False)
    load = lax.psum_scatter(load, "rows", scatter_dimension=0, tiled=False)
    read_part = lax.all_to_all(load[2 * eight :].reshape(n, eight, out_share), "chan", 0, 0, tiled=False)
    load = jnp.concatenate([load[: 2 * eight], read_part.reshape(n * eight, out_share)], axis=0)
    half_all = lax.all_gather(load, ("x", "rows"), axis=0, tiled=False)
    half_got = other_core(half_all)
    first = jnp.where(core == 0, half_all, half_got).astype(F32)
    second = jnp.where(core == 0, half_got, half_all).astype(F32)
    post_reduce_out = first[:, : 2 * eight].reshape(share, ch)
    post_expand_out = second[:, : 2 * eight].reshape(share, n, share).transpose(1, 0, 2).reshape(ch, share)
    readout_out = jnp.stack([first[:, 2 * eight :], second[:, 2 * eight :]]).reshape(2, 16, n, eight, out_share)
    readout_out = readout_out.transpose(0, 1, 3, 2, 4).reshape(share, n * out_share)

    expanded_grad, convolved_grad, top, bottom, pre_gain_grad = pre_backward(
        order, returned, up_m, normal_pre, pre_std, pre_gain_row, convolved, pre_expand
    )
    grad_above = lax.ppermute(bottom, "rows", down_pairs)
    grad_below = lax.ppermute(top, "rows", up_pairs)
    pre_expand_grad = dot(convolved_act.reshape(-1, ch), expanded_grad.reshape(-1, ch), TN).astype(BF)
    reduced_grad, pre_taps_grad = pre_conv_backward(convolved_grad, grad_above, grad_below, reduced, pre_taps)
    pre_reduce_grad = dot(flat_features, reduced_grad.reshape(-1, ch), TN).astype(BF)
    feature_grad = feature_backward(order, reduced_grad, pre_reduce, returned, up_m).reshape(features.shape)

    small = small_rows(pre_taps_grad, pre_gain_grad, post_taps_grad, post_gain_grad)
    mine = [pre_reduce_grad, pre_expand_grad]
    theirs = [other_core(lax.dynamic_index_in_dim(g.reshape(2, ch // 2, ch), 1 - core, 0, keepdims=False)) for g in mine]
    load = join_halves(core_at, mine, theirs, small, other_core(small), 64)
    chips = ("x", "rows", "chan")
    load = sum_and_copy(lax.all_to_all(load, chips, 0, 0, tiled=False))
    load = lax.all_to_all(load, chips, 0, 0, tiled=False).reshape(ch // 2, -1)
    pre_reduce_out, pre_expand_out, small_out = finish_pre(core_at, load, other_core(load), ch)
    per = ch // LANES
    cut = [0, 9 * per, 10 * per, 19 * per, 20 * per]
    pre_conv_out, pre_gain_out, post_conv_out, post_gain_out = [small_out[a:b] for a, b in zip(cut, cut[1:])]
    return (
        tokens,
        feature_grad,
        pre_reduce_out,
        pre_conv_out.reshape(3, 3, ch),
        pre_expand_out,
        pre_gain_out.reshape(ch),
        post_reduce_out,
        post_conv_out.reshape(3, 3, ch),
        post_expand_out,
        lax.dynamic_slice_in_dim(post_gain_out.reshape(ch), chan * share, share, 0),
        readout_out,
    )


def solution(mesh):
    grid = Mesh(mesh.devices.reshape(4, 2, 4, 4), ("x", "core", "rows", "chan"))
    images = P(("x", "core", "chan"), "rows", None, None)
    grids = P(("x", "core", "rows"), None, None, "chan")
    return jax.shard_map(
        body,
        mesh=grid,
        in_specs=(
            images,
            P(("x", "core", "rows")),
            P(),
            P(),
            P(),
            P(),
            P("chan", None),
            P(),
            P(None, "chan"),
            P("chan"),
            P(),
            grids,
        ),
        out_specs=(grids, images, P(), P(), P(), P(), P("chan", None), P(), P(None, "chan"), P("chan"), P("chan", None)),
        check_vma=False,
    )
```

```python
import functools

import jax
import jax.numpy as jnp
import numpy as np
from jax import lax
from jax.experimental import pallas as pl
from jax.experimental.pallas import tpu as pltpu
from jax.sharding import Mesh, PartitionSpec as P

SLOT = 4
EPS = 1e-06
BF = jnp.bfloat16
F32 = jnp.float32
LANES = 128
VMEM_LIMIT = 56 * 1024 * 1024
NN = ((1,), (0,))
NT = ((1,), (1,))
TN = ((0,), (0,))


def dot(a, b, dims=NN):
    return lax.dot_general(a, b, (dims, ((), ())), preferred_element_type=F32)


def sigmoid(v):
    return 0.5 * jnp.tanh(0.5 * v) + 0.5


def silu(v):
    return v * sigmoid(v)


def silu_slope(v):
    s = sigmoid(v)
    return s * (1.0 + v * (1.0 - s))


def gelu_parts(v):
    c = 0.7978845608028654
    square = v * v
    t = jnp.tanh(v * (c + (c * 0.044715) * square))
    half = 0.5 * (1.0 + t)
    slope = half + 0.5 * v * (1.0 - t * t) * (c + (3.0 * c * 0.044715) * square)
    return v * half, slope


def chunks(count, body, width=LANES):
    def step(i, carry):
        body(pl.ds(pl.multiple_of(i * width, width), width))
        return carry

    lax.fori_loop(0, count, step, 0)


def call(kernel, *, grid, ins, outs, scratch=(), prefetch=0, name):
    def spec(shape, block, index):
        if block is None:
            block, index = shape, lambda *_: (0,) * len(shape)
        return pl.BlockSpec(block, index)

    arrays = [i[0] for i in ins]
    in_specs = [spec(a.shape, b, m) for a, b, m in ins]
    out_specs = [spec(s.shape, b, m) for s, b, m in outs]

    def run(*scalars):
        return pl.pallas_call(
            kernel,
            grid_spec=pltpu.PrefetchScalarGridSpec(
                num_scalar_prefetch=prefetch,
                grid=grid,
                in_specs=in_specs,
                out_specs=out_specs,
                scratch_shapes=list(scratch),
            ),
            out_shape=[s[0] for s in outs],
            compiler_params=pltpu.CompilerParams(
                dimension_semantics=("arbitrary",) * len(grid), vmem_limit_bytes=VMEM_LIMIT
            ),
            cost_estimate=pl.CostEstimate(flops=1, bytes_accessed=1, transcendentals=0),
            name=name,
        )(*scalars, *arrays)

    return run


def shape(dims, dtype):
    return jax.ShapeDtypeStruct(dims, dtype)


def columns_moved(t, by, first, last):
    rows = t.shape[0]
    return pltpu.roll(t, by % rows, 0) * (first if by > 0 else last)


def edge_masks(rows, width, depth):
    at = lax.broadcasted_iota(jnp.int32, (rows, LANES), 0) % (width * depth)
    return (at >= depth).astype(F32), (at < (width - 1) * depth).astype(F32)


def pre_forward(order, reduced, above, below, features, pre_reduce, taps, pre_expand, gain, pool):
    slots, cells, ch = reduced.shape
    high, wide = features.shape[1], features.shape[2]
    n = order.shape[0]
    part = slots // n

    def kernel(order_ref, red, up_ref, down_ref, feat, wr, tap, we, gn, pool_ref, conv_out, act_out, norm_out, std_out, *rest):
        pooled_out, (halo, exp, sums) = rest[:-3], rest[-3:]
        k = pl.program_id(0)

        @pl.when(k == 0)
        def _():
            for side, ref in enumerate((up_ref, down_ref)):
                halo[side] = dot(ref[...].reshape(slots * wide, ch), wr[...]).reshape(slots, wide, ch)

        first, last = edge_masks(wide, wide, 1)
        at = order_ref[k] * part
        for u in range(part):

            def conv(lanes):
                w = [tap[pl.ds(i, 1), lanes] for i in range(9)]
                rows = [halo[0, at + u, :, lanes]]
                rows += [red[u, pl.ds(i * wide, wide), lanes] for i in range(high)]
                rows += [halo[1, at + u, :, lanes]]
                rows = [silu(r).astype(BF).astype(F32) for r in rows]
                acts = []
                for i in range(high):
                    t = [sum(rows[i + a] * w[3 * a + b] for a in range(3)) for b in range(3)]
                    c = t[1] + columns_moved(t[0], 1, first, last) + columns_moved(t[2], -1, first, last)
                    conv_out[u, pl.ds(i * wide, wide), lanes] = c
                    acts.append(silu(c))
                act_out[u, :, lanes] = jnp.concatenate(acts, 0).astype(BF)

            chunks(ch // LANES, conv)

        exp[...] = dot(act_out[...].reshape(part * cells, ch), we[...])

        def norm(p, carry):
            u, i = p // (high // 2), p % (high // 2)
            total = [0.0] * (wide // 8)
            for half in range(2):
                f = feat[u, 2 * i + half].astype(F32)
                for t in range(wide // 8):
                    row = (2 * i + half) * wide + 8 * t
                    e = exp[pl.ds(pl.multiple_of(u * cells + row, 8), 8), :]
                    mean = jnp.mean(e, -1, keepdims=True)
                    square = jnp.mean(e * e, -1, keepdims=True)
                    std = lax.rsqrt(square - mean * mean + EPS)
                    nrm = (e - mean) * std
                    norm_out[u, pl.ds(pl.multiple_of(row, 8), 8), :] = nrm
                    std_out[u, pl.ds(pl.multiple_of(row, 8), 8), :] = std
                    total[t] = total[t] + f[8 * t : 8 * t + 8] + silu(nrm * gn[...])
            for t in range(wide // 8):
                sums[pl.ds(pl.multiple_of(p * wide + 8 * t, 8), 8), :] = total[t]
            return carry

        lax.fori_loop(0, part * high // 2, norm, 0)
        s = sums[...]
        hi = s.astype(BF)
        lo = (s - hi.astype(F32)).astype(BF)
        pooled = (dot(pool_ref[...], hi) + dot(pool_ref[...], lo)).astype(BF)
        for i in range(n):

            @pl.when(k == i)
            def _():
                pooled_out[i][...] = pooled

    def by_order(rest):
        return lambda k, order: (order[k],) + (0,) * rest

    pooled_rows = pool.shape[0]
    return call(
        kernel,
        grid=(n,),
        prefetch=1,
        ins=[
            (reduced, (part, cells, ch), by_order(2)),
            (above, None, None),
            (below, None, None),
            (features, (part, high, wide, ch), by_order(3)),
            (pre_reduce, None, None),
            (taps, None, None),
            (pre_expand, None, None),
            (gain, None, None),
            (pool, None, None),
        ],
        outs=[
            (shape((slots, cells, ch), F32), (part, cells, ch), by_order(2)),
            (shape((slots, cells, ch), BF), (part, cells, ch), by_order(2)),
            (shape((slots, cells, ch), F32), (part, cells, ch), by_order(2)),
            (shape((slots, cells, 1), F32), (part, cells, 1), by_order(2)),
        ]
        + [(shape((pooled_rows, ch), BF), None, None)] * n,
        scratch=[
            pltpu.VMEM((2, slots, wide, ch), F32),
            pltpu.VMEM((part * cells, ch), F32),
            pltpu.VMEM((part * cells // 2, ch), F32),
        ],
        name="pre_forward",
    )(order)


def gain_row(w, n, share):
    at = 2 * share
    parts = [w[c, at : at + 16, :].astype(F32)[:1] for c in range(n)]
    return jnp.concatenate([p[:, :share] + p[:, share : 2 * share] for p in parts], 1)


def post_forward(source, moved, weights, taps, pool):
    n, (rows, ch) = len(moved), moved[0].shape
    total = n * rows
    depth = total // (pool * pool)
    share = ch // n

    def kernel(src, *refs):
        got, (w, tap, flat_out, red_out, act_out, conv_out, cact_out, norm_out, std_out, low_out, wide_ref) = refs[:n], refs[n:]
        for k in range(n):
            at = pl.multiple_of(src[k] * rows, 8)
            wide_ref[pl.ds(at, rows), :] = got[k][...].astype(F32)
        gain = gain_row(w, n, share)
        flat_out[...] = wide_ref[...].astype(BF)
        red = 0.0
        for c in range(n):
            red = red + dot(flat_out[:, c * share : (c + 1) * share], w[c, :share])
        red_out[...] = red
        first, last = edge_masks(total, pool, depth)
        step = pool * depth

        def conv(lanes):
            x = silu(red_out[:, lanes]).astype(BF)
            act_out[:, lanes] = x
            x = x.astype(F32)
            moves = [columns_moved(x, depth, first, last), x, columns_moved(x, -depth, first, last)]
            t = [sum(moves[b] * tap[pl.ds(3 * a + b, 1), lanes] for b in range(3)) for a in range(3)]
            none = jnp.zeros((step, LANES), F32)
            c = t[1] + jnp.concatenate([none, t[0][:-step]], 0) + jnp.concatenate([t[2][step:], none], 0)
            conv_out[:, lanes] = c
            cact_out[:, lanes] = silu(c).astype(BF)

        chunks(ch // LANES, conv)
        for c in range(n):
            e = 0.0
            for q in range(n):
                cut = slice(q * share, (q + 1) * share)
                e = e + dot(cact_out[:, cut], w[c, share : 2 * share, cut])
            norm_out[:, c * share : (c + 1) * share] = e

        def norm(i, carry):
            at = pl.ds(pl.multiple_of(i * 16, 16), 16)
            e = norm_out[at, :]
            mean = jnp.mean(e, -1, keepdims=True)
            square = jnp.mean(e * e, -1, keepdims=True)
            std = lax.rsqrt(square - mean * mean + EPS)
            nrm = (e - mean) * std
            norm_out[at, :] = nrm
            std_out[at, :] = std
            low_out[at, :] = (wide_ref[at, :] + silu(nrm * gain)).astype(BF)
            return carry

        lax.fori_loop(0, total // 16, norm, 0)

    wide = shape((total, ch), F32)
    narrow = shape((total, ch), BF)
    return call(
        kernel,
        grid=(1,),
        prefetch=1,
        ins=[(a, None, None) for a in (*moved, weights, taps)],
        outs=[(s, None, None) for s in (narrow, wide, narrow, wide, narrow, wide, shape((total, 1), F32), narrow)],
        scratch=[pltpu.VMEM((total, ch), F32)],
        name="post_forward",
    )(source)


def post_backward(source, low, readout, cots, weights, taps, act, red, conv, nrm, std, pool):
    total, ch = low.shape
    n = cots.shape[0]
    share = ch // n
    out_share = cots.shape[2]
    rows = total // n
    depth = total // (pool * pool)

    def kernel(src, low_ref, ro, cot, w, tap, act_ref, red_ref, conv_ref, norm_ref, std_ref, exp_out, redg_out, taps_out, gain_out, *rest):
        back_out, (grad, cgrad) = rest[:n], rest[n:]
        k = pl.program_id(0)
        logits = dot(low_ref[...], ro[...])
        piece = (cot[0].astype(F32) * gelu_parts(logits)[1]).astype(BF)
        term = dot(piece, ro[...], NT)

        @pl.when(k == 0)
        def _():
            grad[...] = term

        @pl.when(k > 0)
        def _():
            grad[...] += term

        @pl.when(k == n - 1)
        def _():
            gain = gain_row(w, n, share)

            def norm(i, total_gain):
                at = pl.ds(pl.multiple_of(i * 16, 16), 16)
                nm = norm_ref[at, :]
                ng = grad[at, :] * silu_slope(nm * gain)
                sc = ng * gain
                one = jnp.mean(sc, -1, keepdims=True)
                two = jnp.mean(sc * nm, -1, keepdims=True)
                exp_out[at, :] = (std_ref[at, :] * (sc - one - nm * two)).astype(BF)
                g = ng * nm
                return total_gain + g[:8] + g[8:]

            gain_out[...] = lax.fori_loop(0, total // 16, norm, jnp.zeros((8, ch), F32))
            for q in range(n):
                cut = slice(q * share, (q + 1) * share)
                cg = 0.0
                for c in range(n):
                    cg = cg + dot(exp_out[:, c * share : (c + 1) * share], w[c, share : 2 * share, cut], NT)
                cgrad[:, cut] = cg
            first, last = edge_masks(total, pool, depth)
            step = pool * depth

            def back(lanes):
                g = (cgrad[:, lanes] * silu_slope(conv_ref[:, lanes])).astype(BF).astype(F32)
                x = act_ref[:, lanes].astype(F32)
                moves = [columns_moved(g, -depth, first, last), g, columns_moved(g, depth, first, last)]
                none = jnp.zeros((step, LANES), F32)
                xs = [
                    jnp.concatenate([none, x[:-step]], 0),
                    x,
                    jnp.concatenate([x[step:], none], 0),
                ]
                for a in range(3):
                    for b in range(3):
                        prod = xs[a] * moves[b]
                        taps_out[3 * a + b, :, lanes] = jnp.sum(prod.reshape(total // 8, 8, LANES), 0)
                t = [sum(moves[b] * tap[pl.ds(3 * a + b, 1), lanes] for b in range(3)) for a in range(3)]
                d = t[1] + jnp.concatenate([t[0][step:], none], 0) + jnp.concatenate([none, t[2][:-step]], 0)
                redg_out[:, lanes] = (d * silu_slope(red_ref[:, lanes])).astype(BF)

            chunks(ch // LANES, back)
            for c in range(n):
                cut = slice(c * share, (c + 1) * share)
                grad[:, cut] += dot(redg_out[...], w[c, :share], NT)
            for r in range(n):
                at = pl.ds(pl.multiple_of(src[r] * rows, 8), rows)
                back_out[r][...] = grad[at, :].astype(BF)

    return call(
        kernel,
        grid=(n,),
        prefetch=1,
        ins=[
            (low, None, None),
            (readout, (ch, out_share), lambda k, s: (0, k)),
            (cots, (1, total, out_share), lambda k, s: (k, 0, 0)),
        ]
        + [(a, None, None) for a in (weights, taps, act, red, conv, nrm, std)],
        outs=[
            (s, None, None)
            for s in (
                shape((total, ch), BF),
                shape((total, ch), BF),
                shape((9, 8, ch), F32),
                shape((8, ch), F32),
                *[shape((rows, ch), BF)] * n,
            )
        ],
        scratch=[pltpu.VMEM((total, ch), F32), pltpu.VMEM((total, ch), F32)],
        name="post_backward",
    )(source)


def cotangent_by_image(cotangent, select):
    rows, width = cotangent.shape
    size = select.shape[0]
    pairs = SLOT
    each = size // pairs
    per = 3

    def kernel(x, sel, out):
        for q in range(per):
            y = dot(sel[...], x[pl.ds(q * size, size), :]).astype(BF)
            for s in range(pairs):
                out[s, pl.ds(q * each, each), :] = y[s * each : (s + 1) * each]

    return call(
        kernel,
        grid=(rows // (per * size),),
        ins=[(cotangent, (per * size, width), lambda i: (i, 0)), (select, None, None)],
        outs=[(shape((pairs, rows // pairs, width), BF), (pairs, per * each, width), lambda i: (0, i, 0))],
        name="cotangent_by_image",
    )()[0]


def token_block(chan, source, low, place, readout, cotangent, live):
    pairs, ch = len(low), low[0].shape[1]
    rows, width = cotangent.shape
    size = place.shape[0]
    each = size // pairs
    per = 3

    def kernel(chan_ref, src, *refs):
        lows, (place_ref, ro, cot, alive, tok_out, piece_out, low_out, by_pair) = refs[:pairs], refs[pairs:]
        for k in range(pairs):
            by_pair[src[k]] = lows[k][...]
        for q in range(per):
            at = pl.ds(q * size, size)
            x = jnp.concatenate([by_pair[s, pl.ds(q * each, each), :] for s in range(pairs)], 0)
            low_out[at, :] = dot(place_ref[...], x).astype(BF)
        logits = dot(low_out[...], ro[...])
        value, slope = gelu_parts(logits)
        tok_out[...] = value.astype(BF)
        piece_out[...] = (cot[...].astype(F32) * alive[...] * slope).astype(BF)

    block = per * size
    row_block = lambda i, c, s: (i, 0)
    return call(
        kernel,
        grid=(rows // block,),
        prefetch=2,
        ins=[
            *[(v, (per * each, ch), lambda i, c, s: (i, 0)) for v in low],
            (place, None, None),
            (readout, (ch, width), lambda i, c, s: (0, c[0])),
            (cotangent, (block, width), row_block),
            (live, None, None),
        ],
        outs=[
            (shape((rows, width), BF), (block, width), row_block),
            (shape((rows, width), BF), (block, width), row_block),
            (shape((rows, ch), BF), (block, ch), row_block),
        ],
        scratch=[pltpu.VMEM((pairs, per * each, ch), BF)],
        name="token_block",
    )(chan, source)


def pre_backward(order, returned, spread_up, nrm, std, gain, conv, pre_expand):
    slots, cells, ch = nrm.shape
    n = order.shape[0]
    part = slots // n
    wide = 24
    rows = part * cells

    def kernel(order_ref, *refs):
        ret, refs = refs[:n], refs[n:]
        up, norm_ref, std_ref, gn, conv_ref, we, exp_out, conv_grad_out, top_out, bottom_out, gain_out, grad, cgrad = refs
        k = pl.program_id(0)
        for i in range(n):

            @pl.when(k == i)
            def _():
                grad[...] = dot(up[...], ret[i][...])

        def norm(i, total_gain):
            u, j = i // (cells // 16), i % (cells // 16)
            at = pl.ds(pl.multiple_of(j * 16, 16), 16)
            nm = norm_ref[u, at, :]
            ng = grad[pl.ds(pl.multiple_of(i * 16, 16), 16), :] * silu_slope(nm * gn[...])
            sc = ng * gn[...]
            one = jnp.mean(sc, -1, keepdims=True)
            two = jnp.mean(sc * nm, -1, keepdims=True)
            exp_out[u, at, :] = (std_ref[u, at, :] * (sc - one - nm * two)).astype(BF)
            g = ng * nm
            return total_gain + g[:8] + g[8:]

        gains = lax.fori_loop(0, rows // 16, norm, jnp.zeros((8, ch), F32))

        @pl.when(k == 0)
        def _():
            gain_out[...] = gains

        @pl.when(k > 0)
        def _():
            gain_out[...] += gains

        cgrad[...] = dot(exp_out[...].reshape(rows, ch), we[...], NT)
        for u in range(part):

            def slope(lanes):
                g = cgrad[pl.ds(u * cells, cells), lanes] * silu_slope(conv_ref[u, :, lanes])
                conv_grad_out[u, :, lanes] = g.astype(BF)
                top_out[u, :, lanes] = g[:wide].astype(BF)
                bottom_out[u, :, lanes] = g[cells - wide :].astype(BF)

            chunks(ch // LANES, slope)

    by_order = lambda k, order: (order[k], 0, 0)
    whole = (part, cells, ch)
    edge = (part, wide, ch)
    return call(
        kernel,
        grid=(n,),
        prefetch=1,
        ins=[
            *[(r, None, None) for r in returned],
            (spread_up, None, None),
            (nrm, whole, by_order),
            (std, (part, cells, 1), by_order),
            (gain, None, None),
            (conv, whole, by_order),
            (pre_expand, None, None),
        ],
        outs=[
            (shape((slots, cells, ch), BF), whole, by_order),
            (shape((slots, cells, ch), BF), whole, by_order),
            (shape((slots, wide, ch), BF), edge, by_order),
            (shape((slots, wide, ch), BF), edge, by_order),
            (shape((8, ch), F32), None, None),
        ],
        scratch=[pltpu.VMEM((rows, ch), F32), pltpu.VMEM((rows, ch), F32)],
        name="pre_backward",
    )(order)


def pre_conv_backward(conv_grad, above, below, reduced, taps):
    slots, cells, ch = reduced.shape
    wide = above.shape[1]
    high = cells // wide

    def kernel(cg, up, down, red, tap, redg_out, taps_out):
        step = pl.program_id(0)
        first, last = edge_masks(wide, wide, 1)

        @pl.when(step == 0)
        def _():
            taps_out[...] = jnp.zeros_like(taps_out)

        def back(lanes):
            w = [tap[pl.ds(i, 1), lanes] for i in range(9)]
            mid = cg[0, :, lanes].astype(F32)
            rows = [up[0, :, lanes].astype(F32)]
            rows += [mid[i * wide : (i + 1) * wide] for i in range(high)]
            rows += [down[0, :, lanes].astype(F32)]
            v = [red[0, pl.ds(i * wide, wide), lanes] for i in range(high)]
            s = [sigmoid(t) for t in v]
            x = [(a * b).astype(BF).astype(F32) for a, b in zip(v, s)]
            d = [0.0] * high
            sums = [0.0] * 9
            for p in range(high + 2):
                g = rows[p]
                moves = [columns_moved(g, -1, first, last), g, columns_moved(g, 1, first, last)]
                for a in range(3):
                    i = p - 1 + a - 1
                    if 0 <= i < high:
                        for b in range(3):
                            d[i] = d[i] + moves[b] * w[3 * a + b]
                            prod = x[i] * moves[b]
                            sums[3 * a + b] = sums[3 * a + b] + (prod[:8] + prod[8:16] + prod[16:])
            out = [d[i] * (s[i] * (1.0 + v[i] * (1.0 - s[i]))) for i in range(high)]
            redg_out[0, :, lanes] = jnp.concatenate(out, 0).astype(BF)
            for i in range(9):
                taps_out[i, :, lanes] += sums[i]

        chunks(ch // LANES, back)

    image = lambda i: (i, 0, 0)
    return call(
        kernel,
        grid=(slots,),
        ins=[
            (conv_grad, (1, cells, ch), image),
            (above, (1, wide, ch), image),
            (below, (1, wide, ch), image),
            (reduced, (1, cells, ch), image),
            (taps, None, None),
        ],
        outs=[
            (shape((slots, cells, ch), BF), (1, cells, ch), image),
            (shape((9, 8, ch), F32), None, None),
        ],
        name="pre_conv_backward",
    )()


def feature_backward(order, reduced_grad, pre_reduce, returned, spread_up):
    slots, cells, ch = reduced_grad.shape
    n = order.shape[0]
    part = slots // n

    def kernel(order_ref, rg, wr, up, *refs):
        ret, out = refs[:n], refs[n]
        k = pl.program_id(0)
        for i in range(n):

            @pl.when(k == i)
            def _():
                out[...] = dot(up[...], ret[i][...]).reshape(part, cells, ch)

        out[...] += dot(rg[...].reshape(part * cells, ch), wr[...], NT).reshape(part, cells, ch)

    by_order = lambda k, order: (order[k], 0, 0)
    whole = (part, cells, ch)
    return call(
        kernel,
        grid=(n,),
        prefetch=1,
        ins=[
            (reduced_grad, whole, by_order),
            (pre_reduce, None, None),
            (spread_up, None, None),
            *[(r, None, None) for r in returned],
        ],
        outs=[(shape((slots, cells, ch), F32), whole, by_order)],
        name="feature_backward",
    )(order)[0]


def post_weight_grads(flat, reduced_grad, act, expanded_grad, n):
    total, ch = flat.shape
    share = ch // n

    def kernel(x, g, a, e, out):
        for c in range(n):
            cut = slice(c * share, (c + 1) * share)
            out[c, :, :ch] = dot(x[:, cut], g[...], TN).astype(BF)
            for q in range(n):
                rows = slice(q * share, (q + 1) * share)
                out[c, :, ch + q * share : ch + (q + 1) * share] = dot(a[:, rows], e[:, cut], TN).astype(BF)

    return call(
        kernel,
        grid=(1,),
        ins=[(v, None, None) for v in (flat, reduced_grad, act, expanded_grad)],
        outs=[(shape((n, share, 2 * ch), BF), None, None)],
        name="post_weight_grads",
    )()[0]


def spread(n, k):
    return [(a * n + b, b * n + (a + k) % n) for a in range(n) for b in range(n)]


def other_core(values):
    return lax.ppermute(values, "core", [(0, 1), (1, 0)])


def small_rows(*grads):
    ch = grads[0].shape[-1]
    counts = [g.shape[0] if g.ndim == 3 else 1 for g in grads]
    per = ch // LANES

    def kernel(*refs):
        out = refs[-1]
        at = 0
        for ref, count in zip(refs, counts):
            for i in range(count):
                v = jnp.sum(ref[i] if len(ref.shape) == 3 else ref[...], 0, keepdims=True)
                for q in range(per):
                    out[pl.ds(at, 1), :] = v[:, q * LANES : (q + 1) * LANES]
                    at += 1

    return call(
        kernel,
        grid=(1,),
        ins=[(g, None, None) for g in grads],
        outs=[(shape((sum(counts) * per, LANES), F32), None, None)],
        name="small_rows",
    )()[0]


def join_halves(core, mine, theirs, small, their_small, parts):
    rows, ch = mine[0].shape
    half = rows // 2
    width = len(mine) * ch + LANES
    count = small.shape[0]
    m = len(mine)

    def kernel(core_ref, *refs):
        own, got = refs[:m], refs[m : 2 * m]
        sm, got_sm, out = refs[2 * m :]
        for i in range(m):
            out[:, i * ch : (i + 1) * ch] = (own[i][...].astype(F32) + got[i][...].astype(F32)).astype(BF)
        first = (core_ref[0] == 0).astype(F32)
        total = (sm[...] + got_sm[...]) * first
        pad = jnp.zeros((half - count, LANES), F32)
        out[:, m * ch :] = jnp.concatenate([total, pad], 0).astype(BF)

    return call(
        kernel,
        grid=(1,),
        prefetch=1,
        ins=[(v, (half, ch), lambda i, c: (c[0], 0)) for v in mine]
        + [(v, None, None) for v in (*theirs, small, their_small)],
        outs=[(shape((half, width), BF), None, None)],
        name="join_halves",
    )(core)[0].reshape(parts, half // parts, width)


def sum_and_copy(blocks):
    parts, rows, width = blocks.shape

    def kernel(x, out):
        def cut(lanes):
            total = jnp.sum(x[:, :, lanes].astype(F32), 0).astype(BF)
            out[:, :, lanes] = jnp.broadcast_to(total[None], (parts, rows, LANES))

        chunks(width // LANES, cut)

    return call(
        kernel,
        grid=(1,),
        ins=[(blocks, None, None)],
        outs=[(shape(blocks.shape, BF), None, None)],
        name="sum_and_copy",
    )()[0]


def finish_pre(core, own, got, ch):
    half, width = own.shape
    m = (width - LANES) // ch

    def kernel(core_ref, a, b, *outs):
        h = pl.program_id(0)

        def write(ref):
            for i in range(m):
                outs[i][...] = ref[:, i * ch : (i + 1) * ch].astype(F32)

            @pl.when(h == 0)
            def _():
                outs[m][...] = ref[:, m * ch :].astype(F32)

        @pl.when(h == core_ref[0])
        def _():
            write(a)

        @pl.when(h != core_ref[0])
        def _():
            write(b)

    return call(
        kernel,
        grid=(2,),
        prefetch=1,
        ins=[(own, None, None), (got, None, None)],
        outs=[(shape((2 * half, ch), F32), (half, ch), lambda h, c: (h, 0)) for _ in range(m)]
        + [(shape((half, LANES), F32), None, None)],
        name="finish_pre",
    )(core)


def finish_post(gathered, n, share):
    groups, rows, ch = gathered.shape
    eight = share // groups
    per = 4

    def kernel(x, reduce_out, expand_out, read_out):
        for g in range(per):
            at = pl.ds(g * eight, eight)
            v = x[g].astype(F32)
            reduce_out[at, :] = v[:eight]
            for q in range(n):
                expand_out[q, at, :] = v[eight : 2 * eight, q * share : (q + 1) * share]
                read_out[at, q * ch : (q + 1) * ch] = v[(2 + q) * eight : (3 + q) * eight]

    return call(
        kernel,
        grid=(groups // per,),
        ins=[(gathered, (per, rows, ch), lambda i: (i, 0, 0))],
        outs=[
            (shape((share, ch), F32), (per * eight, ch), lambda i: (i, 0)),
            (shape((n, share, share), F32), (n, per * eight, share), lambda i: (0, i, 0)),
            (shape((share, n * ch), F32), (per * eight, n * ch), lambda i: (i, 0)),
        ],
        name="finish_post",
    )()


def after(values, *earlier):
    return lax.optimization_barrier((values, *earlier))[0]


def pool_matrix(part, high, wide):
    half = wide // 2
    m = np.zeros((high // 2 * half * part, part * (high // 2) * wide), np.float32)
    for u in range(part):
        for i in range(high // 2):
            for j in range(wide):
                m[(i * half + j // 2) * part + u, (u * (high // 2) + i) * wide + j] = 0.25
    return m


def spread_matrix(part, high, wide):
    half = wide // 2
    m = np.zeros((part * high * wide, high // 2 * half * part), np.float32)
    for u in range(part):
        for i in range(high):
            for j in range(wide):
                m[(u * high + i) * wide + j, ((i // 2) * half + j // 2) * part + u] = 0.25
    return m


def place_matrix(cells, slots, pairs):
    per = slots // pairs
    m = np.zeros((cells * slots, cells * slots), np.float32)
    for c in range(cells):
        for s in range(slots):
            m[c * slots + s, (s // per) * cells * per + c * per + s % per] = 1.0
    return m


def body(features, counts, pre_reduce, pre_conv, pre_expand, pre_gain, post_reduce, post_conv, post_expand, post_gain, readout, cotangent):
    n = lax.axis_size("chan")
    row = lax.axis_index("rows").astype(jnp.int32)
    chan = lax.axis_index("chan").astype(jnp.int32)
    core = lax.axis_index("core").astype(jnp.int32)
    eighth = lax.axis_index(("x", "core"))
    ch = pre_reduce.shape[0]
    slots, high, wide = features.shape[0], features.shape[1], features.shape[2]
    part = slots // n
    cells = high * wide
    pool = wide // 2
    share = ch // n
    out_share = cotangent.shape[3]
    steps = jnp.arange(n, dtype=jnp.int32)
    order = (row + steps) % n
    source = (chan - steps) % n
    rank = jnp.full((1,), chan, jnp.int32)
    core_at = jnp.full((1,), core, jnp.int32)
    pre_taps = pre_conv.astype(F32).reshape(9, ch)
    post_taps = post_conv.astype(F32).reshape(9, ch)
    pre_gain_row = pre_gain.reshape(1, ch)
    pool_m = jnp.asarray(pool_matrix(part, high, wide), BF)
    up_m = jnp.asarray(spread_matrix(part, high, wide), BF)
    place = jnp.asarray(place_matrix(16, slots, n), BF)

    ends = n - 1
    down_pairs = [(i, i + 1) for i in range(ends)]
    up_pairs = [(i + 1, i) for i in range(ends)]
    above = lax.ppermute(features[:, -1], "rows", down_pairs)
    below = lax.ppermute(features[:, 0], "rows", up_pairs)
    gain_hi = post_gain.astype(BF)
    gain_lo = (post_gain - gain_hi.astype(F32)).astype(BF)
    gain_row = jnp.concatenate([gain_hi, gain_lo, jnp.zeros((ch - 2 * share,), BF)])[None]
    square = post_expand.reshape(n, share, share)
    shards = jnp.concatenate(
        [post_reduce, jnp.concatenate([square[q] for q in range(n)], axis=1), jnp.pad(gain_row, ((0, 63), (0, 0)))], axis=0
    )
    eighths = shards.reshape(8, -1, ch)
    full = lax.all_gather(lax.dynamic_index_in_dim(eighths, eighth, 0, keepdims=False), ("chan", "x", "core"), axis=0, tiled=True)
    full = full.reshape(n, 2 * share + 64, ch)
    live = (jnp.arange(SLOT)[None, :] < counts[:, None]).astype(F32).reshape(slots)
    select = place.T * jnp.tile(live.astype(BF), 16)[None, :]
    cot_rows = cotangent.transpose(1, 2, 0, 3).reshape(-1, out_share)
    cots = lax.all_to_all(cotangent_by_image(cot_rows, select), "chan", 0, 0, tiled=False)

    flat_features = features.reshape(slots * cells, ch)
    reduced = dot(flat_features, pre_reduce).reshape(slots, cells, ch)
    convolved, convolved_act, normal_pre, pre_std, *pooled = pre_forward(
        order, reduced, above, below, features, pre_reduce, pre_taps, pre_expand, pre_gain_row, pool_m
    )

    moved = [lax.ppermute(pooled[k], ("rows", "chan"), spread(n, k)) for k in range(n)]
    flat, post_reduced, post_act, post_convolved, post_cact, post_normal, post_std, low = post_forward(
        source, moved, full, post_taps, pool
    )
    lows = [low] + [lax.ppermute(low, "chan", [(i, (i + k) % n) for i in range(n)]) for k in range(1, n)]
    post_expanded_grad, post_reduced_grad, post_taps_grad, post_gain_grad, *back = post_backward(
        source, low, readout, cots, full, post_taps, post_act, post_reduced, post_convolved, post_normal, post_std, pool
    )

    returned = [lax.ppermute(back[k], ("rows", "chan"), [(d, s) for s, d in spread(n, k)]) for k in range(n)]

    post_load = post_weight_grads(flat, post_reduced_grad, post_cact, post_expanded_grad, n)
    post_sum = lax.psum_scatter(post_load, "chan", scatter_dimension=0, tiled=False)

    alive = jnp.broadcast_to(jnp.tile(live, 48)[:, None], (48 * slots, 1))
    lows = after(lows, post_load)
    tokens, piece, low_here = token_block(rank, source, lows, place, readout, cot_rows, alive)
    readout_grad = dot(low_here, piece, TN).astype(BF)
    tokens = tokens.reshape(pool, pool, slots, out_share).transpose(2, 0, 1, 3)

    returned = after(returned, readout_grad)
    expanded_grad, convolved_grad, top, bottom, pre_gain_grad = pre_backward(
        order, returned, up_m, normal_pre, pre_std, pre_gain_row, convolved, pre_expand
    )
    grad_above = lax.ppermute(bottom, "rows", down_pairs)
    grad_below = lax.ppermute(top, "rows", up_pairs)

    eight = share // 32
    read_rows = after(readout_grad, bottom).reshape(n, 8, 4, eight, out_share).transpose(1, 2, 0, 3, 4)
    load = jnp.concatenate(
        [
            post_sum[:, :ch].reshape(8, 4, eight, ch),
            post_sum[:, ch:].reshape(8, 4, eight, ch),
            read_rows.reshape(8, 4, n * eight, out_share),
        ],
        axis=2,
    )
    load = lax.psum_scatter(load, ("x", "core"), scatter_dimension=0, tiled=False)
    load = lax.psum_scatter(load, "rows", scatter_dimension=0, tiled=False)
    read_part = lax.all_to_all(load[2 * eight :].reshape(n, eight, out_share), "chan", 0, 0, tiled=False)
    load = jnp.concatenate([load[: 2 * eight], read_part.reshape(n * eight, out_share)], axis=0)
    gathered = lax.all_gather(load, ("x", "core", "rows"), axis=0, tiled=False)
    post_reduce_out, post_expand_out, readout_out = finish_post(gathered, n, share)

    act_rows = after(convolved_act, bottom).reshape(-1, ch)
    pre_expand_grad = dot(act_rows, expanded_grad.reshape(-1, ch), TN).astype(BF)
    convolved_grad = after(convolved_grad, pre_expand_grad)
    reduced_grad, pre_taps_grad = pre_conv_backward(convolved_grad, grad_above, grad_below, reduced, pre_taps)
    pre_reduce_grad = dot(flat_features, reduced_grad.reshape(-1, ch), TN).astype(BF)
    feature_grad = feature_backward(order, after(reduced_grad, pre_reduce_grad), pre_reduce, returned, up_m).reshape(features.shape)

    small = small_rows(pre_taps_grad, pre_gain_grad, post_taps_grad, post_gain_grad)
    mine = [pre_reduce_grad, pre_expand_grad]
    theirs = [other_core(lax.dynamic_index_in_dim(g.reshape(2, ch // 2, ch), 1 - core, 0, keepdims=False)) for g in mine]
    load = join_halves(core_at, mine, theirs, small, other_core(small), 64)
    chips = ("x", "rows", "chan")
    load = sum_and_copy(lax.all_to_all(load, chips, 0, 0, tiled=False))
    load = lax.all_to_all(load, chips, 0, 0, tiled=False).reshape(ch // 2, -1)
    pre_reduce_out, pre_expand_out, small_out = finish_pre(core_at, load, other_core(load), ch)
    per = ch // LANES
    cut = [0, 9 * per, 10 * per, 19 * per, 20 * per]
    pre_conv_out, pre_gain_out, post_conv_out, post_gain_out = [small_out[a:b] for a, b in zip(cut, cut[1:])]
    return (
        tokens,
        feature_grad,
        pre_reduce_out,
        pre_conv_out.reshape(3, 3, ch),
        pre_expand_out,
        pre_gain_out.reshape(ch),
        post_reduce_out,
        post_conv_out.reshape(3, 3, ch),
        post_expand_out.reshape(ch, share),
        lax.dynamic_slice_in_dim(post_gain_out.reshape(ch), chan * share, share, 0),
        readout_out,
    )


def solution(mesh):
    grid = Mesh(mesh.devices.reshape(4, 2, 4, 4), ("x", "core", "rows", "chan"))
    images = P(("x", "core", "chan"), "rows", None, None)
    grids = P(("x", "core", "rows"), None, None, "chan")
    return jax.shard_map(
        body,
        mesh=grid,
        in_specs=(
            images,
            P(("x", "core", "rows")),
            P(),
            P(),
            P(),
            P(),
            P("chan", None),
            P(),
            P(None, "chan"),
            P("chan"),
            P(),
            grids,
        ),
        out_specs=(grids, images, P(), P(), P(), P(), P("chan", None), P(), P(None, "chan"), P("chan"), P("chan", None)),
        check_vma=False,
    )
```

```python
import functools

import jax
import jax.numpy as jnp
import numpy as np
from jax import lax
from jax.experimental import pallas as pl
from jax.experimental.pallas import tpu as pltpu
from jax.sharding import Mesh, PartitionSpec as P

SLOT = 4
EPS = 1e-06
BF = jnp.bfloat16
F32 = jnp.float32
LANES = 128
VMEM_LIMIT = 56 * 1024 * 1024
NN = ((1,), (0,))
NT = ((1,), (1,))
TN = ((0,), (0,))


def dot(a, b, dims=NN):
    return lax.dot_general(a, b, (dims, ((), ())), preferred_element_type=F32)


def sigmoid(v):
    return 0.5 * jnp.tanh(0.5 * v) + 0.5


def silu(v):
    return v * sigmoid(v)


def silu_slope(v):
    s = sigmoid(v)
    return s * (1.0 + v * (1.0 - s))


def gelu_parts(v):
    c = 0.7978845608028654
    square = v * v
    t = jnp.tanh(v * (c + (c * 0.044715) * square))
    half = 0.5 * (1.0 + t)
    slope = half + 0.5 * v * (1.0 - t * t) * (c + (3.0 * c * 0.044715) * square)
    return v * half, slope


def chunks(count, body, width=LANES):
    def step(i, carry):
        body(pl.ds(pl.multiple_of(i * width, width), width))
        return carry

    lax.fori_loop(0, count, step, 0)


def call(kernel, *, grid, ins, outs, scratch=(), prefetch=0, aliased=(), cost=1, name):
    def spec(shape, block, index):
        if block is None:
            block, index = shape, lambda *_: (0,) * len(shape)
        return pl.BlockSpec(block, index)

    arrays = [i[0] for i in ins] + list(aliased)
    in_specs = [spec(a.shape, b, m) for a, b, m in ins] + [pl.BlockSpec(memory_space=pl.ANY)] * len(aliased)
    out_specs = [spec(s.shape, b, m) for s, b, m in outs]

    def run(*scalars):
        return pl.pallas_call(
            kernel,
            grid_spec=pltpu.PrefetchScalarGridSpec(
                num_scalar_prefetch=prefetch,
                grid=grid,
                in_specs=in_specs,
                out_specs=out_specs,
                scratch_shapes=list(scratch),
            ),
            out_shape=[s[0] for s in outs],
            compiler_params=pltpu.CompilerParams(
                dimension_semantics=("arbitrary",) * len(grid), vmem_limit_bytes=VMEM_LIMIT
            ),
            input_output_aliases={prefetch + len(ins) + i: i for i in range(len(aliased))},
            cost_estimate=pl.CostEstimate(flops=cost, bytes_accessed=1, transcendentals=0),
            name=name,
        )(*scalars, *arrays)

    return run


def shape(dims, dtype):
    return jax.ShapeDtypeStruct(dims, dtype)


def columns_moved(t, by, first, last):
    rows = t.shape[0]
    return pltpu.roll(t, by % rows, 0) * (first if by > 0 else last)


def edge_masks(rows, width, depth):
    at = lax.broadcasted_iota(jnp.int32, (rows, LANES), 0) % (width * depth)
    return (at >= depth).astype(F32), (at < (width - 1) * depth).astype(F32)


def pre_forward(order, above, below, features, pre_reduce, taps, pre_expand, gain, pool, earlier=()):
    slots, high, wide, ch = features.shape
    cells = high * wide
    n = order.shape[0]
    part = 2

    def kernel(order_ref, up_ref, down_ref, feat, wr, tap, we, gn, pool_ref, *rest):
        red, conv_out, act_out, norm_out, std_out, *rest = rest[len(earlier) :]
        pooled_out, (halo, exp, sums) = rest[:n], rest[n:]
        k = pl.program_id(0)
        red[...] = dot(feat[...].reshape(part * cells, ch), wr[...]).reshape(part, cells, ch)
        for side, ref in enumerate((up_ref, down_ref)):
            halo[side] = dot(ref[...].reshape(part * wide, ch), wr[...]).reshape(part, wide, ch)
        first, last = edge_masks(wide, wide, 1)
        for u in range(part):

            def conv(lanes):
                w = [tap[pl.ds(i, 1), lanes] for i in range(9)]
                rows = [halo[0, u, :, lanes]]
                rows += [red[u, pl.ds(i * wide, wide), lanes] for i in range(high)]
                rows += [halo[1, u, :, lanes]]
                rows = [silu(r).astype(BF).astype(F32) for r in rows]
                acts = []
                for i in range(high):
                    t = [sum(rows[i + a] * w[3 * a + b] for a in range(3)) for b in range(3)]
                    c = t[1] + columns_moved(t[0], 1, first, last) + columns_moved(t[2], -1, first, last)
                    conv_out[u, pl.ds(i * wide, wide), lanes] = c
                    acts.append(silu(c))
                act_out[u, :, lanes] = jnp.concatenate(acts, 0).astype(BF)

            chunks(ch // LANES, conv)

        exp[...] = dot(act_out[...].reshape(part * cells, ch), we[...])

        def norm(p, carry):
            u, i = p // (high // 2), p % (high // 2)
            total = [0.0] * (wide // 8)
            for half in range(2):
                f = feat[u, 2 * i + half].astype(F32)
                for t in range(wide // 8):
                    row = (2 * i + half) * wide + 8 * t
                    e = exp[pl.ds(pl.multiple_of(u * cells + row, 8), 8), :]
                    mean = jnp.mean(e, -1, keepdims=True)
                    square = jnp.mean(e * e, -1, keepdims=True)
                    std = lax.rsqrt(square - mean * mean + EPS)
                    nrm = (e - mean) * std
                    norm_out[u, pl.ds(pl.multiple_of(row, 8), 8), :] = nrm
                    std_out[u, pl.ds(pl.multiple_of(row, 8), 8), :] = std
                    total[t] = total[t] + f[8 * t : 8 * t + 8] + silu(nrm * gn[...])
            for t in range(wide // 8):
                sums[pl.ds(pl.multiple_of(p * wide + 8 * t, 8), 8), :] = total[t]
            return carry

        lax.fori_loop(0, part * high // 2, norm, 0)
        s = sums[...]
        hi = s.astype(BF)
        lo = (s - hi.astype(F32)).astype(BF)
        pooled = (dot(pool_ref[...], hi) + dot(pool_ref[...], lo)).astype(BF)
        for i in range(n):

            @pl.when(k == i)
            def _():
                pooled_out[i][...] = pooled

    def by_order(rest):
        return lambda k, order: (order[k],) + (0,) * rest

    pooled_rows = pool.shape[0]
    block = (part, cells, ch)
    return call(
        kernel,
        grid=(n,),
        prefetch=1,
        ins=[
            (above, (part, wide, ch), by_order(2)),
            (below, (part, wide, ch), by_order(2)),
            (features, (part, high, wide, ch), by_order(3)),
            (pre_reduce, None, None),
            (taps, None, None),
            (pre_expand, None, None),
            (gain, None, None),
            (pool, None, None),
        ],
        outs=[
            (shape((slots, cells, ch), F32), block, by_order(2)),
            (shape((slots, cells, ch), F32), block, by_order(2)),
            (shape((slots, cells, ch), BF), block, by_order(2)),
            (shape((slots, cells, ch), F32), block, by_order(2)),
            (shape((slots, cells, 1), F32), (part, cells, 1), by_order(2)),
        ]
        + [(shape((pooled_rows, ch), BF), None, None)] * n,
        scratch=[
            pltpu.VMEM((2, part, wide, ch), F32),
            pltpu.VMEM((part * cells, ch), F32),
            pltpu.VMEM((part * cells // 2, ch), F32),
        ],
        aliased=earlier,
        name="pre_forward",
    )(order)


def gain_row(w, n, share):
    at = 2 * share
    parts = [w[c, at : at + 16, :].astype(F32)[:1] for c in range(n)]
    return jnp.concatenate([p[:, :share] + p[:, share : 2 * share] for p in parts], 1)


def post_forward(source, moved, weights, taps, pool):
    n, (rows, ch) = len(moved), moved[0].shape
    total = n * rows
    depth = total // (pool * pool)
    share = ch // n

    def kernel(src, *refs):
        got, (w, tap, flat_out, red_out, act_out, conv_out, cact_out, norm_out, std_out, low_out, wide_ref) = refs[:n], refs[n:]
        for k in range(n):
            at = pl.multiple_of(src[k] * rows, 8)
            wide_ref[pl.ds(at, rows), :] = got[k][...].astype(F32)
        gain = gain_row(w, n, share)
        flat_out[...] = wide_ref[...].astype(BF)
        red = 0.0
        for c in range(n):
            red = red + dot(flat_out[:, c * share : (c + 1) * share], w[c, :share])
        red_out[...] = red
        first, last = edge_masks(total, pool, depth)
        step = pool * depth

        def conv(lanes):
            x = silu(red_out[:, lanes]).astype(BF)
            act_out[:, lanes] = x
            x = x.astype(F32)
            moves = [columns_moved(x, depth, first, last), x, columns_moved(x, -depth, first, last)]
            t = [sum(moves[b] * tap[pl.ds(3 * a + b, 1), lanes] for b in range(3)) for a in range(3)]
            none = jnp.zeros((step, LANES), F32)
            c = t[1] + jnp.concatenate([none, t[0][:-step]], 0) + jnp.concatenate([t[2][step:], none], 0)
            conv_out[:, lanes] = c
            cact_out[:, lanes] = silu(c).astype(BF)

        chunks(ch // LANES, conv)
        for c in range(n):
            e = 0.0
            for q in range(n):
                cut = slice(q * share, (q + 1) * share)
                e = e + dot(cact_out[:, cut], w[c, share : 2 * share, cut])
            norm_out[:, c * share : (c + 1) * share] = e

        def norm(i, carry):
            at = pl.ds(pl.multiple_of(i * 16, 16), 16)
            e = norm_out[at, :]
            mean = jnp.mean(e, -1, keepdims=True)
            square = jnp.mean(e * e, -1, keepdims=True)
            std = lax.rsqrt(square - mean * mean + EPS)
            nrm = (e - mean) * std
            norm_out[at, :] = nrm
            std_out[at, :] = std
            low_out[at, :] = (wide_ref[at, :] + silu(nrm * gain)).astype(BF)
            return carry

        lax.fori_loop(0, total // 16, norm, 0)

    wide = shape((total, ch), F32)
    narrow = shape((total, ch), BF)
    return call(
        kernel,
        grid=(1,),
        prefetch=1,
        ins=[(a, None, None) for a in (*moved, weights, taps)],
        outs=[(s, None, None) for s in (narrow, wide, narrow, wide, narrow, wide, shape((total, 1), F32), narrow)],
        scratch=[pltpu.VMEM((total, ch), F32)],
        name="post_forward",
    )(source)


def readout_backward(low, readout, cots):
    total, ch = low.shape
    n, _, out_share = cots.shape

    def kernel(low_ref, ro, cot, grad):
        k = pl.program_id(0)
        logits = dot(low_ref[...], ro[...])
        piece = (cot[0].astype(F32) * gelu_parts(logits)[1]).astype(BF)
        term = dot(piece, ro[...], NT)

        @pl.when(k == 0)
        def _():
            grad[...] = term

        @pl.when(k > 0)
        def _():
            grad[...] += term

    return call(
        kernel,
        grid=(n,),
        ins=[
            (low, None, None),
            (readout, (ch, out_share), lambda k: (0, k)),
            (cots, (1, total, out_share), lambda k: (k, 0, 0)),
        ],
        outs=[(shape((total, ch), F32), None, None)],
        name="readout_backward",
    )()[0]


def post_backward(source, refined_grad, weights, taps, act, red, conv, nrm, std, pool):
    total, ch = act.shape
    n = weights.shape[0]
    share = ch // n
    rows = total // n
    depth = total // (pool * pool)

    def kernel(src, rg, w, tap, act_ref, red_ref, conv_ref, norm_ref, std_ref, exp_out, redg_out, taps_out, gain_out, *rest):
        back_out, (grad, cgrad) = rest[:n], rest[n:]
        gain = gain_row(w, n, share)

        def norm(i, total_gain):
            at = pl.ds(pl.multiple_of(i * 16, 16), 16)
            nm = norm_ref[at, :]
            ng = rg[at, :] * silu_slope(nm * gain)
            sc = ng * gain
            one = jnp.mean(sc, -1, keepdims=True)
            two = jnp.mean(sc * nm, -1, keepdims=True)
            exp_out[at, :] = (std_ref[at, :] * (sc - one - nm * two)).astype(BF)
            g = ng * nm
            return total_gain + g[:8] + g[8:]

        gain_out[...] = lax.fori_loop(0, total // 16, norm, jnp.zeros((8, ch), F32))
        for q in range(n):
            cut = slice(q * share, (q + 1) * share)
            cg = 0.0
            for c in range(n):
                cg = cg + dot(exp_out[:, c * share : (c + 1) * share], w[c, share : 2 * share, cut], NT)
            cgrad[:, cut] = cg
        first, last = edge_masks(total, pool, depth)
        step = pool * depth

        def back(lanes):
            g = (cgrad[:, lanes] * silu_slope(conv_ref[:, lanes])).astype(BF).astype(F32)
            x = act_ref[:, lanes].astype(F32)
            moves = [columns_moved(g, -depth, first, last), g, columns_moved(g, depth, first, last)]
            none = jnp.zeros((step, LANES), F32)
            xs = [
                jnp.concatenate([none, x[:-step]], 0),
                x,
                jnp.concatenate([x[step:], none], 0),
            ]
            for a in range(3):
                for b in range(3):
                    prod = xs[a] * moves[b]
                    taps_out[3 * a + b, :, lanes] = jnp.sum(prod.reshape(total // 8, 8, LANES), 0)
            t = [sum(moves[b] * tap[pl.ds(3 * a + b, 1), lanes] for b in range(3)) for a in range(3)]
            d = t[1] + jnp.concatenate([t[0][step:], none], 0) + jnp.concatenate([none, t[2][:-step]], 0)
            redg_out[:, lanes] = (d * silu_slope(red_ref[:, lanes])).astype(BF)

        chunks(ch // LANES, back)
        for c in range(n):
            cut = slice(c * share, (c + 1) * share)
            grad[:, cut] = rg[:, cut] + dot(redg_out[...], w[c, :share], NT)
        for r in range(n):
            at = pl.ds(pl.multiple_of(src[r] * rows, 8), rows)
            back_out[r][...] = grad[at, :].astype(BF)

    return call(
        kernel,
        grid=(1,),
        prefetch=1,
        ins=[(a, None, None) for a in (refined_grad, weights, taps, act, red, conv, nrm, std)],
        outs=[
            (s, None, None)
            for s in (
                shape((total, ch), BF),
                shape((total, ch), BF),
                shape((9, 8, ch), F32),
                shape((8, ch), F32),
                *[shape((rows, ch), BF)] * n,
            )
        ],
        scratch=[pltpu.VMEM((total, ch), F32), pltpu.VMEM((total, ch), F32)],
        name="post_backward",
    )(source)


def cotangent_by_image(cotangent, select):
    rows, width = cotangent.shape
    size = select.shape[0]
    pairs = SLOT
    each = size // pairs
    per = 3

    def kernel(x, sel, out):
        for q in range(per):
            y = dot(sel[...], x[pl.ds(q * size, size), :]).astype(BF)
            for s in range(pairs):
                out[s, pl.ds(q * each, each), :] = y[s * each : (s + 1) * each]

    return call(
        kernel,
        grid=(rows // (per * size),),
        ins=[(cotangent, (per * size, width), lambda i: (i, 0)), (select, None, None)],
        outs=[(shape((pairs, rows // pairs, width), BF), (pairs, per * each, width), lambda i: (0, i, 0))],
        name="cotangent_by_image",
    )()[0]


def token_block(chan, source, low, place, readout, cotangent, live):
    pairs, ch = len(low), low[0].shape[1]
    rows, width = cotangent.shape
    size = place.shape[0]
    each = size // pairs
    per = 3

    def kernel(chan_ref, src, *refs):
        lows, (place_ref, ro, cot, alive, tok_out, piece_out, low_out, by_pair) = refs[:pairs], refs[pairs:]
        for k in range(pairs):
            by_pair[src[k]] = lows[k][...]
        for q in range(per):
            at = pl.ds(q * size, size)
            x = jnp.concatenate([by_pair[s, pl.ds(q * each, each), :] for s in range(pairs)], 0)
            low_out[at, :] = dot(place_ref[...], x).astype(BF)
        logits = dot(low_out[...], ro[...])
        value, slope = gelu_parts(logits)
        tok_out[...] = value.astype(BF)
        piece_out[...] = (cot[...].astype(F32) * alive[...] * slope).astype(BF)

    block = per * size
    row_block = lambda i, c, s: (i, 0)
    return call(
        kernel,
        grid=(rows // block,),
        prefetch=2,
        ins=[
            *[(v, (per * each, ch), lambda i, c, s: (i, 0)) for v in low],
            (place, None, None),
            (readout, (ch, width), lambda i, c, s: (0, c[0])),
            (cotangent, (block, width), row_block),
            (live, None, None),
        ],
        outs=[
            (shape((rows, width), BF), (block, width), row_block),
            (shape((rows, width), BF), (block, width), row_block),
            (shape((rows, ch), BF), (block, ch), row_block),
        ],
        scratch=[pltpu.VMEM((pairs, per * each, ch), BF)],
        name="token_block",
    )(chan, source)


def pre_backward(order, returned, spread_up, nrm, std, gain, conv, pre_expand):
    slots, cells, ch = nrm.shape
    n = order.shape[0]
    part = slots // n
    wide = 24
    rows = part * cells

    def kernel(order_ref, *refs):
        ret, refs = refs[:n], refs[n:]
        up, norm_ref, std_ref, gn, conv_ref, we, exp_out, conv_grad_out, top_out, bottom_out, gain_out, grad, cgrad = refs
        k = pl.program_id(0)
        for i in range(n):

            @pl.when(k == i)
            def _():
                grad[...] = dot(up[...], ret[i][...])

        def norm(i, total_gain):
            u, j = i // (cells // 16), i % (cells // 16)
            at = pl.ds(pl.multiple_of(j * 16, 16), 16)
            nm = norm_ref[u, at, :]
            ng = grad[pl.ds(pl.multiple_of(i * 16, 16), 16), :] * silu_slope(nm * gn[...])
            sc = ng * gn[...]
            one = jnp.mean(sc, -1, keepdims=True)
            two = jnp.mean(sc * nm, -1, keepdims=True)
            exp_out[u, at, :] = (std_ref[u, at, :] * (sc - one - nm * two)).astype(BF)
            g = ng * nm
            return total_gain + g[:8] + g[8:]

        gains = lax.fori_loop(0, rows // 16, norm, jnp.zeros((8, ch), F32))

        @pl.when(k == 0)
        def _():
            gain_out[...] = gains

        @pl.when(k > 0)
        def _():
            gain_out[...] += gains

        cgrad[...] = dot(exp_out[...].reshape(rows, ch), we[...], NT)
        for u in range(part):

            def slope(lanes):
                g = cgrad[pl.ds(u * cells, cells), lanes] * silu_slope(conv_ref[u, :, lanes])
                conv_grad_out[u, :, lanes] = g.astype(BF)
                top_out[u, :, lanes] = g[:wide].astype(BF)
                bottom_out[u, :, lanes] = g[cells - wide :].astype(BF)

            chunks(ch // LANES, slope)

    by_order = lambda k, order: (order[k], 0, 0)
    whole = (part, cells, ch)
    edge = (part, wide, ch)
    return call(
        kernel,
        grid=(n,),
        prefetch=1,
        ins=[
            *[(r, None, None) for r in returned],
            (spread_up, None, None),
            (nrm, whole, by_order),
            (std, (part, cells, 1), by_order),
            (gain, None, None),
            (conv, whole, by_order),
            (pre_expand, None, None),
        ],
        outs=[
            (shape((slots, cells, ch), BF), whole, by_order),
            (shape((slots, cells, ch), BF), whole, by_order),
            (shape((slots, wide, ch), BF), edge, by_order),
            (shape((slots, wide, ch), BF), edge, by_order),
            (shape((8, ch), F32), None, None),
        ],
        scratch=[pltpu.VMEM((rows, ch), F32), pltpu.VMEM((rows, ch), F32)],
        name="pre_backward",
    )(order)


def pre_conv_backward(conv_grad, above, below, reduced, taps):
    slots, cells, ch = reduced.shape
    wide = above.shape[1]
    high = cells // wide

    def kernel(cg, up, down, red, tap, redg_out, taps_out):
        step = pl.program_id(0)
        first, last = edge_masks(wide, wide, 1)

        @pl.when(step == 0)
        def _():
            taps_out[...] = jnp.zeros_like(taps_out)

        def back(lanes):
            w = [tap[pl.ds(i, 1), lanes] for i in range(9)]
            mid = cg[0, :, lanes].astype(F32)
            rows = [up[0, :, lanes].astype(F32)]
            rows += [mid[i * wide : (i + 1) * wide] for i in range(high)]
            rows += [down[0, :, lanes].astype(F32)]
            v = [red[0, pl.ds(i * wide, wide), lanes] for i in range(high)]
            s = [sigmoid(t) for t in v]
            x = [(a * b).astype(BF).astype(F32) for a, b in zip(v, s)]
            d = [0.0] * high
            sums = [0.0] * 9
            for p in range(high + 2):
                g = rows[p]
                moves = [columns_moved(g, -1, first, last), g, columns_moved(g, 1, first, last)]
                for a in range(3):
                    i = p - 1 + a - 1
                    if 0 <= i < high:
                        for b in range(3):
                            d[i] = d[i] + moves[b] * w[3 * a + b]
                            prod = x[i] * moves[b]
                            sums[3 * a + b] = sums[3 * a + b] + (prod[:8] + prod[8:16] + prod[16:])
            out = [d[i] * (s[i] * (1.0 + v[i] * (1.0 - s[i]))) for i in range(high)]
            redg_out[0, :, lanes] = jnp.concatenate(out, 0).astype(BF)
            for i in range(9):
                taps_out[i, :, lanes] += sums[i]

        chunks(ch // LANES, back)

    image = lambda i: (i, 0, 0)
    return call(
        kernel,
        grid=(slots,),
        ins=[
            (conv_grad, (1, cells, ch), image),
            (above, (1, wide, ch), image),
            (below, (1, wide, ch), image),
            (reduced, (1, cells, ch), image),
            (taps, None, None),
        ],
        outs=[
            (shape((slots, cells, ch), BF), (1, cells, ch), image),
            (shape((9, 8, ch), F32), None, None),
        ],
        name="pre_conv_backward",
    )()


def feature_backward(order, reduced_grad, pre_reduce, returned, spread_up):
    slots, cells, ch = reduced_grad.shape
    n = order.shape[0]
    part = slots // n

    def kernel(order_ref, rg, wr, up, *refs):
        ret, out = refs[:n], refs[n]
        k = pl.program_id(0)
        for i in range(n):

            @pl.when(k == i)
            def _():
                out[...] = dot(up[...], ret[i][...]).reshape(part, cells, ch)

        out[...] += dot(rg[...].reshape(part * cells, ch), wr[...], NT).reshape(part, cells, ch)

    by_order = lambda k, order: (order[k], 0, 0)
    whole = (part, cells, ch)
    return call(
        kernel,
        grid=(n,),
        prefetch=1,
        ins=[
            (reduced_grad, whole, by_order),
            (pre_reduce, None, None),
            (spread_up, None, None),
            *[(r, None, None) for r in returned],
        ],
        outs=[(shape((slots, cells, ch), F32), whole, by_order)],
        cost=9 * 10**9,
        name="feature_backward",
    )(order)[0]


def post_weight_grads(flat, reduced_grad, act, expanded_grad, n):
    total, ch = flat.shape
    share = ch // n
    rows = share // 8

    def kernel(x, g, a, e, out):
        for c in range(n):
            cut = slice(c * share, (c + 1) * share)
            v = dot(x[:, cut], g[...], TN).astype(BF)
            for d in range(8):
                out[d, c, :, :ch] = v[d * rows : (d + 1) * rows]
            for q in range(n):
                v = dot(a[:, q * share : (q + 1) * share], e[:, cut], TN).astype(BF)
                for d in range(8):
                    out[d, c, :, ch + q * share : ch + (q + 1) * share] = v[d * rows : (d + 1) * rows]

    return call(
        kernel,
        grid=(1,),
        ins=[(v, None, None) for v in (flat, reduced_grad, act, expanded_grad)],
        outs=[(shape((8, n, rows, 3 * ch), BF), (8, n, rows, 2 * ch), lambda i: (0, 0, 0, 0))],
        name="post_weight_grads",
    )()[0]


def readout_weight_grad(low, piece, load):
    total, ch = low.shape
    width = piece.shape[1]
    parts, n, rows, _ = load.shape
    share = ch // n

    def kernel(x, g, old, out):
        v = dot(x[...], g[...], TN).astype(BF)
        for d in range(parts):
            out[d, 0] = v[d * rows : (d + 1) * rows]

    return call(
        kernel,
        grid=(n,),
        ins=[(low, (total, share), lambda c: (0, c)), (piece, None, None)],
        outs=[(shape(load.shape, BF), (parts, 1, rows, width), lambda c: (0, c, 0, 2))],
        aliased=(load,),
        name="readout_weight_grad",
    )()[0]


def spread(n, k):
    return [(a * n + b, b * n + (a + k) % n) for a in range(n) for b in range(n)]


def other_core(values):
    return lax.ppermute(values, "core", [(0, 1), (1, 0)])


def small_rows(*grads):
    ch = grads[0].shape[-1]
    counts = [g.shape[0] if g.ndim == 3 else 1 for g in grads]
    per = ch // LANES

    def kernel(*refs):
        out = refs[-1]
        at = 0
        for ref, count in zip(refs, counts):
            for i in range(count):
                v = jnp.sum(ref[i] if len(ref.shape) == 3 else ref[...], 0, keepdims=True)
                for q in range(per):
                    out[pl.ds(at, 1), :] = v[:, q * LANES : (q + 1) * LANES]
                    at += 1

    return call(
        kernel,
        grid=(1,),
        ins=[(g, None, None) for g in grads],
        outs=[(shape((sum(counts) * per, LANES), F32), None, None)],
        name="small_rows",
    )()[0]


def join_halves(core, mine, theirs, small, their_small, parts):
    rows, ch = mine[0].shape
    half = rows // 2
    width = len(mine) * ch + LANES
    count = small.shape[0]
    m = len(mine)

    def kernel(core_ref, *refs):
        own, got = refs[:m], refs[m : 2 * m]
        sm, got_sm, out = refs[2 * m :]
        for i in range(m):
            out[:, i * ch : (i + 1) * ch] = (own[i][...].astype(F32) + got[i][...].astype(F32)).astype(BF)
        first = (core_ref[0] == 0).astype(F32)
        total = (sm[...] + got_sm[...]) * first
        pad = jnp.zeros((half - count, LANES), F32)
        out[:, m * ch :] = jnp.concatenate([total, pad], 0).astype(BF)

    return call(
        kernel,
        grid=(1,),
        prefetch=1,
        ins=[(v, (half, ch), lambda i, c: (c[0], 0)) for v in mine]
        + [(v, None, None) for v in (*theirs, small, their_small)],
        outs=[(shape((half, width), BF), None, None)],
        name="join_halves",
    )(core)[0].reshape(parts, half // parts, width)


def sum_and_copy(blocks):
    parts, rows, width = blocks.shape

    def kernel(x, out):
        def cut(lanes):
            total = jnp.sum(x[:, :, lanes].astype(F32), 0).astype(BF)
            out[:, :, lanes] = jnp.broadcast_to(total[None], (parts, rows, LANES))

        chunks(width // LANES, cut)

    return call(
        kernel,
        grid=(1,),
        ins=[(blocks, None, None)],
        outs=[(shape(blocks.shape, BF), None, None)],
        name="sum_and_copy",
    )()[0]


def finish_pre(core, own, got, ch):
    half, width = own.shape
    m = (width - LANES) // ch

    def kernel(core_ref, a, b, *outs):
        h = pl.program_id(0)

        def write(ref):
            for i in range(m):
                outs[i][...] = ref[:, i * ch : (i + 1) * ch].astype(F32)

            @pl.when(h == 0)
            def _():
                outs[m][...] = ref[:, m * ch :].astype(F32)

        @pl.when(h == core_ref[0])
        def _():
            write(a)

        @pl.when(h != core_ref[0])
        def _():
            write(b)

    return call(
        kernel,
        grid=(2,),
        prefetch=1,
        ins=[(own, None, None), (got, None, None)],
        outs=[(shape((2 * half, ch), F32), (half, ch), lambda h, c: (h, 0)) for _ in range(m)]
        + [(shape((half, LANES), F32), None, None)],
        name="finish_pre",
    )(core)


def finish_post(gathered, n):
    share, width = gathered.shape
    ch = width // (n + 2)
    per = 64

    def kernel(x, reduce_out, expand_out, read_out):
        reduce_out[...] = x[:, :ch].astype(F32)
        for q in range(n):
            expand_out[q] = x[:, ch + q * share : ch + (q + 1) * share].astype(F32)
        read_out[...] = x[:, 2 * ch :].astype(F32)

    return call(
        kernel,
        grid=(share // per,),
        ins=[(gathered, (per, width), lambda i: (i, 0))],
        outs=[
            (shape((share, ch), F32), (per, ch), lambda i: (i, 0)),
            (shape((n, share, share), F32), (n, per, share), lambda i: (0, i, 0)),
            (shape((share, n * ch), F32), (per, n * ch), lambda i: (i, 0)),
        ],
        cost=6 * 10**9,
        name="finish_post",
    )()


def after(values, *earlier):
    return lax.optimization_barrier((values, *earlier))[0]


def pool_matrix(part, high, wide):
    half = wide // 2
    m = np.zeros((high // 2 * half * part, part * (high // 2) * wide), np.float32)
    for u in range(part):
        for i in range(high // 2):
            for j in range(wide):
                m[(i * half + j // 2) * part + u, (u * (high // 2) + i) * wide + j] = 0.25
    return m


def spread_matrix(part, high, wide):
    half = wide // 2
    m = np.zeros((part * high * wide, high // 2 * half * part), np.float32)
    for u in range(part):
        for i in range(high):
            for j in range(wide):
                m[(u * high + i) * wide + j, ((i // 2) * half + j // 2) * part + u] = 0.25
    return m


def place_matrix(cells, slots, pairs):
    per = slots // pairs
    m = np.zeros((cells * slots, cells * slots), np.float32)
    for c in range(cells):
        for s in range(slots):
            m[c * slots + s, (s // per) * cells * per + c * per + s % per] = 1.0
    return m


def body(features, counts, pre_reduce, pre_conv, pre_expand, pre_gain, post_reduce, post_conv, post_expand, post_gain, readout, cotangent):
    n = lax.axis_size("chan")
    row = lax.axis_index("rows").astype(jnp.int32)
    chan = lax.axis_index("chan").astype(jnp.int32)
    core = lax.axis_index("core").astype(jnp.int32)
    eighth = lax.axis_index(("x", "core"))
    ch = pre_reduce.shape[0]
    slots, high, wide = features.shape[0], features.shape[1], features.shape[2]
    part = slots // n
    cells = high * wide
    pool = wide // 2
    share = ch // n
    out_share = cotangent.shape[3]
    steps = jnp.arange(n, dtype=jnp.int32)
    order = (row + steps) % n
    source = (chan - steps) % n
    rank = jnp.full((1,), chan, jnp.int32)
    core_at = jnp.full((1,), core, jnp.int32)
    pre_taps = pre_conv.astype(F32).reshape(9, ch)
    post_taps = post_conv.astype(F32).reshape(9, ch)
    pre_gain_row = pre_gain.reshape(1, ch)
    pool_m = jnp.asarray(pool_matrix(part, high, wide), BF)
    up_m = jnp.asarray(spread_matrix(part, high, wide), BF)
    place = jnp.asarray(place_matrix(16, slots, n), BF)

    ends = n - 1
    down_pairs = [(i, i + 1) for i in range(ends)]
    up_pairs = [(i + 1, i) for i in range(ends)]
    above = lax.ppermute(features[:, -1], "rows", down_pairs)
    below = lax.ppermute(features[:, 0], "rows", up_pairs)
    gain_hi = post_gain.astype(BF)
    gain_lo = (post_gain - gain_hi.astype(F32)).astype(BF)
    gain_row = jnp.concatenate([gain_hi, gain_lo, jnp.zeros((ch - 2 * share,), BF)])[None]
    square = post_expand.reshape(n, share, share)
    shards = jnp.concatenate(
        [post_reduce, jnp.concatenate([square[q] for q in range(n)], axis=1), jnp.pad(gain_row, ((0, 63), (0, 0)))], axis=0
    )
    eighths = shards.reshape(8, -1, ch)
    full = lax.all_gather(lax.dynamic_index_in_dim(eighths, eighth, 0, keepdims=False), ("chan", "x", "core"), axis=0, tiled=True)
    full = full.reshape(n, 2 * share + 64, ch)
    live = (jnp.arange(SLOT)[None, :] < counts[:, None]).astype(F32).reshape(slots)
    select = place.T * jnp.tile(live.astype(BF), 16)[None, :]
    cot_rows = cotangent.transpose(1, 2, 0, 3).reshape(-1, out_share)
    cots = lax.all_to_all(cotangent_by_image(cot_rows, select), "chan", 0, 0, tiled=False)

    flat_features = features.reshape(slots * cells, ch)
    fixed = (features, pre_reduce, pre_taps, pre_expand, pre_gain_row, pool_m)
    half = n // 2
    kept, pooled = (), []
    for h in range(2):
        *kept, = pre_forward(order[h * half : (h + 1) * half], above, below, *fixed, earlier=tuple(kept))
        pooled += kept[5:]
        kept = kept[:5]
    reduced, convolved, convolved_act, normal_pre, pre_std = kept

    moved = [lax.ppermute(pooled[k], ("rows", "chan"), spread(n, k)) for k in range(n)]
    flat, post_reduced, post_act, post_convolved, post_cact, post_normal, post_std, low = post_forward(
        source, moved, full, post_taps, pool
    )
    lows = [low] + [lax.ppermute(low, "chan", [(i, (i + k) % n) for i in range(n)]) for k in range(1, n)]
    refined_grad = readout_backward(low, readout, cots)
    refined_grad, lows[1], lows[3] = lax.optimization_barrier((refined_grad, lows[1], lows[3]))
    post_expanded_grad, post_reduced_grad, post_taps_grad, post_gain_grad, *back = post_backward(
        source, refined_grad, full, post_taps, post_act, post_reduced, post_convolved, post_normal, post_std, pool
    )

    returned = [lax.ppermute(back[k], ("rows", "chan"), [(d, s) for s, d in spread(n, k)]) for k in range(n)]

    load = post_weight_grads(flat, post_reduced_grad, post_cact, post_expanded_grad, n)

    alive = jnp.broadcast_to(jnp.tile(live, 48)[:, None], (48 * slots, 1))
    lows = after(lows, load)
    tokens, piece, low_here = token_block(rank, source, lows, place, readout, cot_rows, alive)
    load = readout_weight_grad(low_here, piece, load)
    tokens = tokens.reshape(pool, pool, slots, out_share).transpose(2, 0, 1, 3)
    returned = after(returned, load)
    eight = share // 32
    rest = lax.psum_scatter(load, ("x", "core"), scatter_dimension=0, tiled=False)

    expanded_grad, convolved_grad, top, bottom, pre_gain_grad = pre_backward(
        order, returned, up_m, normal_pre, pre_std, pre_gain_row, convolved, pre_expand
    )
    grad_above = lax.ppermute(bottom, "rows", down_pairs)
    grad_below = lax.ppermute(top, "rows", up_pairs)
    act_rows = after(convolved_act, bottom).reshape(-1, ch)
    pre_expand_grad = dot(act_rows, expanded_grad.reshape(-1, ch), TN).astype(BF)
    convolved_grad = after(convolved_grad, pre_expand_grad)
    reduced_grad, pre_taps_grad = pre_conv_backward(convolved_grad, grad_above, grad_below, reduced, pre_taps)
    pre_reduce_grad = dot(flat_features, reduced_grad.reshape(-1, ch), TN).astype(BF)
    feature_grad = feature_backward(order, after(reduced_grad, pre_reduce_grad), pre_reduce, returned, up_m).reshape(features.shape)

    small = small_rows(pre_taps_grad, pre_gain_grad, post_taps_grad, post_gain_grad)
    mine = [pre_reduce_grad, pre_expand_grad]
    theirs = [other_core(lax.dynamic_index_in_dim(g.reshape(2, ch // 2, ch), 1 - core, 0, keepdims=False)) for g in mine]
    load = join_halves(core_at, mine, theirs, small, other_core(small), 64)
    chips = ("x", "rows", "chan")
    pieces = after(lax.all_to_all(load, chips, 0, 0, tiled=False), feature_grad)

    rest = after(rest, load).reshape(n, 4, eight, 3 * ch).transpose(1, 0, 2, 3)
    rest = lax.psum_scatter(rest, "rows", scatter_dimension=0, tiled=False)
    rest = lax.all_to_all(rest, "chan", 0, 0, tiled=False)
    summed = jnp.sum(rest[:, :, : 2 * ch].astype(F32), axis=0).astype(BF)
    rest = jnp.concatenate([summed] + [rest[c, :, 2 * ch :] for c in range(n)], axis=1)
    rest = lax.all_gather(rest, ("x", "core", "rows"), axis=0, tiled=True)
    post_reduce_out, post_expand_out, readout_out = finish_post(rest, n)

    load = sum_and_copy(pieces)
    load = lax.all_to_all(load, chips, 0, 0, tiled=False).reshape(ch // 2, -1)
    pre_reduce_out, pre_expand_out, small_out = finish_pre(core_at, load, other_core(load), ch)
    per = ch // LANES
    cut = [0, 9 * per, 10 * per, 19 * per, 20 * per]
    pre_conv_out, pre_gain_out, post_conv_out, post_gain_out = [small_out[a:b] for a, b in zip(cut, cut[1:])]
    return (
        tokens,
        feature_grad,
        pre_reduce_out,
        pre_conv_out.reshape(3, 3, ch),
        pre_expand_out,
        pre_gain_out.reshape(ch),
        post_reduce_out,
        post_conv_out.reshape(3, 3, ch),
        post_expand_out.reshape(ch, share),
        lax.dynamic_slice_in_dim(post_gain_out.reshape(ch), chan * share, share, 0),
        readout_out,
    )


def solution(mesh):
    grid = Mesh(mesh.devices.reshape(4, 2, 4, 4), ("x", "core", "rows", "chan"))
    images = P(("x", "core", "chan"), "rows", None, None)
    grids = P(("x", "core", "rows"), None, None, "chan")
    return jax.shard_map(
        body,
        mesh=grid,
        in_specs=(
            images,
            P(("x", "core", "rows")),
            P(),
            P(),
            P(),
            P(),
            P("chan", None),
            P(),
            P(None, "chan"),
            P("chan"),
            P(),
            grids,
        ),
        out_specs=(grids, images, P(), P(), P(), P(), P("chan", None), P(), P(None, "chan"), P("chan"), P("chan", None)),
        check_vma=False,
    )
```

```python
import functools

import jax
import jax.numpy as jnp
import numpy as np
from jax import lax
from jax.experimental import pallas as pl
from jax.experimental.pallas import tpu as pltpu
from jax.sharding import Mesh, PartitionSpec as P

SLOT = 4
EPS = 1e-06
BF = jnp.bfloat16
F32 = jnp.float32
LANES = 128
VMEM_LIMIT = 56 * 1024 * 1024
NN = ((1,), (0,))
NT = ((1,), (1,))
TN = ((0,), (0,))


def dot(a, b, dims=NN):
    return lax.dot_general(a, b, (dims, ((), ())), preferred_element_type=F32)


def sigmoid(v):
    return 0.5 * jnp.tanh(0.5 * v) + 0.5


def silu(v):
    return v * sigmoid(v)


def silu_slope(v):
    s = sigmoid(v)
    return s * (1.0 + v * (1.0 - s))


def gelu_parts(v):
    c = 0.7978845608028654
    square = v * v
    t = jnp.tanh(v * (c + (c * 0.044715) * square))
    half = 0.5 * (1.0 + t)
    slope = half + 0.5 * v * (1.0 - t * t) * (c + (3.0 * c * 0.044715) * square)
    return v * half, slope


def chunks(count, body, width=LANES):
    def step(i, carry):
        body(pl.ds(pl.multiple_of(i * width, width), width))
        return carry

    lax.fori_loop(0, count, step, 0)


def call(kernel, *, grid, ins, outs, scratch=(), prefetch=0, aliased=(), cost=1, name):
    def spec(shape, block, index):
        if block is None:
            block, index = shape, lambda *_: (0,) * len(shape)
        return pl.BlockSpec(block, index)

    arrays = [i[0] for i in ins] + list(aliased)
    in_specs = [spec(a.shape, b, m) for a, b, m in ins] + [pl.BlockSpec(memory_space=pl.ANY)] * len(aliased)
    out_specs = [spec(s.shape, b, m) for s, b, m in outs]

    def run(*scalars):
        return pl.pallas_call(
            kernel,
            grid_spec=pltpu.PrefetchScalarGridSpec(
                num_scalar_prefetch=prefetch,
                grid=grid,
                in_specs=in_specs,
                out_specs=out_specs,
                scratch_shapes=list(scratch),
            ),
            out_shape=[s[0] for s in outs],
            compiler_params=pltpu.CompilerParams(
                dimension_semantics=("arbitrary",) * len(grid), vmem_limit_bytes=VMEM_LIMIT
            ),
            input_output_aliases={prefetch + len(ins) + i: i for i in range(len(aliased))},
            cost_estimate=pl.CostEstimate(flops=cost, bytes_accessed=1, transcendentals=0),
            name=name,
        )(*scalars, *arrays)

    return run


def shape(dims, dtype):
    return jax.ShapeDtypeStruct(dims, dtype)


def columns_moved(t, by, first, last):
    rows = t.shape[0]
    return pltpu.roll(t, by % rows, 0) * (first if by > 0 else last)


def edge_masks(rows, width, depth):
    at = lax.broadcasted_iota(jnp.int32, (rows, LANES), 0) % (width * depth)
    return (at >= depth).astype(F32), (at < (width - 1) * depth).astype(F32)


def pre_forward(order, reduced, above, below, features, pre_reduce, taps, pre_expand, gain, pool, earlier=()):
    slots, high, wide, ch = features.shape
    cells = high * wide
    n = order.shape[0]
    part = 2

    def kernel(order_ref, red, up_ref, down_ref, feat, wr, tap, we, gn, pool_ref, *rest):
        conv_out, act_out, norm_out, std_out, *rest = rest[len(earlier) :]
        pooled_out, (halo, exp, sums) = rest[:n], rest[n:]
        k = pl.program_id(0)
        for side, ref in enumerate((up_ref, down_ref)):
            halo[side] = dot(ref[...].reshape(part * wide, ch), wr[...]).reshape(part, wide, ch)
        first, last = edge_masks(wide, wide, 1)
        for u in range(part):

            def conv(lanes):
                w = [tap[pl.ds(i, 1), lanes] for i in range(9)]
                rows = [halo[0, u, :, lanes]]
                rows += [red[u, pl.ds(i * wide, wide), lanes] for i in range(high)]
                rows += [halo[1, u, :, lanes]]
                rows = [silu(r).astype(BF).astype(F32) for r in rows]
                acts = []
                for i in range(high):
                    t = [sum(rows[i + a] * w[3 * a + b] for a in range(3)) for b in range(3)]
                    c = t[1] + columns_moved(t[0], 1, first, last) + columns_moved(t[2], -1, first, last)
                    conv_out[u, pl.ds(i * wide, wide), lanes] = c
                    acts.append(silu(c))
                act_out[u, :, lanes] = jnp.concatenate(acts, 0).astype(BF)

            chunks(ch // LANES, conv)

        exp[...] = dot(act_out[...].reshape(part * cells, ch), we[...])

        def norm(p, carry):
            u, i = p // (high // 2), p % (high // 2)
            total = [0.0] * (wide // 8)
            for half in range(2):
                f = feat[u, 2 * i + half].astype(F32)
                for t in range(wide // 8):
                    row = (2 * i + half) * wide + 8 * t
                    e = exp[pl.ds(pl.multiple_of(u * cells + row, 8), 8), :]
                    mean = jnp.mean(e, -1, keepdims=True)
                    square = jnp.mean(e * e, -1, keepdims=True)
                    std = lax.rsqrt(square - mean * mean + EPS)
                    nrm = (e - mean) * std
                    norm_out[u, pl.ds(pl.multiple_of(row, 8), 8), :] = nrm
                    std_out[u, pl.ds(pl.multiple_of(row, 8), 8), :] = std
                    total[t] = total[t] + f[8 * t : 8 * t + 8] + silu(nrm * gn[...])
            for t in range(wide // 8):
                sums[pl.ds(pl.multiple_of(p * wide + 8 * t, 8), 8), :] = total[t]
            return carry

        lax.fori_loop(0, part * high // 2, norm, 0)
        s = sums[...]
        hi = s.astype(BF)
        lo = (s - hi.astype(F32)).astype(BF)
        pooled = (dot(pool_ref[...], hi) + dot(pool_ref[...], lo)).astype(BF)
        for i in range(n):

            @pl.when(k == i)
            def _():
                pooled_out[i][...] = pooled

    def by_order(rest):
        return lambda k, order: (order[k],) + (0,) * rest

    pooled_rows = pool.shape[0]
    block = (part, cells, ch)
    return call(
        kernel,
        grid=(n,),
        prefetch=1,
        ins=[
            (reduced, block, by_order(2)),
            (above, (part, wide, ch), by_order(2)),
            (below, (part, wide, ch), by_order(2)),
            (features, (part, high, wide, ch), by_order(3)),
            (pre_reduce, None, None),
            (taps, None, None),
            (pre_expand, None, None),
            (gain, None, None),
            (pool, None, None),
        ],
        outs=[
            (shape((slots, cells, ch), F32), block, by_order(2)),
            (shape((slots, cells, ch), BF), block, by_order(2)),
            (shape((slots, cells, ch), F32), block, by_order(2)),
            (shape((slots, cells, 1), F32), (part, cells, 1), by_order(2)),
        ]
        + [(shape((pooled_rows, ch), BF), None, None)] * n,
        scratch=[
            pltpu.VMEM((2, part, wide, ch), F32),
            pltpu.VMEM((part * cells, ch), F32),
            pltpu.VMEM((part * cells // 2, ch), F32),
        ],
        aliased=earlier,
        name="pre_forward",
    )(order)


def gain_row(w, n, share):
    at = 2 * share
    parts = [w[c, at : at + 16, :].astype(F32)[:1] for c in range(n)]
    return jnp.concatenate([p[:, :share] + p[:, share : 2 * share] for p in parts], 1)


def post_forward(source, moved, weights, taps, pool):
    n, (rows, ch) = len(moved), moved[0].shape
    total = n * rows
    depth = total // (pool * pool)
    share = ch // n

    def kernel(src, *refs):
        got, (w, tap, flat_out, red_out, act_out, conv_out, cact_out, norm_out, std_out, low_out, wide_ref) = refs[:n], refs[n:]
        for k in range(n):
            at = pl.multiple_of(src[k] * rows, 8)
            wide_ref[pl.ds(at, rows), :] = got[k][...].astype(F32)
        gain = gain_row(w, n, share)
        flat_out[...] = wide_ref[...].astype(BF)
        red = 0.0
        for c in range(n):
            red = red + dot(flat_out[:, c * share : (c + 1) * share], w[c, :share])
        red_out[...] = red
        first, last = edge_masks(total, pool, depth)
        step = pool * depth

        def conv(lanes):
            x = silu(red_out[:, lanes]).astype(BF)
            act_out[:, lanes] = x
            x = x.astype(F32)
            moves = [columns_moved(x, depth, first, last), x, columns_moved(x, -depth, first, last)]
            t = [sum(moves[b] * tap[pl.ds(3 * a + b, 1), lanes] for b in range(3)) for a in range(3)]
            none = jnp.zeros((step, LANES), F32)
            c = t[1] + jnp.concatenate([none, t[0][:-step]], 0) + jnp.concatenate([t[2][step:], none], 0)
            conv_out[:, lanes] = c
            cact_out[:, lanes] = silu(c).astype(BF)

        chunks(ch // LANES, conv)
        for c in range(n):
            e = 0.0
            for q in range(n):
                cut = slice(q * share, (q + 1) * share)
                e = e + dot(cact_out[:, cut], w[c, share : 2 * share, cut])
            norm_out[:, c * share : (c + 1) * share] = e

        def norm(i, carry):
            at = pl.ds(pl.multiple_of(i * 16, 16), 16)
            e = norm_out[at, :]
            mean = jnp.mean(e, -1, keepdims=True)
            square = jnp.mean(e * e, -1, keepdims=True)
            std = lax.rsqrt(square - mean * mean + EPS)
            nrm = (e - mean) * std
            norm_out[at, :] = nrm
            std_out[at, :] = std
            low_out[at, :] = (wide_ref[at, :] + silu(nrm * gain)).astype(BF)
            return carry

        lax.fori_loop(0, total // 16, norm, 0)

    wide = shape((total, ch), F32)
    narrow = shape((total, ch), BF)
    return call(
        kernel,
        grid=(1,),
        prefetch=1,
        ins=[(a, None, None) for a in (*moved, weights, taps)],
        outs=[(s, None, None) for s in (narrow, wide, narrow, wide, narrow, wide, shape((total, 1), F32), narrow)],
        scratch=[pltpu.VMEM((total, ch), F32)],
        name="post_forward",
    )(source)


def readout_backward(low, readout, cots):
    total, ch = low.shape
    n, _, out_share = cots.shape

    def kernel(low_ref, ro, cot, grad):
        k = pl.program_id(0)
        logits = dot(low_ref[...], ro[...])
        piece = (cot[0].astype(F32) * gelu_parts(logits)[1]).astype(BF)
        term = dot(piece, ro[...], NT)

        @pl.when(k == 0)
        def _():
            grad[...] = term

        @pl.when(k > 0)
        def _():
            grad[...] += term

    return call(
        kernel,
        grid=(n,),
        ins=[
            (low, None, None),
            (readout, (ch, out_share), lambda k: (0, k)),
            (cots, (1, total, out_share), lambda k: (k, 0, 0)),
        ],
        outs=[(shape((total, ch), F32), None, None)],
        name="readout_backward",
    )()[0]


def post_backward(source, refined_grad, weights, taps, act, red, conv, nrm, std, pool):
    total, ch = act.shape
    n = weights.shape[0]
    share = ch // n
    rows = total // n
    depth = total // (pool * pool)

    def kernel(src, rg, w, tap, act_ref, red_ref, conv_ref, norm_ref, std_ref, exp_out, redg_out, taps_out, gain_out, *rest):
        back_out, (grad, cgrad) = rest[:n], rest[n:]
        gain = gain_row(w, n, share)

        def norm(i, total_gain):
            at = pl.ds(pl.multiple_of(i * 16, 16), 16)
            nm = norm_ref[at, :]
            ng = rg[at, :] * silu_slope(nm * gain)
            sc = ng * gain
            one = jnp.mean(sc, -1, keepdims=True)
            two = jnp.mean(sc * nm, -1, keepdims=True)
            exp_out[at, :] = (std_ref[at, :] * (sc - one - nm * two)).astype(BF)
            g = ng * nm
            return total_gain + g[:8] + g[8:]

        gain_out[...] = lax.fori_loop(0, total // 16, norm, jnp.zeros((8, ch), F32))
        for q in range(n):
            cut = slice(q * share, (q + 1) * share)
            cg = 0.0
            for c in range(n):
                cg = cg + dot(exp_out[:, c * share : (c + 1) * share], w[c, share : 2 * share, cut], NT)
            cgrad[:, cut] = cg
        first, last = edge_masks(total, pool, depth)
        step = pool * depth

        def back(lanes):
            g = (cgrad[:, lanes] * silu_slope(conv_ref[:, lanes])).astype(BF).astype(F32)
            x = act_ref[:, lanes].astype(F32)
            moves = [columns_moved(g, -depth, first, last), g, columns_moved(g, depth, first, last)]
            none = jnp.zeros((step, LANES), F32)
            xs = [
                jnp.concatenate([none, x[:-step]], 0),
                x,
                jnp.concatenate([x[step:], none], 0),
            ]
            for a in range(3):
                for b in range(3):
                    prod = xs[a] * moves[b]
                    taps_out[3 * a + b, :, lanes] = jnp.sum(prod.reshape(total // 8, 8, LANES), 0)
            t = [sum(moves[b] * tap[pl.ds(3 * a + b, 1), lanes] for b in range(3)) for a in range(3)]
            d = t[1] + jnp.concatenate([t[0][step:], none], 0) + jnp.concatenate([none, t[2][:-step]], 0)
            redg_out[:, lanes] = (d * silu_slope(red_ref[:, lanes])).astype(BF)

        chunks(ch // LANES, back)
        for c in range(n):
            cut = slice(c * share, (c + 1) * share)
            grad[:, cut] = rg[:, cut] + dot(redg_out[...], w[c, :share], NT)
        for r in range(n):
            at = pl.ds(pl.multiple_of(src[r] * rows, 8), rows)
            back_out[r][...] = grad[at, :].astype(BF)

    return call(
        kernel,
        grid=(1,),
        prefetch=1,
        ins=[(a, None, None) for a in (refined_grad, weights, taps, act, red, conv, nrm, std)],
        outs=[
            (s, None, None)
            for s in (
                shape((total, ch), BF),
                shape((total, ch), BF),
                shape((9, 8, ch), F32),
                shape((8, ch), F32),
                *[shape((rows, ch), BF)] * n,
            )
        ],
        scratch=[pltpu.VMEM((total, ch), F32), pltpu.VMEM((total, ch), F32)],
        name="post_backward",
    )(source)


def cotangent_by_image(cotangent, select):
    rows, width = cotangent.shape
    size = select.shape[0]
    pairs = SLOT
    each = size // pairs
    per = 3

    def kernel(x, sel, out):
        for q in range(per):
            y = dot(sel[...], x[pl.ds(q * size, size), :]).astype(BF)
            for s in range(pairs):
                out[s, pl.ds(q * each, each), :] = y[s * each : (s + 1) * each]

    return call(
        kernel,
        grid=(rows // (per * size),),
        ins=[(cotangent, (per * size, width), lambda i: (i, 0)), (select, None, None)],
        outs=[(shape((pairs, rows // pairs, width), BF), (pairs, per * each, width), lambda i: (0, i, 0))],
        name="cotangent_by_image",
    )()[0]


def token_block(chan, source, low, place, readout, cotangent, live):
    pairs, ch = len(low), low[0].shape[1]
    rows, width = cotangent.shape
    size = place.shape[0]
    each = size // pairs
    per = 3

    def kernel(chan_ref, src, *refs):
        lows, (place_ref, ro, cot, alive, tok_out, piece_out, low_out, by_pair) = refs[:pairs], refs[pairs:]
        for k in range(pairs):
            by_pair[src[k]] = lows[k][...]
        for q in range(per):
            at = pl.ds(q * size, size)
            x = jnp.concatenate([by_pair[s, pl.ds(q * each, each), :] for s in range(pairs)], 0)
            low_out[at, :] = dot(place_ref[...], x).astype(BF)
        logits = dot(low_out[...], ro[...])
        value, slope = gelu_parts(logits)
        tok_out[...] = value.astype(BF)
        piece_out[...] = (cot[...].astype(F32) * alive[...] * slope).astype(BF)

    block = per * size
    row_block = lambda i, c, s: (i, 0)
    return call(
        kernel,
        grid=(rows // block,),
        prefetch=2,
        ins=[
            *[(v, (per * each, ch), lambda i, c, s: (i, 0)) for v in low],
            (place, None, None),
            (readout, (ch, width), lambda i, c, s: (0, c[0])),
            (cotangent, (block, width), row_block),
            (live, None, None),
        ],
        outs=[
            (shape((rows, width), BF), (block, width), row_block),
            (shape((rows, width), BF), (block, width), row_block),
            (shape((rows, ch), BF), (block, ch), row_block),
        ],
        scratch=[pltpu.VMEM((pairs, per * each, ch), BF)],
        name="token_block",
    )(chan, source)


def pre_backward(order, returned, spread_up, nrm, std, gain, conv, pre_expand):
    slots, cells, ch = nrm.shape
    n = order.shape[0]
    part = slots // n
    wide = 24
    rows = part * cells

    def kernel(order_ref, *refs):
        ret, refs = refs[:n], refs[n:]
        up, norm_ref, std_ref, gn, conv_ref, we, exp_out, conv_grad_out, top_out, bottom_out, gain_out, grad, cgrad = refs
        k = pl.program_id(0)
        for i in range(n):

            @pl.when(k == i)
            def _():
                grad[...] = dot(up[...], ret[i][...])

        def norm(i, total_gain):
            u, j = i // (cells // 16), i % (cells // 16)
            at = pl.ds(pl.multiple_of(j * 16, 16), 16)
            nm = norm_ref[u, at, :]
            ng = grad[pl.ds(pl.multiple_of(i * 16, 16), 16), :] * silu_slope(nm * gn[...])
            sc = ng * gn[...]
            one = jnp.mean(sc, -1, keepdims=True)
            two = jnp.mean(sc * nm, -1, keepdims=True)
            exp_out[u, at, :] = (std_ref[u, at, :] * (sc - one - nm * two)).astype(BF)
            g = ng * nm
            return total_gain + g[:8] + g[8:]

        gains = lax.fori_loop(0, rows // 16, norm, jnp.zeros((8, ch), F32))

        @pl.when(k == 0)
        def _():
            gain_out[...] = gains

        @pl.when(k > 0)
        def _():
            gain_out[...] += gains

        cgrad[...] = dot(exp_out[...].reshape(rows, ch), we[...], NT)
        for u in range(part):

            def slope(lanes):
                g = cgrad[pl.ds(u * cells, cells), lanes] * silu_slope(conv_ref[u, :, lanes])
                conv_grad_out[u, :, lanes] = g.astype(BF)
                top_out[u, :, lanes] = g[:wide].astype(BF)
                bottom_out[u, :, lanes] = g[cells - wide :].astype(BF)

            chunks(ch // LANES, slope)

    by_order = lambda k, order: (order[k], 0, 0)
    whole = (part, cells, ch)
    edge = (part, wide, ch)
    return call(
        kernel,
        grid=(n,),
        prefetch=1,
        ins=[
            *[(r, None, None) for r in returned],
            (spread_up, None, None),
            (nrm, whole, by_order),
            (std, (part, cells, 1), by_order),
            (gain, None, None),
            (conv, whole, by_order),
            (pre_expand, None, None),
        ],
        outs=[
            (shape((slots, cells, ch), BF), whole, by_order),
            (shape((slots, cells, ch), BF), whole, by_order),
            (shape((slots, wide, ch), BF), edge, by_order),
            (shape((slots, wide, ch), BF), edge, by_order),
            (shape((8, ch), F32), None, None),
        ],
        scratch=[pltpu.VMEM((rows, ch), F32), pltpu.VMEM((rows, ch), F32)],
        name="pre_backward",
    )(order)


def pre_conv_backward(conv_grad, above, below, reduced, taps):
    slots, cells, ch = reduced.shape
    wide = above.shape[1]
    high = cells // wide

    def kernel(cg, up, down, red, tap, redg_out, taps_out):
        step = pl.program_id(0)
        first, last = edge_masks(wide, wide, 1)

        @pl.when(step == 0)
        def _():
            taps_out[...] = jnp.zeros_like(taps_out)

        def back(lanes):
            w = [tap[pl.ds(i, 1), lanes] for i in range(9)]
            mid = cg[0, :, lanes].astype(F32)
            rows = [up[0, :, lanes].astype(F32)]
            rows += [mid[i * wide : (i + 1) * wide] for i in range(high)]
            rows += [down[0, :, lanes].astype(F32)]
            v = [red[0, pl.ds(i * wide, wide), lanes] for i in range(high)]
            s = [sigmoid(t) for t in v]
            x = [(a * b).astype(BF).astype(F32) for a, b in zip(v, s)]
            d = [0.0] * high
            sums = [0.0] * 9
            for p in range(high + 2):
                g = rows[p]
                moves = [columns_moved(g, -1, first, last), g, columns_moved(g, 1, first, last)]
                for a in range(3):
                    i = p - 1 + a - 1
                    if 0 <= i < high:
                        for b in range(3):
                            d[i] = d[i] + moves[b] * w[3 * a + b]
                            prod = x[i] * moves[b]
                            sums[3 * a + b] = sums[3 * a + b] + (prod[:8] + prod[8:16] + prod[16:])
            out = [d[i] * (s[i] * (1.0 + v[i] * (1.0 - s[i]))) for i in range(high)]
            redg_out[0, :, lanes] = jnp.concatenate(out, 0).astype(BF)
            for i in range(9):
                taps_out[i, :, lanes] += sums[i]

        chunks(ch // LANES, back)

    image = lambda i: (i, 0, 0)
    return call(
        kernel,
        grid=(slots,),
        ins=[
            (conv_grad, (1, cells, ch), image),
            (above, (1, wide, ch), image),
            (below, (1, wide, ch), image),
            (reduced, (1, cells, ch), image),
            (taps, None, None),
        ],
        outs=[
            (shape((slots, cells, ch), BF), (1, cells, ch), image),
            (shape((9, 8, ch), F32), None, None),
        ],
        name="pre_conv_backward",
    )()


def feature_backward(order, reduced_grad, pre_reduce, returned, spread_up):
    slots, cells, ch = reduced_grad.shape
    n = order.shape[0]
    part = slots // n

    def kernel(order_ref, rg, wr, up, *refs):
        ret, out = refs[:n], refs[n]
        k = pl.program_id(0)
        for i in range(n):

            @pl.when(k == i)
            def _():
                out[...] = dot(up[...], ret[i][...]).reshape(part, cells, ch)

        out[...] += dot(rg[...].reshape(part * cells, ch), wr[...], NT).reshape(part, cells, ch)

    by_order = lambda k, order: (order[k], 0, 0)
    whole = (part, cells, ch)
    return call(
        kernel,
        grid=(n,),
        prefetch=1,
        ins=[
            (reduced_grad, whole, by_order),
            (pre_reduce, None, None),
            (spread_up, None, None),
            *[(r, None, None) for r in returned],
        ],
        outs=[(shape((slots, cells, ch), F32), whole, by_order)],
        cost=9 * 10**9,
        name="feature_backward",
    )(order)[0]


def post_weight_grads(flat, reduced_grad, act, expanded_grad, n):
    total, ch = flat.shape
    share = ch // n
    rows = share // 8

    def kernel(x, g, a, e, out):
        for c in range(n):
            cut = slice(c * share, (c + 1) * share)
            v = dot(x[:, cut], g[...], TN).astype(BF)
            for d in range(8):
                out[d, c, :, :ch] = v[d * rows : (d + 1) * rows]
            for q in range(n):
                v = dot(a[:, q * share : (q + 1) * share], e[:, cut], TN).astype(BF)
                for d in range(8):
                    out[d, c, :, ch + q * share : ch + (q + 1) * share] = v[d * rows : (d + 1) * rows]

    return call(
        kernel,
        grid=(1,),
        ins=[(v, None, None) for v in (flat, reduced_grad, act, expanded_grad)],
        outs=[(shape((8, n, rows, 3 * ch), BF), (8, n, rows, 2 * ch), lambda i: (0, 0, 0, 0))],
        name="post_weight_grads",
    )()[0]


def readout_weight_grad(low, piece, load):
    total, ch = low.shape
    width = piece.shape[1]
    parts, n, rows, _ = load.shape
    share = ch // n

    def kernel(x, g, old, out):
        v = dot(x[...], g[...], TN).astype(BF)
        for d in range(parts):
            out[d, 0] = v[d * rows : (d + 1) * rows]

    return call(
        kernel,
        grid=(n,),
        ins=[(low, (total, share), lambda c: (0, c)), (piece, None, None)],
        outs=[(shape(load.shape, BF), (parts, 1, rows, width), lambda c: (0, c, 0, 2))],
        aliased=(load,),
        name="readout_weight_grad",
    )()[0]


def spread(n, k):
    return [(a * n + b, b * n + (a + k) % n) for a in range(n) for b in range(n)]


def other_core(values):
    return lax.ppermute(values, "core", [(0, 1), (1, 0)])


def small_rows(*grads):
    ch = grads[0].shape[-1]
    counts = [g.shape[0] if g.ndim == 3 else 1 for g in grads]
    per = ch // LANES

    def kernel(*refs):
        out = refs[-1]
        at = 0
        for ref, count in zip(refs, counts):
            for i in range(count):
                v = jnp.sum(ref[i] if len(ref.shape) == 3 else ref[...], 0, keepdims=True)
                for q in range(per):
                    out[pl.ds(at, 1), :] = v[:, q * LANES : (q + 1) * LANES]
                    at += 1

    return call(
        kernel,
        grid=(1,),
        ins=[(g, None, None) for g in grads],
        outs=[(shape((sum(counts) * per, LANES), F32), None, None)],
        name="small_rows",
    )()[0]


def join_halves(core, mine, theirs, small, their_small, parts):
    rows, ch = mine[0].shape
    half = rows // 2
    width = len(mine) * ch + LANES
    count = small.shape[0]
    m = len(mine)

    def kernel(core_ref, *refs):
        own, got = refs[:m], refs[m : 2 * m]
        sm, got_sm, out = refs[2 * m :]
        for i in range(m):
            out[:, i * ch : (i + 1) * ch] = (own[i][...].astype(F32) + got[i][...].astype(F32)).astype(BF)
        first = (core_ref[0] == 0).astype(F32)
        total = (sm[...] + got_sm[...]) * first
        pad = jnp.zeros((half - count, LANES), F32)
        out[:, m * ch :] = jnp.concatenate([total, pad], 0).astype(BF)

    return call(
        kernel,
        grid=(1,),
        prefetch=1,
        ins=[(v, (half, ch), lambda i, c: (c[0], 0)) for v in mine]
        + [(v, None, None) for v in (*theirs, small, their_small)],
        outs=[(shape((half, width), BF), None, None)],
        name="join_halves",
    )(core)[0].reshape(parts, half // parts, width)


def sum_and_copy(blocks):
    parts, rows, width = blocks.shape

    def kernel(x, out):
        def cut(lanes):
            total = jnp.sum(x[:, :, lanes].astype(F32), 0).astype(BF)
            out[:, :, lanes] = jnp.broadcast_to(total[None], (parts, rows, LANES))

        chunks(width // LANES, cut)

    return call(
        kernel,
        grid=(1,),
        ins=[(blocks, None, None)],
        outs=[(shape(blocks.shape, BF), None, None)],
        name="sum_and_copy",
    )()[0]


def finish_pre(place, half_rows, ch, earlier=()):
    half, width = half_rows.shape
    m = (width - LANES) // ch

    def kernel(place_ref, x, *outs):
        outs = outs[len(earlier) :]
        for i in range(m):
            outs[i][...] = x[:, i * ch : (i + 1) * ch].astype(F32)
        outs[m][...] = x[:, m * ch :].astype(F32)

    return call(
        kernel,
        grid=(1,),
        prefetch=1,
        ins=[(half_rows, None, None)],
        outs=[(shape((2 * half, ch), F32), (half, ch), lambda i, c: (c[0], 0)) for _ in range(m)]
        + [(shape((half, LANES), F32), None, None)],
        aliased=earlier,
        name="finish_pre",
    )(place)


def finish_post(gathered, n):
    share, width = gathered.shape
    ch = width // (n + 2)
    per = 64

    def kernel(x, reduce_out, expand_out, read_out):
        reduce_out[...] = x[:, :ch].astype(F32)
        for q in range(n):
            expand_out[q] = x[:, ch + q * share : ch + (q + 1) * share].astype(F32)
        read_out[...] = x[:, 2 * ch :].astype(F32)

    return call(
        kernel,
        grid=(share // per,),
        ins=[(gathered, (per, width), lambda i: (i, 0))],
        outs=[
            (shape((share, ch), F32), (per, ch), lambda i: (i, 0)),
            (shape((n, share, share), F32), (n, per, share), lambda i: (0, i, 0)),
            (shape((share, n * ch), F32), (per, n * ch), lambda i: (i, 0)),
        ],
        cost=6 * 10**9,
        name="finish_post",
    )()


def after(values, *earlier):
    return lax.optimization_barrier((values, *earlier))[0]


def pool_matrix(part, high, wide):
    half = wide // 2
    m = np.zeros((high // 2 * half * part, part * (high // 2) * wide), np.float32)
    for u in range(part):
        for i in range(high // 2):
            for j in range(wide):
                m[(i * half + j // 2) * part + u, (u * (high // 2) + i) * wide + j] = 0.25
    return m


def spread_matrix(part, high, wide):
    half = wide // 2
    m = np.zeros((part * high * wide, high // 2 * half * part), np.float32)
    for u in range(part):
        for i in range(high):
            for j in range(wide):
                m[(u * high + i) * wide + j, ((i // 2) * half + j // 2) * part + u] = 0.25
    return m


def place_matrix(cells, slots, pairs):
    per = slots // pairs
    m = np.zeros((cells * slots, cells * slots), np.float32)
    for c in range(cells):
        for s in range(slots):
            m[c * slots + s, (s // per) * cells * per + c * per + s % per] = 1.0
    return m


def body(features, counts, pre_reduce, pre_conv, pre_expand, pre_gain, post_reduce, post_conv, post_expand, post_gain, readout, cotangent):
    n = lax.axis_size("chan")
    row = lax.axis_index("rows").astype(jnp.int32)
    chan = lax.axis_index("chan").astype(jnp.int32)
    core = lax.axis_index("core").astype(jnp.int32)
    eighth = lax.axis_index(("x", "core"))
    ch = pre_reduce.shape[0]
    slots, high, wide = features.shape[0], features.shape[1], features.shape[2]
    part = slots // n
    cells = high * wide
    pool = wide // 2
    share = ch // n
    out_share = cotangent.shape[3]
    steps = jnp.arange(n, dtype=jnp.int32)
    order = (row + steps) % n
    source = (chan - steps) % n
    rank = jnp.full((1,), chan, jnp.int32)
    core_at = jnp.full((1,), core, jnp.int32)
    pre_taps = pre_conv.astype(F32).reshape(9, ch)
    post_taps = post_conv.astype(F32).reshape(9, ch)
    pre_gain_row = pre_gain.reshape(1, ch)
    pool_m = jnp.asarray(pool_matrix(part, high, wide), BF)
    up_m = jnp.asarray(spread_matrix(part, high, wide), BF)
    place = jnp.asarray(place_matrix(16, slots, n), BF)

    ends = n - 1
    down_pairs = [(i, i + 1) for i in range(ends)]
    up_pairs = [(i + 1, i) for i in range(ends)]
    above = lax.ppermute(features[:, -1], "rows", down_pairs)
    below = lax.ppermute(features[:, 0], "rows", up_pairs)
    gain_hi = post_gain.astype(BF)
    gain_lo = (post_gain - gain_hi.astype(F32)).astype(BF)
    gain_row = jnp.concatenate([gain_hi, gain_lo, jnp.zeros((ch - 2 * share,), BF)])[None]
    square = post_expand.reshape(n, share, share)
    shards = jnp.concatenate(
        [post_reduce, jnp.concatenate([square[q] for q in range(n)], axis=1), jnp.pad(gain_row, ((0, 63), (0, 0)))], axis=0
    )
    eighths = shards.reshape(8, -1, ch)
    full = lax.all_gather(lax.dynamic_index_in_dim(eighths, eighth, 0, keepdims=False), ("chan", "x", "core"), axis=0, tiled=True)
    full = full.reshape(n, 2 * share + 64, ch)
    flat_features = features.reshape(slots * cells, ch)
    reduced = dot(flat_features, pre_reduce).reshape(slots, cells, ch)
    live = (jnp.arange(SLOT)[None, :] < counts[:, None]).astype(F32).reshape(slots)
    select = place.T * jnp.tile(live.astype(BF), 16)[None, :]
    cot_rows = cotangent.transpose(1, 2, 0, 3).reshape(-1, out_share)
    cots = lax.all_to_all(cotangent_by_image(after(cot_rows, reduced), select), "chan", 0, 0, tiled=False)

    fixed = (reduced, above, below, features, pre_reduce, pre_taps, pre_expand, pre_gain_row, pool_m)
    half = n // 2
    kept, pooled = (), []
    for h in range(2):
        *kept, = pre_forward(order[h * half : (h + 1) * half], *fixed, earlier=tuple(kept))
        pooled += kept[4:]
        kept = kept[:4]
    convolved, convolved_act, normal_pre, pre_std = kept

    moved = [lax.ppermute(pooled[k], ("rows", "chan"), spread(n, k)) for k in range(n)]
    flat, post_reduced, post_act, post_convolved, post_cact, post_normal, post_std, low = post_forward(
        source, moved, full, post_taps, pool
    )
    lows = [low] + [lax.ppermute(low, "chan", [(i, (i + k) % n) for i in range(n)]) for k in range(1, n)]
    refined_grad = readout_backward(low, readout, cots)
    refined_grad, lows[1], lows[3] = lax.optimization_barrier((refined_grad, lows[1], lows[3]))
    post_expanded_grad, post_reduced_grad, post_taps_grad, post_gain_grad, *back = post_backward(
        source, refined_grad, full, post_taps, post_act, post_reduced, post_convolved, post_normal, post_std, pool
    )

    returned = [lax.ppermute(back[k], ("rows", "chan"), [(d, s) for s, d in spread(n, k)]) for k in range(n)]

    load = post_weight_grads(flat, post_reduced_grad, post_cact, post_expanded_grad, n)

    alive = jnp.broadcast_to(jnp.tile(live, 48)[:, None], (48 * slots, 1))
    lows = after(lows, load, returned[:2])
    tokens, piece, low_here = token_block(rank, source, lows, place, readout, cot_rows, alive)
    load = readout_weight_grad(low_here, after(piece, returned[2:]), load)
    tokens = tokens.reshape(pool, pool, slots, out_share).transpose(2, 0, 1, 3)
    returned = after(returned, load)
    eight = share // 32
    rest = lax.psum_scatter(load, ("x", "core"), scatter_dimension=0, tiled=False)

    expanded_grad, convolved_grad, top, bottom, pre_gain_grad = pre_backward(
        order, returned, up_m, normal_pre, pre_std, pre_gain_row, convolved, pre_expand
    )
    grad_above = lax.ppermute(bottom, "rows", down_pairs)
    grad_below = lax.ppermute(top, "rows", up_pairs)
    act_rows = after(convolved_act, bottom).reshape(-1, ch)
    pre_expand_grad = dot(act_rows, expanded_grad.reshape(-1, ch), TN).astype(BF)
    convolved_grad = after(convolved_grad, pre_expand_grad)
    reduced_grad, pre_taps_grad = pre_conv_backward(convolved_grad, grad_above, grad_below, reduced, pre_taps)
    rest = after(rest, reduced_grad).reshape(n, 4, eight, 3 * ch).transpose(1, 0, 2, 3)
    small = small_rows(pre_taps_grad, pre_gain_grad, post_taps_grad, post_gain_grad)
    flat_features = after(flat_features, rest, small)
    rest = lax.psum_scatter(rest, "rows", scatter_dimension=0, tiled=False)

    pre_reduce_grad = dot(flat_features, reduced_grad.reshape(-1, ch), TN).astype(BF)
    feature_grad = feature_backward(order, after(reduced_grad, pre_reduce_grad), pre_reduce, returned, up_m).reshape(features.shape)

    mine = [pre_reduce_grad, pre_expand_grad]
    theirs = [other_core(lax.dynamic_index_in_dim(g.reshape(2, ch // 2, ch), 1 - core, 0, keepdims=False)) for g in mine]
    load = join_halves(core_at, mine, theirs, small, other_core(small), 64)
    chips = ("x", "rows", "chan")
    pieces = after(lax.all_to_all(load, chips, 0, 0, tiled=False), feature_grad)

    rest = lax.all_to_all(after(rest, feature_grad), "chan", 0, 0, tiled=False)
    summed = jnp.sum(rest[:, :, : 2 * ch].astype(F32), axis=0).astype(BF)
    rest = jnp.concatenate([summed] + [rest[c, :, 2 * ch :] for c in range(n)], axis=1)
    rest = lax.all_gather(rest, ("x", "core", "rows"), axis=0, tiled=True)
    post_reduce_out, post_expand_out, readout_out = finish_post(rest, n)

    load = sum_and_copy(pieces)
    load = lax.all_to_all(load, chips, 0, 0, tiled=False).reshape(ch // 2, -1)
    theirs = other_core(load)
    *own, small_own = finish_pre(core_at, load, ch)
    theirs = after(theirs, small_own)
    pre_reduce_out, pre_expand_out, small_their = finish_pre(1 - core_at, theirs, ch, earlier=tuple(own))
    small_out = jnp.where(core == 0, small_own, small_their)
    per = ch // LANES
    cut = [0, 9 * per, 10 * per, 19 * per, 20 * per]
    pre_conv_out, pre_gain_out, post_conv_out, post_gain_out = [small_out[a:b] for a, b in zip(cut, cut[1:])]
    return (
        tokens,
        feature_grad,
        pre_reduce_out,
        pre_conv_out.reshape(3, 3, ch),
        pre_expand_out,
        pre_gain_out.reshape(ch),
        post_reduce_out,
        post_conv_out.reshape(3, 3, ch),
        post_expand_out.reshape(ch, share),
        lax.dynamic_slice_in_dim(post_gain_out.reshape(ch), chan * share, share, 0),
        readout_out,
    )


def solution(mesh):
    grid = Mesh(mesh.devices.reshape(4, 2, 4, 4), ("x", "core", "rows", "chan"))
    images = P(("x", "core", "chan"), "rows", None, None)
    grids = P(("x", "core", "rows"), None, None, "chan")
    return jax.shard_map(
        body,
        mesh=grid,
        in_specs=(
            images,
            P(("x", "core", "rows")),
            P(),
            P(),
            P(),
            P(),
            P("chan", None),
            P(),
            P(None, "chan"),
            P("chan"),
            P(),
            grids,
        ),
        out_specs=(grids, images, P(), P(), P(), P(), P("chan", None), P(), P(None, "chan"), P("chan"), P("chan", None)),
        check_vma=False,
    )
```

```python
import functools

import jax
import jax.numpy as jnp
import numpy as np
from jax import lax
from jax.experimental import pallas as pl
from jax.experimental.pallas import tpu as pltpu
from jax.sharding import Mesh, PartitionSpec as P

SLOT = 4
EPS = 1e-06
BF = jnp.bfloat16
F32 = jnp.float32
LANES = 128
VMEM_LIMIT = 56 * 1024 * 1024
NN = ((1,), (0,))
NT = ((1,), (1,))
TN = ((0,), (0,))


def dot(a, b, dims=NN):
    return lax.dot_general(a, b, (dims, ((), ())), preferred_element_type=F32)


def sigmoid(v):
    return 0.5 * jnp.tanh(0.5 * v) + 0.5


def silu(v):
    return v * sigmoid(v)


def silu_slope(v):
    s = sigmoid(v)
    return s * (1.0 + v * (1.0 - s))


def gelu_parts(v):
    c = 0.7978845608028654
    square = v * v
    t = jnp.tanh(v * (c + (c * 0.044715) * square))
    half = 0.5 * (1.0 + t)
    slope = half + 0.5 * v * (1.0 - t * t) * (c + (3.0 * c * 0.044715) * square)
    return v * half, slope


def chunks(count, body, width=LANES):
    def step(i, carry):
        body(pl.ds(pl.multiple_of(i * width, width), width))
        return carry

    lax.fori_loop(0, count, step, 0)


def call(kernel, *, grid, ins, outs, scratch=(), prefetch=0, aliased=(), cost=1, name):
    def spec(shape, block, index):
        if block is None:
            block, index = shape, lambda *_: (0,) * len(shape)
        return pl.BlockSpec(block, index)

    arrays = [i[0] for i in ins] + list(aliased)
    in_specs = [spec(a.shape, b, m) for a, b, m in ins] + [pl.BlockSpec(memory_space=pl.ANY)] * len(aliased)
    out_specs = [spec(s.shape, b, m) for s, b, m in outs]

    def run(*scalars):
        return pl.pallas_call(
            kernel,
            grid_spec=pltpu.PrefetchScalarGridSpec(
                num_scalar_prefetch=prefetch,
                grid=grid,
                in_specs=in_specs,
                out_specs=out_specs,
                scratch_shapes=list(scratch),
            ),
            out_shape=[s[0] for s in outs],
            compiler_params=pltpu.CompilerParams(
                dimension_semantics=("arbitrary",) * len(grid), vmem_limit_bytes=VMEM_LIMIT
            ),
            input_output_aliases={prefetch + len(ins) + i: i for i in range(len(aliased))},
            cost_estimate=pl.CostEstimate(flops=cost, bytes_accessed=1, transcendentals=0),
            name=name,
        )(*scalars, *arrays)

    return run


def shape(dims, dtype):
    return jax.ShapeDtypeStruct(dims, dtype)


def columns_moved(t, by, first, last):
    rows = t.shape[0]
    return pltpu.roll(t, by % rows, 0) * (first if by > 0 else last)


def edge_masks(rows, width, depth):
    at = lax.broadcasted_iota(jnp.int32, (rows, LANES), 0) % (width * depth)
    return (at >= depth).astype(F32), (at < (width - 1) * depth).astype(F32)


def pre_forward(order, reduced, above, below, features, pre_reduce, taps, pre_expand, gain, pool, earlier=()):
    slots, high, wide, ch = features.shape
    cells = high * wide
    n = order.shape[0]
    part = 2

    def kernel(order_ref, red, up_ref, down_ref, feat, wr, tap, we, gn, pool_ref, *rest):
        conv_out, act_out, norm_out, std_out, *rest = rest[len(earlier) :]
        pooled_out, (halo, exp, sums) = rest[:n], rest[n:]
        k = pl.program_id(0)
        for side, ref in enumerate((up_ref, down_ref)):
            halo[side] = dot(ref[...].reshape(part * wide, ch), wr[...]).reshape(part, wide, ch)
        first, last = edge_masks(wide, wide, 1)
        for u in range(part):

            def conv(lanes):
                w = [tap[pl.ds(i, 1), lanes] for i in range(9)]
                rows = [halo[0, u, :, lanes]]
                rows += [red[u, pl.ds(i * wide, wide), lanes] for i in range(high)]
                rows += [halo[1, u, :, lanes]]
                rows = [silu(r).astype(BF).astype(F32) for r in rows]
                acts = []
                for i in range(high):
                    t = [sum(rows[i + a] * w[3 * a + b] for a in range(3)) for b in range(3)]
                    c = t[1] + columns_moved(t[0], 1, first, last) + columns_moved(t[2], -1, first, last)
                    conv_out[u, pl.ds(i * wide, wide), lanes] = c
                    acts.append(silu(c))
                act_out[u, :, lanes] = jnp.concatenate(acts, 0).astype(BF)

            chunks(ch // LANES, conv)

        exp[...] = dot(act_out[...].reshape(part * cells, ch), we[...])

        def norm(p, carry):
            u, i = p // (high // 2), p % (high // 2)
            total = [0.0] * (wide // 8)
            for half in range(2):
                f = feat[u, 2 * i + half].astype(F32)
                for t in range(wide // 8):
                    row = (2 * i + half) * wide + 8 * t
                    e = exp[pl.ds(pl.multiple_of(u * cells + row, 8), 8), :]
                    mean = jnp.mean(e, -1, keepdims=True)
                    square = jnp.mean(e * e, -1, keepdims=True)
                    std = lax.rsqrt(square - mean * mean + EPS)
                    nrm = (e - mean) * std
                    norm_out[u, pl.ds(pl.multiple_of(row, 8), 8), :] = nrm
                    std_out[u, pl.ds(pl.multiple_of(row, 8), 8), :] = std
                    total[t] = total[t] + f[8 * t : 8 * t + 8] + silu(nrm * gn[...])
            for t in range(wide // 8):
                sums[pl.ds(pl.multiple_of(p * wide + 8 * t, 8), 8), :] = total[t]
            return carry

        lax.fori_loop(0, part * high // 2, norm, 0)
        s = sums[...]
        hi = s.astype(BF)
        lo = (s - hi.astype(F32)).astype(BF)
        pooled = (dot(pool_ref[...], hi) + dot(pool_ref[...], lo)).astype(BF)
        for i in range(n):

            @pl.when(k == i)
            def _():
                pooled_out[i][...] = pooled

    def by_order(rest):
        return lambda k, order: (order[k],) + (0,) * rest

    pooled_rows = pool.shape[0]
    block = (part, cells, ch)
    return call(
        kernel,
        grid=(n,),
        prefetch=1,
        ins=[
            (reduced, block, by_order(2)),
            (above, (part, wide, ch), by_order(2)),
            (below, (part, wide, ch), by_order(2)),
            (features, (part, high, wide, ch), by_order(3)),
            (pre_reduce, None, None),
            (taps, None, None),
            (pre_expand, None, None),
            (gain, None, None),
            (pool, None, None),
        ],
        outs=[
            (shape((slots, cells, ch), F32), block, by_order(2)),
            (shape((slots, cells, ch), BF), block, by_order(2)),
            (shape((slots, cells, ch), F32), block, by_order(2)),
            (shape((slots, cells, 1), F32), (part, cells, 1), by_order(2)),
        ]
        + [(shape((pooled_rows, ch), BF), None, None)] * n,
        scratch=[
            pltpu.VMEM((2, part, wide, ch), F32),
            pltpu.VMEM((part * cells, ch), F32),
            pltpu.VMEM((part * cells // 2, ch), F32),
        ],
        aliased=earlier,
        name="pre_forward",
    )(order)


def gain_row(w, n, share):
    at = 2 * share
    parts = [w[c, at : at + 16, :].astype(F32)[:1] for c in range(n)]
    return jnp.concatenate([p[:, :share] + p[:, share : 2 * share] for p in parts], 1)


def post_forward(source, moved, weights, taps, pool):
    n, (rows, ch) = len(moved), moved[0].shape
    total = n * rows
    depth = total // (pool * pool)
    share = ch // n

    def kernel(src, *refs):
        got, (w, tap, flat_out, red_out, act_out, conv_out, cact_out, norm_out, std_out, low_out, wide_ref) = refs[:n], refs[n:]
        for k in range(n):
            at = pl.multiple_of(src[k] * rows, 8)
            wide_ref[pl.ds(at, rows), :] = got[k][...].astype(F32)
        gain = gain_row(w, n, share)
        flat_out[...] = wide_ref[...].astype(BF)
        red = 0.0
        for c in range(n):
            red = red + dot(flat_out[:, c * share : (c + 1) * share], w[c, :share])
        red_out[...] = red
        first, last = edge_masks(total, pool, depth)
        step = pool * depth

        def conv(lanes):
            x = silu(red_out[:, lanes]).astype(BF)
            act_out[:, lanes] = x
            x = x.astype(F32)
            moves = [columns_moved(x, depth, first, last), x, columns_moved(x, -depth, first, last)]
            t = [sum(moves[b] * tap[pl.ds(3 * a + b, 1), lanes] for b in range(3)) for a in range(3)]
            none = jnp.zeros((step, LANES), F32)
            c = t[1] + jnp.concatenate([none, t[0][:-step]], 0) + jnp.concatenate([t[2][step:], none], 0)
            conv_out[:, lanes] = c
            cact_out[:, lanes] = silu(c).astype(BF)

        chunks(ch // LANES, conv)
        for c in range(n):
            e = 0.0
            for q in range(n):
                cut = slice(q * share, (q + 1) * share)
                e = e + dot(cact_out[:, cut], w[c, share : 2 * share, cut])
            norm_out[:, c * share : (c + 1) * share] = e

        def norm(i, carry):
            at = pl.ds(pl.multiple_of(i * 16, 16), 16)
            e = norm_out[at, :]
            mean = jnp.mean(e, -1, keepdims=True)
            square = jnp.mean(e * e, -1, keepdims=True)
            std = lax.rsqrt(square - mean * mean + EPS)
            nrm = (e - mean) * std
            norm_out[at, :] = nrm
            std_out[at, :] = std
            low_out[at, :] = (wide_ref[at, :] + silu(nrm * gain)).astype(BF)
            return carry

        lax.fori_loop(0, total // 16, norm, 0)

    wide = shape((total, ch), F32)
    narrow = shape((total, ch), BF)
    return call(
        kernel,
        grid=(1,),
        prefetch=1,
        ins=[(a, None, None) for a in (*moved, weights, taps)],
        outs=[(s, None, None) for s in (narrow, wide, narrow, wide, narrow, wide, shape((total, 1), F32), narrow)],
        scratch=[pltpu.VMEM((total, ch), F32)],
        name="post_forward",
    )(source)


def readout_backward(source, low, readout, cots):
    total, ch = low.shape
    n, out_share = len(cots), cots[0].shape[1]

    def kernel(src, low_ref, ro, *rest):
        cot, grad = rest[:n], rest[n]
        k = pl.program_id(0)
        logits = dot(low_ref[...], ro[...])
        slope = gelu_parts(logits)[1]
        for i in range(n):

            @pl.when(k == i)
            def _():
                piece = (cot[i][...].astype(F32) * slope).astype(BF)
                term = dot(piece, ro[...], NT)
                grad[...] = term if i == 0 else grad[...] + term

    return call(
        kernel,
        grid=(n,),
        prefetch=1,
        ins=[(low, None, None), (readout, (ch, out_share), lambda k, s: (0, s[k]))] + [(c, None, None) for c in cots],
        outs=[(shape((total, ch), F32), None, None)],
        name="readout_backward",
    )(source)[0]


def post_backward(source, refined_grad, weights, taps, act, red, conv, nrm, std, pool):
    total, ch = act.shape
    n = weights.shape[0]
    share = ch // n
    rows = total // n
    depth = total // (pool * pool)

    def kernel(src, rg, w, tap, act_ref, red_ref, conv_ref, norm_ref, std_ref, exp_out, redg_out, taps_out, gain_out, *rest):
        back_out, (grad, cgrad) = rest[:n], rest[n:]
        gain = gain_row(w, n, share)

        def norm(i, total_gain):
            at = pl.ds(pl.multiple_of(i * 16, 16), 16)
            nm = norm_ref[at, :]
            ng = rg[at, :] * silu_slope(nm * gain)
            sc = ng * gain
            one = jnp.mean(sc, -1, keepdims=True)
            two = jnp.mean(sc * nm, -1, keepdims=True)
            exp_out[at, :] = (std_ref[at, :] * (sc - one - nm * two)).astype(BF)
            g = ng * nm
            return total_gain + g[:8] + g[8:]

        gain_out[...] = lax.fori_loop(0, total // 16, norm, jnp.zeros((8, ch), F32))
        for q in range(n):
            cut = slice(q * share, (q + 1) * share)
            cg = 0.0
            for c in range(n):
                cg = cg + dot(exp_out[:, c * share : (c + 1) * share], w[c, share : 2 * share, cut], NT)
            cgrad[:, cut] = cg
        first, last = edge_masks(total, pool, depth)
        step = pool * depth

        def back(lanes):
            g = (cgrad[:, lanes] * silu_slope(conv_ref[:, lanes])).astype(BF).astype(F32)
            x = act_ref[:, lanes].astype(F32)
            moves = [columns_moved(g, -depth, first, last), g, columns_moved(g, depth, first, last)]
            none = jnp.zeros((step, LANES), F32)
            xs = [
                jnp.concatenate([none, x[:-step]], 0),
                x,
                jnp.concatenate([x[step:], none], 0),
            ]
            for a in range(3):
                for b in range(3):
                    prod = xs[a] * moves[b]
                    taps_out[3 * a + b, :, lanes] = jnp.sum(prod.reshape(total // 8, 8, LANES), 0)
            t = [sum(moves[b] * tap[pl.ds(3 * a + b, 1), lanes] for b in range(3)) for a in range(3)]
            d = t[1] + jnp.concatenate([t[0][step:], none], 0) + jnp.concatenate([none, t[2][:-step]], 0)
            redg_out[:, lanes] = (d * silu_slope(red_ref[:, lanes])).astype(BF)

        chunks(ch // LANES, back)
        for c in range(n):
            cut = slice(c * share, (c + 1) * share)
            grad[:, cut] = rg[:, cut] + dot(redg_out[...], w[c, :share], NT)
        for r in range(n):
            at = pl.ds(pl.multiple_of(src[r] * rows, 8), rows)
            back_out[r][...] = grad[at, :].astype(BF)

    return call(
        kernel,
        grid=(1,),
        prefetch=1,
        ins=[(a, None, None) for a in (refined_grad, weights, taps, act, red, conv, nrm, std)],
        outs=[
            (s, None, None)
            for s in (
                shape((total, ch), BF),
                shape((total, ch), BF),
                shape((9, 8, ch), F32),
                shape((8, ch), F32),
                *[shape((rows, ch), BF)] * n,
            )
        ],
        scratch=[pltpu.VMEM((total, ch), F32), pltpu.VMEM((total, ch), F32)],
        name="post_backward",
    )(source)


def cotangent_by_image(cotangent, select, pairs):
    rows, width = cotangent.shape
    size = select.shape[0]
    each = size // pairs
    per = 3

    def kernel(x, sel, *outs):
        for q in range(per):
            y = dot(sel[...], x[pl.ds(q * size, size), :]).astype(BF)
            for s in range(pairs):
                outs[s][pl.ds(q * each, each), :] = y[s * each : (s + 1) * each]

    return call(
        kernel,
        grid=(rows // (per * size),),
        ins=[(cotangent, (per * size, width), lambda i: (i, 0)), (select, None, None)],
        outs=[(shape((rows // pairs, width), BF), (per * each, width), lambda i: (i, 0))] * pairs,
        name="cotangent_by_image",
    )()


def token_block(chan, source, low, place, readout, cotangent, live):
    pairs, ch = len(low), low[0].shape[1]
    rows, width = cotangent.shape
    size = place.shape[0]
    each = size // pairs
    per = 3

    def kernel(chan_ref, src, *refs):
        lows, (place_ref, ro, cot, alive, tok_out, piece_out, low_out, by_pair) = refs[:pairs], refs[pairs:]
        for k in range(pairs):
            by_pair[src[k]] = lows[k][...]
        for q in range(per):
            at = pl.ds(q * size, size)
            x = jnp.concatenate([by_pair[s, pl.ds(q * each, each), :] for s in range(pairs)], 0)
            low_out[at, :] = dot(place_ref[...], x).astype(BF)
        logits = dot(low_out[...], ro[...])
        value, slope = gelu_parts(logits)
        tok_out[...] = value.astype(BF)
        piece_out[...] = (cot[...].astype(F32) * alive[...] * slope).astype(BF)

    block = per * size
    row_block = lambda i, c, s: (i, 0)
    return call(
        kernel,
        grid=(rows // block,),
        prefetch=2,
        ins=[
            *[(v, (per * each, ch), lambda i, c, s: (i, 0)) for v in low],
            (place, None, None),
            (readout, (ch, width), lambda i, c, s: (0, c[0])),
            (cotangent, (block, width), row_block),
            (live, None, None),
        ],
        outs=[
            (shape((rows, width), BF), (block, width), row_block),
            (shape((rows, width), BF), (block, width), row_block),
            (shape((rows, ch), BF), (block, ch), row_block),
        ],
        scratch=[pltpu.VMEM((pairs, per * each, ch), BF)],
        name="token_block",
    )(chan, source)


def pre_backward(order, returned, spread_up, nrm, std, gain, conv, pre_expand):
    slots, cells, ch = nrm.shape
    n = order.shape[0]
    part = slots // n
    wide = 24
    rows = part * cells

    def kernel(order_ref, *refs):
        ret, refs = refs[:n], refs[n:]
        up, norm_ref, std_ref, gn, conv_ref, we, exp_out, conv_grad_out, top_out, bottom_out, gain_out, grad, cgrad = refs
        k = pl.program_id(0)
        for i in range(n):

            @pl.when(k == i)
            def _():
                grad[...] = dot(up[...], ret[i][...])

        def norm(i, total_gain):
            u, j = i // (cells // 16), i % (cells // 16)
            at = pl.ds(pl.multiple_of(j * 16, 16), 16)
            nm = norm_ref[u, at, :]
            ng = grad[pl.ds(pl.multiple_of(i * 16, 16), 16), :] * silu_slope(nm * gn[...])
            sc = ng * gn[...]
            one = jnp.mean(sc, -1, keepdims=True)
            two = jnp.mean(sc * nm, -1, keepdims=True)
            exp_out[u, at, :] = (std_ref[u, at, :] * (sc - one - nm * two)).astype(BF)
            g = ng * nm
            return total_gain + g[:8] + g[8:]

        gains = lax.fori_loop(0, rows // 16, norm, jnp.zeros((8, ch), F32))

        @pl.when(k == 0)
        def _():
            gain_out[...] = gains

        @pl.when(k > 0)
        def _():
            gain_out[...] += gains

        cgrad[...] = dot(exp_out[...].reshape(rows, ch), we[...], NT)
        for u in range(part):

            def slope(lanes):
                g = cgrad[pl.ds(u * cells, cells), lanes] * silu_slope(conv_ref[u, :, lanes])
                conv_grad_out[u, :, lanes] = g.astype(BF)
                top_out[u, :, lanes] = g[:wide].astype(BF)
                bottom_out[u, :, lanes] = g[cells - wide :].astype(BF)

            chunks(ch // LANES, slope)

    by_order = lambda k, order: (order[k], 0, 0)
    whole = (part, cells, ch)
    edge = (part, wide, ch)
    return call(
        kernel,
        grid=(n,),
        prefetch=1,
        ins=[
            *[(r, None, None) for r in returned],
            (spread_up, None, None),
            (nrm, whole, by_order),
            (std, (part, cells, 1), by_order),
            (gain, None, None),
            (conv, whole, by_order),
            (pre_expand, None, None),
        ],
        outs=[
            (shape((slots, cells, ch), BF), whole, by_order),
            (shape((slots, cells, ch), BF), whole, by_order),
            (shape((slots, wide, ch), BF), edge, by_order),
            (shape((slots, wide, ch), BF), edge, by_order),
            (shape((8, ch), F32), None, None),
        ],
        scratch=[pltpu.VMEM((rows, ch), F32), pltpu.VMEM((rows, ch), F32)],
        name="pre_backward",
    )(order)


def pre_conv_backward(conv_grad, above, below, reduced, taps):
    slots, cells, ch = reduced.shape
    wide = above.shape[1]
    high = cells // wide

    def kernel(cg, up, down, red, tap, redg_out, taps_out):
        step = pl.program_id(0)
        first, last = edge_masks(wide, wide, 1)

        @pl.when(step == 0)
        def _():
            taps_out[...] = jnp.zeros_like(taps_out)

        def back(lanes):
            w = [tap[pl.ds(i, 1), lanes] for i in range(9)]
            mid = cg[0, :, lanes].astype(F32)
            rows = [up[0, :, lanes].astype(F32)]
            rows += [mid[i * wide : (i + 1) * wide] for i in range(high)]
            rows += [down[0, :, lanes].astype(F32)]
            v = [red[0, pl.ds(i * wide, wide), lanes] for i in range(high)]
            s = [sigmoid(t) for t in v]
            x = [(a * b).astype(BF).astype(F32) for a, b in zip(v, s)]
            d = [0.0] * high
            sums = [0.0] * 9
            for p in range(high + 2):
                g = rows[p]
                moves = [columns_moved(g, -1, first, last), g, columns_moved(g, 1, first, last)]
                for a in range(3):
                    i = p - 1 + a - 1
                    if 0 <= i < high:
                        for b in range(3):
                            d[i] = d[i] + moves[b] * w[3 * a + b]
                            prod = x[i] * moves[b]
                            sums[3 * a + b] = sums[3 * a + b] + (prod[:8] + prod[8:16] + prod[16:])
            out = [d[i] * (s[i] * (1.0 + v[i] * (1.0 - s[i]))) for i in range(high)]
            redg_out[0, :, lanes] = jnp.concatenate(out, 0).astype(BF)
            for i in range(9):
                taps_out[i, :, lanes] += sums[i]

        chunks(ch // LANES, back)

    image = lambda i: (i, 0, 0)
    return call(
        kernel,
        grid=(slots,),
        ins=[
            (conv_grad, (1, cells, ch), image),
            (above, (1, wide, ch), image),
            (below, (1, wide, ch), image),
            (reduced, (1, cells, ch), image),
            (taps, None, None),
        ],
        outs=[
            (shape((slots, cells, ch), BF), (1, cells, ch), image),
            (shape((9, 8, ch), F32), None, None),
        ],
        cost=12 * 10**9,
        name="pre_conv_backward",
    )()


def feature_backward(order, reduced_grad, pre_reduce, returned, spread_up):
    slots, cells, ch = reduced_grad.shape
    n = order.shape[0]
    part = slots // n

    def kernel(order_ref, rg, wr, up, *refs):
        ret, out = refs[:n], refs[n]
        k = pl.program_id(0)
        for i in range(n):

            @pl.when(k == i)
            def _():
                out[...] = dot(up[...], ret[i][...]).reshape(part, cells, ch)

        out[...] += dot(rg[...].reshape(part * cells, ch), wr[...], NT).reshape(part, cells, ch)

    by_order = lambda k, order: (order[k], 0, 0)
    whole = (part, cells, ch)
    return call(
        kernel,
        grid=(n,),
        prefetch=1,
        ins=[
            (reduced_grad, whole, by_order),
            (pre_reduce, None, None),
            (spread_up, None, None),
            *[(r, None, None) for r in returned],
        ],
        outs=[(shape((slots, cells, ch), F32), whole, by_order)],
        cost=9 * 10**9,
        name="feature_backward",
    )(order)[0]


def post_weight_grads(flat, reduced_grad, act, expanded_grad, n):
    total, ch = flat.shape
    share = ch // n
    rows = share // 8

    def kernel(x, g, a, e, out):
        for c in range(n):
            cut = slice(c * share, (c + 1) * share)
            v = dot(x[:, cut], g[...], TN).astype(BF)
            for d in range(8):
                out[d, c, :, :ch] = v[d * rows : (d + 1) * rows]
            for q in range(n):
                v = dot(a[:, q * share : (q + 1) * share], e[:, cut], TN).astype(BF)
                for d in range(8):
                    out[d, c, :, ch + q * share : ch + (q + 1) * share] = v[d * rows : (d + 1) * rows]

    return call(
        kernel,
        grid=(1,),
        ins=[(v, None, None) for v in (flat, reduced_grad, act, expanded_grad)],
        outs=[(shape((8, n, rows, 3 * ch), BF), (8, n, rows, 2 * ch), lambda i: (0, 0, 0, 0))],
        name="post_weight_grads",
    )()[0]


def readout_weight_grad(low, piece, load):
    total, ch = low.shape
    width = piece.shape[1]
    parts, n, rows, _ = load.shape
    share = ch // n

    def kernel(x, g, old, out):
        v = dot(x[...], g[...], TN).astype(BF)
        for d in range(parts):
            out[d, 0] = v[d * rows : (d + 1) * rows]

    return call(
        kernel,
        grid=(n,),
        ins=[(low, (total, share), lambda c: (0, c)), (piece, None, None)],
        outs=[(shape(load.shape, BF), (parts, 1, rows, width), lambda c: (0, c, 0, 2))],
        aliased=(load,),
        name="readout_weight_grad",
    )()[0]


def spread(n, k):
    return [(a * n + b, b * n + (a + k) % n) for a in range(n) for b in range(n)]


def cross(n, k):
    return [(a * n + b, ((b + k) % n) * n + a) for a in range(n) for b in range(n)]


def turn(n, k):
    return [(i, (i + k) % n) for i in range(n)]


def other_core(values):
    return lax.ppermute(values, "core", [(0, 1), (1, 0)])


def small_rows(*grads):
    ch = grads[0].shape[-1]
    counts = [g.shape[0] if g.ndim == 3 else 1 for g in grads]
    per = ch // LANES

    def kernel(*refs):
        out = refs[-1]
        at = 0
        for ref, count in zip(refs, counts):
            for i in range(count):
                v = jnp.sum(ref[i] if len(ref.shape) == 3 else ref[...], 0, keepdims=True)
                for q in range(per):
                    out[pl.ds(at, 1), :] = v[:, q * LANES : (q + 1) * LANES]
                    at += 1

    return call(
        kernel,
        grid=(1,),
        ins=[(g, None, None) for g in grads],
        outs=[(shape((sum(counts) * per, LANES), F32), None, None)],
        name="small_rows",
    )()[0]


def join_halves(core, mine, theirs, parts, small=()):
    rows, ch = mine.shape
    half = rows // 2
    width = ch + (LANES if small else 0)

    def kernel(core_ref, own, got, *refs):
        out = refs[-1]
        out[:, :ch] = (own[...].astype(F32) + got[...].astype(F32)).astype(BF)
        if small:
            first = (core_ref[0] == 0).astype(F32)
            total = (refs[0][...] + refs[1][...]) * first
            pad = jnp.zeros((half - total.shape[0], LANES), F32)
            out[:, ch:] = jnp.concatenate([total, pad], 0).astype(BF)

    return call(
        kernel,
        grid=(1,),
        prefetch=1,
        ins=[(mine, (half, ch), lambda i, c: (c[0], 0)), (theirs, None, None)] + [(v, None, None) for v in small],
        outs=[(shape((half, width), BF), None, None)],
        name="join_halves",
    )(core)[0].reshape(parts, half // parts, width)


def sum_and_copy(blocks):
    parts, rows, width = blocks.shape

    def kernel(x, out):
        def cut(lanes):
            total = jnp.sum(x[:, :, lanes].astype(F32), 0).astype(BF)
            out[:, :, lanes] = jnp.broadcast_to(total[None], (parts, rows, LANES))

        chunks(width // LANES, cut)

    return call(
        kernel,
        grid=(1,),
        ins=[(blocks, None, None)],
        outs=[(shape(blocks.shape, BF), None, None)],
        name="sum_and_copy",
    )()[0]


def finish_pre(place, half_rows, ch, earlier=()):
    half, width = half_rows.shape
    more = width > ch

    def kernel(place_ref, x, *outs):
        outs = outs[len(earlier) :]
        outs[0][...] = x[:, :ch].astype(F32)
        if more:
            outs[1][...] = x[:, ch:].astype(F32)

    return call(
        kernel,
        grid=(1,),
        prefetch=1,
        ins=[(half_rows, None, None)],
        outs=[(shape((2 * half, ch), F32), (half, ch), lambda i, c: (c[0], 0))]
        + ([(shape((half, width - ch), F32), None, None)] if more else []),
        aliased=earlier,
        name="finish_pre",
    )(place)


def finish_post(place, gathered, n, earlier=()):
    groups, per, width = gathered.shape
    share = 2 * groups * per
    ch = width // (n + 2)

    def kernel(place_ref, x, *outs):
        reduce_out, expand_out, read_out = outs[len(earlier) :]
        reduce_out[...] = x[0, :, :ch].astype(F32)
        for q in range(n):
            expand_out[q] = x[0, :, ch + q * share : ch + (q + 1) * share].astype(F32)
        read_out[...] = x[0, :, 2 * ch :].astype(F32)

    at = lambda i, c: (2 * i + c[0], 0)
    return call(
        kernel,
        grid=(groups,),
        prefetch=1,
        ins=[(gathered, (1, per, width), lambda i, c: (i, 0, 0))],
        outs=[
            (shape((share, ch), F32), (per, ch), at),
            (shape((n, share, share), F32), (n, per, share), lambda i, c: (0, 2 * i + c[0], 0)),
            (shape((share, n * ch), F32), (per, n * ch), at),
        ],
        aliased=earlier,
        cost=3 * 10**9,
        name="finish_post",
    )(place)


def after(values, *earlier):
    return lax.optimization_barrier((values, *earlier))[0]


def pool_matrix(part, high, wide):
    half = wide // 2
    m = np.zeros((high // 2 * half * part, part * (high // 2) * wide), np.float32)
    for u in range(part):
        for i in range(high // 2):
            for j in range(wide):
                m[(i * half + j // 2) * part + u, (u * (high // 2) + i) * wide + j] = 0.25
    return m


def spread_matrix(part, high, wide):
    half = wide // 2
    m = np.zeros((part * high * wide, high // 2 * half * part), np.float32)
    for u in range(part):
        for i in range(high):
            for j in range(wide):
                m[(u * high + i) * wide + j, ((i // 2) * half + j // 2) * part + u] = 0.25
    return m


def place_matrix(cells, slots, pairs):
    per = slots // pairs
    m = np.zeros((cells * slots, cells * slots), np.float32)
    for c in range(cells):
        for s in range(slots):
            m[c * slots + s, (s // per) * cells * per + c * per + s % per] = 1.0
    return m


def body(features, counts, pre_reduce, pre_conv, pre_expand, pre_gain, post_reduce, post_conv, post_expand, post_gain, readout, cotangent):
    n = lax.axis_size("chan")
    row = lax.axis_index("rows").astype(jnp.int32)
    chan = lax.axis_index("chan").astype(jnp.int32)
    core = lax.axis_index("core").astype(jnp.int32)
    eighth = lax.axis_index(("x", "core"))
    ch = pre_reduce.shape[0]
    slots, high, wide = features.shape[0], features.shape[1], features.shape[2]
    part = slots // n
    cells = high * wide
    pool = wide // 2
    share = ch // n
    out_share = cotangent.shape[3]
    steps = jnp.arange(n, dtype=jnp.int32)
    order = (row + steps) % n
    source = (row - steps) % n
    lows_at = (chan - steps) % n
    rank = jnp.full((1,), chan, jnp.int32)
    core_at = jnp.full((1,), core, jnp.int32)
    pre_taps = pre_conv.astype(F32).reshape(9, ch)
    post_taps = post_conv.astype(F32).reshape(9, ch)
    pre_gain_row = pre_gain.reshape(1, ch)
    pool_m = jnp.asarray(pool_matrix(part, high, wide), BF)
    up_m = jnp.asarray(spread_matrix(part, high, wide), BF)
    place = jnp.asarray(place_matrix(16, slots, n), BF)

    ends = n - 1
    down_pairs = [(i, i + 1) for i in range(ends)]
    up_pairs = [(i + 1, i) for i in range(ends)]
    above = lax.ppermute(features[:, -1], "rows", down_pairs)
    below = lax.ppermute(features[:, 0], "rows", up_pairs)
    gain_hi = post_gain.astype(BF)
    gain_lo = (post_gain - gain_hi.astype(F32)).astype(BF)
    gain_row = jnp.concatenate([gain_hi, gain_lo, jnp.zeros((ch - 2 * share,), BF)])[None]
    square = post_expand.reshape(n, share, share)
    shards = jnp.concatenate(
        [post_reduce, jnp.concatenate([square[q] for q in range(n)], axis=1), jnp.pad(gain_row, ((0, 63), (0, 0)))], axis=0
    )
    eighths = shards.reshape(8, -1, ch)
    full = lax.all_gather(lax.dynamic_index_in_dim(eighths, eighth, 0, keepdims=False), ("chan", "x", "core"), axis=0, tiled=True)
    full = full.reshape(n, 2 * share + 64, ch)
    flat_features = features.reshape(slots * cells, ch)
    reduced = dot(flat_features, pre_reduce).reshape(slots, cells, ch)
    live = (jnp.arange(SLOT)[None, :] < counts[:, None]).astype(F32).reshape(slots)
    size = 16 * slots
    at = lax.broadcasted_iota(jnp.int32, (size, size), 0)
    column = lax.broadcasted_iota(jnp.int32, (size, size), 1)
    each = size // n
    wanted = (at % each) // part * slots + part * ((chan + at // each) % n) + at % part
    select = jnp.where(column == wanted, jnp.tile(live, 16)[None, :], 0.0).astype(BF)
    cot_rows = cotangent.transpose(1, 2, 0, 3).reshape(-1, out_share)
    sends = cotangent_by_image(after(cot_rows, reduced, above, below), select, n)
    cots = [lax.ppermute(sends[k], ("rows", "chan"), cross(n, k)) for k in range(n)]

    convolved, convolved_act, normal_pre, pre_std, *pooled = pre_forward(
        order, reduced, above, below, features, pre_reduce, pre_taps, pre_expand, pre_gain_row, pool_m
    )

    moved = [pooled[0]] + [lax.ppermute(pooled[k], "rows", turn(n, k)) for k in range(1, n)]
    flat, post_reduced, post_act, post_convolved, post_cact, post_normal, post_std, low = post_forward(
        source, moved, full, post_taps, pool
    )
    refined_grad = readout_backward(source, low, readout, cots)
    lows = [lax.ppermute(low, ("rows", "chan"), spread(n, k)) for k in range(n - 1)]
    lows += [lax.ppermute(after(low, refined_grad), ("rows", "chan"), spread(n, n - 1))]
    refined_grad, lows[0] = lax.optimization_barrier((refined_grad, lows[0]))
    post_expanded_grad, post_reduced_grad, post_taps_grad, post_gain_grad, *back = post_backward(
        source, refined_grad, full, post_taps, post_act, post_reduced, post_convolved, post_normal, post_std, pool
    )

    returned = [back[0]] + [lax.ppermute(back[k], "rows", turn(n, -k)) for k in range(1, n)]

    flat = after(flat, lows[1], lows[2])
    load = post_weight_grads(flat, post_reduced_grad, post_cact, post_expanded_grad, n)

    alive = jnp.broadcast_to(jnp.tile(live, 48)[:, None], (48 * slots, 1))
    lows = after(lows, load, returned[1])
    tokens, piece, low_here = token_block(rank, lows_at, lows, place, readout, cot_rows, alive)
    load = readout_weight_grad(low_here, after(piece, returned[2:]), load)
    tokens = tokens.reshape(pool, pool, slots, out_share).transpose(2, 0, 1, 3)
    returned = after(returned, load)
    eight = share // 32
    rest = lax.psum_scatter(load, ("x", "core"), scatter_dimension=0, tiled=False)

    expanded_grad, convolved_grad, top, bottom, pre_gain_grad = pre_backward(
        order, returned, up_m, normal_pre, pre_std, pre_gain_row, convolved, pre_expand
    )
    grad_above = lax.ppermute(bottom, "rows", down_pairs)
    grad_below = lax.ppermute(top, "rows", up_pairs)
    chips = ("x", "rows", "chan")

    def halves(grad):
        return other_core(lax.dynamic_index_in_dim(grad.reshape(2, ch // 2, ch), 1 - core, 0, keepdims=False))

    act_rows = after(convolved_act, bottom).reshape(-1, ch)
    pre_expand_grad = dot(act_rows, expanded_grad.reshape(-1, ch), TN).astype(BF)
    expand_load = join_halves(core_at, pre_expand_grad, halves(pre_expand_grad), 64)
    expand_parts = lax.all_to_all(expand_load, chips, 0, 0, tiled=False)
    convolved_grad = after(convolved_grad, expand_load)
    reduced_grad, pre_taps_grad = pre_conv_backward(convolved_grad, grad_above, grad_below, reduced, pre_taps)

    rest = after(rest, reduced_grad).reshape(n, 4, eight, 3 * ch).transpose(1, 0, 2, 3)
    small = small_rows(pre_taps_grad, pre_gain_grad, post_taps_grad, post_gain_grad)
    expand_parts = sum_and_copy(after(expand_parts, rest, small))
    flat_features = after(flat_features, expand_parts)
    rest = lax.psum_scatter(rest, "rows", scatter_dimension=0, tiled=False)
    expand_all = lax.all_to_all(expand_parts, chips, 0, 0, tiled=False).reshape(ch // 2, -1)

    pre_reduce_grad = dot(flat_features, reduced_grad.reshape(-1, ch), TN).astype(BF)
    reduce_load = join_halves(core_at, pre_reduce_grad, halves(pre_reduce_grad), 64, (small, other_core(small)))
    reduce_parts = lax.all_to_all(reduce_load, chips, 0, 0, tiled=False)
    feature_grad = feature_backward(order, after(reduced_grad, reduce_load), pre_reduce, returned, up_m).reshape(features.shape)

    rest = lax.all_to_all(after(rest, feature_grad), "chan", 0, 0, tiled=False)
    summed = jnp.sum(rest[:, :, : 2 * ch].astype(F32), axis=0).astype(BF)
    rest = jnp.concatenate([summed] + [rest[c, :, 2 * ch :] for c in range(n)], axis=1)
    reduce_parts = sum_and_copy(after(reduce_parts, rest))
    rest = lax.all_gather(rest, ("x", "rows"), axis=0, tiled=False).reshape(4, 4 * eight, -1)
    reduce_all = lax.all_to_all(reduce_parts, chips, 0, 0, tiled=False).reshape(ch // 2, -1)

    def finish(kernel, values, *sizes):
        theirs = other_core(values)
        own = kernel(core_at, values, *sizes)
        theirs = after(theirs, *own)
        return own, theirs

    own, theirs = finish(finish_pre, after(expand_all, reduce_parts), ch)
    pre_expand_out = finish_pre(1 - core_at, theirs, ch, earlier=tuple(own))[0]
    own, theirs = finish(finish_pre, reduce_all, ch)
    pre_reduce_out, small_their = finish_pre(1 - core_at, theirs, ch, earlier=tuple(own[:1]))
    small_out = jnp.where(core == 0, own[1], small_their)
    own, theirs = finish(finish_post, rest, n)
    post_reduce_out, post_expand_out, readout_out = finish_post(1 - core_at, theirs, n, earlier=tuple(own))
    per = ch // LANES
    cut = [0, 9 * per, 10 * per, 19 * per, 20 * per]
    pre_conv_out, pre_gain_out, post_conv_out, post_gain_out = [small_out[a:b] for a, b in zip(cut, cut[1:])]
    return (
        tokens,
        feature_grad,
        pre_reduce_out,
        pre_conv_out.reshape(3, 3, ch),
        pre_expand_out,
        pre_gain_out.reshape(ch),
        post_reduce_out,
        post_conv_out.reshape(3, 3, ch),
        post_expand_out.reshape(ch, share),
        lax.dynamic_slice_in_dim(post_gain_out.reshape(ch), chan * share, share, 0),
        readout_out,
    )


def solution(mesh):
    grid = Mesh(mesh.devices.reshape(4, 2, 4, 4), ("x", "core", "rows", "chan"))
    images = P(("x", "core", "chan"), "rows", None, None)
    grids = P(("x", "core", "rows"), None, None, "chan")
    return jax.shard_map(
        body,
        mesh=grid,
        in_specs=(
            images,
            P(("x", "core", "rows")),
            P(),
            P(),
            P(),
            P(),
            P("chan", None),
            P(),
            P(None, "chan"),
            P("chan"),
            P(),
            grids,
        ),
        out_specs=(grids, images, P(), P(), P(), P(), P("chan", None), P(), P(None, "chan"), P("chan"), P("chan", None)),
        check_vma=False,
    )
```

```python
import functools

import jax
import jax.numpy as jnp
import numpy as np
from jax import lax
from jax.experimental import pallas as pl
from jax.experimental.pallas import tpu as pltpu
from jax.sharding import Mesh, PartitionSpec as P

SLOT = 4
EPS = 1e-06
BF = jnp.bfloat16
F32 = jnp.float32
LANES = 128
VMEM_LIMIT = 56 * 1024 * 1024
NN = ((1,), (0,))
NT = ((1,), (1,))
TN = ((0,), (0,))


def dot(a, b, dims=NN):
    return lax.dot_general(a, b, (dims, ((), ())), preferred_element_type=F32)


def sigmoid(v):
    return 0.5 * jnp.tanh(0.5 * v) + 0.5


def silu(v):
    return v * sigmoid(v)


def silu_slope(v):
    s = sigmoid(v)
    return s * (1.0 + v * (1.0 - s))


def gelu_parts(v):
    c = 0.7978845608028654
    square = v * v
    t = jnp.tanh(v * (c + (c * 0.044715) * square))
    half = 0.5 * (1.0 + t)
    slope = half + 0.5 * v * (1.0 - t * t) * (c + (3.0 * c * 0.044715) * square)
    return v * half, slope


def chunks(count, body, width=LANES):
    def step(i, carry):
        body(pl.ds(pl.multiple_of(i * width, width), width))
        return carry

    lax.fori_loop(0, count, step, 0)


def call(kernel, *, grid, ins, outs, scratch=(), prefetch=0, aliased=(), cost=1, name):
    def spec(shape, block, index):
        if block is None:
            block, index = shape, lambda *_: (0,) * len(shape)
        return pl.BlockSpec(block, index)

    arrays = [i[0] for i in ins] + list(aliased)
    in_specs = [spec(a.shape, b, m) for a, b, m in ins] + [pl.BlockSpec(memory_space=pl.ANY)] * len(aliased)
    out_specs = [spec(s.shape, b, m) for s, b, m in outs]

    def run(*scalars):
        return pl.pallas_call(
            kernel,
            grid_spec=pltpu.PrefetchScalarGridSpec(
                num_scalar_prefetch=prefetch,
                grid=grid,
                in_specs=in_specs,
                out_specs=out_specs,
                scratch_shapes=list(scratch),
            ),
            out_shape=[s[0] for s in outs],
            compiler_params=pltpu.CompilerParams(
                dimension_semantics=("arbitrary",) * len(grid), vmem_limit_bytes=VMEM_LIMIT
            ),
            input_output_aliases={prefetch + len(ins) + i: i for i in range(len(aliased))},
            cost_estimate=pl.CostEstimate(flops=cost, bytes_accessed=1, transcendentals=0),
            name=name,
        )(*scalars, *arrays)

    return run


def shape(dims, dtype):
    return jax.ShapeDtypeStruct(dims, dtype)


def columns_moved(t, by, first, last):
    rows = t.shape[0]
    return pltpu.roll(t, by % rows, 0) * (first if by > 0 else last)


def edge_masks(rows, width, depth):
    at = lax.broadcasted_iota(jnp.int32, (rows, LANES), 0) % (width * depth)
    return (at >= depth).astype(F32), (at < (width - 1) * depth).astype(F32)


def pre_forward(order, reduced, above, below, features, pre_reduce, taps, pre_expand, gain, pool, earlier=()):
    slots, high, wide, ch = features.shape
    cells = high * wide
    n = order.shape[0]
    part = 2

    def kernel(order_ref, red, up_ref, down_ref, feat, wr, tap, we, gn, pool_ref, *rest):
        conv_out, act_out, norm_out, std_out, *rest = rest[len(earlier) :]
        pooled_out, (halo, exp, sums) = rest[:n], rest[n:]
        k = pl.program_id(0)
        for side, ref in enumerate((up_ref, down_ref)):
            halo[side] = dot(ref[...].reshape(part * wide, ch), wr[...]).reshape(part, wide, ch)
        first, last = edge_masks(wide, wide, 1)
        for u in range(part):

            def conv(lanes):
                w = [tap[pl.ds(i, 1), lanes] for i in range(9)]
                rows = [halo[0, u, :, lanes]]
                rows += [red[u, pl.ds(i * wide, wide), lanes] for i in range(high)]
                rows += [halo[1, u, :, lanes]]
                rows = [silu(r).astype(BF).astype(F32) for r in rows]
                acts = []
                for i in range(high):
                    t = [sum(rows[i + a] * w[3 * a + b] for a in range(3)) for b in range(3)]
                    c = t[1] + columns_moved(t[0], 1, first, last) + columns_moved(t[2], -1, first, last)
                    conv_out[u, pl.ds(i * wide, wide), lanes] = c
                    acts.append(silu(c))
                act_out[u, :, lanes] = jnp.concatenate(acts, 0).astype(BF)

            chunks(ch // LANES, conv)

        exp[...] = dot(act_out[...].reshape(part * cells, ch), we[...])

        def norm(p, carry):
            u, i = p // (high // 2), p % (high // 2)
            total = [0.0] * (wide // 8)
            for half in range(2):
                f = feat[u, 2 * i + half].astype(F32)
                for t in range(wide // 8):
                    row = (2 * i + half) * wide + 8 * t
                    e = exp[pl.ds(pl.multiple_of(u * cells + row, 8), 8), :]
                    mean = jnp.mean(e, -1, keepdims=True)
                    square = jnp.mean(e * e, -1, keepdims=True)
                    std = lax.rsqrt(square - mean * mean + EPS)
                    nrm = (e - mean) * std
                    norm_out[u, pl.ds(pl.multiple_of(row, 8), 8), :] = nrm
                    std_out[u, pl.ds(pl.multiple_of(row, 8), 8), :] = std
                    total[t] = total[t] + f[8 * t : 8 * t + 8] + silu(nrm * gn[...])
            for t in range(wide // 8):
                sums[pl.ds(pl.multiple_of(p * wide + 8 * t, 8), 8), :] = total[t]
            return carry

        lax.fori_loop(0, part * high // 2, norm, 0)
        s = sums[...]
        hi = s.astype(BF)
        lo = (s - hi.astype(F32)).astype(BF)
        pooled = (dot(pool_ref[...], hi) + dot(pool_ref[...], lo)).astype(BF)
        for i in range(n):

            @pl.when(k == i)
            def _():
                pooled_out[i][...] = pooled

    def by_order(rest):
        return lambda k, order: (order[k],) + (0,) * rest

    pooled_rows = pool.shape[0]
    block = (part, cells, ch)
    return call(
        kernel,
        grid=(n,),
        prefetch=1,
        ins=[
            (reduced, block, by_order(2)),
            (above, (part, wide, ch), by_order(2)),
            (below, (part, wide, ch), by_order(2)),
            (features, (part, high, wide, ch), by_order(3)),
            (pre_reduce, None, None),
            (taps, None, None),
            (pre_expand, None, None),
            (gain, None, None),
            (pool, None, None),
        ],
        outs=[
            (shape((slots, cells, ch), F32), block, by_order(2)),
            (shape((slots, cells, ch), BF), block, by_order(2)),
            (shape((slots, cells, ch), F32), block, by_order(2)),
            (shape((slots, cells, 1), F32), (part, cells, 1), by_order(2)),
        ]
        + [(shape((pooled_rows, ch), BF), None, None)] * n,
        scratch=[
            pltpu.VMEM((2, part, wide, ch), F32),
            pltpu.VMEM((part * cells, ch), F32),
            pltpu.VMEM((part * cells // 2, ch), F32),
        ],
        aliased=earlier,
        name="pre_forward",
    )(order)


def gain_row(w, n, share):
    at = 2 * share
    parts = [w[c, at : at + 16, :].astype(F32)[:1] for c in range(n)]
    return jnp.concatenate([p[:, :share] + p[:, share : 2 * share] for p in parts], 1)


def post_forward(source, moved, weights, taps, pool):
    n, (rows, ch) = len(moved), moved[0].shape
    total = n * rows
    depth = total // (pool * pool)
    share = ch // n

    def kernel(src, *refs):
        got, (w, tap, flat_out, red_out, act_out, conv_out, cact_out, norm_out, std_out, low_out, wide_ref) = refs[:n], refs[n:]
        for k in range(n):
            at = pl.multiple_of(src[k] * rows, 8)
            wide_ref[pl.ds(at, rows), :] = got[k][...].astype(F32)
        gain = gain_row(w, n, share)
        flat_out[...] = wide_ref[...].astype(BF)
        red = 0.0
        for c in range(n):
            red = red + dot(flat_out[:, c * share : (c + 1) * share], w[c, :share])
        red_out[...] = red
        first, last = edge_masks(total, pool, depth)
        step = pool * depth

        def conv(lanes):
            x = silu(red_out[:, lanes]).astype(BF)
            act_out[:, lanes] = x
            x = x.astype(F32)
            moves = [columns_moved(x, depth, first, last), x, columns_moved(x, -depth, first, last)]
            t = [sum(moves[b] * tap[pl.ds(3 * a + b, 1), lanes] for b in range(3)) for a in range(3)]
            none = jnp.zeros((step, LANES), F32)
            c = t[1] + jnp.concatenate([none, t[0][:-step]], 0) + jnp.concatenate([t[2][step:], none], 0)
            conv_out[:, lanes] = c
            cact_out[:, lanes] = silu(c).astype(BF)

        chunks(ch // LANES, conv)
        for c in range(n):
            e = 0.0
            for q in range(n):
                cut = slice(q * share, (q + 1) * share)
                e = e + dot(cact_out[:, cut], w[c, share : 2 * share, cut])
            norm_out[:, c * share : (c + 1) * share] = e

        def norm(i, carry):
            at = pl.ds(pl.multiple_of(i * 16, 16), 16)
            e = norm_out[at, :]
            mean = jnp.mean(e, -1, keepdims=True)
            square = jnp.mean(e * e, -1, keepdims=True)
            std = lax.rsqrt(square - mean * mean + EPS)
            nrm = (e - mean) * std
            norm_out[at, :] = nrm
            std_out[at, :] = std
            low_out[at, :] = (wide_ref[at, :] + silu(nrm * gain)).astype(BF)
            return carry

        lax.fori_loop(0, total // 16, norm, 0)

    wide = shape((total, ch), F32)
    narrow = shape((total, ch), BF)
    return call(
        kernel,
        grid=(1,),
        prefetch=1,
        ins=[(a, None, None) for a in (*moved, weights, taps)],
        outs=[(s, None, None) for s in (narrow, wide, narrow, wide, narrow, wide, shape((total, 1), F32), narrow)],
        scratch=[pltpu.VMEM((total, ch), F32)],
        name="post_forward",
    )(source)


def readout_backward(low, readout, cots):
    total, ch = low.shape
    n, _, out_share = cots.shape

    def kernel(low_ref, ro, cot, grad):
        k = pl.program_id(0)
        logits = dot(low_ref[...], ro[...])
        piece = (cot[0].astype(F32) * gelu_parts(logits)[1]).astype(BF)
        term = dot(piece, ro[...], NT)

        @pl.when(k == 0)
        def _():
            grad[...] = term

        @pl.when(k > 0)
        def _():
            grad[...] += term

    return call(
        kernel,
        grid=(n,),
        ins=[
            (low, None, None),
            (readout, (ch, out_share), lambda k: (0, k)),
            (cots, (1, total, out_share), lambda k: (k, 0, 0)),
        ],
        outs=[(shape((total, ch), F32), None, None)],
        name="readout_backward",
    )()[0]


def post_backward(source, refined_grad, weights, taps, act, red, conv, nrm, std, pool):
    total, ch = act.shape
    n = weights.shape[0]
    share = ch // n
    rows = total // n
    depth = total // (pool * pool)

    def kernel(src, rg, w, tap, act_ref, red_ref, conv_ref, norm_ref, std_ref, exp_out, redg_out, taps_out, gain_out, *rest):
        back_out, (grad, cgrad) = rest[:n], rest[n:]
        gain = gain_row(w, n, share)

        def norm(i, total_gain):
            at = pl.ds(pl.multiple_of(i * 16, 16), 16)
            nm = norm_ref[at, :]
            ng = rg[at, :] * silu_slope(nm * gain)
            sc = ng * gain
            one = jnp.mean(sc, -1, keepdims=True)
            two = jnp.mean(sc * nm, -1, keepdims=True)
            exp_out[at, :] = (std_ref[at, :] * (sc - one - nm * two)).astype(BF)
            g = ng * nm
            return total_gain + g[:8] + g[8:]

        gain_out[...] = lax.fori_loop(0, total // 16, norm, jnp.zeros((8, ch), F32))
        for q in range(n):
            cut = slice(q * share, (q + 1) * share)
            cg = 0.0
            for c in range(n):
                cg = cg + dot(exp_out[:, c * share : (c + 1) * share], w[c, share : 2 * share, cut], NT)
            cgrad[:, cut] = cg
        first, last = edge_masks(total, pool, depth)
        step = pool * depth

        def back(lanes):
            g = (cgrad[:, lanes] * silu_slope(conv_ref[:, lanes])).astype(BF).astype(F32)
            x = act_ref[:, lanes].astype(F32)
            moves = [columns_moved(g, -depth, first, last), g, columns_moved(g, depth, first, last)]
            none = jnp.zeros((step, LANES), F32)
            xs = [
                jnp.concatenate([none, x[:-step]], 0),
                x,
                jnp.concatenate([x[step:], none], 0),
            ]
            for a in range(3):
                for b in range(3):
                    prod = xs[a] * moves[b]
                    taps_out[3 * a + b, :, lanes] = jnp.sum(prod.reshape(total // 8, 8, LANES), 0)
            t = [sum(moves[b] * tap[pl.ds(3 * a + b, 1), lanes] for b in range(3)) for a in range(3)]
            d = t[1] + jnp.concatenate([t[0][step:], none], 0) + jnp.concatenate([none, t[2][:-step]], 0)
            redg_out[:, lanes] = (d * silu_slope(red_ref[:, lanes])).astype(BF)

        chunks(ch // LANES, back)
        for c in range(n):
            cut = slice(c * share, (c + 1) * share)
            grad[:, cut] = rg[:, cut] + dot(redg_out[...], w[c, :share], NT)
        for r in range(n):
            at = pl.ds(pl.multiple_of(src[r] * rows, 8), rows)
            back_out[r][...] = grad[at, :].astype(BF)

    return call(
        kernel,
        grid=(1,),
        prefetch=1,
        ins=[(a, None, None) for a in (refined_grad, weights, taps, act, red, conv, nrm, std)],
        outs=[
            (s, None, None)
            for s in (
                shape((total, ch), BF),
                shape((total, ch), BF),
                shape((9, 8, ch), F32),
                shape((8, ch), F32),
                *[shape((rows, ch), BF)] * n,
            )
        ],
        scratch=[pltpu.VMEM((total, ch), F32), pltpu.VMEM((total, ch), F32)],
        name="post_backward",
    )(source)


def cotangent_by_image(cotangent, select):
    rows, width = cotangent.shape
    size = select.shape[0]
    pairs = SLOT
    each = size // pairs
    per = 3

    def kernel(x, sel, out):
        for q in range(per):
            y = dot(sel[...], x[pl.ds(q * size, size), :]).astype(BF)
            for s in range(pairs):
                out[s, pl.ds(q * each, each), :] = y[s * each : (s + 1) * each]

    return call(
        kernel,
        grid=(rows // (per * size),),
        ins=[(cotangent, (per * size, width), lambda i: (i, 0)), (select, None, None)],
        outs=[(shape((pairs, rows // pairs, width), BF), (pairs, per * each, width), lambda i: (0, i, 0))],
        name="cotangent_by_image",
    )()[0]


def token_block(chan, source, low, place, readout, cotangent, live):
    pairs, ch = len(low), low[0].shape[1]
    rows, width = cotangent.shape
    size = place.shape[0]
    each = size // pairs
    per = 3

    def kernel(chan_ref, src, *refs):
        lows, (place_ref, ro, cot, alive, tok_out, piece_out, low_out, by_pair) = refs[:pairs], refs[pairs:]
        for k in range(pairs):
            by_pair[src[k]] = lows[k][...]
        for q in range(per):
            at = pl.ds(q * size, size)
            x = jnp.concatenate([by_pair[s, pl.ds(q * each, each), :] for s in range(pairs)], 0)
            low_out[at, :] = dot(place_ref[...], x).astype(BF)
        logits = dot(low_out[...], ro[...])
        value, slope = gelu_parts(logits)
        tok_out[...] = value.astype(BF)
        piece_out[...] = (cot[...].astype(F32) * alive[...] * slope).astype(BF)

    block = per * size
    row_block = lambda i, c, s: (i, 0)
    return call(
        kernel,
        grid=(rows // block,),
        prefetch=2,
        ins=[
            *[(v, (per * each, ch), lambda i, c, s: (i, 0)) for v in low],
            (place, None, None),
            (readout, (ch, width), lambda i, c, s: (0, c[0])),
            (cotangent, (block, width), row_block),
            (live, None, None),
        ],
        outs=[
            (shape((rows, width), BF), (block, width), row_block),
            (shape((rows, width), BF), (block, width), row_block),
            (shape((rows, ch), BF), (block, ch), row_block),
        ],
        scratch=[pltpu.VMEM((pairs, per * each, ch), BF)],
        name="token_block",
    )(chan, source)


def pre_backward(order, returned, spread_up, nrm, std, gain, conv, pre_expand):
    slots, cells, ch = nrm.shape
    n = order.shape[0]
    part = slots // n
    wide = 24
    rows = part * cells

    def kernel(order_ref, *refs):
        ret, refs = refs[:n], refs[n:]
        up, norm_ref, std_ref, gn, conv_ref, we, exp_out, conv_grad_out, top_out, bottom_out, gain_out, grad, cgrad = refs
        k = pl.program_id(0)
        for i in range(n):

            @pl.when(k == i)
            def _():
                grad[...] = dot(up[...], ret[i][...])

        def norm(i, total_gain):
            u, j = i // (cells // 16), i % (cells // 16)
            at = pl.ds(pl.multiple_of(j * 16, 16), 16)
            nm = norm_ref[u, at, :]
            ng = grad[pl.ds(pl.multiple_of(i * 16, 16), 16), :] * silu_slope(nm * gn[...])
            sc = ng * gn[...]
            one = jnp.mean(sc, -1, keepdims=True)
            two = jnp.mean(sc * nm, -1, keepdims=True)
            exp_out[u, at, :] = (std_ref[u, at, :] * (sc - one - nm * two)).astype(BF)
            g = ng * nm
            return total_gain + g[:8] + g[8:]

        gains = lax.fori_loop(0, rows // 16, norm, jnp.zeros((8, ch), F32))

        @pl.when(k == 0)
        def _():
            gain_out[...] = gains

        @pl.when(k > 0)
        def _():
            gain_out[...] += gains

        cgrad[...] = dot(exp_out[...].reshape(rows, ch), we[...], NT)
        for u in range(part):

            def slope(lanes):
                g = cgrad[pl.ds(u * cells, cells), lanes] * silu_slope(conv_ref[u, :, lanes])
                conv_grad_out[u, :, lanes] = g.astype(BF)
                top_out[u, :, lanes] = g[:wide].astype(BF)
                bottom_out[u, :, lanes] = g[cells - wide :].astype(BF)

            chunks(ch // LANES, slope)

    by_order = lambda k, order: (order[k], 0, 0)
    whole = (part, cells, ch)
    edge = (part, wide, ch)
    return call(
        kernel,
        grid=(n,),
        prefetch=1,
        ins=[
            *[(r, None, None) for r in returned],
            (spread_up, None, None),
            (nrm, whole, by_order),
            (std, (part, cells, 1), by_order),
            (gain, None, None),
            (conv, whole, by_order),
            (pre_expand, None, None),
        ],
        outs=[
            (shape((slots, cells, ch), BF), whole, by_order),
            (shape((slots, cells, ch), BF), whole, by_order),
            (shape((slots, wide, ch), BF), edge, by_order),
            (shape((slots, wide, ch), BF), edge, by_order),
            (shape((8, ch), F32), None, None),
        ],
        scratch=[pltpu.VMEM((rows, ch), F32), pltpu.VMEM((rows, ch), F32)],
        name="pre_backward",
    )(order)


def pre_conv_backward(conv_grad, above, below, reduced, taps):
    slots, cells, ch = reduced.shape
    wide = above.shape[1]
    high = cells // wide

    def kernel(cg, up, down, red, tap, redg_out, taps_out):
        step = pl.program_id(0)
        first, last = edge_masks(wide, wide, 1)

        @pl.when(step == 0)
        def _():
            taps_out[...] = jnp.zeros_like(taps_out)

        def back(lanes):
            w = [tap[pl.ds(i, 1), lanes] for i in range(9)]
            mid = cg[0, :, lanes].astype(F32)
            rows = [up[0, :, lanes].astype(F32)]
            rows += [mid[i * wide : (i + 1) * wide] for i in range(high)]
            rows += [down[0, :, lanes].astype(F32)]
            v = [red[0, pl.ds(i * wide, wide), lanes] for i in range(high)]
            s = [sigmoid(t) for t in v]
            x = [(a * b).astype(BF).astype(F32) for a, b in zip(v, s)]
            d = [0.0] * high
            sums = [0.0] * 9
            for p in range(high + 2):
                g = rows[p]
                moves = [columns_moved(g, -1, first, last), g, columns_moved(g, 1, first, last)]
                for a in range(3):
                    i = p - 1 + a - 1
                    if 0 <= i < high:
                        for b in range(3):
                            d[i] = d[i] + moves[b] * w[3 * a + b]
                            prod = x[i] * moves[b]
                            sums[3 * a + b] = sums[3 * a + b] + (prod[:8] + prod[8:16] + prod[16:])
            out = [d[i] * (s[i] * (1.0 + v[i] * (1.0 - s[i]))) for i in range(high)]
            redg_out[0, :, lanes] = jnp.concatenate(out, 0).astype(BF)
            for i in range(9):
                taps_out[i, :, lanes] += sums[i]

        chunks(ch // LANES, back)

    image = lambda i: (i, 0, 0)
    return call(
        kernel,
        grid=(slots,),
        ins=[
            (conv_grad, (1, cells, ch), image),
            (above, (1, wide, ch), image),
            (below, (1, wide, ch), image),
            (reduced, (1, cells, ch), image),
            (taps, None, None),
        ],
        outs=[
            (shape((slots, cells, ch), BF), (1, cells, ch), image),
            (shape((9, 8, ch), F32), None, None),
        ],
        name="pre_conv_backward",
    )()


def feature_backward(order, reduced_grad, pre_reduce, returned, spread_up):
    slots, cells, ch = reduced_grad.shape
    n = order.shape[0]
    part = slots // n

    def kernel(order_ref, rg, wr, up, *refs):
        ret, out = refs[:n], refs[n]
        k = pl.program_id(0)
        for i in range(n):

            @pl.when(k == i)
            def _():
                out[...] = dot(up[...], ret[i][...]).reshape(part, cells, ch)

        out[...] += dot(rg[...].reshape(part * cells, ch), wr[...], NT).reshape(part, cells, ch)

    by_order = lambda k, order: (order[k], 0, 0)
    whole = (part, cells, ch)
    return call(
        kernel,
        grid=(n,),
        prefetch=1,
        ins=[
            (reduced_grad, whole, by_order),
            (pre_reduce, None, None),
            (spread_up, None, None),
            *[(r, None, None) for r in returned],
        ],
        outs=[(shape((slots, cells, ch), F32), whole, by_order)],
        name="feature_backward",
    )(order)[0]


def post_weight_grads(flat, reduced_grad, act, expanded_grad, n):
    total, ch = flat.shape
    share = ch // n
    rows = share // 8

    def kernel(x, g, a, e, out):
        for c in range(n):
            cut = slice(c * share, (c + 1) * share)
            v = dot(x[:, cut], g[...], TN).astype(BF)
            for d in range(8):
                out[d, c, :, :ch] = v[d * rows : (d + 1) * rows]
            for q in range(n):
                v = dot(a[:, q * share : (q + 1) * share], e[:, cut], TN).astype(BF)
                for d in range(8):
                    out[d, c, :, ch + q * share : ch + (q + 1) * share] = v[d * rows : (d + 1) * rows]

    return call(
        kernel,
        grid=(1,),
        ins=[(v, None, None) for v in (flat, reduced_grad, act, expanded_grad)],
        outs=[(shape((8, n, rows, 3 * ch), BF), (8, n, rows, 2 * ch), lambda i: (0, 0, 0, 0))],
        name="post_weight_grads",
    )()[0]


def readout_weight_grad(low, piece, load):
    total, ch = low.shape
    width = piece.shape[1]
    parts, n, rows, _ = load.shape
    share = ch // n

    def kernel(x, g, old, out):
        v = dot(x[...], g[...], TN).astype(BF)
        for d in range(parts):
            out[d, 0] = v[d * rows : (d + 1) * rows]

    return call(
        kernel,
        grid=(n,),
        ins=[(low, (total, share), lambda c: (0, c)), (piece, None, None)],
        outs=[(shape(load.shape, BF), (parts, 1, rows, width), lambda c: (0, c, 0, 2))],
        aliased=(load,),
        name="readout_weight_grad",
    )()[0]


def spread(n, k):
    return [(a * n + b, b * n + (a + k) % n) for a in range(n) for b in range(n)]


def other_core(values):
    return lax.ppermute(values, "core", [(0, 1), (1, 0)])


def small_rows(*grads):
    ch = grads[0].shape[-1]
    counts = [g.shape[0] if g.ndim == 3 else 1 for g in grads]
    per = ch // LANES

    def kernel(*refs):
        out = refs[-1]
        at = 0
        for ref, count in zip(refs, counts):
            for i in range(count):
                v = jnp.sum(ref[i] if len(ref.shape) == 3 else ref[...], 0, keepdims=True)
                for q in range(per):
                    out[pl.ds(at, 1), :] = v[:, q * LANES : (q + 1) * LANES]
                    at += 1

    return call(
        kernel,
        grid=(1,),
        ins=[(g, None, None) for g in grads],
        outs=[(shape((sum(counts) * per, LANES), F32), None, None)],
        name="small_rows",
    )()[0]


def join_halves(core, mine, theirs, small, their_small, parts):
    rows, ch = mine[0].shape
    half = rows // 2
    width = len(mine) * ch + LANES
    count = small.shape[0]
    m = len(mine)

    def kernel(core_ref, *refs):
        own, got = refs[:m], refs[m : 2 * m]
        sm, got_sm, out = refs[2 * m :]
        for i in range(m):
            out[:, i * ch : (i + 1) * ch] = (own[i][...].astype(F32) + got[i][...].astype(F32)).astype(BF)
        first = (core_ref[0] == 0).astype(F32)
        total = (sm[...] + got_sm[...]) * first
        pad = jnp.zeros((half - count, LANES), F32)
        out[:, m * ch :] = jnp.concatenate([total, pad], 0).astype(BF)

    return call(
        kernel,
        grid=(1,),
        prefetch=1,
        ins=[(v, (half, ch), lambda i, c: (c[0], 0)) for v in mine]
        + [(v, None, None) for v in (*theirs, small, their_small)],
        outs=[(shape((half, width), BF), None, None)],
        name="join_halves",
    )(core)[0].reshape(parts, half // parts, width)


def sum_and_copy(blocks):
    parts, rows, width = blocks.shape

    def kernel(x, out):
        def cut(lanes):
            total = jnp.sum(x[:, :, lanes].astype(F32), 0).astype(BF)
            out[:, :, lanes] = jnp.broadcast_to(total[None], (parts, rows, LANES))

        chunks(width // LANES, cut)

    return call(
        kernel,
        grid=(1,),
        ins=[(blocks, None, None)],
        outs=[(shape(blocks.shape, BF), None, None)],
        name="sum_and_copy",
    )()[0]


def finish_pre(place, half_rows, ch, earlier=()):
    half, width = half_rows.shape
    m = (width - LANES) // ch

    def kernel(place_ref, x, *outs):
        outs = outs[len(earlier) :]
        for i in range(m):
            outs[i][...] = x[:, i * ch : (i + 1) * ch].astype(F32)
        outs[m][...] = x[:, m * ch :].astype(F32)

    return call(
        kernel,
        grid=(1,),
        prefetch=1,
        ins=[(half_rows, None, None)],
        outs=[(shape((2 * half, ch), F32), (half, ch), lambda i, c: (c[0], 0)) for _ in range(m)]
        + [(shape((half, LANES), F32), None, None)],
        aliased=earlier,
        name="finish_pre",
    )(place)


def finish_post(place, gathered, n, earlier=()):
    groups, per, width = gathered.shape
    share = 2 * groups * per
    ch = width // (n + 2)

    def kernel(place_ref, x, *outs):
        reduce_out, expand_out, read_out = outs[len(earlier) :]
        reduce_out[...] = x[0, :, :ch].astype(F32)
        for q in range(n):
            expand_out[q] = x[0, :, ch + q * share : ch + (q + 1) * share].astype(F32)
        read_out[...] = x[0, :, 2 * ch :].astype(F32)

    at = lambda i, c: (2 * i + c[0], 0)
    return call(
        kernel,
        grid=(groups,),
        prefetch=1,
        ins=[(gathered, (1, per, width), lambda i, c: (i, 0, 0))],
        outs=[
            (shape((share, ch), F32), (per, ch), at),
            (shape((n, share, share), F32), (n, per, share), lambda i, c: (0, 2 * i + c[0], 0)),
            (shape((share, n * ch), F32), (per, n * ch), at),
        ],
        aliased=earlier,
        name="finish_post",
    )(place)


def after(values, *earlier):
    return lax.optimization_barrier((values, *earlier))[0]


def pool_matrix(part, high, wide):
    half = wide // 2
    m = np.zeros((high // 2 * half * part, part * (high // 2) * wide), np.float32)
    for u in range(part):
        for i in range(high // 2):
            for j in range(wide):
                m[(i * half + j // 2) * part + u, (u * (high // 2) + i) * wide + j] = 0.25
    return m


def spread_matrix(part, high, wide):
    half = wide // 2
    m = np.zeros((part * high * wide, high // 2 * half * part), np.float32)
    for u in range(part):
        for i in range(high):
            for j in range(wide):
                m[(u * high + i) * wide + j, ((i // 2) * half + j // 2) * part + u] = 0.25
    return m


def place_matrix(cells, slots, pairs):
    per = slots // pairs
    m = np.zeros((cells * slots, cells * slots), np.float32)
    for c in range(cells):
        for s in range(slots):
            m[c * slots + s, (s // per) * cells * per + c * per + s % per] = 1.0
    return m


def body(features, counts, pre_reduce, pre_conv, pre_expand, pre_gain, post_reduce, post_conv, post_expand, post_gain, readout, cotangent):
    n = lax.axis_size("chan")
    row = lax.axis_index("rows").astype(jnp.int32)
    chan = lax.axis_index("chan").astype(jnp.int32)
    core = lax.axis_index("core").astype(jnp.int32)
    ch = pre_reduce.shape[0]
    slots, high, wide = features.shape[0], features.shape[1], features.shape[2]
    part = slots // n
    cells = high * wide
    pool = wide // 2
    share = ch // n
    out_share = cotangent.shape[3]
    steps = jnp.arange(n, dtype=jnp.int32)
    order = (row + steps) % n
    source = (chan - steps) % n
    rank = jnp.full((1,), chan, jnp.int32)
    core_at = jnp.full((1,), core, jnp.int32)
    pre_taps = pre_conv.astype(F32).reshape(9, ch)
    post_taps = post_conv.astype(F32).reshape(9, ch)
    pre_gain_row = pre_gain.reshape(1, ch)
    pool_m = jnp.asarray(pool_matrix(part, high, wide), BF)
    up_m = jnp.asarray(spread_matrix(part, high, wide), BF)
    place = jnp.asarray(place_matrix(16, slots, n), BF)

    ends = n - 1
    down_pairs = [(i, i + 1) for i in range(ends)]
    up_pairs = [(i + 1, i) for i in range(ends)]
    above = lax.ppermute(features[:, -1], "rows", down_pairs)
    below = lax.ppermute(features[:, 0], "rows", up_pairs)
    gain_hi = post_gain.astype(BF)
    gain_lo = (post_gain - gain_hi.astype(F32)).astype(BF)
    gain_row = jnp.concatenate([gain_hi, gain_lo, jnp.zeros((ch - 2 * share,), BF)])[None]
    square = post_expand.reshape(n, share, share)
    shards = jnp.concatenate(
        [post_reduce, jnp.concatenate([square[q] for q in range(n)], axis=1), jnp.pad(gain_row, ((0, 63), (0, 0)))], axis=0
    )
    shard = lax.dynamic_index_in_dim(shards.reshape(2, -1, ch), core, 0, keepdims=False)
    full = lax.all_gather(shard, ("chan", "core"), axis=0, tiled=True)
    full = full.reshape(n, 2 * share + 64, ch)
    flat_features = features.reshape(slots * cells, ch)
    reduced = dot(flat_features, pre_reduce).reshape(slots, cells, ch)
    live = (jnp.arange(SLOT)[None, :] < counts[:, None]).astype(F32).reshape(slots)
    select = place.T * jnp.tile(live.astype(BF), 16)[None, :]
    cot_rows = cotangent.transpose(1, 2, 0, 3).reshape(-1, out_share)
    cots = lax.all_to_all(cotangent_by_image(after(cot_rows, reduced, above, below), select), "chan", 0, 0, tiled=False)

    convolved, convolved_act, normal_pre, pre_std, *pooled = pre_forward(
        order, reduced, above, below, features, pre_reduce, pre_taps, pre_expand, pre_gain_row, pool_m
    )

    pooled = after(pooled, cots)
    moved = [lax.ppermute(pooled[k], ("rows", "chan"), spread(n, k)) for k in range(n)]
    flat, post_reduced, post_act, post_convolved, post_cact, post_normal, post_std, low = post_forward(
        source, moved, full, post_taps, pool
    )
    lows = [low] + [lax.ppermute(low, "chan", [(i, (i + k) % n) for i in range(n)]) for k in range(1, n)]
    refined_grad = readout_backward(low, readout, cots)
    post_expanded_grad, post_reduced_grad, post_taps_grad, post_gain_grad, *back = post_backward(
        source, refined_grad, full, post_taps, post_act, post_reduced, post_convolved, post_normal, post_std, pool
    )

    returned = [lax.ppermute(back[k], ("rows", "chan"), [(d, s) for s, d in spread(n, k)]) for k in range(n)]

    flat = after(flat, lows)
    load = post_weight_grads(flat, post_reduced_grad, post_cact, post_expanded_grad, n)

    alive = jnp.broadcast_to(jnp.tile(live, 48)[:, None], (48 * slots, 1))
    lows = after(lows, load, returned[:2])
    tokens, piece, low_here = token_block(rank, source, lows, place, readout, cot_rows, alive)
    load = readout_weight_grad(low_here, after(piece, returned[2:]), load)
    tokens = tokens.reshape(pool, pool, slots, out_share).transpose(2, 0, 1, 3)
    returned = after(returned, load)
    eight = share // 32
    rest = lax.psum_scatter(load, ("x", "core"), scatter_dimension=0, tiled=False)

    expanded_grad, convolved_grad, top, bottom, pre_gain_grad = pre_backward(
        order, returned, up_m, normal_pre, pre_std, pre_gain_row, convolved, pre_expand
    )
    grad_above = lax.ppermute(bottom, "rows", down_pairs)
    grad_below = lax.ppermute(top, "rows", up_pairs)
    act_rows = after(convolved_act, bottom).reshape(-1, ch)
    pre_expand_grad = dot(act_rows, expanded_grad.reshape(-1, ch), TN).astype(BF)
    convolved_grad = after(convolved_grad, pre_expand_grad)
    reduced_grad, pre_taps_grad = pre_conv_backward(convolved_grad, grad_above, grad_below, reduced, pre_taps)
    small = small_rows(pre_taps_grad, pre_gain_grad, post_taps_grad, post_gain_grad)
    pre_reduce_grad = dot(after(flat_features, small), reduced_grad.reshape(-1, ch), TN).astype(BF)

    chips = ("x", "rows", "chan")
    mine = [pre_reduce_grad, pre_expand_grad]
    theirs = [other_core(lax.dynamic_index_in_dim(g.reshape(2, ch // 2, ch), 1 - core, 0, keepdims=False)) for g in mine]
    rest = after(rest, *mine).reshape(n, 4, eight, 3 * ch).transpose(1, 0, 2, 3)
    theirs = after(theirs, rest)
    rest = lax.psum_scatter(rest, "rows", scatter_dimension=0, tiled=False)
    load = join_halves(core_at, mine, theirs, small, other_core(small), 64)
    pieces = lax.all_to_all(load, chips, 0, 0, tiled=False)
    feature_grad = feature_backward(order, after(reduced_grad, load), pre_reduce, returned, up_m).reshape(features.shape)

    rest = after(rest, feature_grad)
    block_at = lax.broadcasted_iota(jnp.int32, (1, 1, n * ch), 2) // ch
    padded = jnp.where(block_at == chan, jnp.tile(rest[:, :, 2 * ch :], (1, 1, n)), jnp.zeros((), BF))
    rest = jnp.concatenate([rest[:, :, : 2 * ch], padded], axis=2)
    pieces = after(pieces, rest)
    rest = lax.psum_scatter(rest, "chan", scatter_dimension=0, tiled=False)
    load = sum_and_copy(pieces)
    load_all = lax.all_to_all(load, chips, 0, 0, tiled=False).reshape(ch // 2, -1)
    rest = lax.all_gather(rest, ("x", "rows"), axis=0, tiled=False).reshape(4, 4 * eight, -1)

    def finish(kernel, values, *sizes):
        theirs = other_core(values)
        own = kernel(core_at, values, *sizes)
        theirs = after(theirs, *own)
        return own, theirs

    own, theirs = finish(finish_pre, load_all, ch)
    pre_reduce_out, pre_expand_out, small_their = finish_pre(1 - core_at, theirs, ch, earlier=tuple(own[:2]))
    small_out = jnp.where(core == 0, own[2], small_their)
    own, theirs = finish(finish_post, rest, n)
    post_reduce_out, post_expand_out, readout_out = finish_post(1 - core_at, theirs, n, earlier=tuple(own))
    per = ch // LANES
    cut = [0, 9 * per, 10 * per, 19 * per, 20 * per]
    pre_conv_out, pre_gain_out, post_conv_out, post_gain_out = [small_out[a:b] for a, b in zip(cut, cut[1:])]
    return (
        tokens,
        feature_grad,
        pre_reduce_out,
        pre_conv_out.reshape(3, 3, ch),
        pre_expand_out,
        pre_gain_out.reshape(ch),
        post_reduce_out,
        post_conv_out.reshape(3, 3, ch),
        post_expand_out.reshape(ch, share),
        lax.dynamic_slice_in_dim(post_gain_out.reshape(ch), chan * share, share, 0),
        readout_out,
    )


def solution(mesh):
    grid = Mesh(mesh.devices.reshape(4, 2, 4, 4), ("x", "core", "rows", "chan"))
    images = P(("x", "core", "chan"), "rows", None, None)
    grids = P(("x", "core", "rows"), None, None, "chan")
    return jax.shard_map(
        body,
        mesh=grid,
        in_specs=(
            images,
            P(("x", "core", "rows")),
            P(),
            P(),
            P(),
            P(),
            P("chan", None),
            P(),
            P(None, "chan"),
            P("chan"),
            P(),
            grids,
        ),
        out_specs=(grids, images, P(), P(), P(), P(), P("chan", None), P(), P(None, "chan"), P("chan"), P("chan", None)),
        check_vma=False,
    )
```

```python
import functools

import jax
import jax.numpy as jnp
import numpy as np
from jax import lax
from jax.experimental import pallas as pl
from jax.experimental.pallas import tpu as pltpu
from jax.sharding import Mesh, PartitionSpec as P

SLOT = 4
EPS = 1e-06
BF = jnp.bfloat16
F32 = jnp.float32
LANES = 128
VMEM_LIMIT = 56 * 1024 * 1024
NN = ((1,), (0,))
NT = ((1,), (1,))
TN = ((0,), (0,))


def dot(a, b, dims=NN):
    return lax.dot_general(a, b, (dims, ((), ())), preferred_element_type=F32)


def sigmoid(v):
    return 0.5 * jnp.tanh(0.5 * v) + 0.5


def silu(v):
    return v * sigmoid(v)


def silu_slope(v):
    s = sigmoid(v)
    return s * (1.0 + v * (1.0 - s))


def gelu_parts(v):
    c = 0.7978845608028654
    square = v * v
    t = jnp.tanh(v * (c + (c * 0.044715) * square))
    half = 0.5 * (1.0 + t)
    slope = half + 0.5 * v * (1.0 - t * t) * (c + (3.0 * c * 0.044715) * square)
    return v * half, slope


def chunks(count, body, width=LANES):
    def step(i, carry):
        body(pl.ds(pl.multiple_of(i * width, width), width))
        return carry

    lax.fori_loop(0, count, step, 0)


def call(kernel, *, grid, ins, outs, scratch=(), prefetch=0, aliased=(), cost=1, name):
    def spec(shape, block, index):
        if block is None:
            block, index = shape, lambda *_: (0,) * len(shape)
        return pl.BlockSpec(block, index)

    arrays = [i[0] for i in ins] + list(aliased)
    in_specs = [spec(a.shape, b, m) for a, b, m in ins] + [pl.BlockSpec(memory_space=pl.ANY)] * len(aliased)
    out_specs = [spec(s.shape, b, m) for s, b, m in outs]

    def run(*scalars):
        return pl.pallas_call(
            kernel,
            grid_spec=pltpu.PrefetchScalarGridSpec(
                num_scalar_prefetch=prefetch,
                grid=grid,
                in_specs=in_specs,
                out_specs=out_specs,
                scratch_shapes=list(scratch),
            ),
            out_shape=[s[0] for s in outs],
            compiler_params=pltpu.CompilerParams(
                dimension_semantics=("arbitrary",) * len(grid), vmem_limit_bytes=VMEM_LIMIT
            ),
            input_output_aliases={prefetch + len(ins) + i: i for i in range(len(aliased))},
            cost_estimate=pl.CostEstimate(flops=cost, bytes_accessed=1, transcendentals=0),
            name=name,
        )(*scalars, *arrays)

    return run


def shape(dims, dtype):
    return jax.ShapeDtypeStruct(dims, dtype)


def columns_moved(t, by, first, last):
    rows = t.shape[0]
    return pltpu.roll(t, by % rows, 0) * (first if by > 0 else last)


def edge_masks(rows, width, depth):
    at = lax.broadcasted_iota(jnp.int32, (rows, LANES), 0) % (width * depth)
    return (at >= depth).astype(F32), (at < (width - 1) * depth).astype(F32)


def pre_forward(order, reduced, above, below, features, pre_reduce, taps, pre_expand, gain, pool, earlier=()):
    slots, high, wide, ch = features.shape
    cells = high * wide
    n = order.shape[0]
    part = 2

    def kernel(order_ref, red, up_ref, down_ref, feat, wr, tap, we, gn, pool_ref, *rest):
        conv_out, act_out, norm_out, std_out, *rest = rest[len(earlier) :]
        pooled_out, (halo, exp, sums) = rest[:n], rest[n:]
        k = pl.program_id(0)
        for side, ref in enumerate((up_ref, down_ref)):
            halo[side] = dot(ref[...].reshape(part * wide, ch), wr[...]).reshape(part, wide, ch)
        first, last = edge_masks(wide, wide, 1)
        for u in range(part):

            def conv(lanes):
                w = [tap[pl.ds(i, 1), lanes] for i in range(9)]
                rows = [halo[0, u, :, lanes]]
                rows += [red[u, pl.ds(i * wide, wide), lanes] for i in range(high)]
                rows += [halo[1, u, :, lanes]]
                rows = [silu(r).astype(BF).astype(F32) for r in rows]
                acts = []
                for i in range(high):
                    t = [sum(rows[i + a] * w[3 * a + b] for a in range(3)) for b in range(3)]
                    c = t[1] + columns_moved(t[0], 1, first, last) + columns_moved(t[2], -1, first, last)
                    conv_out[u, pl.ds(i * wide, wide), lanes] = c
                    acts.append(silu(c))
                act_out[u, :, lanes] = jnp.concatenate(acts, 0).astype(BF)

            chunks(ch // LANES, conv)

        exp[...] = dot(act_out[...].reshape(part * cells, ch), we[...])

        def norm(p, carry):
            u, i = p // (high // 2), p % (high // 2)
            total = [0.0] * (wide // 8)
            for half in range(2):
                f = feat[u, 2 * i + half].astype(F32)
                for t in range(wide // 8):
                    row = (2 * i + half) * wide + 8 * t
                    e = exp[pl.ds(pl.multiple_of(u * cells + row, 8), 8), :]
                    mean = jnp.mean(e, -1, keepdims=True)
                    square = jnp.mean(e * e, -1, keepdims=True)
                    std = lax.rsqrt(square - mean * mean + EPS)
                    nrm = (e - mean) * std
                    norm_out[u, pl.ds(pl.multiple_of(row, 8), 8), :] = nrm
                    std_out[u, pl.ds(pl.multiple_of(row, 8), 8), :] = std
                    total[t] = total[t] + f[8 * t : 8 * t + 8] + silu(nrm * gn[...])
            for t in range(wide // 8):
                sums[pl.ds(pl.multiple_of(p * wide + 8 * t, 8), 8), :] = total[t]
            return carry

        lax.fori_loop(0, part * high // 2, norm, 0)
        s = sums[...]
        hi = s.astype(BF)
        lo = (s - hi.astype(F32)).astype(BF)
        pooled = (dot(pool_ref[...], hi) + dot(pool_ref[...], lo)).astype(BF)
        for i in range(n):

            @pl.when(k == i)
            def _():
                pooled_out[i][...] = pooled

    def by_order(rest):
        return lambda k, order: (order[k],) + (0,) * rest

    pooled_rows = pool.shape[0]
    block = (part, cells, ch)
    return call(
        kernel,
        grid=(n,),
        prefetch=1,
        ins=[
            (reduced, block, by_order(2)),
            (above, (part, wide, ch), by_order(2)),
            (below, (part, wide, ch), by_order(2)),
            (features, (part, high, wide, ch), by_order(3)),
            (pre_reduce, None, None),
            (taps, None, None),
            (pre_expand, None, None),
            (gain, None, None),
            (pool, None, None),
        ],
        outs=[
            (shape((slots, cells, ch), F32), block, by_order(2)),
            (shape((slots, cells, ch), BF), block, by_order(2)),
            (shape((slots, cells, ch), F32), block, by_order(2)),
            (shape((slots, cells, 1), F32), (part, cells, 1), by_order(2)),
        ]
        + [(shape((pooled_rows, ch), BF), None, None)] * n,
        scratch=[
            pltpu.VMEM((2, part, wide, ch), F32),
            pltpu.VMEM((part * cells, ch), F32),
            pltpu.VMEM((part * cells // 2, ch), F32),
        ],
        aliased=earlier,
        name="pre_forward",
    )(order)


def gain_row(w, n, share):
    at = 2 * share
    parts = [w[c, at : at + 16, :].astype(F32)[:1] for c in range(n)]
    return jnp.concatenate([p[:, :share] + p[:, share : 2 * share] for p in parts], 1)


def post_forward(source, moved, weights, taps, pool):
    n, (rows, ch) = len(moved), moved[0].shape
    total = n * rows
    depth = total // (pool * pool)
    share = ch // n

    def kernel(src, *refs):
        got, (w, tap, flat_out, red_out, act_out, conv_out, cact_out, norm_out, std_out, low_out, wide_ref) = refs[:n], refs[n:]
        for k in range(n):
            at = pl.multiple_of(src[k] * rows, 8)
            wide_ref[pl.ds(at, rows), :] = got[k][...].astype(F32)
        gain = gain_row(w, n, share)
        flat_out[...] = wide_ref[...].astype(BF)
        red = 0.0
        for c in range(n):
            red = red + dot(flat_out[:, c * share : (c + 1) * share], w[c, :share])
        red_out[...] = red
        first, last = edge_masks(total, pool, depth)
        step = pool * depth

        def conv(lanes):
            x = silu(red_out[:, lanes]).astype(BF)
            act_out[:, lanes] = x
            x = x.astype(F32)
            moves = [columns_moved(x, depth, first, last), x, columns_moved(x, -depth, first, last)]
            t = [sum(moves[b] * tap[pl.ds(3 * a + b, 1), lanes] for b in range(3)) for a in range(3)]
            none = jnp.zeros((step, LANES), F32)
            c = t[1] + jnp.concatenate([none, t[0][:-step]], 0) + jnp.concatenate([t[2][step:], none], 0)
            conv_out[:, lanes] = c
            cact_out[:, lanes] = silu(c).astype(BF)

        chunks(ch // LANES, conv)
        for c in range(n):
            e = 0.0
            for q in range(n):
                cut = slice(q * share, (q + 1) * share)
                e = e + dot(cact_out[:, cut], w[c, share : 2 * share, cut])
            norm_out[:, c * share : (c + 1) * share] = e

        def norm(i, carry):
            at = pl.ds(pl.multiple_of(i * 16, 16), 16)
            e = norm_out[at, :]
            mean = jnp.mean(e, -1, keepdims=True)
            square = jnp.mean(e * e, -1, keepdims=True)
            std = lax.rsqrt(square - mean * mean + EPS)
            nrm = (e - mean) * std
            norm_out[at, :] = nrm
            std_out[at, :] = std
            low_out[at, :] = (wide_ref[at, :] + silu(nrm * gain)).astype(BF)
            return carry

        lax.fori_loop(0, total // 16, norm, 0)

    wide = shape((total, ch), F32)
    narrow = shape((total, ch), BF)
    return call(
        kernel,
        grid=(1,),
        prefetch=1,
        ins=[(a, None, None) for a in (*moved, weights, taps)],
        outs=[(s, None, None) for s in (narrow, wide, narrow, wide, narrow, wide, shape((total, 1), F32), narrow)],
        scratch=[pltpu.VMEM((total, ch), F32)],
        name="post_forward",
    )(source)


def readout_backward(low, readout, cots):
    total, ch = low.shape
    n, _, out_share = cots.shape

    def kernel(low_ref, ro, cot, grad):
        k = pl.program_id(0)
        logits = dot(low_ref[...], ro[...])
        piece = (cot[0].astype(F32) * gelu_parts(logits)[1]).astype(BF)
        term = dot(piece, ro[...], NT)

        @pl.when(k == 0)
        def _():
            grad[...] = term

        @pl.when(k > 0)
        def _():
            grad[...] += term

    return call(
        kernel,
        grid=(n,),
        ins=[
            (low, None, None),
            (readout, (ch, out_share), lambda k: (0, k)),
            (cots, (1, total, out_share), lambda k: (k, 0, 0)),
        ],
        outs=[(shape((total, ch), F32), None, None)],
        name="readout_backward",
    )()[0]


def post_backward(source, refined_grad, weights, taps, act, red, conv, nrm, std, pool):
    total, ch = act.shape
    n = weights.shape[0]
    share = ch // n
    rows = total // n
    depth = total // (pool * pool)

    def kernel(src, rg, w, tap, act_ref, red_ref, conv_ref, norm_ref, std_ref, exp_out, redg_out, taps_out, gain_out, *rest):
        back_out, (grad, cgrad) = rest[:n], rest[n:]
        gain = gain_row(w, n, share)

        def norm(i, total_gain):
            at = pl.ds(pl.multiple_of(i * 16, 16), 16)
            nm = norm_ref[at, :]
            ng = rg[at, :] * silu_slope(nm * gain)
            sc = ng * gain
            one = jnp.mean(sc, -1, keepdims=True)
            two = jnp.mean(sc * nm, -1, keepdims=True)
            exp_out[at, :] = (std_ref[at, :] * (sc - one - nm * two)).astype(BF)
            g = ng * nm
            return total_gain + g[:8] + g[8:]

        gain_out[...] = lax.fori_loop(0, total // 16, norm, jnp.zeros((8, ch), F32))
        for q in range(n):
            cut = slice(q * share, (q + 1) * share)
            cg = 0.0
            for c in range(n):
                cg = cg + dot(exp_out[:, c * share : (c + 1) * share], w[c, share : 2 * share, cut], NT)
            cgrad[:, cut] = cg
        first, last = edge_masks(total, pool, depth)
        step = pool * depth

        def back(lanes):
            g = (cgrad[:, lanes] * silu_slope(conv_ref[:, lanes])).astype(BF).astype(F32)
            x = act_ref[:, lanes].astype(F32)
            moves = [columns_moved(g, -depth, first, last), g, columns_moved(g, depth, first, last)]
            none = jnp.zeros((step, LANES), F32)
            xs = [
                jnp.concatenate([none, x[:-step]], 0),
                x,
                jnp.concatenate([x[step:], none], 0),
            ]
            for a in range(3):
                for b in range(3):
                    prod = xs[a] * moves[b]
                    taps_out[3 * a + b, :, lanes] = jnp.sum(prod.reshape(total // 8, 8, LANES), 0)
            t = [sum(moves[b] * tap[pl.ds(3 * a + b, 1), lanes] for b in range(3)) for a in range(3)]
            d = t[1] + jnp.concatenate([t[0][step:], none], 0) + jnp.concatenate([none, t[2][:-step]], 0)
            redg_out[:, lanes] = (d * silu_slope(red_ref[:, lanes])).astype(BF)

        chunks(ch // LANES, back)
        for c in range(n):
            cut = slice(c * share, (c + 1) * share)
            grad[:, cut] = rg[:, cut] + dot(redg_out[...], w[c, :share], NT)
        for r in range(n):
            at = pl.ds(pl.multiple_of(src[r] * rows, 8), rows)
            back_out[r][...] = grad[at, :].astype(BF)

    return call(
        kernel,
        grid=(1,),
        prefetch=1,
        ins=[(a, None, None) for a in (refined_grad, weights, taps, act, red, conv, nrm, std)],
        outs=[
            (s, None, None)
            for s in (
                shape((total, ch), BF),
                shape((total, ch), BF),
                shape((9, 8, ch), F32),
                shape((8, ch), F32),
                *[shape((rows, ch), BF)] * n,
            )
        ],
        scratch=[pltpu.VMEM((total, ch), F32), pltpu.VMEM((total, ch), F32)],
        name="post_backward",
    )(source)


def cotangent_by_image(cotangent, select):
    rows, width = cotangent.shape
    size = select.shape[0]
    pairs = SLOT
    each = size // pairs
    per = 3

    def kernel(x, sel, out):
        for q in range(per):
            y = dot(sel[...], x[pl.ds(q * size, size), :]).astype(BF)
            for s in range(pairs):
                out[s, pl.ds(q * each, each), :] = y[s * each : (s + 1) * each]

    return call(
        kernel,
        grid=(rows // (per * size),),
        ins=[(cotangent, (per * size, width), lambda i: (i, 0)), (select, None, None)],
        outs=[(shape((pairs, rows // pairs, width), BF), (pairs, per * each, width), lambda i: (0, i, 0))],
        name="cotangent_by_image",
    )()[0]


def token_block(chan, source, low, place, readout, cotangent, live):
    pairs, ch = len(low), low[0].shape[1]
    rows, width = cotangent.shape
    size = place.shape[0]
    each = size // pairs
    per = 3

    def kernel(chan_ref, src, *refs):
        lows, (place_ref, ro, cot, alive, tok_out, piece_out, low_out, by_pair) = refs[:pairs], refs[pairs:]
        for k in range(pairs):
            by_pair[src[k]] = lows[k][...]
        for q in range(per):
            at = pl.ds(q * size, size)
            x = jnp.concatenate([by_pair[s, pl.ds(q * each, each), :] for s in range(pairs)], 0)
            low_out[at, :] = dot(place_ref[...], x).astype(BF)
        logits = dot(low_out[...], ro[...])
        value, slope = gelu_parts(logits)
        tok_out[...] = value.astype(BF)
        piece_out[...] = (cot[...].astype(F32) * alive[...] * slope).astype(BF)

    block = per * size
    row_block = lambda i, c, s: (i, 0)
    return call(
        kernel,
        grid=(rows // block,),
        prefetch=2,
        ins=[
            *[(v, (per * each, ch), lambda i, c, s: (i, 0)) for v in low],
            (place, None, None),
            (readout, (ch, width), lambda i, c, s: (0, c[0])),
            (cotangent, (block, width), row_block),
            (live, None, None),
        ],
        outs=[
            (shape((rows, width), BF), (block, width), row_block),
            (shape((rows, width), BF), (block, width), row_block),
            (shape((rows, ch), BF), (block, ch), row_block),
        ],
        scratch=[pltpu.VMEM((pairs, per * each, ch), BF)],
        name="token_block",
    )(chan, source)


def pre_backward(order, returned, spread_up, nrm, std, gain, conv, pre_expand):
    slots, cells, ch = nrm.shape
    n = order.shape[0]
    part = slots // n
    wide = 24
    rows = part * cells

    def kernel(order_ref, *refs):
        ret, refs = refs[:n], refs[n:]
        up, norm_ref, std_ref, gn, conv_ref, we, exp_out, conv_grad_out, top_out, bottom_out, gain_out, grad, cgrad = refs
        k = pl.program_id(0)
        for i in range(n):

            @pl.when(k == i)
            def _():
                grad[...] = dot(up[...], ret[i][...])

        def norm(i, total_gain):
            u, j = i // (cells // 16), i % (cells // 16)
            at = pl.ds(pl.multiple_of(j * 16, 16), 16)
            nm = norm_ref[u, at, :]
            ng = grad[pl.ds(pl.multiple_of(i * 16, 16), 16), :] * silu_slope(nm * gn[...])
            sc = ng * gn[...]
            one = jnp.mean(sc, -1, keepdims=True)
            two = jnp.mean(sc * nm, -1, keepdims=True)
            exp_out[u, at, :] = (std_ref[u, at, :] * (sc - one - nm * two)).astype(BF)
            g = ng * nm
            return total_gain + g[:8] + g[8:]

        gains = lax.fori_loop(0, rows // 16, norm, jnp.zeros((8, ch), F32))

        @pl.when(k == 0)
        def _():
            gain_out[...] = gains

        @pl.when(k > 0)
        def _():
            gain_out[...] += gains

        cgrad[...] = dot(exp_out[...].reshape(rows, ch), we[...], NT)
        for u in range(part):

            def slope(lanes):
                g = cgrad[pl.ds(u * cells, cells), lanes] * silu_slope(conv_ref[u, :, lanes])
                conv_grad_out[u, :, lanes] = g.astype(BF)
                top_out[u, :, lanes] = g[:wide].astype(BF)
                bottom_out[u, :, lanes] = g[cells - wide :].astype(BF)

            chunks(ch // LANES, slope)

    by_order = lambda k, order: (order[k], 0, 0)
    whole = (part, cells, ch)
    edge = (part, wide, ch)
    return call(
        kernel,
        grid=(n,),
        prefetch=1,
        ins=[
            *[(r, None, None) for r in returned],
            (spread_up, None, None),
            (nrm, whole, by_order),
            (std, (part, cells, 1), by_order),
            (gain, None, None),
            (conv, whole, by_order),
            (pre_expand, None, None),
        ],
        outs=[
            (shape((slots, cells, ch), BF), whole, by_order),
            (shape((slots, cells, ch), BF), whole, by_order),
            (shape((slots, wide, ch), BF), edge, by_order),
            (shape((slots, wide, ch), BF), edge, by_order),
            (shape((8, ch), F32), None, None),
        ],
        scratch=[pltpu.VMEM((rows, ch), F32), pltpu.VMEM((rows, ch), F32)],
        name="pre_backward",
    )(order)


def pre_conv_backward(conv_grad, above, below, reduced, taps):
    slots, cells, ch = reduced.shape
    wide = above.shape[1]
    high = cells // wide

    def kernel(cg, up, down, red, tap, redg_out, taps_out):
        step = pl.program_id(0)
        first, last = edge_masks(wide, wide, 1)

        @pl.when(step == 0)
        def _():
            taps_out[...] = jnp.zeros_like(taps_out)

        def back(lanes):
            w = [tap[pl.ds(i, 1), lanes] for i in range(9)]
            mid = cg[0, :, lanes].astype(F32)
            rows = [up[0, :, lanes].astype(F32)]
            rows += [mid[i * wide : (i + 1) * wide] for i in range(high)]
            rows += [down[0, :, lanes].astype(F32)]
            v = [red[0, pl.ds(i * wide, wide), lanes] for i in range(high)]
            s = [sigmoid(t) for t in v]
            x = [(a * b).astype(BF).astype(F32) for a, b in zip(v, s)]
            d = [0.0] * high
            sums = [0.0] * 9
            for p in range(high + 2):
                g = rows[p]
                moves = [columns_moved(g, -1, first, last), g, columns_moved(g, 1, first, last)]
                for a in range(3):
                    i = p - 1 + a - 1
                    if 0 <= i < high:
                        for b in range(3):
                            d[i] = d[i] + moves[b] * w[3 * a + b]
                            prod = x[i] * moves[b]
                            sums[3 * a + b] = sums[3 * a + b] + (prod[:8] + prod[8:16] + prod[16:])
            out = [d[i] * (s[i] * (1.0 + v[i] * (1.0 - s[i]))) for i in range(high)]
            redg_out[0, :, lanes] = jnp.concatenate(out, 0).astype(BF)
            for i in range(9):
                taps_out[i, :, lanes] += sums[i]

        chunks(ch // LANES, back)

    image = lambda i: (i, 0, 0)
    return call(
        kernel,
        grid=(slots,),
        ins=[
            (conv_grad, (1, cells, ch), image),
            (above, (1, wide, ch), image),
            (below, (1, wide, ch), image),
            (reduced, (1, cells, ch), image),
            (taps, None, None),
        ],
        outs=[
            (shape((slots, cells, ch), BF), (1, cells, ch), image),
            (shape((9, 8, ch), F32), None, None),
        ],
        name="pre_conv_backward",
    )()


def feature_backward(order, reduced_grad, pre_reduce, returned, spread_up):
    slots, cells, ch = reduced_grad.shape
    n = order.shape[0]
    part = slots // n

    def kernel(order_ref, rg, wr, up, *refs):
        ret, out = refs[:n], refs[n]
        k = pl.program_id(0)
        for i in range(n):

            @pl.when(k == i)
            def _():
                out[...] = dot(up[...], ret[i][...]).reshape(part, cells, ch)

        out[...] += dot(rg[...].reshape(part * cells, ch), wr[...], NT).reshape(part, cells, ch)

    by_order = lambda k, order: (order[k], 0, 0)
    whole = (part, cells, ch)
    return call(
        kernel,
        grid=(n,),
        prefetch=1,
        ins=[
            (reduced_grad, whole, by_order),
            (pre_reduce, None, None),
            (spread_up, None, None),
            *[(r, None, None) for r in returned],
        ],
        outs=[(shape((slots, cells, ch), F32), whole, by_order)],
        name="feature_backward",
    )(order)[0]


def post_weight_grads(flat, reduced_grad, act, expanded_grad, n):
    total, ch = flat.shape
    share = ch // n
    rows = share // 8

    def kernel(x, g, a, e, out):
        for c in range(n):
            cut = slice(c * share, (c + 1) * share)
            v = dot(x[:, cut], g[...], TN).astype(BF)
            for d in range(8):
                out[d, c, :, :ch] = v[d * rows : (d + 1) * rows]
            for q in range(n):
                v = dot(a[:, q * share : (q + 1) * share], e[:, cut], TN).astype(BF)
                for d in range(8):
                    out[d, c, :, ch + q * share : ch + (q + 1) * share] = v[d * rows : (d + 1) * rows]

    return call(
        kernel,
        grid=(1,),
        ins=[(v, None, None) for v in (flat, reduced_grad, act, expanded_grad)],
        outs=[(shape((8, n, rows, 3 * ch), BF), (8, n, rows, 2 * ch), lambda i: (0, 0, 0, 0))],
        name="post_weight_grads",
    )()[0]


def readout_weight_grad(low, piece, load):
    total, ch = low.shape
    width = piece.shape[1]
    parts, n, rows, _ = load.shape
    share = ch // n

    def kernel(x, g, old, out):
        v = dot(x[...], g[...], TN).astype(BF)
        for d in range(parts):
            out[d, 0] = v[d * rows : (d + 1) * rows]

    return call(
        kernel,
        grid=(n,),
        ins=[(low, (total, share), lambda c: (0, c)), (piece, None, None)],
        outs=[(shape(load.shape, BF), (parts, 1, rows, width), lambda c: (0, c, 0, 2))],
        aliased=(load,),
        name="readout_weight_grad",
    )()[0]


def spread(n, k):
    return [(a * n + b, b * n + (a + k) % n) for a in range(n) for b in range(n)]


def other_core(values):
    return lax.ppermute(values, "core", [(0, 1), (1, 0)])


def small_rows(*grads):
    ch = grads[0].shape[-1]
    counts = [g.shape[0] if g.ndim == 3 else 1 for g in grads]
    per = ch // LANES

    def kernel(*refs):
        out = refs[-1]
        at = 0
        for ref, count in zip(refs, counts):
            for i in range(count):
                v = jnp.sum(ref[i] if len(ref.shape) == 3 else ref[...], 0, keepdims=True)
                for q in range(per):
                    out[pl.ds(at, 1), :] = v[:, q * LANES : (q + 1) * LANES]
                    at += 1

    return call(
        kernel,
        grid=(1,),
        ins=[(g, None, None) for g in grads],
        outs=[(shape((sum(counts) * per, LANES), F32), None, None)],
        name="small_rows",
    )()[0]


def join_halves(core, mine, theirs, small, their_small, parts):
    rows, ch = mine[0].shape
    half = rows // 2
    width = len(mine) * ch + LANES
    count = small.shape[0]
    m = len(mine)
    steps = 2
    block = half // steps

    def kernel(core_ref, *refs):
        own, got = refs[:m], refs[m : 2 * m]
        sm, got_sm, out = refs[2 * m :]
        for i in range(m):
            out[:, i * ch : (i + 1) * ch] = (own[i][...].astype(F32) + got[i][...].astype(F32)).astype(BF)
        first = ((core_ref[0] == 0) & (pl.program_id(0) == 0)).astype(F32)
        total = (sm[...] + got_sm[...]) * first
        pad = jnp.zeros((block - count, LANES), F32)
        out[:, m * ch :] = jnp.concatenate([total, pad], 0).astype(BF)

    return call(
        kernel,
        grid=(steps,),
        prefetch=1,
        ins=[(v, (block, ch), lambda i, c: (c[0] * steps + i, 0)) for v in mine]
        + [(v, (block, ch), lambda i, c: (i, 0)) for v in theirs]
        + [(v, None, None) for v in (small, their_small)],
        outs=[(shape((half, width), BF), (block, width), lambda i, c: (i, 0))],
        name="join_halves",
    )(core)[0].reshape(parts, half // parts, width)


def sum_and_copy(blocks):
    parts, rows, width = blocks.shape

    def kernel(x, out):
        def cut(lanes):
            total = jnp.sum(x[:, :, lanes].astype(F32), 0).astype(BF)
            out[:, :, lanes] = jnp.broadcast_to(total[None], (parts, rows, LANES))

        chunks(width // LANES, cut)

    return call(
        kernel,
        grid=(1,),
        ins=[(blocks, None, None)],
        outs=[(shape(blocks.shape, BF), None, None)],
        name="sum_and_copy",
    )()[0]


def sum_parts(blocks, n):
    parts, rows, width = blocks.shape
    ch = width // 3

    def kernel(x, out):
        for lanes in range(0, width, ch):
            for at in range(lanes, lanes + ch, 2 * LANES):
                cut = slice(at, at + 2 * LANES)
                by_chan = [sum(x[p, :, cut].astype(F32) for p in range(c, parts, n)) for c in range(n)]
                if lanes < 2 * ch:
                    out[:, cut] = sum(by_chan).astype(BF)
                else:
                    for c in range(n):
                        out[:, at + c * ch : at + c * ch + 2 * LANES] = by_chan[c].astype(BF)

    return call(
        kernel,
        grid=(1,),
        ins=[(blocks, None, None)],
        outs=[(shape((rows, 2 * ch + n * ch), BF), None, None)],
        name="sum_parts",
    )()[0]


def finish_pre(place, half_rows, ch, earlier=()):
    half, width = half_rows.shape
    m = (width - LANES) // ch
    steps = 4
    block = half // steps

    def kernel(place_ref, x, *outs):
        outs = outs[len(earlier) :]
        for i in range(m):
            outs[i][...] = x[:, i * ch : (i + 1) * ch].astype(F32)
        outs[m][...] = x[:, m * ch :].astype(F32)

    return call(
        kernel,
        grid=(steps,),
        prefetch=1,
        ins=[(half_rows, (block, width), lambda i, c: (i, 0))],
        outs=[(shape((2 * half, ch), F32), (block, ch), lambda i, c: (c[0] * steps + i, 0)) for _ in range(m)]
        + [(shape((half, LANES), F32), (block, LANES), lambda i, c: (i, 0))],
        aliased=earlier,
        name="finish_pre",
    )(place)


def finish_post(place, gathered, n, earlier=()):
    groups, per, width = gathered.shape
    share = 2 * groups * per
    ch = width // (n + 2)

    def kernel(place_ref, x, *outs):
        reduce_out, expand_out, read_out = outs[len(earlier) :]
        reduce_out[...] = x[0, :, :ch].astype(F32)
        for q in range(n):
            expand_out[q] = x[0, :, ch + q * share : ch + (q + 1) * share].astype(F32)
        read_out[...] = x[0, :, 2 * ch :].astype(F32)

    at = lambda i, c: (2 * i + c[0], 0)
    return call(
        kernel,
        grid=(groups,),
        prefetch=1,
        ins=[(gathered, (1, per, width), lambda i, c: (i, 0, 0))],
        outs=[
            (shape((share, ch), F32), (per, ch), at),
            (shape((n, share, share), F32), (n, per, share), lambda i, c: (0, 2 * i + c[0], 0)),
            (shape((share, n * ch), F32), (per, n * ch), at),
        ],
        aliased=earlier,
        name="finish_post",
    )(place)


def after(values, *earlier):
    return lax.optimization_barrier((values, *earlier))[0]


def pool_matrix(part, high, wide):
    half = wide // 2
    m = np.zeros((high // 2 * half * part, part * (high // 2) * wide), np.float32)
    for u in range(part):
        for i in range(high // 2):
            for j in range(wide):
                m[(i * half + j // 2) * part + u, (u * (high // 2) + i) * wide + j] = 0.25
    return m


def spread_matrix(part, high, wide):
    half = wide // 2
    m = np.zeros((part * high * wide, high // 2 * half * part), np.float32)
    for u in range(part):
        for i in range(high):
            for j in range(wide):
                m[(u * high + i) * wide + j, ((i // 2) * half + j // 2) * part + u] = 0.25
    return m


def place_matrix(cells, slots, pairs):
    per = slots // pairs
    m = np.zeros((cells * slots, cells * slots), np.float32)
    for c in range(cells):
        for s in range(slots):
            m[c * slots + s, (s // per) * cells * per + c * per + s % per] = 1.0
    return m


def body(features, counts, pre_reduce, pre_conv, pre_expand, pre_gain, post_reduce, post_conv, post_expand, post_gain, readout, cotangent):
    n = lax.axis_size("chan")
    row = lax.axis_index("rows").astype(jnp.int32)
    chan = lax.axis_index("chan").astype(jnp.int32)
    core = lax.axis_index("core").astype(jnp.int32)
    ch = pre_reduce.shape[0]
    slots, high, wide = features.shape[0], features.shape[1], features.shape[2]
    part = slots // n
    cells = high * wide
    pool = wide // 2
    share = ch // n
    out_share = cotangent.shape[3]
    steps = jnp.arange(n, dtype=jnp.int32)
    order = (row + steps) % n
    source = (chan - steps) % n
    rank = jnp.full((1,), chan, jnp.int32)
    core_at = jnp.full((1,), core, jnp.int32)
    pre_taps = pre_conv.astype(F32).reshape(9, ch)
    post_taps = post_conv.astype(F32).reshape(9, ch)
    pre_gain_row = pre_gain.reshape(1, ch)
    pool_m = jnp.asarray(pool_matrix(part, high, wide), BF)
    up_m = jnp.asarray(spread_matrix(part, high, wide), BF)
    place = jnp.asarray(place_matrix(16, slots, n), BF)

    ends = n - 1
    down_pairs = [(i, i + 1) for i in range(ends)]
    up_pairs = [(i + 1, i) for i in range(ends)]
    above = lax.ppermute(features[:, -1], "rows", down_pairs)
    below = lax.ppermute(features[:, 0], "rows", up_pairs)
    gain_hi = post_gain.astype(BF)
    gain_lo = (post_gain - gain_hi.astype(F32)).astype(BF)
    gain_row = jnp.concatenate([gain_hi, gain_lo, jnp.zeros((ch - 2 * share,), BF)])[None]
    square = post_expand.reshape(n, share, share)
    shards = jnp.concatenate(
        [post_reduce, jnp.concatenate([square[q] for q in range(n)], axis=1), jnp.pad(gain_row, ((0, 63), (0, 0)))], axis=0
    )
    shard = lax.dynamic_index_in_dim(shards.reshape(2, -1, ch), core, 0, keepdims=False)
    full = lax.all_gather(shard, ("chan", "core"), axis=0, tiled=True)
    full = full.reshape(n, 2 * share + 64, ch)
    flat_features = features.reshape(slots * cells, ch)
    reduced = dot(flat_features, pre_reduce).reshape(slots, cells, ch)
    live = (jnp.arange(SLOT)[None, :] < counts[:, None]).astype(F32).reshape(slots)
    select = place.T * jnp.tile(live.astype(BF), 16)[None, :]
    cot_rows = cotangent.transpose(1, 2, 0, 3).reshape(-1, out_share)
    cots = lax.all_to_all(cotangent_by_image(after(cot_rows, reduced, above, below), select), "chan", 0, 0, tiled=False)

    convolved, convolved_act, normal_pre, pre_std, *pooled = pre_forward(
        order, reduced, above, below, features, pre_reduce, pre_taps, pre_expand, pre_gain_row, pool_m
    )

    pooled = after(pooled, cots)
    moved = [lax.ppermute(pooled[k], ("rows", "chan"), spread(n, k)) for k in range(n)]
    flat, post_reduced, post_act, post_convolved, post_cact, post_normal, post_std, low = post_forward(
        source, moved, full, post_taps, pool
    )
    lows = [low] + [lax.ppermute(low, "chan", [(i, (i + k) % n) for i in range(n)]) for k in range(1, n)]
    refined_grad = readout_backward(low, readout, cots)
    post_expanded_grad, post_reduced_grad, post_taps_grad, post_gain_grad, *back = post_backward(
        source, refined_grad, full, post_taps, post_act, post_reduced, post_convolved, post_normal, post_std, pool
    )

    returned = [lax.ppermute(back[k], ("rows", "chan"), [(d, s) for s, d in spread(n, k)]) for k in range(n)]

    flat = after(flat, lows)
    load = post_weight_grads(flat, post_reduced_grad, post_cact, post_expanded_grad, n)

    alive = jnp.broadcast_to(jnp.tile(live, 48)[:, None], (48 * slots, 1))
    lows = after(lows, load, returned[:2])
    tokens, piece, low_here = token_block(rank, source, lows, place, readout, cot_rows, alive)
    load = readout_weight_grad(low_here, after(piece, returned[2:]), load)
    tokens = tokens.reshape(pool, pool, slots, out_share).transpose(2, 0, 1, 3)
    returned = after(returned, load)
    eight = share // 32
    rest = lax.psum_scatter(load, ("x", "core"), scatter_dimension=0, tiled=False)

    expanded_grad, convolved_grad, top, bottom, pre_gain_grad = pre_backward(
        order, returned, up_m, normal_pre, pre_std, pre_gain_row, convolved, pre_expand
    )
    grad_above = lax.ppermute(bottom, "rows", down_pairs)
    grad_below = lax.ppermute(top, "rows", up_pairs)
    act_rows = after(convolved_act, bottom).reshape(-1, ch)
    pre_expand_grad = dot(act_rows, expanded_grad.reshape(-1, ch), TN).astype(BF)
    convolved_grad = after(convolved_grad, pre_expand_grad)
    reduced_grad, pre_taps_grad = pre_conv_backward(convolved_grad, grad_above, grad_below, reduced, pre_taps)
    small = small_rows(pre_taps_grad, pre_gain_grad, post_taps_grad, post_gain_grad)
    pre_reduce_grad = dot(after(flat_features, small), reduced_grad.reshape(-1, ch), TN).astype(BF)

    chips = ("x", "rows", "chan")
    mine = [pre_reduce_grad, pre_expand_grad]
    theirs = [other_core(lax.dynamic_index_in_dim(g.reshape(2, ch // 2, ch), 1 - core, 0, keepdims=False)) for g in mine]
    rest = after(rest, *mine).reshape(n, 4, eight, 3 * ch).transpose(1, 0, 2, 3)
    theirs = after(theirs, rest)
    rest = lax.all_to_all(rest.reshape(4 * n, eight, 3 * ch), ("rows", "chan"), 0, 0, tiled=False)
    load = join_halves(core_at, mine, theirs, small, other_core(small), 64)
    pieces = lax.all_to_all(load, chips, 0, 0, tiled=False)
    feature_grad = feature_backward(order, after(reduced_grad, load), pre_reduce, returned, up_m).reshape(features.shape)

    rest = sum_parts(after(rest, feature_grad), n)
    pieces = after(pieces, rest)
    load = sum_and_copy(pieces)
    load_all = lax.all_to_all(load, chips, 0, 0, tiled=False).reshape(ch // 2, -1)
    rest = lax.all_gather(rest, ("x", "rows"), axis=0, tiled=False).reshape(4, 4 * eight, -1)

    def finish(kernel, values, *sizes):
        theirs = other_core(values)
        own = kernel(core_at, values, *sizes)
        theirs = after(theirs, *own)
        return own, theirs

    own, theirs = finish(finish_pre, load_all, ch)
    pre_reduce_out, pre_expand_out, small_their = finish_pre(1 - core_at, theirs, ch, earlier=tuple(own[:2]))
    small_out = jnp.where(core == 0, own[2], small_their)
    own, theirs = finish(finish_post, rest, n)
    post_reduce_out, post_expand_out, readout_out = finish_post(1 - core_at, theirs, n, earlier=tuple(own))
    per = ch // LANES
    cut = [0, 9 * per, 10 * per, 19 * per, 20 * per]
    pre_conv_out, pre_gain_out, post_conv_out, post_gain_out = [small_out[a:b] for a, b in zip(cut, cut[1:])]
    return (
        tokens,
        feature_grad,
        pre_reduce_out,
        pre_conv_out.reshape(3, 3, ch),
        pre_expand_out,
        pre_gain_out.reshape(ch),
        post_reduce_out,
        post_conv_out.reshape(3, 3, ch),
        post_expand_out.reshape(ch, share),
        lax.dynamic_slice_in_dim(post_gain_out.reshape(ch), chan * share, share, 0),
        readout_out,
    )


def solution(mesh):
    grid = Mesh(mesh.devices.reshape(4, 2, 4, 4), ("x", "core", "rows", "chan"))
    images = P(("x", "core", "chan"), "rows", None, None)
    grids = P(("x", "core", "rows"), None, None, "chan")
    return jax.shard_map(
        body,
        mesh=grid,
        in_specs=(
            images,
            P(("x", "core", "rows")),
            P(),
            P(),
            P(),
            P(),
            P("chan", None),
            P(),
            P(None, "chan"),
            P("chan"),
            P(),
            grids,
        ),
        out_specs=(grids, images, P(), P(), P(), P(), P("chan", None), P(), P(None, "chan"), P("chan"), P("chan", None)),
        check_vma=False,
    )
```

```python
import functools

import jax
import jax.numpy as jnp
import numpy as np
from jax import lax
from jax.experimental import pallas as pl
from jax.experimental.pallas import tpu as pltpu
from jax.sharding import Mesh, PartitionSpec as P

SLOT = 4
EPS = 1e-06
BF = jnp.bfloat16
F32 = jnp.float32
LANES = 128
VMEM_LIMIT = 56 * 1024 * 1024
NN = ((1,), (0,))
NT = ((1,), (1,))
TN = ((0,), (0,))


def dot(a, b, dims=NN):
    return lax.dot_general(a, b, (dims, ((), ())), preferred_element_type=F32)


def sigmoid(v):
    return 0.5 * jnp.tanh(0.5 * v) + 0.5


def silu(v):
    return v * sigmoid(v)


def silu_slope(v):
    s = sigmoid(v)
    return s * (1.0 + v * (1.0 - s))


def gelu_parts(v):
    c = 0.7978845608028654
    square = v * v
    t = jnp.tanh(v * (c + (c * 0.044715) * square))
    half = 0.5 * (1.0 + t)
    slope = half + 0.5 * v * (1.0 - t * t) * (c + (3.0 * c * 0.044715) * square)
    return v * half, slope


def chunks(count, body, width=LANES):
    for i in range(count):
        body(pl.ds(i * width, width))


def call(kernel, *, grid, ins, outs, scratch=(), prefetch=0, aliased=(), cost=1, name):
    def spec(shape, block, index):
        if block is None:
            block, index = shape, lambda *_: (0,) * len(shape)
        return pl.BlockSpec(block, index)

    arrays = [i[0] for i in ins] + list(aliased)
    in_specs = [spec(a.shape, b, m) for a, b, m in ins] + [pl.BlockSpec(memory_space=pl.ANY)] * len(aliased)
    out_specs = [spec(s.shape, b, m) for s, b, m in outs]

    def run(*scalars):
        return pl.pallas_call(
            kernel,
            grid_spec=pltpu.PrefetchScalarGridSpec(
                num_scalar_prefetch=prefetch,
                grid=grid,
                in_specs=in_specs,
                out_specs=out_specs,
                scratch_shapes=list(scratch),
            ),
            out_shape=[s[0] for s in outs],
            compiler_params=pltpu.CompilerParams(
                dimension_semantics=("arbitrary",) * len(grid), vmem_limit_bytes=VMEM_LIMIT
            ),
            input_output_aliases={prefetch + len(ins) + i: i for i in range(len(aliased))},
            cost_estimate=pl.CostEstimate(flops=cost, bytes_accessed=1, transcendentals=0),
            name=name,
        )(*scalars, *arrays)

    return run


def shape(dims, dtype):
    return jax.ShapeDtypeStruct(dims, dtype)


def columns_moved(t, by, first, last):
    rows = t.shape[0]
    return pltpu.roll(t, by % rows, 0) * (first if by > 0 else last)


def edge_masks(rows, width, depth):
    at = lax.broadcasted_iota(jnp.int32, (rows, LANES), 0) % (width * depth)
    return (at >= depth).astype(F32), (at < (width - 1) * depth).astype(F32)


def pre_forward(order, above, below, features, pre_reduce, taps, pre_expand, gain, pool):
    slots, high, wide, ch = features.shape
    cells = high * wide
    n = order.shape[0]
    part = slots // n
    rows_all = part * cells

    def kernel(order_ref, up_ref, down_ref, feat, wr, tap, we, gn, pool_ref, red_out, conv_out, act_out, norm_out, std_out, *rest):
        pooled_out, (red, halo, exp, sums) = rest[:n], rest[n:]
        k = pl.program_id(0)
        for side, ref in enumerate((up_ref, down_ref)):
            halo[side] = dot(ref[...].reshape(part * wide, ch), wr[...]).reshape(part, wide, ch)
        red[...] = dot(feat[...].reshape(rows_all, ch), wr[...]).reshape(part, cells, ch)
        red_out[...] = red[...].astype(BF)
        first, last = edge_masks(wide, wide, 1)
        for u in range(part):

            def conv(lanes):
                w = [tap[pl.ds(i, 1), lanes] for i in range(9)]
                rows = [halo[0, u, :, lanes]]
                rows += [red[u, pl.ds(i * wide, wide), lanes] for i in range(high)]
                rows += [halo[1, u, :, lanes]]
                rows = [silu(r).astype(BF).astype(F32) for r in rows]
                out = []
                for i in range(high):
                    t = [sum(rows[i + a] * w[3 * a + b] for a in range(3)) for b in range(3)]
                    out.append(t[1] + columns_moved(t[0], 1, first, last) + columns_moved(t[2], -1, first, last))
                conv_out[u, :, lanes] = jnp.concatenate(out, 0).astype(BF)
                act_out[u, :, lanes] = jnp.concatenate([silu(c) for c in out], 0).astype(BF)

            chunks(ch // LANES, conv)

        exp[...] = dot(act_out[...].reshape(rows_all, ch), we[...])

        def norm(p, carry):
            u, i = p // (high // 2), p % (high // 2)
            tiles = wide // 8
            f = [feat[u, 2 * i + half].astype(F32) for half in range(2)]
            nrms, blends = [], []
            for t in range(2 * tiles):
                e = exp[pl.ds(p * 2 * wide + 8 * t, 8), :]
                mean = jnp.mean(e, -1, keepdims=True)
                square = jnp.mean(e * e, -1, keepdims=True)
                std = lax.rsqrt(square - mean * mean + EPS)
                nrm = (e - mean) * std
                std_out[u, pl.ds(i * 2 * wide + 8 * t, 8), :] = std
                nrms.append(nrm)
                at = t % tiles
                blends.append(f[t // tiles][8 * at : 8 * at + 8] + silu(nrm * gn[...]))
                if t % 2 == 1:
                    both = jnp.concatenate(nrms[-2:], 0).astype(BF)
                    norm_out[u, pl.ds(i * 2 * wide + 8 * (t - 1), 16), :] = both
            for t in range(tiles):
                sums[pl.ds(p * wide + 8 * t, 8), :] = blends[t] + blends[tiles + t]
            return carry

        for p in range(part * high // 2):
            norm(p, 0)
        s = sums[...]
        hi = s.astype(BF)
        lo = (s - hi.astype(F32)).astype(BF)
        pooled = (dot(pool_ref[...], hi) + dot(pool_ref[...], lo)).astype(BF)
        for i in range(n):

            @pl.when(k == i)
            def _():
                pooled_out[i][...] = pooled

    def by_order(rest):
        return lambda k, order: (order[k],) + (0,) * rest

    pooled_rows = pool.shape[0]
    block = (part, cells, ch)
    return call(
        kernel,
        grid=(n,),
        prefetch=1,
        ins=[
            (above, (part, wide, ch), by_order(2)),
            (below, (part, wide, ch), by_order(2)),
            (features, (part, high, wide, ch), by_order(3)),
            (pre_reduce, None, None),
            (taps, None, None),
            (pre_expand, None, None),
            (gain, None, None),
            (pool, None, None),
        ],
        outs=[(shape((slots, cells, ch), BF), block, by_order(2))] * 4
        + [(shape((slots, cells, 1), F32), (part, cells, 1), by_order(2))]
        + [(shape((pooled_rows, ch), BF), None, None)] * n,
        scratch=[
            pltpu.VMEM((part, cells, ch), F32),
            pltpu.VMEM((2, part, wide, ch), F32),
            pltpu.VMEM((rows_all, ch), F32),
            pltpu.VMEM((rows_all // 2, ch), F32),
        ],
        name="pre_forward",
    )(order)


def gain_row(w, n, share):
    at = 2 * share
    parts = [w[c, at : at + 16, :].astype(F32)[:1] for c in range(n)]
    return jnp.concatenate([p[:, :share] + p[:, share : 2 * share] for p in parts], 1)


def post_forward(source, moved, weights, taps, pool):
    n, (rows, ch) = len(moved), moved[0].shape
    total = n * rows
    depth = total // (pool * pool)
    share = ch // n

    def kernel(src, *refs):
        got, refs = refs[:n], refs[n:]
        w, tap, flat_out, red_out, act_out, conv_out, cact_out, norm_out, std_out, low_out, wide_ref, red, exp = refs
        for k in range(n):
            at = pl.multiple_of(src[k] * rows, 8)
            wide_ref[pl.ds(at, rows), :] = got[k][...].astype(F32)
        gain = gain_row(w, n, share)
        flat_out[...] = wide_ref[...].astype(BF)
        total_red = 0.0
        for c in range(n):
            total_red = total_red + dot(flat_out[:, c * share : (c + 1) * share], w[c, :share])
        red[...] = total_red
        first, last = edge_masks(total, pool, depth)
        step = pool * depth

        def conv(lanes):
            v = red[:, lanes]
            red_out[:, lanes] = v.astype(BF)
            x = silu(v).astype(BF)
            act_out[:, lanes] = x
            x = x.astype(F32)
            moves = [columns_moved(x, depth, first, last), x, columns_moved(x, -depth, first, last)]
            t = [sum(moves[b] * tap[pl.ds(3 * a + b, 1), lanes] for b in range(3)) for a in range(3)]
            none = jnp.zeros((step, LANES), F32)
            c = t[1] + jnp.concatenate([none, t[0][:-step]], 0) + jnp.concatenate([t[2][step:], none], 0)
            conv_out[:, lanes] = c.astype(BF)
            cact_out[:, lanes] = silu(c).astype(BF)

        chunks(ch // LANES, conv)
        for c in range(n):
            e = 0.0
            for q in range(n):
                cut = slice(q * share, (q + 1) * share)
                e = e + dot(cact_out[:, cut], w[c, share : 2 * share, cut])
            exp[:, c * share : (c + 1) * share] = e

        def norm(i, carry):
            for t in range(3):
                at = pl.ds(i * 48 + 16 * t, 16)
                e = exp[at, :]
                mean = jnp.mean(e, -1, keepdims=True)
                square = jnp.mean(e * e, -1, keepdims=True)
                std = lax.rsqrt(square - mean * mean + EPS)
                nrm = (e - mean) * std
                norm_out[at, :] = nrm.astype(BF)
                std_out[at, :] = std
                low_out[at, :] = (wide_ref[at, :] + silu(nrm * gain)).astype(BF)
            return carry

        for i in range(total // 48):
            norm(i, 0)

    narrow = shape((total, ch), BF)
    return call(
        kernel,
        grid=(1,),
        prefetch=1,
        ins=[(a, None, None) for a in (*moved, weights, taps)],
        outs=[(s, None, None) for s in (narrow, narrow, narrow, narrow, narrow, narrow, shape((total, 1), F32), narrow)],
        scratch=[pltpu.VMEM((total, ch), F32)] * 3,
        name="post_forward",
    )(source)


def readout_backward(low, readout, cots):
    total, ch = low.shape
    n, _, out_share = cots.shape

    def kernel(low_ref, ro, cot, grad):
        k = pl.program_id(0)
        logits = dot(low_ref[...], ro[...])
        piece = (cot[0].astype(F32) * gelu_parts(logits)[1]).astype(BF)
        term = dot(piece, ro[...], NT)

        @pl.when(k == 0)
        def _():
            grad[...] = term

        @pl.when(k > 0)
        def _():
            grad[...] += term

    return call(
        kernel,
        grid=(n,),
        ins=[
            (low, None, None),
            (readout, (ch, out_share), lambda k: (0, k)),
            (cots, (1, total, out_share), lambda k: (k, 0, 0)),
        ],
        outs=[(shape((total, ch), F32), None, None)],
        name="readout_backward",
    )()[0]


def post_backward(source, refined_grad, weights, taps, act, red, conv, nrm, std, pool):
    total, ch = act.shape
    n = weights.shape[0]
    share = ch // n
    rows = total // n
    depth = total // (pool * pool)

    def kernel(src, rg, w, tap, act_ref, red_ref, conv_ref, norm_ref, std_ref, exp_out, redg_out, taps_out, gain_out, *rest):
        back_out, (grad, cgrad) = rest[:n], rest[n:]
        gain = gain_row(w, n, share)

        def norm(i, total_gain):
            for t in range(3):
                at = pl.ds(i * 48 + 16 * t, 16)
                nm = norm_ref[at, :].astype(F32)
                ng = rg[at, :] * silu_slope(nm * gain)
                sc = ng * gain
                one = jnp.mean(sc, -1, keepdims=True)
                two = jnp.mean(sc * nm, -1, keepdims=True)
                exp_out[at, :] = (std_ref[at, :] * (sc - one - nm * two)).astype(BF)
                g = ng * nm
                total_gain = total_gain + g[:8] + g[8:]
            return total_gain

        gains = jnp.zeros((8, ch), F32)
        for i in range(total // 48):
            gains = norm(i, gains)
        gain_out[...] = gains
        for q in range(n):
            cut = slice(q * share, (q + 1) * share)
            cg = 0.0
            for c in range(n):
                cg = cg + dot(exp_out[:, c * share : (c + 1) * share], w[c, share : 2 * share, cut], NT)
            cgrad[:, cut] = cg
        first, last = edge_masks(total, pool, depth)
        step = pool * depth

        def back(lanes):
            g = (cgrad[:, lanes] * silu_slope(conv_ref[:, lanes].astype(F32))).astype(BF).astype(F32)
            x = act_ref[:, lanes].astype(F32)
            moves = [columns_moved(g, -depth, first, last), g, columns_moved(g, depth, first, last)]
            none = jnp.zeros((step, LANES), F32)
            xs = [
                jnp.concatenate([none, x[:-step]], 0),
                x,
                jnp.concatenate([x[step:], none], 0),
            ]
            for a in range(3):
                for b in range(3):
                    prod = xs[a] * moves[b]
                    taps_out[3 * a + b, :, lanes] = jnp.sum(prod.reshape(total // 8, 8, LANES), 0)
            t = [sum(moves[b] * tap[pl.ds(3 * a + b, 1), lanes] for b in range(3)) for a in range(3)]
            d = t[1] + jnp.concatenate([t[0][step:], none], 0) + jnp.concatenate([none, t[2][:-step]], 0)
            redg_out[:, lanes] = (d * silu_slope(red_ref[:, lanes].astype(F32))).astype(BF)

        chunks(ch // LANES, back)
        for c in range(n):
            cut = slice(c * share, (c + 1) * share)
            grad[:, cut] = rg[:, cut] + dot(redg_out[...], w[c, :share], NT)
        for r in range(n):
            at = pl.ds(pl.multiple_of(src[r] * rows, 8), rows)
            back_out[r][...] = grad[at, :].astype(BF)

    return call(
        kernel,
        grid=(1,),
        prefetch=1,
        ins=[(a, None, None) for a in (refined_grad, weights, taps, act, red, conv, nrm, std)],
        outs=[
            (s, None, None)
            for s in (
                shape((total, ch), BF),
                shape((total, ch), BF),
                shape((9, 8, ch), F32),
                shape((8, ch), F32),
                *[shape((rows, ch), BF)] * n,
            )
        ],
        scratch=[pltpu.VMEM((total, ch), F32), pltpu.VMEM((total, ch), F32)],
        name="post_backward",
    )(source)


def cotangent_by_image(cotangent, select):
    rows, width = cotangent.shape
    size = select.shape[0]
    pairs = SLOT
    each = size // pairs
    per = 3

    def kernel(x, sel, out):
        for q in range(per):
            y = dot(sel[...], x[pl.ds(q * size, size), :]).astype(BF)
            for s in range(pairs):
                out[s, pl.ds(q * each, each), :] = y[s * each : (s + 1) * each]

    return call(
        kernel,
        grid=(rows // (per * size),),
        ins=[(cotangent, (per * size, width), lambda i: (i, 0)), (select, None, None)],
        outs=[(shape((pairs, rows // pairs, width), BF), (pairs, per * each, width), lambda i: (0, i, 0))],
        name="cotangent_by_image",
    )()[0]


def token_block(chan, source, low, place, readout, cotangent):
    pairs, (rows, ch) = len(low), low[0].shape
    width = cotangent.shape[2]
    size = place.shape[0]
    each = size // pairs
    per = 3
    block = per * each

    def kernel(chan_ref, src, *refs):
        lows, (place_ref, ro, cot, tok_out, piece_out) = refs[:pairs], refs[pairs:]
        logits = dot(jnp.concatenate([v[...] for v in lows], 0), ro[...])
        value, slope = gelu_parts(logits)
        value = value.astype(BF)
        for k in range(pairs):
            piece_out[k] = (cot[src[k]].astype(F32) * slope[k * block : (k + 1) * block]).astype(BF)
        for q in range(per):
            x = jnp.concatenate([value[k * block + q * each : k * block + (q + 1) * each] for k in range(pairs)], 0)
            tok_out[pl.ds(q * size, size), :] = dot(place_ref[...], x).astype(BF)

    by_pair = lambda i, c, s: (0, i, 0)
    return call(
        kernel,
        grid=(rows // block,),
        prefetch=2,
        ins=[
            *[(v, (block, ch), lambda i, c, s: (i, 0)) for v in low],
            (place, None, None),
            (readout, (ch, width), lambda i, c, s: (0, c[0])),
            (cotangent, (pairs, block, width), by_pair),
        ],
        outs=[
            (shape((pairs * rows, width), BF), (pairs * block, width), lambda i, c, s: (i, 0)),
            (shape((pairs, rows, width), BF), (pairs, block, width), by_pair),
        ],
        name="token_block",
    )(chan, source)


def pre_backward(order, returned, spread_up, nrm, std, gain, conv, pre_expand):
    slots, cells, ch = nrm.shape
    n = order.shape[0]
    part = slots // n
    wide = 24
    rows = part * cells

    def kernel(order_ref, *refs):
        ret, refs = refs[:n], refs[n:]
        up, norm_ref, std_ref, gn, conv_ref, we, exp_out, conv_grad_out, top_out, bottom_out, gain_out, grad, cgrad = refs
        k = pl.program_id(0)
        for i in range(n):

            @pl.when(k == i)
            def _():
                grad[...] = dot(up[...], ret[i][...])

        def norm(i, total_gain):
            u, j = i // (cells // 48), i % (cells // 48)
            for t in range(3):
                at = pl.ds(j * 48 + 16 * t, 16)
                nm = norm_ref[u, at, :].astype(F32)
                ng = grad[pl.ds(i * 48 + 16 * t, 16), :] * silu_slope(nm * gn[...])
                sc = ng * gn[...]
                one = jnp.mean(sc, -1, keepdims=True)
                two = jnp.mean(sc * nm, -1, keepdims=True)
                exp_out[u, at, :] = (std_ref[u, at, :] * (sc - one - nm * two)).astype(BF)
                g = ng * nm
                total_gain = total_gain + g[:8] + g[8:]
            return total_gain

        gains = jnp.zeros((8, ch), F32)
        for i in range(rows // 48):
            gains = norm(i, gains)

        @pl.when(k == 0)
        def _():
            gain_out[...] = gains

        @pl.when(k > 0)
        def _():
            gain_out[...] += gains

        cgrad[...] = dot(exp_out[...].reshape(rows, ch), we[...], NT)
        for u in range(part):

            def slope(lanes):
                g = cgrad[pl.ds(u * cells, cells), lanes] * silu_slope(conv_ref[u, :, lanes].astype(F32))
                conv_grad_out[u, :, lanes] = g.astype(BF)
                top_out[u, :, lanes] = g[:wide].astype(BF)
                bottom_out[u, :, lanes] = g[cells - wide :].astype(BF)

            chunks(ch // LANES, slope)

    by_order = lambda k, order: (order[k], 0, 0)
    whole = (part, cells, ch)
    edge = (part, wide, ch)
    return call(
        kernel,
        grid=(n,),
        prefetch=1,
        ins=[
            *[(r, None, None) for r in returned],
            (spread_up, None, None),
            (nrm, whole, by_order),
            (std, (part, cells, 1), by_order),
            (gain, None, None),
            (conv, whole, by_order),
            (pre_expand, None, None),
        ],
        outs=[
            (shape((slots, cells, ch), BF), whole, by_order),
            (shape((slots, cells, ch), BF), whole, by_order),
            (shape((slots, wide, ch), BF), edge, by_order),
            (shape((slots, wide, ch), BF), edge, by_order),
            (shape((8, ch), F32), None, None),
        ],
        scratch=[pltpu.VMEM((rows, ch), F32), pltpu.VMEM((rows, ch), F32)],
        name="pre_backward",
    )(order)


def pre_conv_backward(conv_grad, above, below, reduced, taps):
    slots, cells, ch = reduced.shape
    wide = above.shape[1]
    high = cells // wide

    def kernel(cg, up, down, red, tap, redg_out, taps_out):
        step = pl.program_id(0)
        first, last = edge_masks(wide, wide, 1)

        @pl.when(step == 0)
        def _():
            taps_out[...] = jnp.zeros_like(taps_out)

        def back(lanes):
            w = [tap[pl.ds(i, 1), lanes] for i in range(9)]
            mid = cg[0, :, lanes].astype(F32)
            rows = [up[0, :, lanes].astype(F32)]
            rows += [mid[i * wide : (i + 1) * wide] for i in range(high)]
            rows += [down[0, :, lanes].astype(F32)]
            whole = red[0, :, lanes].astype(F32)
            v = [whole[i * wide : (i + 1) * wide] for i in range(high)]
            s = [sigmoid(t) for t in v]
            x = [(a * b).astype(BF).astype(F32) for a, b in zip(v, s)]
            d = [0.0] * high
            sums = [0.0] * 9
            for p in range(high + 2):
                g = rows[p]
                moves = [columns_moved(g, -1, first, last), g, columns_moved(g, 1, first, last)]
                for a in range(3):
                    i = p - 1 + a - 1
                    if 0 <= i < high:
                        for b in range(3):
                            d[i] = d[i] + moves[b] * w[3 * a + b]
                            prod = x[i] * moves[b]
                            sums[3 * a + b] = sums[3 * a + b] + (prod[:8] + prod[8:16] + prod[16:])
            out = [d[i] * (s[i] * (1.0 + v[i] * (1.0 - s[i]))) for i in range(high)]
            redg_out[0, :, lanes] = jnp.concatenate(out, 0).astype(BF)
            for i in range(9):
                taps_out[i, :, lanes] += sums[i]

        chunks(ch // LANES, back)

    image = lambda i: (i, 0, 0)
    return call(
        kernel,
        grid=(slots,),
        ins=[
            (conv_grad, (1, cells, ch), image),
            (above, (1, wide, ch), image),
            (below, (1, wide, ch), image),
            (reduced, (1, cells, ch), image),
            (taps, None, None),
        ],
        outs=[
            (shape((slots, cells, ch), BF), (1, cells, ch), image),
            (shape((9, 8, ch), F32), None, None),
        ],
        name="pre_conv_backward",
    )()


def feature_backward(order, reduced_grad, pre_reduce, returned, spread_up):
    slots, cells, ch = reduced_grad.shape
    n = order.shape[0]
    part = slots // n

    def kernel(order_ref, rg, wr, up, *refs):
        ret, out = refs[:n], refs[n]
        k = pl.program_id(0)
        for i in range(n):

            @pl.when(k == i)
            def _():
                out[...] = dot(up[...], ret[i][...]).reshape(part, cells, ch)

        out[...] += dot(rg[...].reshape(part * cells, ch), wr[...], NT).reshape(part, cells, ch)

    by_order = lambda k, order: (order[k], 0, 0)
    whole = (part, cells, ch)
    return call(
        kernel,
        grid=(n,),
        prefetch=1,
        ins=[
            (reduced_grad, whole, by_order),
            (pre_reduce, None, None),
            (spread_up, None, None),
            *[(r, None, None) for r in returned],
        ],
        outs=[(shape((slots, cells, ch), F32), whole, by_order)],
        name="feature_backward",
    )(order)[0]


def post_weight_grads(flat, reduced_grad, act, expanded_grad, n):
    total, ch = flat.shape
    share = ch // n
    rows = share // 8

    def kernel(x, g, a, e, out):
        for c in range(n):
            cut = slice(c * share, (c + 1) * share)
            v = dot(x[:, cut], g[...], TN).astype(BF)
            for d in range(8):
                out[d, c, :, :ch] = v[d * rows : (d + 1) * rows]
            for q in range(n):
                v = dot(a[:, q * share : (q + 1) * share], e[:, cut], TN).astype(BF)
                for d in range(8):
                    out[d, c, :, ch + q * share : ch + (q + 1) * share] = v[d * rows : (d + 1) * rows]

    return call(
        kernel,
        grid=(1,),
        ins=[(v, None, None) for v in (flat, reduced_grad, act, expanded_grad)],
        outs=[(shape((8, n, rows, 3 * ch), BF), (8, n, rows, 2 * ch), lambda i: (0, 0, 0, 0))],
        name="post_weight_grads",
    )()[0]


def readout_weight_grad(low, piece, load):
    pairs, total, width = piece.shape
    parts, n, rows, _ = load.shape
    share = low[0].shape[1] // n

    def kernel(*refs):
        x, (g, old, out) = refs[:pairs], refs[pairs:]
        x = jnp.concatenate([v[...] for v in x], 0)
        v = dot(x, g[...].reshape(pairs * total, width), TN).astype(BF)
        for d in range(parts):
            out[d, 0] = v[d * rows : (d + 1) * rows]

    return call(
        kernel,
        grid=(n,),
        ins=[(v, (total, share), lambda c: (0, c)) for v in low] + [(piece, None, None)],
        outs=[(shape(load.shape, BF), (parts, 1, rows, width), lambda c: (0, c, 0, 2))],
        aliased=(load,),
        name="readout_weight_grad",
    )()[0]


def spread(n, k):
    return [(a * n + b, b * n + (a + k) % n) for a in range(n) for b in range(n)]


def other_core(values):
    return lax.ppermute(values, "core", [(0, 1), (1, 0)])


def small_rows(*grads):
    ch = grads[0].shape[-1]
    counts = [g.shape[0] if g.ndim == 3 else 1 for g in grads]
    per = ch // LANES

    def kernel(*refs):
        out = refs[-1]
        at = 0
        for ref, count in zip(refs, counts):
            for i in range(count):
                v = jnp.sum(ref[i] if len(ref.shape) == 3 else ref[...], 0, keepdims=True)
                for q in range(per):
                    out[pl.ds(at, 1), :] = v[:, q * LANES : (q + 1) * LANES]
                    at += 1

    return call(
        kernel,
        grid=(1,),
        ins=[(g, None, None) for g in grads],
        outs=[(shape((sum(counts) * per, LANES), F32), None, None)],
        name="small_rows",
    )()[0]


def join_halves(core, mine, theirs, small, their_small, parts):
    rows, ch = mine[0].shape
    half = rows // 2
    width = len(mine) * ch + LANES
    count = small.shape[0]
    m = len(mine)
    steps = 2
    block = half // steps

    def kernel(core_ref, *refs):
        own, got = refs[:m], refs[m : 2 * m]
        sm, got_sm, out = refs[2 * m :]
        for i in range(m):
            out[:, i * ch : (i + 1) * ch] = (own[i][...].astype(F32) + got[i][...].astype(F32)).astype(BF)
        first = ((core_ref[0] == 0) & (pl.program_id(0) == 0)).astype(F32)
        total = (sm[...] + got_sm[...]) * first
        pad = jnp.zeros((block - count, LANES), F32)
        out[:, m * ch :] = jnp.concatenate([total, pad], 0).astype(BF)

    return call(
        kernel,
        grid=(steps,),
        prefetch=1,
        ins=[(v, (block, ch), lambda i, c: (c[0] * steps + i, 0)) for v in mine]
        + [(v, (block, ch), lambda i, c: (i, 0)) for v in theirs]
        + [(v, None, None) for v in (small, their_small)],
        outs=[(shape((half, width), BF), (block, width), lambda i, c: (i, 0))],
        name="join_halves",
    )(core)[0].reshape(parts, half // parts, width)


def sum_and_copy(blocks):
    parts, rows, width = blocks.shape

    def kernel(x, out):
        def cut(lanes):
            total = jnp.sum(x[:, :, lanes].astype(F32), 0).astype(BF)
            out[:, :, lanes] = jnp.broadcast_to(total[None], (parts, rows, LANES))

        chunks(width // LANES, cut)

    return call(
        kernel,
        grid=(1,),
        ins=[(blocks, None, None)],
        outs=[(shape(blocks.shape, BF), None, None)],
        name="sum_and_copy",
    )()[0]


def sum_parts(blocks, n):
    parts, rows, width = blocks.shape
    ch = width // 3

    def kernel(x, out):
        for lanes in range(0, width, ch):
            for at in range(lanes, lanes + ch, 2 * LANES):
                cut = slice(at, at + 2 * LANES)
                by_chan = [sum(x[p, :, cut].astype(F32) for p in range(c, parts, n)) for c in range(n)]
                if lanes < 2 * ch:
                    out[:, cut] = sum(by_chan).astype(BF)
                else:
                    for c in range(n):
                        out[:, at + c * ch : at + c * ch + 2 * LANES] = by_chan[c].astype(BF)

    return call(
        kernel,
        grid=(1,),
        ins=[(blocks, None, None)],
        outs=[(shape((rows, 2 * ch + n * ch), BF), None, None)],
        name="sum_parts",
    )()[0]


def finish_pre(place, half_rows, ch, earlier=()):
    half, width = half_rows.shape
    m = (width - LANES) // ch
    steps = 4
    block = half // steps

    def kernel(place_ref, x, *outs):
        outs = outs[len(earlier) :]
        for i in range(m):
            outs[i][...] = x[:, i * ch : (i + 1) * ch].astype(F32)
        outs[m][...] = x[:, m * ch :].astype(F32)

    return call(
        kernel,
        grid=(steps,),
        prefetch=1,
        ins=[(half_rows, (block, width), lambda i, c: (i, 0))],
        outs=[(shape((2 * half, ch), F32), (block, ch), lambda i, c: (c[0] * steps + i, 0)) for _ in range(m)]
        + [(shape((half, LANES), F32), (block, LANES), lambda i, c: (i, 0))],
        aliased=earlier,
        name="finish_pre",
    )(place)


def finish_post(place, gathered, n, earlier=()):
    groups, per, width = gathered.shape
    share = 2 * groups * per
    ch = width // (n + 2)

    def kernel(place_ref, x, *outs):
        reduce_out, expand_out, read_out = outs[len(earlier) :]
        reduce_out[...] = x[0, :, :ch].astype(F32)
        for q in range(n):
            expand_out[q] = x[0, :, ch + q * share : ch + (q + 1) * share].astype(F32)
        read_out[...] = x[0, :, 2 * ch :].astype(F32)

    at = lambda i, c: (2 * i + c[0], 0)
    return call(
        kernel,
        grid=(groups,),
        prefetch=1,
        ins=[(gathered, (1, per, width), lambda i, c: (i, 0, 0))],
        outs=[
            (shape((share, ch), F32), (per, ch), at),
            (shape((n, share, share), F32), (n, per, share), lambda i, c: (0, 2 * i + c[0], 0)),
            (shape((share, n * ch), F32), (per, n * ch), at),
        ],
        aliased=earlier,
        name="finish_post",
    )(place)


def after(values, *earlier):
    return lax.optimization_barrier((values, *earlier))[0]


def pool_matrix(part, high, wide):
    half = wide // 2
    m = np.zeros((high // 2 * half * part, part * (high // 2) * wide), np.float32)
    for u in range(part):
        for i in range(high // 2):
            for j in range(wide):
                m[(i * half + j // 2) * part + u, (u * (high // 2) + i) * wide + j] = 0.25
    return m


def spread_matrix(part, high, wide):
    half = wide // 2
    m = np.zeros((part * high * wide, high // 2 * half * part), np.float32)
    for u in range(part):
        for i in range(high):
            for j in range(wide):
                m[(u * high + i) * wide + j, ((i // 2) * half + j // 2) * part + u] = 0.25
    return m


def place_matrix(cells, slots, pairs):
    per = slots // pairs
    m = np.zeros((cells * slots, cells * slots), np.float32)
    for c in range(cells):
        for s in range(slots):
            m[c * slots + s, (s // per) * cells * per + c * per + s % per] = 1.0
    return m


def body(features, counts, pre_reduce, pre_conv, pre_expand, pre_gain, post_reduce, post_conv, post_expand, post_gain, readout, cotangent):
    n = lax.axis_size("chan")
    row = lax.axis_index("rows").astype(jnp.int32)
    chan = lax.axis_index("chan").astype(jnp.int32)
    core = lax.axis_index("core").astype(jnp.int32)
    ch = pre_reduce.shape[0]
    slots, high, wide = features.shape[0], features.shape[1], features.shape[2]
    part = slots // n
    cells = high * wide
    pool = wide // 2
    share = ch // n
    out_share = cotangent.shape[3]
    steps = jnp.arange(n, dtype=jnp.int32)
    order = (row + steps) % n
    source = (chan - steps) % n
    rank = jnp.full((1,), chan, jnp.int32)
    core_at = jnp.full((1,), core, jnp.int32)
    pre_taps = pre_conv.astype(F32).reshape(9, ch)
    post_taps = post_conv.astype(F32).reshape(9, ch)
    pre_gain_row = pre_gain.reshape(1, ch)
    pool_m = jnp.asarray(pool_matrix(part, high, wide), BF)
    up_m = jnp.asarray(spread_matrix(part, high, wide), BF)
    place = jnp.asarray(place_matrix(16, slots, n), BF)

    ends = n - 1
    down_pairs = [(i, i + 1) for i in range(ends)]
    up_pairs = [(i + 1, i) for i in range(ends)]
    above = lax.ppermute(features[:, -1], "rows", down_pairs)
    below = lax.ppermute(features[:, 0], "rows", up_pairs)
    gain_hi = post_gain.astype(BF)
    gain_lo = (post_gain - gain_hi.astype(F32)).astype(BF)
    gain_row = jnp.concatenate([gain_hi, gain_lo, jnp.zeros((ch - 2 * share,), BF)])[None]
    square = post_expand.reshape(n, share, share)
    shards = jnp.concatenate(
        [post_reduce, jnp.concatenate([square[q] for q in range(n)], axis=1), jnp.pad(gain_row, ((0, 63), (0, 0)))], axis=0
    )
    shard = lax.dynamic_index_in_dim(shards.reshape(2, -1, ch), core, 0, keepdims=False)
    full = lax.all_gather(shard, ("chan", "core"), axis=0, tiled=True)
    full = full.reshape(n, 2 * share + 64, ch)
    flat_features = features.reshape(slots * cells, ch)
    live = (jnp.arange(SLOT)[None, :] < counts[:, None]).astype(F32).reshape(slots)
    select = place.T * jnp.tile(live.astype(BF), 16)[None, :]
    cot_rows = cotangent.transpose(1, 2, 0, 3).reshape(-1, out_share)
    sends = cotangent_by_image(cot_rows, select)
    cots = lax.all_to_all(after(sends, above, below), "chan", 0, 0, tiled=False)

    reduced, convolved, convolved_act, normal_pre, pre_std, *pooled = pre_forward(
        order, above, below, features, pre_reduce, pre_taps, pre_expand, pre_gain_row, pool_m
    )

    pooled = after(pooled, cots)
    moved = [lax.ppermute(pooled[k], ("rows", "chan"), spread(n, k)) for k in range(n)]
    flat, post_reduced, post_act, post_convolved, post_cact, post_normal, post_std, low = post_forward(
        source, moved, full, post_taps, pool
    )
    lows = [low] + [lax.ppermute(low, "chan", [(i, (i + k) % n) for i in range(n)]) for k in range(1, n)]
    refined_grad = readout_backward(low, readout, cots)
    post_expanded_grad, post_reduced_grad, post_taps_grad, post_gain_grad, *back = post_backward(
        source, refined_grad, full, post_taps, post_act, post_reduced, post_convolved, post_normal, post_std, pool
    )

    returned = [lax.ppermute(back[k], ("rows", "chan"), [(d, s) for s, d in spread(n, k)]) for k in range(n)]

    flat = after(flat, lows)
    load = post_weight_grads(flat, post_reduced_grad, post_cact, post_expanded_grad, n)

    at = lax.broadcasted_iota(jnp.int32, (16 * slots, 16 * slots), 0)
    column = lax.broadcasted_iota(jnp.int32, (16 * slots, 16 * slots), 1)
    each = 16 * part
    wanted = (column % each) // part * slots + part * ((chan - column // each) % n) + column % part
    place_here = jnp.where(at == wanted, 1.0, 0.0).astype(BF)
    lows = after(lows, load, returned[:2])
    tokens, piece = token_block(rank, source, lows, place_here, readout, sends)
    load = readout_weight_grad(lows, after(piece, returned[2:]), load)
    tokens = tokens.reshape(pool, pool, slots, out_share).transpose(2, 0, 1, 3)
    returned = after(returned, load)
    eight = share // 32
    rest = lax.psum_scatter(load, ("x", "core"), scatter_dimension=0, tiled=False)

    expanded_grad, convolved_grad, top, bottom, pre_gain_grad = pre_backward(
        order, returned, up_m, normal_pre, pre_std, pre_gain_row, convolved, pre_expand
    )
    grad_above = lax.ppermute(bottom, "rows", down_pairs)
    grad_below = lax.ppermute(top, "rows", up_pairs)
    act_rows = after(convolved_act, bottom).reshape(-1, ch)
    pre_expand_grad = dot(act_rows, expanded_grad.reshape(-1, ch), TN).astype(BF)
    convolved_grad = after(convolved_grad, pre_expand_grad)
    reduced_grad, pre_taps_grad = pre_conv_backward(convolved_grad, grad_above, grad_below, reduced, pre_taps)

    rest = after(rest, reduced_grad).reshape(n, 4, eight, 3 * ch).transpose(1, 0, 2, 3).reshape(4 * n, eight, 3 * ch)
    small = small_rows(pre_taps_grad, pre_gain_grad, post_taps_grad, post_gain_grad)
    flat_features = after(flat_features, small, rest)
    rest = lax.all_to_all(rest, ("rows", "chan"), 0, 0, tiled=False)
    pre_reduce_grad = dot(flat_features, reduced_grad.reshape(-1, ch), TN).astype(BF)
    rest = sum_parts(after(rest, pre_reduce_grad), n)

    chips = ("x", "rows", "chan")
    mine = [pre_reduce_grad, pre_expand_grad]
    theirs = [other_core(lax.dynamic_index_in_dim(g.reshape(2, ch // 2, ch), 1 - core, 0, keepdims=False)) for g in mine]
    load = join_halves(core_at, mine, after(theirs, rest), small, other_core(small), 64)
    rest = lax.all_gather(rest, ("x", "rows"), axis=0, tiled=False).reshape(4, 4 * eight, -1)
    pieces = lax.all_to_all(load, chips, 0, 0, tiled=False)
    feature_grad = feature_backward(order, after(reduced_grad, load), pre_reduce, returned, up_m).reshape(features.shape)
    pieces, rest = lax.optimization_barrier((pieces, rest, feature_grad))[:2]
    load = sum_and_copy(pieces)
    load_all = lax.all_to_all(load, chips, 0, 0, tiled=False).reshape(ch // 2, -1)

    def finish(kernel, values, *sizes):
        theirs = other_core(values)
        own = kernel(core_at, values, *sizes)
        theirs = after(theirs, *own)
        return own, theirs

    own, theirs = finish(finish_post, after(rest, load), n)
    post_out = finish_post(1 - core_at, theirs, n, earlier=tuple(own))
    post_reduce_out, post_expand_out, readout_out = post_out
    own, theirs = finish(finish_pre, after(load_all, *post_out), ch)
    pre_reduce_out, pre_expand_out, small_their = finish_pre(1 - core_at, theirs, ch, earlier=tuple(own[:2]))
    small_out = jnp.where(core == 0, own[2], small_their)
    per = ch // LANES
    cut = [0, 9 * per, 10 * per, 19 * per, 20 * per]
    pre_conv_out, pre_gain_out, post_conv_out, post_gain_out = [small_out[a:b] for a, b in zip(cut, cut[1:])]
    return (
        tokens,
        feature_grad,
        pre_reduce_out,
        pre_conv_out.reshape(3, 3, ch),
        pre_expand_out,
        pre_gain_out.reshape(ch),
        post_reduce_out,
        post_conv_out.reshape(3, 3, ch),
        post_expand_out.reshape(ch, share),
        lax.dynamic_slice_in_dim(post_gain_out.reshape(ch), chan * share, share, 0),
        readout_out,
    )


def solution(mesh):
    grid = Mesh(mesh.devices.reshape(4, 2, 4, 4), ("x", "core", "rows", "chan"))
    images = P(("x", "core", "chan"), "rows", None, None)
    grids = P(("x", "core", "rows"), None, None, "chan")
    return jax.shard_map(
        body,
        mesh=grid,
        in_specs=(
            images,
            P(("x", "core", "rows")),
            P(),
            P(),
            P(),
            P(),
            P("chan", None),
            P(),
            P(None, "chan"),
            P("chan"),
            P(),
            grids,
        ),
        out_specs=(grids, images, P(), P(), P(), P(), P("chan", None), P(), P(None, "chan"), P("chan"), P("chan", None)),
        check_vma=False,
    )
```

```python
import functools

import jax
import jax.numpy as jnp
import numpy as np
from jax import lax
from jax.experimental import pallas as pl
from jax.experimental.pallas import tpu as pltpu
from jax.sharding import Mesh, PartitionSpec as P

SLOT = 4
EPS = 1e-06
BF = jnp.bfloat16
F32 = jnp.float32
LANES = 128
VMEM_LIMIT = 56 * 1024 * 1024
NN = ((1,), (0,))
NT = ((1,), (1,))
TN = ((0,), (0,))


def dot(a, b, dims=NN):
    return lax.dot_general(a, b, (dims, ((), ())), preferred_element_type=F32)


def sigmoid(v):
    return 0.5 * jnp.tanh(0.5 * v) + 0.5


def silu(v):
    return v * sigmoid(v)


def silu_slope(v):
    s = sigmoid(v)
    return s * (1.0 + v * (1.0 - s))


def gelu_parts(v):
    c = 0.7978845608028654
    square = v * v
    t = jnp.tanh(v * (c + (c * 0.044715) * square))
    half = 0.5 * (1.0 + t)
    slope = half + 0.5 * v * (1.0 - t * t) * (c + (3.0 * c * 0.044715) * square)
    return v * half, slope


def chunks(count, body, width=LANES):
    for i in range(count):
        body(pl.ds(i * width, width))


def call(kernel, *, grid, ins, outs, scratch=(), prefetch=0, aliased=(), cost=1, name):
    def spec(shape, block, index):
        if block is None:
            block, index = shape, lambda *_: (0,) * len(shape)
        return pl.BlockSpec(block, index)

    arrays = [i[0] for i in ins] + list(aliased)
    in_specs = [spec(a.shape, b, m) for a, b, m in ins] + [pl.BlockSpec(memory_space=pl.ANY)] * len(aliased)
    out_specs = [spec(s.shape, b, m) for s, b, m in outs]

    def run(*scalars):
        return pl.pallas_call(
            kernel,
            grid_spec=pltpu.PrefetchScalarGridSpec(
                num_scalar_prefetch=prefetch,
                grid=grid,
                in_specs=in_specs,
                out_specs=out_specs,
                scratch_shapes=list(scratch),
            ),
            out_shape=[s[0] for s in outs],
            compiler_params=pltpu.CompilerParams(
                dimension_semantics=("arbitrary",) * len(grid), vmem_limit_bytes=VMEM_LIMIT
            ),
            input_output_aliases={prefetch + len(ins) + i: i for i in range(len(aliased))},
            cost_estimate=pl.CostEstimate(flops=cost, bytes_accessed=1, transcendentals=0),
            name=name,
        )(*scalars, *arrays)

    return run


def shape(dims, dtype):
    return jax.ShapeDtypeStruct(dims, dtype)


def columns_moved(t, by, first, last):
    rows = t.shape[0]
    return pltpu.roll(t, by % rows, 0) * (first if by > 0 else last)


def edge_masks(rows, width, depth):
    at = lax.broadcasted_iota(jnp.int32, (rows, LANES), 0) % (width * depth)
    return (at >= depth).astype(F32), (at < (width - 1) * depth).astype(F32)


def pre_forward(order, above, below, features, pre_reduce, taps, pre_expand, gain, pool):
    slots, high, wide, ch = features.shape
    cells = high * wide
    n = order.shape[0]
    part = slots // n
    rows_all = part * cells

    def kernel(order_ref, up_ref, down_ref, feat, wr, tap, we, gn, pool_ref, red_out, conv_out, act_out, norm_out, std_out, *rest):
        pooled_out, (red, halo, exp, sums) = rest[:n], rest[n:]
        k = pl.program_id(0)
        for side, ref in enumerate((up_ref, down_ref)):
            halo[side] = dot(ref[...].reshape(part * wide, ch), wr[...]).reshape(part, wide, ch)
        red[...] = dot(feat[...].reshape(rows_all, ch), wr[...]).reshape(part, cells, ch)
        red_out[...] = red[...].astype(BF)
        first, last = edge_masks(wide, wide, 1)
        for u in range(part):

            def conv(lanes):
                w = [tap[pl.ds(i, 1), lanes] for i in range(9)]
                rows = [halo[0, u, :, lanes]]
                rows += [red[u, pl.ds(i * wide, wide), lanes] for i in range(high)]
                rows += [halo[1, u, :, lanes]]
                rows = [silu(r).astype(BF).astype(F32) for r in rows]
                out = []
                for i in range(high):
                    t = [sum(rows[i + a] * w[3 * a + b] for a in range(3)) for b in range(3)]
                    out.append(t[1] + columns_moved(t[0], 1, first, last) + columns_moved(t[2], -1, first, last))
                conv_out[u, :, lanes] = jnp.concatenate(out, 0).astype(BF)
                act_out[u, :, lanes] = jnp.concatenate([silu(c) for c in out], 0).astype(BF)

            chunks(ch // LANES, conv)

        exp[...] = dot(act_out[...].reshape(rows_all, ch), we[...])

        def norm(p, carry):
            u, i = p // (high // 2), p % (high // 2)
            tiles = wide // 8
            f = [feat[u, 2 * i + half].astype(F32) for half in range(2)]
            nrms, blends = [], []
            for t in range(2 * tiles):
                e = exp[pl.ds(p * 2 * wide + 8 * t, 8), :]
                mean = jnp.mean(e, -1, keepdims=True)
                square = jnp.mean(e * e, -1, keepdims=True)
                std = lax.rsqrt(square - mean * mean + EPS)
                nrm = (e - mean) * std
                std_out[u, pl.ds(i * 2 * wide + 8 * t, 8), :] = std
                nrms.append(nrm)
                at = t % tiles
                blends.append(f[t // tiles][8 * at : 8 * at + 8] + silu(nrm * gn[...]))
                if t % 2 == 1:
                    both = jnp.concatenate(nrms[-2:], 0).astype(BF)
                    norm_out[u, pl.ds(i * 2 * wide + 8 * (t - 1), 16), :] = both
            for t in range(tiles):
                sums[pl.ds(p * wide + 8 * t, 8), :] = blends[t] + blends[tiles + t]
            return carry

        for p in range(part * high // 2):
            norm(p, 0)
        s = sums[...]
        hi = s.astype(BF)
        lo = (s - hi.astype(F32)).astype(BF)
        pooled = (dot(pool_ref[...], hi) + dot(pool_ref[...], lo)).astype(BF)
        for i in range(n):

            @pl.when(k == i)
            def _():
                pooled_out[i][...] = pooled

    def by_order(rest):
        return lambda k, order: (order[k],) + (0,) * rest

    pooled_rows = pool.shape[0]
    block = (part, cells, ch)
    return call(
        kernel,
        grid=(n,),
        prefetch=1,
        ins=[
            (above, (part, wide, ch), by_order(2)),
            (below, (part, wide, ch), by_order(2)),
            (features, (part, high, wide, ch), by_order(3)),
            (pre_reduce, None, None),
            (taps, None, None),
            (pre_expand, None, None),
            (gain, None, None),
            (pool, None, None),
        ],
        outs=[(shape((slots, cells, ch), BF), block, by_order(2))] * 4
        + [(shape((slots, cells, 1), F32), (part, cells, 1), by_order(2))]
        + [(shape((pooled_rows, ch), BF), None, None)] * n,
        scratch=[
            pltpu.VMEM((part, cells, ch), F32),
            pltpu.VMEM((2, part, wide, ch), F32),
            pltpu.VMEM((rows_all, ch), F32),
            pltpu.VMEM((rows_all // 2, ch), F32),
        ],
        name="pre_forward",
    )(order)


def gain_row(w, n, share):
    at = 2 * share
    parts = [w[c, at : at + 16, :].astype(F32)[:1] for c in range(n)]
    return jnp.concatenate([p[:, :share] + p[:, share : 2 * share] for p in parts], 1)


def post_forward(source, moved, weights, taps, pool):
    n, (rows, ch) = len(moved), moved[0].shape
    total = n * rows
    depth = total // (pool * pool)
    share = ch // n

    def kernel(src, *refs):
        got, refs = refs[:n], refs[n:]
        w, tap, flat_out, red_out, act_out, conv_out, cact_out, norm_out, std_out, low_out, wide_ref, red, exp = refs
        for k in range(n):
            at = pl.multiple_of(src[k] * rows, 8)
            wide_ref[pl.ds(at, rows), :] = got[k][...].astype(F32)
        gain = gain_row(w, n, share)
        flat_out[...] = wide_ref[...].astype(BF)
        total_red = 0.0
        for c in range(n):
            total_red = total_red + dot(flat_out[:, c * share : (c + 1) * share], w[c, :share])
        red[...] = total_red
        first, last = edge_masks(total, pool, depth)
        step = pool * depth

        def conv(lanes):
            v = red[:, lanes]
            red_out[:, lanes] = v.astype(BF)
            x = silu(v).astype(BF)
            act_out[:, lanes] = x
            x = x.astype(F32)
            moves = [columns_moved(x, depth, first, last), x, columns_moved(x, -depth, first, last)]
            t = [sum(moves[b] * tap[pl.ds(3 * a + b, 1), lanes] for b in range(3)) for a in range(3)]
            none = jnp.zeros((step, LANES), F32)
            c = t[1] + jnp.concatenate([none, t[0][:-step]], 0) + jnp.concatenate([t[2][step:], none], 0)
            conv_out[:, lanes] = c.astype(BF)
            cact_out[:, lanes] = silu(c).astype(BF)

        chunks(ch // LANES, conv)
        for c in range(n):
            e = 0.0
            for q in range(n):
                cut = slice(q * share, (q + 1) * share)
                e = e + dot(cact_out[:, cut], w[c, share : 2 * share, cut])
            exp[:, c * share : (c + 1) * share] = e

        def norm(i, carry):
            for t in range(3):
                at = pl.ds(i * 48 + 16 * t, 16)
                e = exp[at, :]
                mean = jnp.mean(e, -1, keepdims=True)
                square = jnp.mean(e * e, -1, keepdims=True)
                std = lax.rsqrt(square - mean * mean + EPS)
                nrm = (e - mean) * std
                norm_out[at, :] = nrm.astype(BF)
                std_out[at, :] = std
                low_out[at, :] = (wide_ref[at, :] + silu(nrm * gain)).astype(BF)
            return carry

        for i in range(total // 48):
            norm(i, 0)

    narrow = shape((total, ch), BF)
    return call(
        kernel,
        grid=(1,),
        prefetch=1,
        ins=[(a, None, None) for a in (*moved, weights, taps)],
        outs=[(s, None, None) for s in (narrow, narrow, narrow, narrow, narrow, narrow, shape((total, 1), F32), narrow)],
        scratch=[pltpu.VMEM((total, ch), F32)] * 3,
        name="post_forward",
    )(source)


def readout_backward(source, low, readout, cots):
    total, ch = low.shape
    n, out_share = len(cots), cots[0].shape[1]

    def kernel(src, low_ref, ro, *rest):
        cot, grad = rest[:n], rest[n]
        k = pl.program_id(0)
        logits = dot(low_ref[...], ro[...])
        slope = gelu_parts(logits)[1]
        for i in range(n):

            @pl.when(k == i)
            def _():
                piece = (cot[i][...].astype(F32) * slope).astype(BF)
                term = dot(piece, ro[...], NT)
                grad[...] = term if i == 0 else grad[...] + term

    return call(
        kernel,
        grid=(n,),
        prefetch=1,
        ins=[(low, None, None), (readout, (ch, out_share), lambda k, s: (0, s[k]))] + [(c, None, None) for c in cots],
        outs=[(shape((total, ch), F32), None, None)],
        name="readout_backward",
    )(source)[0]


def post_backward(source, refined_grad, weights, taps, act, red, conv, nrm, std, pool):
    total, ch = act.shape
    n = weights.shape[0]
    share = ch // n
    rows = total // n
    depth = total // (pool * pool)

    def kernel(src, rg, w, tap, act_ref, red_ref, conv_ref, norm_ref, std_ref, exp_out, redg_out, taps_out, gain_out, *rest):
        back_out, (grad, cgrad) = rest[:n], rest[n:]
        gain = gain_row(w, n, share)

        def norm(i, total_gain):
            for t in range(3):
                at = pl.ds(i * 48 + 16 * t, 16)
                nm = norm_ref[at, :].astype(F32)
                ng = rg[at, :] * silu_slope(nm * gain)
                sc = ng * gain
                one = jnp.mean(sc, -1, keepdims=True)
                two = jnp.mean(sc * nm, -1, keepdims=True)
                exp_out[at, :] = (std_ref[at, :] * (sc - one - nm * two)).astype(BF)
                g = ng * nm
                total_gain = total_gain + g[:8] + g[8:]
            return total_gain

        gains = jnp.zeros((8, ch), F32)
        for i in range(total // 48):
            gains = norm(i, gains)
        gain_out[...] = gains
        for q in range(n):
            cut = slice(q * share, (q + 1) * share)
            cg = 0.0
            for c in range(n):
                cg = cg + dot(exp_out[:, c * share : (c + 1) * share], w[c, share : 2 * share, cut], NT)
            cgrad[:, cut] = cg
        first, last = edge_masks(total, pool, depth)
        step = pool * depth

        def back(lanes):
            g = (cgrad[:, lanes] * silu_slope(conv_ref[:, lanes].astype(F32))).astype(BF).astype(F32)
            x = act_ref[:, lanes].astype(F32)
            moves = [columns_moved(g, -depth, first, last), g, columns_moved(g, depth, first, last)]
            none = jnp.zeros((step, LANES), F32)
            xs = [
                jnp.concatenate([none, x[:-step]], 0),
                x,
                jnp.concatenate([x[step:], none], 0),
            ]
            for a in range(3):
                for b in range(3):
                    prod = xs[a] * moves[b]
                    taps_out[3 * a + b, :, lanes] = jnp.sum(prod.reshape(total // 8, 8, LANES), 0)
            t = [sum(moves[b] * tap[pl.ds(3 * a + b, 1), lanes] for b in range(3)) for a in range(3)]
            d = t[1] + jnp.concatenate([t[0][step:], none], 0) + jnp.concatenate([none, t[2][:-step]], 0)
            redg_out[:, lanes] = (d * silu_slope(red_ref[:, lanes].astype(F32))).astype(BF)

        chunks(ch // LANES, back)
        for c in range(n):
            cut = slice(c * share, (c + 1) * share)
            grad[:, cut] = rg[:, cut] + dot(redg_out[...], w[c, :share], NT)
        for r in range(n):
            at = pl.ds(pl.multiple_of(src[r] * rows, 8), rows)
            back_out[r][...] = grad[at, :].astype(BF)

    return call(
        kernel,
        grid=(1,),
        prefetch=1,
        ins=[(a, None, None) for a in (refined_grad, weights, taps, act, red, conv, nrm, std)],
        outs=[
            (s, None, None)
            for s in (
                shape((total, ch), BF),
                shape((total, ch), BF),
                shape((9, 8, ch), F32),
                shape((8, ch), F32),
                *[shape((rows, ch), BF)] * n,
            )
        ],
        scratch=[pltpu.VMEM((total, ch), F32), pltpu.VMEM((total, ch), F32)],
        name="post_backward",
    )(source)


def cotangent_by_image(cotangent, select, pairs):
    rows, width = cotangent.shape
    size = select.shape[0]
    each = size // pairs
    per = 3

    def kernel(x, sel, *outs):
        for q in range(per):
            y = dot(sel[...], x[pl.ds(q * size, size), :]).astype(BF)
            for s in range(pairs):
                outs[s][pl.ds(q * each, each), :] = y[s * each : (s + 1) * each]

    return call(
        kernel,
        grid=(rows // (per * size),),
        ins=[(cotangent, (per * size, width), lambda i: (i, 0)), (select, None, None)],
        outs=[(shape((rows // pairs, width), BF), (per * each, width), lambda i: (i, 0))] * pairs,
        name="cotangent_by_image",
    )()


def token_block(chan, source, pair_of, low, place, readout, cotangent):
    pairs, (rows, ch) = len(low), low[0].shape
    width = cotangent[0].shape[1]
    size = place.shape[0]
    each = size // pairs
    per = 3
    block = per * each

    def kernel(chan_ref, src, pair, *refs):
        lows, cots, (place_ref, ro, tok_out, piece_out, cot) = refs[:pairs], refs[pairs : 2 * pairs], refs[2 * pairs :]
        for k in range(pairs):
            cot[pair[k]] = cots[k][...]
        logits = dot(jnp.concatenate([v[...] for v in lows], 0), ro[...])
        value, slope = gelu_parts(logits)
        value = value.astype(BF)
        for k in range(pairs):
            piece_out[k] = (cot[src[k]].astype(F32) * slope[k * block : (k + 1) * block]).astype(BF)
        for q in range(per):
            x = jnp.concatenate([value[k * block + q * each : k * block + (q + 1) * each] for k in range(pairs)], 0)
            tok_out[pl.ds(q * size, size), :] = dot(place_ref[...], x).astype(BF)

    rows_at = lambda i, c, s, p: (i, 0)
    return call(
        kernel,
        grid=(rows // block,),
        prefetch=3,
        ins=[
            *[(v, (block, ch), rows_at) for v in low],
            *[(v, (block, width), rows_at) for v in cotangent],
            (place, None, None),
            (readout, (ch, width), lambda i, c, s, p: (0, c[0])),
        ],
        outs=[
            (shape((pairs * rows, width), BF), (pairs * block, width), rows_at),
            (shape((pairs, rows, width), BF), (pairs, block, width), lambda i, c, s, p: (0, i, 0)),
        ],
        scratch=[pltpu.VMEM((pairs, block, width), BF)],
        name="token_block",
    )(chan, source, pair_of)


def pre_backward(order, returned, spread_up, nrm, std, gain, conv, pre_expand):
    slots, cells, ch = nrm.shape
    n = order.shape[0]
    part = slots // n
    wide = 24
    rows = part * cells

    def kernel(order_ref, *refs):
        ret, refs = refs[:n], refs[n:]
        up, norm_ref, std_ref, gn, conv_ref, we, exp_out, conv_grad_out, top_out, bottom_out, gain_out, grad, cgrad = refs
        k = pl.program_id(0)
        for i in range(n):

            @pl.when(k == i)
            def _():
                grad[...] = dot(up[...], ret[i][...])

        def norm(i, total_gain):
            u, j = i // (cells // 48), i % (cells // 48)
            for t in range(3):
                at = pl.ds(j * 48 + 16 * t, 16)
                nm = norm_ref[u, at, :].astype(F32)
                ng = grad[pl.ds(i * 48 + 16 * t, 16), :] * silu_slope(nm * gn[...])
                sc = ng * gn[...]
                one = jnp.mean(sc, -1, keepdims=True)
                two = jnp.mean(sc * nm, -1, keepdims=True)
                exp_out[u, at, :] = (std_ref[u, at, :] * (sc - one - nm * two)).astype(BF)
                g = ng * nm
                total_gain = total_gain + g[:8] + g[8:]
            return total_gain

        gains = jnp.zeros((8, ch), F32)
        for i in range(rows // 48):
            gains = norm(i, gains)

        @pl.when(k == 0)
        def _():
            gain_out[...] = gains

        @pl.when(k > 0)
        def _():
            gain_out[...] += gains

        cgrad[...] = dot(exp_out[...].reshape(rows, ch), we[...], NT)
        for u in range(part):

            def slope(lanes):
                g = cgrad[pl.ds(u * cells, cells), lanes] * silu_slope(conv_ref[u, :, lanes].astype(F32))
                conv_grad_out[u, :, lanes] = g.astype(BF)
                top_out[u, :, lanes] = g[:wide].astype(BF)
                bottom_out[u, :, lanes] = g[cells - wide :].astype(BF)

            chunks(ch // LANES, slope)

    by_order = lambda k, order: (order[k], 0, 0)
    whole = (part, cells, ch)
    edge = (part, wide, ch)
    return call(
        kernel,
        grid=(n,),
        prefetch=1,
        ins=[
            *[(r, None, None) for r in returned],
            (spread_up, None, None),
            (nrm, whole, by_order),
            (std, (part, cells, 1), by_order),
            (gain, None, None),
            (conv, whole, by_order),
            (pre_expand, None, None),
        ],
        outs=[
            (shape((slots, cells, ch), BF), whole, by_order),
            (shape((slots, cells, ch), BF), whole, by_order),
            (shape((slots, wide, ch), BF), edge, by_order),
            (shape((slots, wide, ch), BF), edge, by_order),
            (shape((8, ch), F32), None, None),
        ],
        scratch=[pltpu.VMEM((rows, ch), F32), pltpu.VMEM((rows, ch), F32)],
        name="pre_backward",
    )(order)


def pre_conv_backward(conv_grad, above, below, reduced, taps):
    slots, cells, ch = reduced.shape
    wide = above.shape[1]
    high = cells // wide

    def kernel(cg, up, down, red, tap, redg_out, taps_out):
        step = pl.program_id(0)
        first, last = edge_masks(wide, wide, 1)

        @pl.when(step == 0)
        def _():
            taps_out[...] = jnp.zeros_like(taps_out)

        def back(lanes):
            w = [tap[pl.ds(i, 1), lanes] for i in range(9)]
            mid = cg[0, :, lanes].astype(F32)
            rows = [up[0, :, lanes].astype(F32)]
            rows += [mid[i * wide : (i + 1) * wide] for i in range(high)]
            rows += [down[0, :, lanes].astype(F32)]
            whole = red[0, :, lanes].astype(F32)
            v = [whole[i * wide : (i + 1) * wide] for i in range(high)]
            s = [sigmoid(t) for t in v]
            x = [(a * b).astype(BF).astype(F32) for a, b in zip(v, s)]
            d = [0.0] * high
            sums = [0.0] * 9
            for p in range(high + 2):
                g = rows[p]
                moves = [columns_moved(g, -1, first, last), g, columns_moved(g, 1, first, last)]
                for a in range(3):
                    i = p - 1 + a - 1
                    if 0 <= i < high:
                        for b in range(3):
                            d[i] = d[i] + moves[b] * w[3 * a + b]
                            prod = x[i] * moves[b]
                            sums[3 * a + b] = sums[3 * a + b] + (prod[:8] + prod[8:16] + prod[16:])
            out = [d[i] * (s[i] * (1.0 + v[i] * (1.0 - s[i]))) for i in range(high)]
            redg_out[0, :, lanes] = jnp.concatenate(out, 0).astype(BF)
            for i in range(9):
                taps_out[i, :, lanes] += sums[i]

        chunks(ch // LANES, back)

    image = lambda i: (i, 0, 0)
    return call(
        kernel,
        grid=(slots,),
        ins=[
            (conv_grad, (1, cells, ch), image),
            (above, (1, wide, ch), image),
            (below, (1, wide, ch), image),
            (reduced, (1, cells, ch), image),
            (taps, None, None),
        ],
        outs=[
            (shape((slots, cells, ch), BF), (1, cells, ch), image),
            (shape((9, 8, ch), F32), None, None),
        ],
        name="pre_conv_backward",
    )()


def feature_backward(order, reduced_grad, pre_reduce, returned, spread_up):
    slots, cells, ch = reduced_grad.shape
    n = order.shape[0]
    part = slots // n

    def kernel(order_ref, rg, wr, up, *refs):
        ret, out = refs[:n], refs[n]
        k = pl.program_id(0)
        for i in range(n):

            @pl.when(k == i)
            def _():
                out[...] = dot(up[...], ret[i][...]).reshape(part, cells, ch)

        out[...] += dot(rg[...].reshape(part * cells, ch), wr[...], NT).reshape(part, cells, ch)

    by_order = lambda k, order: (order[k], 0, 0)
    whole = (part, cells, ch)
    return call(
        kernel,
        grid=(n,),
        prefetch=1,
        ins=[
            (reduced_grad, whole, by_order),
            (pre_reduce, None, None),
            (spread_up, None, None),
            *[(r, None, None) for r in returned],
        ],
        outs=[(shape((slots, cells, ch), F32), whole, by_order)],
        name="feature_backward",
    )(order)[0]


def post_weight_grads(flat, reduced_grad, act, expanded_grad, n):
    total, ch = flat.shape
    share = ch // n
    rows = share // 8

    def kernel(x, g, a, e, out):
        for c in range(n):
            cut = slice(c * share, (c + 1) * share)
            v = dot(x[:, cut], g[...], TN).astype(BF)
            for d in range(8):
                out[d, c, :, :ch] = v[d * rows : (d + 1) * rows]
            for q in range(n):
                v = dot(a[:, q * share : (q + 1) * share], e[:, cut], TN).astype(BF)
                for d in range(8):
                    out[d, c, :, ch + q * share : ch + (q + 1) * share] = v[d * rows : (d + 1) * rows]

    return call(
        kernel,
        grid=(1,),
        ins=[(v, None, None) for v in (flat, reduced_grad, act, expanded_grad)],
        outs=[(shape((8, n, rows, 3 * ch), BF), (8, n, rows, 2 * ch), lambda i: (0, 0, 0, 0))],
        name="post_weight_grads",
    )()[0]


def readout_weight_grad(low, piece, load):
    pairs, total, width = piece.shape
    parts, n, rows, _ = load.shape
    share = low[0].shape[1] // n

    def kernel(*refs):
        x, (g, old, out) = refs[:pairs], refs[pairs:]
        x = jnp.concatenate([v[...] for v in x], 0)
        v = dot(x, g[...].reshape(pairs * total, width), TN).astype(BF)
        for d in range(parts):
            out[d, 0] = v[d * rows : (d + 1) * rows]

    return call(
        kernel,
        grid=(n,),
        ins=[(v, (total, share), lambda c: (0, c)) for v in low] + [(piece, None, None)],
        outs=[(shape(load.shape, BF), (parts, 1, rows, width), lambda c: (0, c, 0, 2))],
        aliased=(load,),
        name="readout_weight_grad",
    )()[0]


def cross(n, k):
    return [(a * n + b, ((b + k) % n) * n + a) for a in range(n) for b in range(n)]


def turn(n, k):
    return [(i, (i + k) % n) for i in range(n)]


def other_core(values):
    return lax.ppermute(values, "core", [(0, 1), (1, 0)])


def small_rows(*grads):
    ch = grads[0].shape[-1]
    counts = [g.shape[0] if g.ndim == 3 else 1 for g in grads]
    per = ch // LANES

    def kernel(*refs):
        out = refs[-1]
        at = 0
        for ref, count in zip(refs, counts):
            for i in range(count):
                v = jnp.sum(ref[i] if len(ref.shape) == 3 else ref[...], 0, keepdims=True)
                for q in range(per):
                    out[pl.ds(at, 1), :] = v[:, q * LANES : (q + 1) * LANES]
                    at += 1

    return call(
        kernel,
        grid=(1,),
        ins=[(g, None, None) for g in grads],
        outs=[(shape((sum(counts) * per, LANES), F32), None, None)],
        name="small_rows",
    )()[0]


def join_halves(core, mine, theirs, small, their_small, parts):
    rows, ch = mine[0].shape
    half = rows // 2
    width = len(mine) * ch + LANES
    count = small.shape[0]
    m = len(mine)
    steps = 2
    block = half // steps

    def kernel(core_ref, *refs):
        own, got = refs[:m], refs[m : 2 * m]
        sm, got_sm, out = refs[2 * m :]
        for i in range(m):
            out[:, i * ch : (i + 1) * ch] = (own[i][...].astype(F32) + got[i][...].astype(F32)).astype(BF)
        first = ((core_ref[0] == 0) & (pl.program_id(0) == 0)).astype(F32)
        total = (sm[...] + got_sm[...]) * first
        pad = jnp.zeros((block - count, LANES), F32)
        out[:, m * ch :] = jnp.concatenate([total, pad], 0).astype(BF)

    return call(
        kernel,
        grid=(steps,),
        prefetch=1,
        ins=[(v, (block, ch), lambda i, c: (c[0] * steps + i, 0)) for v in mine]
        + [(v, (block, ch), lambda i, c: (i, 0)) for v in theirs]
        + [(v, None, None) for v in (small, their_small)],
        outs=[(shape((half, width), BF), (block, width), lambda i, c: (i, 0))],
        name="join_halves",
    )(core)[0].reshape(parts, half // parts, width)


def sum_and_copy(blocks):
    parts, rows, width = blocks.shape

    def kernel(x, out):
        def cut(lanes):
            total = jnp.sum(x[:, :, lanes].astype(F32), 0).astype(BF)
            out[:, :, lanes] = jnp.broadcast_to(total[None], (parts, rows, LANES))

        chunks(width // LANES, cut)

    return call(
        kernel,
        grid=(1,),
        ins=[(blocks, None, None)],
        outs=[(shape(blocks.shape, BF), None, None)],
        name="sum_and_copy",
    )()[0]


def sum_parts(blocks, n):
    parts, rows, width = blocks.shape
    ch = width // 3

    def kernel(x, out):
        for lanes in range(0, width, ch):
            for at in range(lanes, lanes + ch, 2 * LANES):
                cut = slice(at, at + 2 * LANES)
                by_chan = [sum(x[p, :, cut].astype(F32) for p in range(c, parts, n)) for c in range(n)]
                if lanes < 2 * ch:
                    out[:, cut] = sum(by_chan).astype(BF)
                else:
                    for c in range(n):
                        out[:, at + c * ch : at + c * ch + 2 * LANES] = by_chan[c].astype(BF)

    return call(
        kernel,
        grid=(1,),
        ins=[(blocks, None, None)],
        outs=[(shape((rows, 2 * ch + n * ch), BF), None, None)],
        name="sum_parts",
    )()[0]


def finish_pre(place, half_rows, ch, earlier=()):
    half, width = half_rows.shape
    m = (width - LANES) // ch
    steps = 4
    block = half // steps

    def kernel(place_ref, x, *outs):
        outs = outs[len(earlier) :]
        for i in range(m):
            outs[i][...] = x[:, i * ch : (i + 1) * ch].astype(F32)
        outs[m][...] = x[:, m * ch :].astype(F32)

    return call(
        kernel,
        grid=(steps,),
        prefetch=1,
        ins=[(half_rows, (block, width), lambda i, c: (i, 0))],
        outs=[(shape((2 * half, ch), F32), (block, ch), lambda i, c: (c[0] * steps + i, 0)) for _ in range(m)]
        + [(shape((half, LANES), F32), (block, LANES), lambda i, c: (i, 0))],
        aliased=earlier,
        name="finish_pre",
    )(place)


def finish_post(place, gathered, n, earlier=()):
    groups, per, width = gathered.shape
    share = 2 * groups * per
    ch = width // (n + 2)

    def kernel(place_ref, x, *outs):
        reduce_out, expand_out, read_out = outs[len(earlier) :]
        reduce_out[...] = x[0, :, :ch].astype(F32)
        for q in range(n):
            expand_out[q] = x[0, :, ch + q * share : ch + (q + 1) * share].astype(F32)
        read_out[...] = x[0, :, 2 * ch :].astype(F32)

    at = lambda i, c: (2 * i + c[0], 0)
    return call(
        kernel,
        grid=(groups,),
        prefetch=1,
        ins=[(gathered, (1, per, width), lambda i, c: (i, 0, 0))],
        outs=[
            (shape((share, ch), F32), (per, ch), at),
            (shape((n, share, share), F32), (n, per, share), lambda i, c: (0, 2 * i + c[0], 0)),
            (shape((share, n * ch), F32), (per, n * ch), at),
        ],
        aliased=earlier,
        name="finish_post",
    )(place)


def after(values, *earlier):
    return lax.optimization_barrier((values, *earlier))[0]


def pool_matrix(part, high, wide):
    half = wide // 2
    m = np.zeros((high // 2 * half * part, part * (high // 2) * wide), np.float32)
    for u in range(part):
        for i in range(high // 2):
            for j in range(wide):
                m[(i * half + j // 2) * part + u, (u * (high // 2) + i) * wide + j] = 0.25
    return m


def spread_matrix(part, high, wide):
    half = wide // 2
    m = np.zeros((part * high * wide, high // 2 * half * part), np.float32)
    for u in range(part):
        for i in range(high):
            for j in range(wide):
                m[(u * high + i) * wide + j, ((i // 2) * half + j // 2) * part + u] = 0.25
    return m


def body(features, counts, pre_reduce, pre_conv, pre_expand, pre_gain, post_reduce, post_conv, post_expand, post_gain, readout, cotangent):
    n = lax.axis_size("chan")
    row = lax.axis_index("rows").astype(jnp.int32)
    chan = lax.axis_index("chan").astype(jnp.int32)
    core = lax.axis_index("core").astype(jnp.int32)
    ch = pre_reduce.shape[0]
    slots, high, wide = features.shape[0], features.shape[1], features.shape[2]
    part = slots // n
    cells = high * wide
    pool = wide // 2
    share = ch // n
    out_share = cotangent.shape[3]
    steps = jnp.arange(n, dtype=jnp.int32)
    order = (row + steps) % n
    source = (row - steps) % n
    pair_of = (chan + steps) % n
    rank = jnp.full((1,), chan, jnp.int32)
    core_at = jnp.full((1,), core, jnp.int32)
    pre_taps = pre_conv.astype(F32).reshape(9, ch)
    post_taps = post_conv.astype(F32).reshape(9, ch)
    pre_gain_row = pre_gain.reshape(1, ch)
    pool_m = jnp.asarray(pool_matrix(part, high, wide), BF)
    up_m = jnp.asarray(spread_matrix(part, high, wide), BF)

    ends = n - 1
    down_pairs = [(i, i + 1) for i in range(ends)]
    up_pairs = [(i + 1, i) for i in range(ends)]
    above = lax.ppermute(features[:, -1], "rows", down_pairs)
    below = lax.ppermute(features[:, 0], "rows", up_pairs)
    gain_hi = post_gain.astype(BF)
    gain_lo = (post_gain - gain_hi.astype(F32)).astype(BF)
    gain_row = jnp.concatenate([gain_hi, gain_lo, jnp.zeros((ch - 2 * share,), BF)])[None]
    square = post_expand.reshape(n, share, share)
    shards = jnp.concatenate(
        [post_reduce, jnp.concatenate([square[q] for q in range(n)], axis=1), jnp.pad(gain_row, ((0, 63), (0, 0)))], axis=0
    )
    shard = lax.dynamic_index_in_dim(shards.reshape(2, -1, ch), core, 0, keepdims=False)
    full = lax.all_gather(shard, ("chan", "core"), axis=0, tiled=True)
    full = full.reshape(n, 2 * share + 64, ch)
    flat_features = features.reshape(slots * cells, ch)
    live = (jnp.arange(SLOT)[None, :] < counts[:, None]).astype(F32).reshape(slots)
    size, each = 16 * slots, 16 * part
    at = lax.broadcasted_iota(jnp.int32, (size, size), 0)
    column = lax.broadcasted_iota(jnp.int32, (size, size), 1)
    wanted = (at % each) // part * slots + part * ((chan + at // each) % n) + at % part
    select = jnp.where(column == wanted, jnp.tile(live, 16)[None, :], 0.0).astype(BF)
    wanted = (column % each) // part * slots + part * ((row - column // each) % n) + column % part
    place = jnp.where(at == wanted, 1.0, 0.0).astype(BF)
    cot_rows = cotangent.transpose(1, 2, 0, 3).reshape(-1, out_share)
    sends = cotangent_by_image(cot_rows, select, n)
    away = after(sends, above, below)
    cots = [lax.ppermute(away[k], ("rows", "chan"), cross(n, k)) for k in range(n)]

    reduced, convolved, convolved_act, normal_pre, pre_std, *pooled = pre_forward(
        order, above, below, features, pre_reduce, pre_taps, pre_expand, pre_gain_row, pool_m
    )

    pooled = after(pooled, cots)
    moved = [pooled[0]] + [lax.ppermute(pooled[k], "rows", turn(n, k)) for k in range(1, n)]
    flat, post_reduced, post_act, post_convolved, post_cact, post_normal, post_std, low = post_forward(
        source, moved, full, post_taps, pool
    )
    lows = [low] + [lax.ppermute(low, "chan", turn(n, k)) for k in range(1, n)]
    refined_grad = readout_backward(source, low, readout, cots)
    post_expanded_grad, post_reduced_grad, post_taps_grad, post_gain_grad, *back = post_backward(
        source, refined_grad, full, post_taps, post_act, post_reduced, post_convolved, post_normal, post_std, pool
    )

    returned = [back[0]] + [lax.ppermute(back[k], "rows", turn(n, -k)) for k in range(1, n)]

    flat = after(flat, lows)
    load = post_weight_grads(flat, post_reduced_grad, post_cact, post_expanded_grad, n)

    stacked = jnp.stack(after(lows, load))
    lows = [lax.dynamic_index_in_dim(stacked, (chan - row - k) % n, 0, keepdims=False) for k in range(n)]
    lows = [lows[0]] + [lax.ppermute(lows[k], "rows", turn(n, k)) for k in range(1, n)]

    expanded_grad, convolved_grad, top, bottom, pre_gain_grad = pre_backward(
        order, returned, up_m, normal_pre, pre_std, pre_gain_row, convolved, pre_expand
    )
    top, bottom, lows[1], lows[3] = lax.optimization_barrier((top, bottom, lows[1], lows[3]))
    grad_above = lax.ppermute(bottom, "rows", down_pairs)
    grad_below = lax.ppermute(top, "rows", up_pairs)
    act_rows = after(convolved_act, bottom).reshape(-1, ch)
    pre_expand_grad = dot(act_rows, expanded_grad.reshape(-1, ch), TN).astype(BF)

    lows = after(lows, pre_expand_grad)
    tokens, piece = token_block(rank, source, pair_of, lows, place, readout, sends)
    load = readout_weight_grad(lows, piece, load)
    tokens = tokens.reshape(pool, pool, slots, out_share).transpose(2, 0, 1, 3)
    eight = share // 32
    convolved_grad = after(convolved_grad, load)
    rest = lax.psum_scatter(load, ("x", "core"), scatter_dimension=0, tiled=False)

    reduced_grad, pre_taps_grad = pre_conv_backward(convolved_grad, grad_above, grad_below, reduced, pre_taps)
    small = small_rows(pre_taps_grad, pre_gain_grad, post_taps_grad, post_gain_grad)
    pre_reduce_grad = dot(after(flat_features, small), reduced_grad.reshape(-1, ch), TN).astype(BF)

    chips = ("x", "rows", "chan")
    mine = [pre_reduce_grad, pre_expand_grad]
    theirs = [other_core(lax.dynamic_index_in_dim(g.reshape(2, ch // 2, ch), 1 - core, 0, keepdims=False)) for g in mine]
    load = join_halves(core_at, mine, theirs, small, other_core(small), 64)
    pieces = lax.all_to_all(load, chips, 0, 0, tiled=False)
    feature_grad = feature_backward(order, after(reduced_grad, load), pre_reduce, returned, up_m).reshape(features.shape)

    rest = after(rest, feature_grad, pieces).reshape(n, 4, eight, 3 * ch).transpose(1, 0, 2, 3).reshape(4 * n, eight, 3 * ch)
    pieces = after(pieces, rest)
    rest = lax.all_to_all(rest, ("rows", "chan"), 0, 0, tiled=False)
    load = sum_and_copy(pieces)
    rest = sum_parts(after(rest, load), n)
    load = after(load, rest)
    rest = lax.all_gather(rest, ("x", "rows"), axis=0, tiled=False).reshape(4, 4 * eight, -1)
    load_all = lax.all_to_all(load, chips, 0, 0, tiled=False).reshape(ch // 2, -1)

    def finish(kernel, values, *sizes):
        theirs = other_core(values)
        own = kernel(core_at, values, *sizes)
        theirs = after(theirs, *own)
        return own, theirs

    own, theirs = finish(finish_pre, load_all, ch)
    pre_reduce_out, pre_expand_out, small_their = finish_pre(1 - core_at, theirs, ch, earlier=tuple(own[:2]))
    small_out = jnp.where(core == 0, own[2], small_their)
    own, theirs = finish(finish_post, after(rest, pre_reduce_out), n)
    post_reduce_out, post_expand_out, readout_out = finish_post(1 - core_at, theirs, n, earlier=tuple(own))
    per = ch // LANES
    cut = [0, 9 * per, 10 * per, 19 * per, 20 * per]
    pre_conv_out, pre_gain_out, post_conv_out, post_gain_out = [small_out[a:b] for a, b in zip(cut, cut[1:])]
    return (
        tokens,
        feature_grad,
        pre_reduce_out,
        pre_conv_out.reshape(3, 3, ch),
        pre_expand_out,
        pre_gain_out.reshape(ch),
        post_reduce_out,
        post_conv_out.reshape(3, 3, ch),
        post_expand_out.reshape(ch, share),
        lax.dynamic_slice_in_dim(post_gain_out.reshape(ch), chan * share, share, 0),
        readout_out,
    )


def solution(mesh):
    grid = Mesh(mesh.devices.reshape(4, 2, 4, 4), ("x", "core", "rows", "chan"))
    images = P(("x", "core", "chan"), "rows", None, None)
    grids = P(("x", "core", "rows"), None, None, "chan")
    return jax.shard_map(
        body,
        mesh=grid,
        in_specs=(
            images,
            P(("x", "core", "rows")),
            P(),
            P(),
            P(),
            P(),
            P("chan", None),
            P(),
            P(None, "chan"),
            P("chan"),
            P(),
            grids,
        ),
        out_specs=(grids, images, P(), P(), P(), P(), P("chan", None), P(), P(None, "chan"), P("chan"), P("chan", None)),
        check_vma=False,
    )
```

```python
import functools

import jax
import jax.numpy as jnp
import numpy as np
from jax import lax
from jax.experimental import pallas as pl
from jax.experimental.pallas import tpu as pltpu
from jax.sharding import Mesh, PartitionSpec as P

SLOT = 4
EPS = 1e-06
BF = jnp.bfloat16
F32 = jnp.float32
LANES = 128
VMEM_LIMIT = 20 * 1024 * 1024
NN = ((1,), (0,))
NT = ((1,), (1,))
TN = ((0,), (0,))


def dot(a, b, dims=NN):
    return lax.dot_general(a, b, (dims, ((), ())), preferred_element_type=F32)


def sigmoid(v):
    return 0.5 * jnp.tanh(0.5 * v) + 0.5


def silu(v):
    return v * sigmoid(v)


def silu_slope(v):
    s = sigmoid(v)
    return s * (1.0 + v * (1.0 - s))


def gelu_parts(v):
    c = 0.7978845608028654
    square = v * v
    t = jnp.tanh(v * (c + (c * 0.044715) * square))
    half = 0.5 * (1.0 + t)
    slope = half + 0.5 * v * (1.0 - t * t) * (c + (3.0 * c * 0.044715) * square)
    return v * half, slope


def chunks(count, body, width=LANES):
    for i in range(count):
        body(pl.ds(i * width, width))


def call(kernel, *, grid, ins, outs, scratch=(), prefetch=0, aliased=(), cost=1, name):
    def spec(shape, block, index):
        if block is None:
            block, index = shape, lambda *_: (0,) * len(shape)
        return pl.BlockSpec(block, index)

    arrays = [i[0] for i in ins] + list(aliased)
    in_specs = [spec(a.shape, b, m) for a, b, m in ins] + [pl.BlockSpec(memory_space=pl.ANY)] * len(aliased)
    out_specs = [spec(s.shape, b, m) for s, b, m in outs]

    def run(*scalars):
        return pl.pallas_call(
            kernel,
            grid_spec=pltpu.PrefetchScalarGridSpec(
                num_scalar_prefetch=prefetch,
                grid=grid,
                in_specs=in_specs,
                out_specs=out_specs,
                scratch_shapes=list(scratch),
            ),
            out_shape=[s[0] for s in outs],
            compiler_params=pltpu.CompilerParams(
                dimension_semantics=("arbitrary",) * len(grid), vmem_limit_bytes=VMEM_LIMIT
            ),
            input_output_aliases={prefetch + len(ins) + i: i for i in range(len(aliased))},
            cost_estimate=pl.CostEstimate(flops=cost, bytes_accessed=1, transcendentals=0),
            name=name,
        )(*scalars, *arrays)

    return run


def shape(dims, dtype):
    return jax.ShapeDtypeStruct(dims, dtype)


def columns_moved(t, by, first, last):
    rows = t.shape[0]
    return pltpu.roll(t, by % rows, 0) * (first if by > 0 else last)


def edge_masks(rows, width, depth):
    at = lax.broadcasted_iota(jnp.int32, (rows, LANES), 0) % (width * depth)
    return (at >= depth).astype(F32), (at < (width - 1) * depth).astype(F32)


def pre_forward(order, above, below, features, pre_reduce, taps, pre_expand, gain, pool):
    slots, high, wide, ch = features.shape
    cells = high * wide
    n = order.shape[0]
    part = slots // n
    rows_all = part * cells

    def kernel(order_ref, up_ref, down_ref, feat, wr, tap, we, gn, pool_ref, red_out, conv_out, act_out, norm_out, std_out, *rest):
        pooled_out, (red, halo, exp, sums) = rest[:n], rest[n:]
        k = pl.program_id(0)
        for side, ref in enumerate((up_ref, down_ref)):
            halo[side] = dot(ref[...].reshape(part * wide, ch), wr[...]).reshape(part, wide, ch)
        red[...] = dot(feat[...].reshape(rows_all, ch), wr[...]).reshape(part, cells, ch)
        red_out[...] = red[...].astype(BF)
        first, last = edge_masks(wide, wide, 1)
        for u in range(part):

            def conv(lanes):
                w = [tap[pl.ds(i, 1), lanes] for i in range(9)]
                rows = [halo[0, u, :, lanes]]
                rows += [red[u, pl.ds(i * wide, wide), lanes] for i in range(high)]
                rows += [halo[1, u, :, lanes]]
                rows = [silu(r).astype(BF).astype(F32) for r in rows]
                out = []
                for i in range(high):
                    t = [sum(rows[i + a] * w[3 * a + b] for a in range(3)) for b in range(3)]
                    out.append(t[1] + columns_moved(t[0], 1, first, last) + columns_moved(t[2], -1, first, last))
                conv_out[u, :, lanes] = jnp.concatenate(out, 0).astype(BF)
                act_out[u, :, lanes] = jnp.concatenate([silu(c) for c in out], 0).astype(BF)

            chunks(ch // LANES, conv)

        exp[...] = dot(act_out[...].reshape(rows_all, ch), we[...])

        def norm(p, carry):
            u, i = p // (high // 2), p % (high // 2)
            tiles = wide // 8
            f = [feat[u, 2 * i + half].astype(F32) for half in range(2)]
            nrms, blends = [], []
            for t in range(2 * tiles):
                e = exp[pl.ds(p * 2 * wide + 8 * t, 8), :]
                mean = jnp.mean(e, -1, keepdims=True)
                square = jnp.mean(e * e, -1, keepdims=True)
                std = lax.rsqrt(square - mean * mean + EPS)
                nrm = (e - mean) * std
                std_out[u, pl.ds(i * 2 * wide + 8 * t, 8), :] = std
                nrms.append(nrm)
                at = t % tiles
                blends.append(f[t // tiles][8 * at : 8 * at + 8] + silu(nrm * gn[...]))
                if t % 2 == 1:
                    both = jnp.concatenate(nrms[-2:], 0).astype(BF)
                    norm_out[u, pl.ds(i * 2 * wide + 8 * (t - 1), 16), :] = both
            for t in range(tiles):
                sums[pl.ds(p * wide + 8 * t, 8), :] = blends[t] + blends[tiles + t]
            return carry

        for p in range(part * high // 2):
            norm(p, 0)
        s = sums[...]
        hi = s.astype(BF)
        lo = (s - hi.astype(F32)).astype(BF)
        pooled = (dot(pool_ref[...], hi) + dot(pool_ref[...], lo)).astype(BF)
        for i in range(n):

            @pl.when(k == i)
            def _():
                pooled_out[i][...] = pooled

    def by_order(rest):
        return lambda k, order: (order[k],) + (0,) * rest

    pooled_rows = pool.shape[0]
    block = (part, cells, ch)
    return call(
        kernel,
        grid=(n,),
        prefetch=1,
        ins=[
            (above, (part, wide, ch), by_order(2)),
            (below, (part, wide, ch), by_order(2)),
            (features, (part, high, wide, ch), by_order(3)),
            (pre_reduce, None, None),
            (taps, None, None),
            (pre_expand, None, None),
            (gain, None, None),
            (pool, None, None),
        ],
        outs=[(shape((slots, cells, ch), BF), block, by_order(2))] * 4
        + [(shape((slots, cells, 1), F32), (part, cells, 1), by_order(2))]
        + [(shape((pooled_rows, ch), BF), None, None)] * n,
        scratch=[
            pltpu.VMEM((part, cells, ch), F32),
            pltpu.VMEM((2, part, wide, ch), F32),
            pltpu.VMEM((rows_all, ch), F32),
            pltpu.VMEM((rows_all // 2, ch), F32),
        ],
        name="pre_forward",
    )(order)


def gain_row(w, n, share):
    at = 2 * share
    parts = [w[c, at : at + 16, :].astype(F32)[:1] for c in range(n)]
    return jnp.concatenate([p[:, :share] + p[:, share : 2 * share] for p in parts], 1)


def post_forward(source, moved, weights, taps, pool):
    n, (rows, ch) = len(moved), moved[0].shape
    total = n * rows
    depth = total // (pool * pool)
    share = ch // n

    def kernel(src, *refs):
        got, refs = refs[:n], refs[n:]
        w, tap, flat_out, red_out, act_out, conv_out, cact_out, norm_out, std_out, low_out, wide_ref, red, exp = refs
        for k in range(n):
            at = pl.multiple_of(src[k] * rows, 8)
            wide_ref[pl.ds(at, rows), :] = got[k][...].astype(F32)
        gain = gain_row(w, n, share)
        flat_out[...] = wide_ref[...].astype(BF)
        total_red = 0.0
        for c in range(n):
            total_red = total_red + dot(flat_out[:, c * share : (c + 1) * share], w[c, :share])
        red[...] = total_red
        first, last = edge_masks(total, pool, depth)
        step = pool * depth

        def conv(lanes):
            v = red[:, lanes]
            red_out[:, lanes] = v.astype(BF)
            x = silu(v).astype(BF)
            act_out[:, lanes] = x
            x = x.astype(F32)
            moves = [columns_moved(x, depth, first, last), x, columns_moved(x, -depth, first, last)]
            t = [sum(moves[b] * tap[pl.ds(3 * a + b, 1), lanes] for b in range(3)) for a in range(3)]
            none = jnp.zeros((step, LANES), F32)
            c = t[1] + jnp.concatenate([none, t[0][:-step]], 0) + jnp.concatenate([t[2][step:], none], 0)
            conv_out[:, lanes] = c.astype(BF)
            cact_out[:, lanes] = silu(c).astype(BF)

        chunks(ch // LANES, conv)
        for c in range(n):
            e = 0.0
            for q in range(n):
                cut = slice(q * share, (q + 1) * share)
                e = e + dot(cact_out[:, cut], w[c, share : 2 * share, cut])
            exp[:, c * share : (c + 1) * share] = e

        def norm(i, carry):
            for t in range(3):
                at = pl.ds(i * 48 + 16 * t, 16)
                e = exp[at, :]
                mean = jnp.mean(e, -1, keepdims=True)
                square = jnp.mean(e * e, -1, keepdims=True)
                std = lax.rsqrt(square - mean * mean + EPS)
                nrm = (e - mean) * std
                norm_out[at, :] = nrm.astype(BF)
                std_out[at, :] = std
                low_out[at, :] = (wide_ref[at, :] + silu(nrm * gain)).astype(BF)
            return carry

        for i in range(total // 48):
            norm(i, 0)

    narrow = shape((total, ch), BF)
    return call(
        kernel,
        grid=(1,),
        prefetch=1,
        ins=[(a, None, None) for a in (*moved, weights, taps)],
        outs=[(s, None, None) for s in (narrow, narrow, narrow, narrow, narrow, narrow, shape((total, 1), F32), narrow)],
        scratch=[pltpu.VMEM((total, ch), F32)] * 3,
        name="post_forward",
    )(source)


def readout_backward(source, low, readout, cots):
    total, ch = low.shape
    n, out_share = len(cots), cots[0].shape[1]

    def kernel(src, low_ref, ro, *rest):
        cot, grad = rest[:n], rest[n]
        k = pl.program_id(0)
        logits = dot(low_ref[...], ro[...])
        slope = gelu_parts(logits)[1]
        for i in range(n):

            @pl.when(k == i)
            def _():
                piece = (cot[i][...].astype(F32) * slope).astype(BF)
                term = dot(piece, ro[...], NT)
                grad[...] = term if i == 0 else grad[...] + term

    return call(
        kernel,
        grid=(n,),
        prefetch=1,
        ins=[(low, None, None), (readout, (ch, out_share), lambda k, s: (0, s[k]))] + [(c, None, None) for c in cots],
        outs=[(shape((total, ch), F32), None, None)],
        name="readout_backward",
    )(source)[0]


def post_backward(source, refined_grad, weights, taps, act, red, conv, nrm, std, pool):
    total, ch = act.shape
    n = weights.shape[0]
    share = ch // n
    rows = total // n
    depth = total // (pool * pool)

    def kernel(src, rg, w, tap, act_ref, red_ref, conv_ref, norm_ref, std_ref, exp_out, redg_out, taps_out, gain_out, *rest):
        back_out, (grad, cgrad) = rest[:n], rest[n:]
        gain = gain_row(w, n, share)

        def norm(i, total_gain):
            for t in range(3):
                at = pl.ds(i * 48 + 16 * t, 16)
                nm = norm_ref[at, :].astype(F32)
                ng = rg[at, :] * silu_slope(nm * gain)
                sc = ng * gain
                one = jnp.mean(sc, -1, keepdims=True)
                two = jnp.mean(sc * nm, -1, keepdims=True)
                exp_out[at, :] = (std_ref[at, :] * (sc - one - nm * two)).astype(BF)
                g = ng * nm
                total_gain = total_gain + g[:8] + g[8:]
            return total_gain

        gains = jnp.zeros((8, ch), F32)
        for i in range(total // 48):
            gains = norm(i, gains)
        gain_out[...] = gains
        for q in range(n):
            cut = slice(q * share, (q + 1) * share)
            cg = 0.0
            for c in range(n):
                cg = cg + dot(exp_out[:, c * share : (c + 1) * share], w[c, share : 2 * share, cut], NT)
            cgrad[:, cut] = cg
        first, last = edge_masks(total, pool, depth)
        step = pool * depth

        def back(lanes):
            g = (cgrad[:, lanes] * silu_slope(conv_ref[:, lanes].astype(F32))).astype(BF).astype(F32)
            x = act_ref[:, lanes].astype(F32)
            moves = [columns_moved(g, -depth, first, last), g, columns_moved(g, depth, first, last)]
            none = jnp.zeros((step, LANES), F32)
            xs = [
                jnp.concatenate([none, x[:-step]], 0),
                x,
                jnp.concatenate([x[step:], none], 0),
            ]
            for a in range(3):
                for b in range(3):
                    prod = xs[a] * moves[b]
                    taps_out[3 * a + b, :, lanes] = jnp.sum(prod.reshape(total // 8, 8, LANES), 0)
            t = [sum(moves[b] * tap[pl.ds(3 * a + b, 1), lanes] for b in range(3)) for a in range(3)]
            d = t[1] + jnp.concatenate([t[0][step:], none], 0) + jnp.concatenate([none, t[2][:-step]], 0)
            redg_out[:, lanes] = (d * silu_slope(red_ref[:, lanes].astype(F32))).astype(BF)

        chunks(ch // LANES, back)
        for c in range(n):
            cut = slice(c * share, (c + 1) * share)
            grad[:, cut] = rg[:, cut] + dot(redg_out[...], w[c, :share], NT)
        for r in range(n):
            at = pl.ds(pl.multiple_of(src[r] * rows, 8), rows)
            back_out[r][...] = grad[at, :].astype(BF)

    return call(
        kernel,
        grid=(1,),
        prefetch=1,
        ins=[(a, None, None) for a in (refined_grad, weights, taps, act, red, conv, nrm, std)],
        outs=[
            (s, None, None)
            for s in (
                shape((total, ch), BF),
                shape((total, ch), BF),
                shape((9, 8, ch), F32),
                shape((8, ch), F32),
                *[shape((rows, ch), BF)] * n,
            )
        ],
        scratch=[pltpu.VMEM((total, ch), F32), pltpu.VMEM((total, ch), F32)],
        name="post_backward",
    )(source)


def cotangent_by_image(cotangent, select, pairs):
    rows, width = cotangent.shape
    size = select.shape[0]
    each = size // pairs
    per = 3

    def kernel(x, sel, *outs):
        for q in range(per):
            y = dot(sel[...], x[pl.ds(q * size, size), :]).astype(BF)
            for s in range(pairs):
                outs[s][pl.ds(q * each, each), :] = y[s * each : (s + 1) * each]

    return call(
        kernel,
        grid=(rows // (per * size),),
        ins=[(cotangent, (per * size, width), lambda i: (i, 0)), (select, None, None)],
        outs=[(shape((rows // pairs, width), BF), (per * each, width), lambda i: (i, 0))] * pairs,
        name="cotangent_by_image",
    )()


def token_block(chan, source, pair_of, low, place, readout, cotangent):
    pairs, (rows, ch) = len(low), low[0].shape
    width = cotangent[0].shape[1]
    size = place.shape[0]
    each = size // pairs
    per = 3
    block = per * each

    def kernel(chan_ref, src, pair, *refs):
        lows, cots, (place_ref, ro, tok_out, piece_out, cot) = refs[:pairs], refs[pairs : 2 * pairs], refs[2 * pairs :]
        for k in range(pairs):
            cot[pair[k]] = cots[k][...]
        logits = dot(jnp.concatenate([v[...] for v in lows], 0), ro[...])
        value, slope = gelu_parts(logits)
        value = value.astype(BF)
        for k in range(pairs):
            piece_out[k] = (cot[src[k]].astype(F32) * slope[k * block : (k + 1) * block]).astype(BF)
        for q in range(per):
            x = jnp.concatenate([value[k * block + q * each : k * block + (q + 1) * each] for k in range(pairs)], 0)
            tok_out[pl.ds(q * size, size), :] = dot(place_ref[...], x).astype(BF)

    rows_at = lambda i, c, s, p: (i, 0)
    return call(
        kernel,
        grid=(rows // block,),
        prefetch=3,
        ins=[
            *[(v, (block, ch), rows_at) for v in low],
            *[(v, (block, width), rows_at) for v in cotangent],
            (place, None, None),
            (readout, (ch, width), lambda i, c, s, p: (0, c[0])),
        ],
        outs=[
            (shape((pairs * rows, width), BF), (pairs * block, width), rows_at),
            (shape((pairs, rows, width), BF), (pairs, block, width), lambda i, c, s, p: (0, i, 0)),
        ],
        scratch=[pltpu.VMEM((pairs, block, width), BF)],
        name="token_block",
    )(chan, source, pair_of)


def pre_backward(order, returned, spread_up, nrm, std, gain, conv, pre_expand):
    slots, cells, ch = nrm.shape
    n = order.shape[0]
    part = slots // n
    wide = 24
    rows = part * cells

    def kernel(order_ref, *refs):
        ret, refs = refs[:n], refs[n:]
        up, norm_ref, std_ref, gn, conv_ref, we, exp_out, conv_grad_out, top_out, bottom_out, gain_out, grad, cgrad = refs
        k = pl.program_id(0)
        for i in range(n):

            @pl.when(k == i)
            def _():
                grad[...] = dot(up[...], ret[i][...])

        def norm(i, total_gain):
            u, j = i // (cells // 48), i % (cells // 48)
            for t in range(3):
                at = pl.ds(j * 48 + 16 * t, 16)
                nm = norm_ref[u, at, :].astype(F32)
                ng = grad[pl.ds(i * 48 + 16 * t, 16), :] * silu_slope(nm * gn[...])
                sc = ng * gn[...]
                one = jnp.mean(sc, -1, keepdims=True)
                two = jnp.mean(sc * nm, -1, keepdims=True)
                exp_out[u, at, :] = (std_ref[u, at, :] * (sc - one - nm * two)).astype(BF)
                g = ng * nm
                total_gain = total_gain + g[:8] + g[8:]
            return total_gain

        gains = jnp.zeros((8, ch), F32)
        for i in range(rows // 48):
            gains = norm(i, gains)

        @pl.when(k == 0)
        def _():
            gain_out[...] = gains

        @pl.when(k > 0)
        def _():
            gain_out[...] += gains

        cgrad[...] = dot(exp_out[...].reshape(rows, ch), we[...], NT)
        for u in range(part):

            def slope(lanes):
                g = cgrad[pl.ds(u * cells, cells), lanes] * silu_slope(conv_ref[u, :, lanes].astype(F32))
                conv_grad_out[u, :, lanes] = g.astype(BF)
                top_out[u, :, lanes] = g[:wide].astype(BF)
                bottom_out[u, :, lanes] = g[cells - wide :].astype(BF)

            chunks(ch // LANES, slope)

    by_order = lambda k, order: (order[k], 0, 0)
    whole = (part, cells, ch)
    edge = (part, wide, ch)
    return call(
        kernel,
        grid=(n,),
        prefetch=1,
        ins=[
            *[(r, None, None) for r in returned],
            (spread_up, None, None),
            (nrm, whole, by_order),
            (std, (part, cells, 1), by_order),
            (gain, None, None),
            (conv, whole, by_order),
            (pre_expand, None, None),
        ],
        outs=[
            (shape((slots, cells, ch), BF), whole, by_order),
            (shape((slots, cells, ch), BF), whole, by_order),
            (shape((slots, wide, ch), BF), edge, by_order),
            (shape((slots, wide, ch), BF), edge, by_order),
            (shape((8, ch), F32), None, None),
        ],
        scratch=[pltpu.VMEM((rows, ch), F32), pltpu.VMEM((rows, ch), F32)],
        name="pre_backward",
    )(order)


def pre_conv_backward(conv_grad, above, below, reduced, taps):
    slots, cells, ch = reduced.shape
    wide = above.shape[1]
    high = cells // wide

    def kernel(cg, up, down, red, tap, redg_out, taps_out):
        step = pl.program_id(0)
        first, last = edge_masks(wide, wide, 1)

        @pl.when(step == 0)
        def _():
            taps_out[...] = jnp.zeros_like(taps_out)

        def back(lanes):
            w = [tap[pl.ds(i, 1), lanes] for i in range(9)]
            mid = cg[0, :, lanes].astype(F32)
            rows = [up[0, :, lanes].astype(F32)]
            rows += [mid[i * wide : (i + 1) * wide] for i in range(high)]
            rows += [down[0, :, lanes].astype(F32)]
            whole = red[0, :, lanes].astype(F32)
            v = [whole[i * wide : (i + 1) * wide] for i in range(high)]
            s = [sigmoid(t) for t in v]
            x = [(a * b).astype(BF).astype(F32) for a, b in zip(v, s)]
            d = [0.0] * high
            sums = [0.0] * 9
            for p in range(high + 2):
                g = rows[p]
                moves = [columns_moved(g, -1, first, last), g, columns_moved(g, 1, first, last)]
                for a in range(3):
                    i = p - 1 + a - 1
                    if 0 <= i < high:
                        for b in range(3):
                            d[i] = d[i] + moves[b] * w[3 * a + b]
                            prod = x[i] * moves[b]
                            sums[3 * a + b] = sums[3 * a + b] + (prod[:8] + prod[8:16] + prod[16:])
            out = [d[i] * (s[i] * (1.0 + v[i] * (1.0 - s[i]))) for i in range(high)]
            redg_out[0, :, lanes] = jnp.concatenate(out, 0).astype(BF)
            for i in range(9):
                taps_out[i, :, lanes] += sums[i]

        chunks(ch // LANES, back)

    image = lambda i: (i, 0, 0)
    return call(
        kernel,
        grid=(slots,),
        ins=[
            (conv_grad, (1, cells, ch), image),
            (above, (1, wide, ch), image),
            (below, (1, wide, ch), image),
            (reduced, (1, cells, ch), image),
            (taps, None, None),
        ],
        outs=[
            (shape((slots, cells, ch), BF), (1, cells, ch), image),
            (shape((9, 8, ch), F32), None, None),
        ],
        name="pre_conv_backward",
    )()


def feature_backward(order, reduced_grad, pre_reduce, returned, spread_up):
    slots, cells, ch = reduced_grad.shape
    n = order.shape[0]
    part = slots // n

    def kernel(order_ref, rg, wr, up, *refs):
        ret, out = refs[:n], refs[n]
        k = pl.program_id(0)
        for i in range(n):

            @pl.when(k == i)
            def _():
                out[...] = dot(up[...], ret[i][...]).reshape(part, cells, ch)

        out[...] += dot(rg[...].reshape(part * cells, ch), wr[...], NT).reshape(part, cells, ch)

    by_order = lambda k, order: (order[k], 0, 0)
    whole = (part, cells, ch)
    return call(
        kernel,
        grid=(n,),
        prefetch=1,
        ins=[
            (reduced_grad, whole, by_order),
            (pre_reduce, None, None),
            (spread_up, None, None),
            *[(r, None, None) for r in returned],
        ],
        outs=[(shape((slots, cells, ch), F32), whole, by_order)],
        name="feature_backward",
    )(order)[0]


def post_weight_grads(flat, reduced_grad, act, expanded_grad, n):
    total, ch = flat.shape
    share = ch // n
    rows = share // 8

    def kernel(x, g, a, e, out):
        for c in range(n):
            cut = slice(c * share, (c + 1) * share)
            v = dot(x[:, cut], g[...], TN).astype(BF)
            for d in range(8):
                out[d, c, :, :ch] = v[d * rows : (d + 1) * rows]
            for q in range(n):
                v = dot(a[:, q * share : (q + 1) * share], e[:, cut], TN).astype(BF)
                for d in range(8):
                    out[d, c, :, ch + q * share : ch + (q + 1) * share] = v[d * rows : (d + 1) * rows]

    return call(
        kernel,
        grid=(1,),
        ins=[(v, None, None) for v in (flat, reduced_grad, act, expanded_grad)],
        outs=[(shape((8, n, rows, 3 * ch), BF), (8, n, rows, 2 * ch), lambda i: (0, 0, 0, 0))],
        name="post_weight_grads",
    )()[0]


def readout_weight_grad(low, piece, load):
    pairs, total, width = piece.shape
    parts, n, rows, _ = load.shape
    share = low[0].shape[1] // n

    def kernel(*refs):
        x, (g, old, out) = refs[:pairs], refs[pairs:]
        x = jnp.concatenate([v[...] for v in x], 0)
        v = dot(x, g[...].reshape(pairs * total, width), TN).astype(BF)
        for d in range(parts):
            out[d, 0] = v[d * rows : (d + 1) * rows]

    return call(
        kernel,
        grid=(n,),
        ins=[(v, (total, share), lambda c: (0, c)) for v in low] + [(piece, None, None)],
        outs=[(shape(load.shape, BF), (parts, 1, rows, width), lambda c: (0, c, 0, 2))],
        aliased=(load,),
        name="readout_weight_grad",
    )()[0]


def cross(n, k):
    return [(a * n + b, ((b + k) % n) * n + a) for a in range(n) for b in range(n)]


def turn(n, k):
    return [(i, (i + k) % n) for i in range(n)]


def other_core(values):
    return lax.ppermute(values, "core", [(0, 1), (1, 0)])


def small_rows(*grads):
    ch = grads[0].shape[-1]
    counts = [g.shape[0] if g.ndim == 3 else 1 for g in grads]
    per = ch // LANES

    def kernel(*refs):
        out = refs[-1]
        at = 0
        for ref, count in zip(refs, counts):
            for i in range(count):
                v = jnp.sum(ref[i] if len(ref.shape) == 3 else ref[...], 0, keepdims=True)
                for q in range(per):
                    out[pl.ds(at, 1), :] = v[:, q * LANES : (q + 1) * LANES]
                    at += 1

    return call(
        kernel,
        grid=(1,),
        ins=[(g, None, None) for g in grads],
        outs=[(shape((sum(counts) * per, LANES), F32), None, None)],
        name="small_rows",
    )()[0]


def join_halves(core, mine, theirs, small, their_small, parts):
    rows, ch = mine[0].shape
    half = rows // 2
    width = len(mine) * ch + LANES
    count = small.shape[0]
    m = len(mine)
    steps = 2
    block = half // steps

    def kernel(core_ref, *refs):
        own, got = refs[:m], refs[m : 2 * m]
        sm, got_sm, out = refs[2 * m :]
        for i in range(m):
            out[:, i * ch : (i + 1) * ch] = (own[i][...].astype(F32) + got[i][...].astype(F32)).astype(BF)
        first = ((core_ref[0] == 0) & (pl.program_id(0) == 0)).astype(F32)
        total = (sm[...] + got_sm[...]) * first
        pad = jnp.zeros((block - count, LANES), F32)
        out[:, m * ch :] = jnp.concatenate([total, pad], 0).astype(BF)

    return call(
        kernel,
        grid=(steps,),
        prefetch=1,
        ins=[(v, (block, ch), lambda i, c: (c[0] * steps + i, 0)) for v in mine]
        + [(v, (block, ch), lambda i, c: (i, 0)) for v in theirs]
        + [(v, None, None) for v in (small, their_small)],
        outs=[(shape((half, width), BF), (block, width), lambda i, c: (i, 0))],
        name="join_halves",
    )(core)[0].reshape(parts, half // parts, width)


def sum_and_copy(blocks):
    parts, rows, width = blocks.shape

    def kernel(x, out):
        def cut(lanes):
            total = jnp.sum(x[:, :, lanes].astype(F32), 0).astype(BF)
            out[:, :, lanes] = jnp.broadcast_to(total[None], (parts, rows, LANES))

        chunks(width // LANES, cut)

    return call(
        kernel,
        grid=(1,),
        ins=[(blocks, None, None)],
        outs=[(shape(blocks.shape, BF), None, None)],
        name="sum_and_copy",
    )()[0]


def sum_parts(blocks, n):
    parts, rows, width = blocks.shape
    ch = width // 3

    def kernel(x, out):
        for lanes in range(0, width, ch):
            for at in range(lanes, lanes + ch, 2 * LANES):
                cut = slice(at, at + 2 * LANES)
                by_chan = [sum(x[p, :, cut].astype(F32) for p in range(c, parts, n)) for c in range(n)]
                if lanes < 2 * ch:
                    out[:, cut] = sum(by_chan).astype(BF)
                else:
                    for c in range(n):
                        out[:, at + c * ch : at + c * ch + 2 * LANES] = by_chan[c].astype(BF)

    return call(
        kernel,
        grid=(1,),
        ins=[(blocks, None, None)],
        outs=[(shape((rows, 2 * ch + n * ch), BF), None, None)],
        name="sum_parts",
    )()[0]


def finish_pre(place, half_rows, ch, earlier=()):
    half, width = half_rows.shape
    m = (width - LANES) // ch
    steps = 4
    block = half // steps

    def kernel(place_ref, x, *outs):
        outs = outs[len(earlier) :]
        for i in range(m):
            outs[i][...] = x[:, i * ch : (i + 1) * ch].astype(F32)
        outs[m][...] = x[:, m * ch :].astype(F32)

    return call(
        kernel,
        grid=(steps,),
        prefetch=1,
        ins=[(half_rows, (block, width), lambda i, c: (i, 0))],
        outs=[(shape((2 * half, ch), F32), (block, ch), lambda i, c: (c[0] * steps + i, 0)) for _ in range(m)]
        + [(shape((half, LANES), F32), (block, LANES), lambda i, c: (i, 0))],
        aliased=earlier,
        name="finish_pre",
    )(place)


def finish_post(place, gathered, n, earlier=()):
    groups, per, width = gathered.shape
    share = 2 * groups * per
    ch = width // (n + 2)

    def kernel(place_ref, x, *outs):
        reduce_out, expand_out, read_out = outs[len(earlier) :]
        reduce_out[...] = x[0, :, :ch].astype(F32)
        for q in range(n):
            expand_out[q] = x[0, :, ch + q * share : ch + (q + 1) * share].astype(F32)
        read_out[...] = x[0, :, 2 * ch :].astype(F32)

    at = lambda i, c: (2 * i + c[0], 0)
    return call(
        kernel,
        grid=(groups,),
        prefetch=1,
        ins=[(gathered, (1, per, width), lambda i, c: (i, 0, 0))],
        outs=[
            (shape((share, ch), F32), (per, ch), at),
            (shape((n, share, share), F32), (n, per, share), lambda i, c: (0, 2 * i + c[0], 0)),
            (shape((share, n * ch), F32), (per, n * ch), at),
        ],
        aliased=earlier,
        name="finish_post",
    )(place)


def after(values, *earlier):
    return lax.optimization_barrier((values, *earlier))[0]


def pool_matrix(part, high, wide):
    half = wide // 2
    m = np.zeros((high // 2 * half * part, part * (high // 2) * wide), np.float32)
    for u in range(part):
        for i in range(high // 2):
            for j in range(wide):
                m[(i * half + j // 2) * part + u, (u * (high // 2) + i) * wide + j] = 0.25
    return m


def spread_matrix(part, high, wide):
    half = wide // 2
    m = np.zeros((part * high * wide, high // 2 * half * part), np.float32)
    for u in range(part):
        for i in range(high):
            for j in range(wide):
                m[(u * high + i) * wide + j, ((i // 2) * half + j // 2) * part + u] = 0.25
    return m


def body(features, counts, pre_reduce, pre_conv, pre_expand, pre_gain, post_reduce, post_conv, post_expand, post_gain, readout, cotangent):
    n = lax.axis_size("chan")
    row = lax.axis_index("rows").astype(jnp.int32)
    chan = lax.axis_index("chan").astype(jnp.int32)
    core = lax.axis_index("core").astype(jnp.int32)
    ch = pre_reduce.shape[0]
    slots, high, wide = features.shape[0], features.shape[1], features.shape[2]
    part = slots // n
    cells = high * wide
    pool = wide // 2
    share = ch // n
    out_share = cotangent.shape[3]
    steps = jnp.arange(n, dtype=jnp.int32)
    order = (row + steps) % n
    source = (row - steps) % n
    pair_of = (chan + steps) % n
    rank = jnp.full((1,), chan, jnp.int32)
    core_at = jnp.full((1,), core, jnp.int32)
    pre_taps = pre_conv.astype(F32).reshape(9, ch)
    post_taps = post_conv.astype(F32).reshape(9, ch)
    pre_gain_row = pre_gain.reshape(1, ch)
    pool_m = jnp.asarray(pool_matrix(part, high, wide), BF)
    up_m = jnp.asarray(spread_matrix(part, high, wide), BF)

    ends = n - 1
    down_pairs = [(i, i + 1) for i in range(ends)]
    up_pairs = [(i + 1, i) for i in range(ends)]
    above = lax.ppermute(features[:, -1], "rows", down_pairs)
    below = lax.ppermute(features[:, 0], "rows", up_pairs)
    gain_hi = post_gain.astype(BF)
    gain_lo = (post_gain - gain_hi.astype(F32)).astype(BF)
    gain_row = jnp.concatenate([gain_hi, gain_lo, jnp.zeros((ch - 2 * share,), BF)])[None]
    square = post_expand.reshape(n, share, share)
    shards = jnp.concatenate(
        [post_reduce, jnp.concatenate([square[q] for q in range(n)], axis=1), jnp.pad(gain_row, ((0, 63), (0, 0)))], axis=0
    )
    shard = lax.dynamic_index_in_dim(shards.reshape(2, -1, ch), core, 0, keepdims=False)
    full = lax.all_gather(shard, ("chan", "core"), axis=0, tiled=True)
    full = full.reshape(n, 2 * share + 64, ch)
    flat_features = features.reshape(slots * cells, ch)
    live = (jnp.arange(SLOT)[None, :] < counts[:, None]).astype(F32).reshape(slots)
    size, each = 16 * slots, 16 * part
    at = lax.broadcasted_iota(jnp.int32, (size, size), 0)
    column = lax.broadcasted_iota(jnp.int32, (size, size), 1)
    wanted = (at % each) // part * slots + part * ((chan + at // each) % n) + at % part
    select = jnp.where(column == wanted, jnp.tile(live, 16)[None, :], 0.0).astype(BF)
    wanted = (column % each) // part * slots + part * ((row - column // each) % n) + column % part
    place = jnp.where(at == wanted, 1.0, 0.0).astype(BF)
    cot_rows = cotangent.transpose(1, 2, 0, 3).reshape(-1, out_share)
    sends = cotangent_by_image(cot_rows, select, n)
    away = after(sends, above, below)
    cots = [lax.ppermute(away[k], ("rows", "chan"), cross(n, k)) for k in range(n)]

    reduced, convolved, convolved_act, normal_pre, pre_std, *pooled = pre_forward(
        order, above, below, features, pre_reduce, pre_taps, pre_expand, pre_gain_row, pool_m
    )

    pooled = after(pooled, cots)
    moved = [pooled[0]] + [lax.ppermute(pooled[k], "rows", turn(n, k)) for k in range(1, n)]
    flat, post_reduced, post_act, post_convolved, post_cact, post_normal, post_std, low = post_forward(
        source, moved, full, post_taps, pool
    )
    lows = [low] + [lax.ppermute(low, "chan", turn(n, k)) for k in range(1, n)]
    refined_grad = readout_backward(source, low, readout, cots)
    post_expanded_grad, post_reduced_grad, post_taps_grad, post_gain_grad, *back = post_backward(
        source, refined_grad, full, post_taps, post_act, post_reduced, post_convolved, post_normal, post_std, pool
    )

    returned = [back[0]] + [lax.ppermute(back[k], "rows", turn(n, -k)) for k in range(1, n)]

    flat = after(flat, lows)
    load = post_weight_grads(flat, post_reduced_grad, post_cact, post_expanded_grad, n)

    stacked = jnp.stack(after(lows, load, returned))
    lows = [lax.dynamic_index_in_dim(stacked, (chan - row - k) % n, 0, keepdims=False) for k in range(n)]
    lows = [lows[0]] + [lax.ppermute(lows[k], "rows", turn(n, k)) for k in range(1, n)]

    expanded_grad, convolved_grad, top, bottom, pre_gain_grad = pre_backward(
        order, returned, up_m, normal_pre, pre_std, pre_gain_row, convolved, pre_expand
    )
    top, bottom, lows[1], lows[3] = lax.optimization_barrier((top, bottom, lows[1], lows[3]))
    grad_above = lax.ppermute(bottom, "rows", down_pairs)
    grad_below = lax.ppermute(top, "rows", up_pairs)
    act_rows = after(convolved_act, bottom).reshape(-1, ch)
    pre_expand_grad = dot(act_rows, expanded_grad.reshape(-1, ch), TN).astype(BF)

    lows = after(lows, pre_expand_grad)
    tokens, piece = token_block(rank, source, pair_of, lows, place, readout, sends)
    load = readout_weight_grad(lows, after(piece, grad_above, grad_below), load)
    tokens = tokens.reshape(pool, pool, slots, out_share).transpose(2, 0, 1, 3)
    eight = share // 32
    convolved_grad = after(convolved_grad, load)
    rest = lax.psum_scatter(load, ("x", "core"), scatter_dimension=0, tiled=False)

    reduced_grad, pre_taps_grad = pre_conv_backward(convolved_grad, grad_above, grad_below, reduced, pre_taps)
    small = small_rows(pre_taps_grad, pre_gain_grad, post_taps_grad, post_gain_grad)
    pre_reduce_grad = dot(after(flat_features, small), reduced_grad.reshape(-1, ch), TN).astype(BF)

    chips = ("x", "rows", "chan")
    mine = [pre_reduce_grad, pre_expand_grad]
    theirs = [other_core(lax.dynamic_index_in_dim(g.reshape(2, ch // 2, ch), 1 - core, 0, keepdims=False)) for g in mine]
    load = join_halves(core_at, mine, theirs, small, other_core(small), 64)
    pieces = lax.all_to_all(load, chips, 0, 0, tiled=False)
    feature_grad = feature_backward(order, after(reduced_grad, load), pre_reduce, returned, up_m).reshape(features.shape)

    rest = after(rest, feature_grad, pieces).reshape(n, 4, eight, 3 * ch).transpose(1, 0, 2, 3).reshape(4 * n, eight, 3 * ch)
    pieces = after(pieces, rest)
    rest = lax.all_to_all(rest, ("rows", "chan"), 0, 0, tiled=False)
    load = sum_and_copy(pieces)
    rest = sum_parts(after(rest, load), n)
    load = after(load, rest)
    rest = lax.all_gather(rest, ("x", "rows"), axis=0, tiled=False).reshape(4, 4 * eight, -1)
    load_all = lax.all_to_all(load, chips, 0, 0, tiled=False).reshape(ch // 2, -1)

    def finish(kernel, values, *sizes):
        theirs = other_core(values)
        own = kernel(core_at, values, *sizes)
        theirs = after(theirs, *own)
        return own, theirs

    own, theirs = finish(finish_pre, load_all, ch)
    pre_reduce_out, pre_expand_out, small_their = finish_pre(1 - core_at, theirs, ch, earlier=tuple(own[:2]))
    small_out = jnp.where(core == 0, own[2], small_their)
    own, theirs = finish(finish_post, after(rest, pre_reduce_out), n)
    post_reduce_out, post_expand_out, readout_out = finish_post(1 - core_at, theirs, n, earlier=tuple(own))
    per = ch // LANES
    cut = [0, 9 * per, 10 * per, 19 * per, 20 * per]
    pre_conv_out, pre_gain_out, post_conv_out, post_gain_out = [small_out[a:b] for a, b in zip(cut, cut[1:])]
    return (
        tokens,
        feature_grad,
        pre_reduce_out,
        pre_conv_out.reshape(3, 3, ch),
        pre_expand_out,
        pre_gain_out.reshape(ch),
        post_reduce_out,
        post_conv_out.reshape(3, 3, ch),
        post_expand_out.reshape(ch, share),
        lax.dynamic_slice_in_dim(post_gain_out.reshape(ch), chan * share, share, 0),
        readout_out,
    )


def solution(mesh):
    grid = Mesh(mesh.devices.reshape(4, 2, 4, 4), ("x", "core", "rows", "chan"))
    images = P(("x", "core", "chan"), "rows", None, None)
    grids = P(("x", "core", "rows"), None, None, "chan")
    return jax.shard_map(
        body,
        mesh=grid,
        in_specs=(
            images,
            P(("x", "core", "rows")),
            P(),
            P(),
            P(),
            P(),
            P("chan", None),
            P(),
            P(None, "chan"),
            P("chan"),
            P(),
            grids,
        ),
        out_specs=(grids, images, P(), P(), P(), P(), P("chan", None), P(), P(None, "chan"), P("chan"), P("chan", None)),
        check_vma=False,
    )
```

```python
import functools

import jax
import jax.numpy as jnp
import numpy as np
from jax import lax
from jax.experimental import pallas as pl
from jax.experimental.pallas import tpu as pltpu
from jax.sharding import Mesh, PartitionSpec as P

SLOT = 4
EPS = 1e-06
BF = jnp.bfloat16
F32 = jnp.float32
LANES = 128
VMEM_LIMIT = 20 * 1024 * 1024
NN = ((1,), (0,))
NT = ((1,), (1,))
TN = ((0,), (0,))


def dot(a, b, dims=NN):
    return lax.dot_general(a, b, (dims, ((), ())), preferred_element_type=F32)


def sigmoid(v):
    return 0.5 * jnp.tanh(0.5 * v) + 0.5


def silu(v):
    return v * sigmoid(v)


def silu_slope(v):
    s = sigmoid(v)
    return s * (1.0 + v * (1.0 - s))


def gelu_parts(v):
    c = 0.7978845608028654
    square = v * v
    t = jnp.tanh(v * (c + (c * 0.044715) * square))
    half = 0.5 * (1.0 + t)
    slope = half + 0.5 * v * (1.0 - t * t) * (c + (3.0 * c * 0.044715) * square)
    return v * half, slope


def chunks(count, body, width=LANES):
    for i in range(count):
        body(pl.ds(i * width, width))


def call(kernel, *, grid, ins, outs, scratch=(), prefetch=0, aliased=(), cost=1, name):
    def spec(shape, block, index):
        if block is None:
            block, index = shape, lambda *_: (0,) * len(shape)
        return pl.BlockSpec(block, index)

    arrays = [i[0] for i in ins] + list(aliased)
    in_specs = [spec(a.shape, b, m) for a, b, m in ins] + [pl.BlockSpec(memory_space=pl.ANY)] * len(aliased)
    out_specs = [spec(s.shape, b, m) for s, b, m in outs]

    def run(*scalars):
        return pl.pallas_call(
            kernel,
            grid_spec=pltpu.PrefetchScalarGridSpec(
                num_scalar_prefetch=prefetch,
                grid=grid,
                in_specs=in_specs,
                out_specs=out_specs,
                scratch_shapes=list(scratch),
            ),
            out_shape=[s[0] for s in outs],
            compiler_params=pltpu.CompilerParams(
                dimension_semantics=("arbitrary",) * len(grid), vmem_limit_bytes=VMEM_LIMIT
            ),
            input_output_aliases={prefetch + len(ins) + i: i for i in range(len(aliased))},
            cost_estimate=pl.CostEstimate(flops=cost, bytes_accessed=1, transcendentals=0),
            name=name,
        )(*scalars, *arrays)

    return run


def shape(dims, dtype):
    return jax.ShapeDtypeStruct(dims, dtype)


def far(values, dtype=None):
    if dtype is None:
        return pltpu.with_memory_space_constraint(values, pltpu.HBM)
    return pltpu.HBM(values, dtype)


def columns_moved(t, by, first, last):
    rows = t.shape[0]
    return pltpu.roll(t, by % rows, 0) * (first if by > 0 else last)


def edge_masks(rows, width, depth):
    at = lax.broadcasted_iota(jnp.int32, (rows, LANES), 0) % (width * depth)
    return (at >= depth).astype(F32), (at < (width - 1) * depth).astype(F32)


def pre_forward(order, above, below, features, pre_reduce, taps, pre_expand, gain, pool):
    slots, high, wide, ch = features.shape
    cells = high * wide
    n = order.shape[0]
    part = slots // n
    rows_all = part * cells

    def kernel(order_ref, up_ref, down_ref, feat, wr, tap, we, gn, pool_ref, red_out, conv_out, act_out, norm_out, std_out, *rest):
        pooled_out, (red, halo, exp, sums) = rest[:n], rest[n:]
        k = pl.program_id(0)
        for side, ref in enumerate((up_ref, down_ref)):
            halo[side] = dot(ref[...].reshape(part * wide, ch), wr[...]).reshape(part, wide, ch)
        red[...] = dot(feat[...].reshape(rows_all, ch), wr[...]).reshape(part, cells, ch)
        red_out[...] = red[...].astype(BF)
        first, last = edge_masks(wide, wide, 1)
        for u in range(part):

            def conv(lanes):
                w = [tap[pl.ds(i, 1), lanes] for i in range(9)]
                rows = [halo[0, u, :, lanes]]
                rows += [red[u, pl.ds(i * wide, wide), lanes] for i in range(high)]
                rows += [halo[1, u, :, lanes]]
                rows = [silu(r).astype(BF).astype(F32) for r in rows]
                out = []
                for i in range(high):
                    t = [sum(rows[i + a] * w[3 * a + b] for a in range(3)) for b in range(3)]
                    out.append(t[1] + columns_moved(t[0], 1, first, last) + columns_moved(t[2], -1, first, last))
                conv_out[u, :, lanes] = jnp.concatenate(out, 0).astype(BF)
                act_out[u, :, lanes] = jnp.concatenate([silu(c) for c in out], 0).astype(BF)

            chunks(ch // LANES, conv)

        exp[...] = dot(act_out[...].reshape(rows_all, ch), we[...])

        def norm(p, carry):
            u, i = p // (high // 2), p % (high // 2)
            tiles = wide // 8
            f = [feat[u, 2 * i + half].astype(F32) for half in range(2)]
            nrms, blends = [], []
            for t in range(2 * tiles):
                e = exp[pl.ds(p * 2 * wide + 8 * t, 8), :]
                mean = jnp.mean(e, -1, keepdims=True)
                square = jnp.mean(e * e, -1, keepdims=True)
                std = lax.rsqrt(square - mean * mean + EPS)
                nrm = (e - mean) * std
                std_out[u, pl.ds(i * 2 * wide + 8 * t, 8), :] = std
                nrms.append(nrm)
                at = t % tiles
                blends.append(f[t // tiles][8 * at : 8 * at + 8] + silu(nrm * gn[...]))
                if t % 2 == 1:
                    both = jnp.concatenate(nrms[-2:], 0).astype(BF)
                    norm_out[u, pl.ds(i * 2 * wide + 8 * (t - 1), 16), :] = both
            for t in range(tiles):
                sums[pl.ds(p * wide + 8 * t, 8), :] = blends[t] + blends[tiles + t]
            return carry

        for p in range(part * high // 2):
            norm(p, 0)
        s = sums[...]
        hi = s.astype(BF)
        lo = (s - hi.astype(F32)).astype(BF)
        pooled = (dot(pool_ref[...], hi) + dot(pool_ref[...], lo)).astype(BF)
        for i in range(n):

            @pl.when(k == i)
            def _():
                pooled_out[i][...] = pooled

    def by_order(rest):
        return lambda k, order: (order[k],) + (0,) * rest

    pooled_rows = pool.shape[0]
    block = (part, cells, ch)
    return call(
        kernel,
        grid=(n,),
        prefetch=1,
        ins=[
            (above, (part, wide, ch), by_order(2)),
            (below, (part, wide, ch), by_order(2)),
            (far(features), (part, high, wide, ch), by_order(3)),
            (far(pre_reduce), None, None),
            (taps, None, None),
            (far(pre_expand), None, None),
            (gain, None, None),
            (pool, None, None),
        ],
        outs=[(far((slots, cells, ch), BF), block, by_order(2))] * 4
        + [(far((slots, cells, 1), F32), (part, cells, 1), by_order(2))]
        + [(shape((pooled_rows, ch), BF), None, None)] * n,
        scratch=[
            pltpu.VMEM((part, cells, ch), F32),
            pltpu.VMEM((2, part, wide, ch), F32),
            pltpu.VMEM((rows_all, ch), F32),
            pltpu.VMEM((rows_all // 2, ch), F32),
        ],
        name="pre_forward",
    )(order)


def gain_row(w, n, share):
    at = 2 * share
    parts = [w[c, at : at + 16, :].astype(F32)[:1] for c in range(n)]
    return jnp.concatenate([p[:, :share] + p[:, share : 2 * share] for p in parts], 1)


def post_forward(source, moved, weights, taps, pool):
    n, (rows, ch) = len(moved), moved[0].shape
    total = n * rows
    depth = total // (pool * pool)
    share = ch // n

    def kernel(src, *refs):
        got, refs = refs[:n], refs[n:]
        w, tap, flat_out, red_out, act_out, conv_out, cact_out, norm_out, std_out, low_out, wide_ref, red, exp = refs
        for k in range(n):
            at = pl.multiple_of(src[k] * rows, 8)
            wide_ref[pl.ds(at, rows), :] = got[k][...].astype(F32)
        gain = gain_row(w, n, share)
        flat_out[...] = wide_ref[...].astype(BF)
        total_red = 0.0
        for c in range(n):
            total_red = total_red + dot(flat_out[:, c * share : (c + 1) * share], w[c, :share])
        red[...] = total_red
        first, last = edge_masks(total, pool, depth)
        step = pool * depth

        def conv(lanes):
            v = red[:, lanes]
            red_out[:, lanes] = v.astype(BF)
            x = silu(v).astype(BF)
            act_out[:, lanes] = x
            x = x.astype(F32)
            moves = [columns_moved(x, depth, first, last), x, columns_moved(x, -depth, first, last)]
            t = [sum(moves[b] * tap[pl.ds(3 * a + b, 1), lanes] for b in range(3)) for a in range(3)]
            none = jnp.zeros((step, LANES), F32)
            c = t[1] + jnp.concatenate([none, t[0][:-step]], 0) + jnp.concatenate([t[2][step:], none], 0)
            conv_out[:, lanes] = c.astype(BF)
            cact_out[:, lanes] = silu(c).astype(BF)

        chunks(ch // LANES, conv)
        for c in range(n):
            e = 0.0
            for q in range(n):
                cut = slice(q * share, (q + 1) * share)
                e = e + dot(cact_out[:, cut], w[c, share : 2 * share, cut])
            exp[:, c * share : (c + 1) * share] = e

        def norm(i, carry):
            for t in range(3):
                at = pl.ds(i * 48 + 16 * t, 16)
                e = exp[at, :]
                mean = jnp.mean(e, -1, keepdims=True)
                square = jnp.mean(e * e, -1, keepdims=True)
                std = lax.rsqrt(square - mean * mean + EPS)
                nrm = (e - mean) * std
                norm_out[at, :] = nrm.astype(BF)
                std_out[at, :] = std
                low_out[at, :] = (wide_ref[at, :] + silu(nrm * gain)).astype(BF)
            return carry

        for i in range(total // 48):
            norm(i, 0)

    narrow = shape((total, ch), BF)
    return call(
        kernel,
        grid=(1,),
        prefetch=1,
        ins=[(a, None, None) for a in (*moved, far(weights), taps)],
        outs=[(s, None, None) for s in (narrow, narrow, narrow, narrow, narrow, narrow, shape((total, 1), F32), narrow)],
        scratch=[pltpu.VMEM((total, ch), F32)] * 3,
        name="post_forward",
    )(source)


def readout_backward(source, low, readout, cots):
    total, ch = low.shape
    n, out_share = len(cots), cots[0].shape[1]

    def kernel(src, low_ref, ro, *rest):
        cot, grad = rest[:n], rest[n]
        k = pl.program_id(0)
        logits = dot(low_ref[...], ro[...])
        slope = gelu_parts(logits)[1]
        for i in range(n):

            @pl.when(k == i)
            def _():
                piece = (cot[i][...].astype(F32) * slope).astype(BF)
                term = dot(piece, ro[...], NT)
                grad[...] = term if i == 0 else grad[...] + term

    return call(
        kernel,
        grid=(n,),
        prefetch=1,
        ins=[(low, None, None), (far(readout), (ch, out_share), lambda k, s: (0, s[k]))] + [(c, None, None) for c in cots],
        outs=[(shape((total, ch), F32), None, None)],
        name="readout_backward",
    )(source)[0]


def post_backward(source, refined_grad, weights, taps, act, red, conv, nrm, std, pool):
    total, ch = act.shape
    n = weights.shape[0]
    share = ch // n
    rows = total // n
    depth = total // (pool * pool)

    def kernel(src, rg, w, tap, act_ref, red_ref, conv_ref, norm_ref, std_ref, exp_out, redg_out, taps_out, gain_out, *rest):
        back_out, (grad, cgrad) = rest[:n], rest[n:]
        gain = gain_row(w, n, share)

        def norm(i, total_gain):
            for t in range(3):
                at = pl.ds(i * 48 + 16 * t, 16)
                nm = norm_ref[at, :].astype(F32)
                ng = rg[at, :] * silu_slope(nm * gain)
                sc = ng * gain
                one = jnp.mean(sc, -1, keepdims=True)
                two = jnp.mean(sc * nm, -1, keepdims=True)
                exp_out[at, :] = (std_ref[at, :] * (sc - one - nm * two)).astype(BF)
                g = ng * nm
                total_gain = total_gain + g[:8] + g[8:]
            return total_gain

        gains = jnp.zeros((8, ch), F32)
        for i in range(total // 48):
            gains = norm(i, gains)
        gain_out[...] = gains
        for q in range(n):
            cut = slice(q * share, (q + 1) * share)
            cg = 0.0
            for c in range(n):
                cg = cg + dot(exp_out[:, c * share : (c + 1) * share], w[c, share : 2 * share, cut], NT)
            cgrad[:, cut] = cg
        first, last = edge_masks(total, pool, depth)
        step = pool * depth

        def back(lanes):
            g = (cgrad[:, lanes] * silu_slope(conv_ref[:, lanes].astype(F32))).astype(BF).astype(F32)
            x = act_ref[:, lanes].astype(F32)
            moves = [columns_moved(g, -depth, first, last), g, columns_moved(g, depth, first, last)]
            none = jnp.zeros((step, LANES), F32)
            xs = [
                jnp.concatenate([none, x[:-step]], 0),
                x,
                jnp.concatenate([x[step:], none], 0),
            ]
            for a in range(3):
                for b in range(3):
                    prod = xs[a] * moves[b]
                    taps_out[3 * a + b, :, lanes] = jnp.sum(prod.reshape(total // 8, 8, LANES), 0)
            t = [sum(moves[b] * tap[pl.ds(3 * a + b, 1), lanes] for b in range(3)) for a in range(3)]
            d = t[1] + jnp.concatenate([t[0][step:], none], 0) + jnp.concatenate([none, t[2][:-step]], 0)
            redg_out[:, lanes] = (d * silu_slope(red_ref[:, lanes].astype(F32))).astype(BF)

        chunks(ch // LANES, back)
        for c in range(n):
            cut = slice(c * share, (c + 1) * share)
            grad[:, cut] = rg[:, cut] + dot(redg_out[...], w[c, :share], NT)
        for r in range(n):
            at = pl.ds(pl.multiple_of(src[r] * rows, 8), rows)
            back_out[r][...] = grad[at, :].astype(BF)

    return call(
        kernel,
        grid=(1,),
        prefetch=1,
        ins=[(a, None, None) for a in (refined_grad, far(weights), taps, act, red, conv, nrm, std)],
        outs=[
            (s, None, None)
            for s in (
                shape((total, ch), BF),
                shape((total, ch), BF),
                shape((9, 8, ch), F32),
                shape((8, ch), F32),
                *[shape((rows, ch), BF)] * n,
            )
        ],
        scratch=[pltpu.VMEM((total, ch), F32), pltpu.VMEM((total, ch), F32)],
        name="post_backward",
    )(source)


def cotangent_by_image(cotangent, select, pairs):
    rows, width = cotangent.shape
    size = select.shape[0]
    each = size // pairs
    per = 3

    def kernel(x, sel, *outs):
        for q in range(per):
            y = dot(sel[...], x[pl.ds(q * size, size), :]).astype(BF)
            for s in range(pairs):
                outs[s][pl.ds(q * each, each), :] = y[s * each : (s + 1) * each]

    return call(
        kernel,
        grid=(rows // (per * size),),
        ins=[(far(cotangent), (per * size, width), lambda i: (i, 0)), (select, None, None)],
        outs=[(shape((rows // pairs, width), BF), (per * each, width), lambda i: (i, 0))] * pairs,
        name="cotangent_by_image",
    )()


def token_block(chan, source, pair_of, low, place, readout, cotangent):
    pairs, (rows, ch) = len(low), low[0].shape
    width = cotangent[0].shape[1]
    size = place.shape[0]
    each = size // pairs
    per = 3
    block = per * each

    def kernel(chan_ref, src, pair, *refs):
        lows, cots, (place_ref, ro, tok_out, piece_out, cot) = refs[:pairs], refs[pairs : 2 * pairs], refs[2 * pairs :]
        for k in range(pairs):
            cot[pair[k]] = cots[k][...]
        logits = dot(jnp.concatenate([v[...] for v in lows], 0), ro[...])
        value, slope = gelu_parts(logits)
        value = value.astype(BF)
        for k in range(pairs):
            piece_out[k] = (cot[src[k]].astype(F32) * slope[k * block : (k + 1) * block]).astype(BF)
        for q in range(per):
            x = jnp.concatenate([value[k * block + q * each : k * block + (q + 1) * each] for k in range(pairs)], 0)
            tok_out[pl.ds(q * size, size), :] = dot(place_ref[...], x).astype(BF)

    rows_at = lambda i, c, s, p: (i, 0)
    return call(
        kernel,
        grid=(rows // block,),
        prefetch=3,
        ins=[
            *[(v, (block, ch), rows_at) for v in low],
            *[(v, (block, width), rows_at) for v in cotangent],
            (place, None, None),
            (far(readout), (ch, width), lambda i, c, s, p: (0, c[0])),
        ],
        outs=[
            (shape((pairs * rows, width), BF), (pairs * block, width), rows_at),
            (shape((pairs, rows, width), BF), (pairs, block, width), lambda i, c, s, p: (0, i, 0)),
        ],
        scratch=[pltpu.VMEM((pairs, block, width), BF)],
        name="token_block",
    )(chan, source, pair_of)


def pre_backward(order, returned, spread_up, nrm, std, gain, conv, pre_expand):
    slots, cells, ch = nrm.shape
    n = order.shape[0]
    part = slots // n
    wide = 24
    rows = part * cells

    def kernel(order_ref, *refs):
        ret, refs = refs[:n], refs[n:]
        up, norm_ref, std_ref, gn, conv_ref, we, exp_out, conv_grad_out, top_out, bottom_out, gain_out, grad, cgrad = refs
        k = pl.program_id(0)
        for i in range(n):

            @pl.when(k == i)
            def _():
                grad[...] = dot(up[...], ret[i][...])

        def norm(i, total_gain):
            u, j = i // (cells // 48), i % (cells // 48)
            for t in range(3):
                at = pl.ds(j * 48 + 16 * t, 16)
                nm = norm_ref[u, at, :].astype(F32)
                ng = grad[pl.ds(i * 48 + 16 * t, 16), :] * silu_slope(nm * gn[...])
                sc = ng * gn[...]
                one = jnp.mean(sc, -1, keepdims=True)
                two = jnp.mean(sc * nm, -1, keepdims=True)
                exp_out[u, at, :] = (std_ref[u, at, :] * (sc - one - nm * two)).astype(BF)
                g = ng * nm
                total_gain = total_gain + g[:8] + g[8:]
            return total_gain

        gains = jnp.zeros((8, ch), F32)
        for i in range(rows // 48):
            gains = norm(i, gains)

        @pl.when(k == 0)
        def _():
            gain_out[...] = gains

        @pl.when(k > 0)
        def _():
            gain_out[...] += gains

        cgrad[...] = dot(exp_out[...].reshape(rows, ch), we[...], NT)
        for u in range(part):

            def slope(lanes):
                g = cgrad[pl.ds(u * cells, cells), lanes] * silu_slope(conv_ref[u, :, lanes].astype(F32))
                conv_grad_out[u, :, lanes] = g.astype(BF)
                top_out[u, :, lanes] = g[:wide].astype(BF)
                bottom_out[u, :, lanes] = g[cells - wide :].astype(BF)

            chunks(ch // LANES, slope)

    by_order = lambda k, order: (order[k], 0, 0)
    whole = (part, cells, ch)
    edge = (part, wide, ch)
    return call(
        kernel,
        grid=(n,),
        prefetch=1,
        ins=[
            *[(r, None, None) for r in returned],
            (spread_up, None, None),
            (far(nrm), whole, by_order),
            (far(std), (part, cells, 1), by_order),
            (gain, None, None),
            (far(conv), whole, by_order),
            (far(pre_expand), None, None),
        ],
        outs=[
            (shape((slots, cells, ch), BF), whole, by_order),
            (shape((slots, cells, ch), BF), whole, by_order),
            (shape((slots, wide, ch), BF), edge, by_order),
            (shape((slots, wide, ch), BF), edge, by_order),
            (shape((8, ch), F32), None, None),
        ],
        scratch=[pltpu.VMEM((rows, ch), F32), pltpu.VMEM((rows, ch), F32)],
        name="pre_backward",
    )(order)


def pre_conv_backward(conv_grad, above, below, reduced, taps):
    slots, cells, ch = reduced.shape
    wide = above.shape[1]
    high = cells // wide

    def kernel(cg, up, down, red, tap, redg_out, taps_out):
        step = pl.program_id(0)
        first, last = edge_masks(wide, wide, 1)

        @pl.when(step == 0)
        def _():
            taps_out[...] = jnp.zeros_like(taps_out)

        def back(lanes):
            w = [tap[pl.ds(i, 1), lanes] for i in range(9)]
            mid = cg[0, :, lanes].astype(F32)
            rows = [up[0, :, lanes].astype(F32)]
            rows += [mid[i * wide : (i + 1) * wide] for i in range(high)]
            rows += [down[0, :, lanes].astype(F32)]
            whole = red[0, :, lanes].astype(F32)
            v = [whole[i * wide : (i + 1) * wide] for i in range(high)]
            s = [sigmoid(t) for t in v]
            x = [(a * b).astype(BF).astype(F32) for a, b in zip(v, s)]
            d = [0.0] * high
            sums = [0.0] * 9
            for p in range(high + 2):
                g = rows[p]
                moves = [columns_moved(g, -1, first, last), g, columns_moved(g, 1, first, last)]
                for a in range(3):
                    i = p - 1 + a - 1
                    if 0 <= i < high:
                        for b in range(3):
                            d[i] = d[i] + moves[b] * w[3 * a + b]
                            prod = x[i] * moves[b]
                            sums[3 * a + b] = sums[3 * a + b] + (prod[:8] + prod[8:16] + prod[16:])
            out = [d[i] * (s[i] * (1.0 + v[i] * (1.0 - s[i]))) for i in range(high)]
            redg_out[0, :, lanes] = jnp.concatenate(out, 0).astype(BF)
            for i in range(9):
                taps_out[i, :, lanes] += sums[i]

        chunks(ch // LANES, back)

    image = lambda i: (i, 0, 0)
    return call(
        kernel,
        grid=(slots,),
        ins=[
            (conv_grad, (1, cells, ch), image),
            (above, (1, wide, ch), image),
            (below, (1, wide, ch), image),
            (far(reduced), (1, cells, ch), image),
            (taps, None, None),
        ],
        outs=[
            (shape((slots, cells, ch), BF), (1, cells, ch), image),
            (shape((9, 8, ch), F32), None, None),
        ],
        name="pre_conv_backward",
    )()


def feature_backward(order, reduced_grad, pre_reduce, returned, spread_up):
    slots, cells, ch = reduced_grad.shape
    n = order.shape[0]
    part = slots // n

    def kernel(order_ref, rg, wr, up, *refs):
        ret, out = refs[:n], refs[n]
        k = pl.program_id(0)
        for i in range(n):

            @pl.when(k == i)
            def _():
                out[...] = dot(up[...], ret[i][...]).reshape(part, cells, ch)

        out[...] += dot(rg[...].reshape(part * cells, ch), wr[...], NT).reshape(part, cells, ch)

    by_order = lambda k, order: (order[k], 0, 0)
    whole = (part, cells, ch)
    return call(
        kernel,
        grid=(n,),
        prefetch=1,
        ins=[
            (reduced_grad, whole, by_order),
            (far(pre_reduce), None, None),
            (spread_up, None, None),
            *[(r, None, None) for r in returned],
        ],
        outs=[(shape((slots, cells, ch), F32), whole, by_order)],
        name="feature_backward",
    )(order)[0]


def post_weight_grads(flat, reduced_grad, act, expanded_grad, n):
    total, ch = flat.shape
    share = ch // n
    rows = share // 8

    def kernel(x, g, a, e, out):
        for c in range(n):
            cut = slice(c * share, (c + 1) * share)
            v = dot(x[:, cut], g[...], TN).astype(BF)
            for d in range(8):
                out[d, c, :, :ch] = v[d * rows : (d + 1) * rows]
            for q in range(n):
                v = dot(a[:, q * share : (q + 1) * share], e[:, cut], TN).astype(BF)
                for d in range(8):
                    out[d, c, :, ch + q * share : ch + (q + 1) * share] = v[d * rows : (d + 1) * rows]

    return call(
        kernel,
        grid=(1,),
        ins=[(v, None, None) for v in (flat, reduced_grad, act, expanded_grad)],
        outs=[(far((8, n, rows, 2 * ch), BF), None, None)],
        name="post_weight_grads",
    )()[0]


def readout_weight_grad(low, piece, n):
    pairs, total, width = piece.shape
    ch = low[0].shape[1]
    share = ch // n
    parts = 8
    rows = share // parts

    def kernel(*refs):
        x, (g, out) = refs[:pairs], refs[pairs:]
        x = jnp.concatenate([v[...] for v in x], 0)
        v = dot(x, g[...].reshape(pairs * total, width), TN).astype(BF)
        for d in range(parts):
            out[d, 0] = v[d * rows : (d + 1) * rows]

    return call(
        kernel,
        grid=(n,),
        ins=[(v, (total, share), lambda c: (0, c)) for v in low] + [(piece, None, None)],
        outs=[(far((parts, n, rows, width), BF), (parts, 1, rows, width), lambda c: (0, c, 0, 0))],
        name="readout_weight_grad",
    )()[0]


def cross(n, k):
    return [(a * n + b, ((b + k) % n) * n + a) for a in range(n) for b in range(n)]


def turn(n, k):
    return [(i, (i + k) % n) for i in range(n)]


def other_core(values):
    return lax.ppermute(values, "core", [(0, 1), (1, 0)])


def small_rows(*grads):
    ch = grads[0].shape[-1]
    counts = [g.shape[0] if g.ndim == 3 else 1 for g in grads]
    per = ch // LANES

    def kernel(*refs):
        out = refs[-1]
        at = 0
        for ref, count in zip(refs, counts):
            for i in range(count):
                v = jnp.sum(ref[i] if len(ref.shape) == 3 else ref[...], 0, keepdims=True)
                for q in range(per):
                    out[pl.ds(at, 1), :] = v[:, q * LANES : (q + 1) * LANES]
                    at += 1

    return call(
        kernel,
        grid=(1,),
        ins=[(g, None, None) for g in grads],
        outs=[(shape((sum(counts) * per, LANES), F32), None, None)],
        name="small_rows",
    )()[0]


def join_halves(core, mine, theirs, small, their_small, parts):
    rows, ch = mine[0].shape
    half = rows // 2
    width = len(mine) * ch + LANES
    count = small.shape[0]
    m = len(mine)
    steps = 2
    block = half // steps

    def kernel(core_ref, *refs):
        own, got = refs[:m], refs[m : 2 * m]
        sm, got_sm, out = refs[2 * m :]
        for i in range(m):
            out[:, i * ch : (i + 1) * ch] = (own[i][...].astype(F32) + got[i][...].astype(F32)).astype(BF)
        first = ((core_ref[0] == 0) & (pl.program_id(0) == 0)).astype(F32)
        total = (sm[...] + got_sm[...]) * first
        pad = jnp.zeros((block - count, LANES), F32)
        out[:, m * ch :] = jnp.concatenate([total, pad], 0).astype(BF)

    return call(
        kernel,
        grid=(steps,),
        prefetch=1,
        ins=[(v, (block, ch), lambda i, c: (c[0] * steps + i, 0)) for v in mine]
        + [(v, (block, ch), lambda i, c: (i, 0)) for v in theirs]
        + [(v, None, None) for v in (small, their_small)],
        outs=[(far((half, width), BF), (block, width), lambda i, c: (i, 0))],
        name="join_halves",
    )(core)[0].reshape(parts, half // parts, width)


def sum_and_copy(blocks):
    parts, rows, width = blocks.shape

    def kernel(x, out):
        def cut(lanes):
            total = jnp.sum(x[:, :, lanes].astype(F32), 0).astype(BF)
            out[:, :, lanes] = jnp.broadcast_to(total[None], (parts, rows, LANES))

        chunks(width // LANES, cut)

    return call(
        kernel,
        grid=(1,),
        ins=[(blocks, None, None)],
        outs=[(far(blocks.shape, BF), None, None)],
        name="sum_and_copy",
    )()[0]


def split_rows(to_row, post, read):
    n, rows, width = post.shape
    ch = read.shape[2]
    each = rows // n

    def kernel(to, a, b, *outs):
        outs, wide = outs[:n], outs[n]
        wide[:, :, :width] = a[...].astype(F32)
        wide[:, :, width:] = b[...].astype(F32)
        for k in range(n):
            outs[k][...] = wide[:, pl.ds(pl.multiple_of(to[k] * each, 8), each), :].astype(BF)

    return call(
        kernel,
        grid=(1,),
        prefetch=1,
        ins=[(post, None, None), (read, None, None)],
        outs=[(shape((n, each, width + ch), BF), None, None)] * n,
        scratch=[pltpu.VMEM((n, rows, width + ch), F32)],
        name="split_rows",
    )(to_row)


def sum_rows(to_chan, blocks):
    n, rows, width = blocks[0].shape

    def kernel(to, *refs):
        outs = refs[n:]
        for k in range(n):
            outs[k][...] = sum(r[to[k]].astype(F32) for r in refs[:n]).astype(BF)

    return call(
        kernel,
        grid=(1,),
        prefetch=1,
        ins=[(b, None, None) for b in blocks],
        outs=[(shape((rows, width), BF), None, None)] * n,
        name="sum_rows",
    )(to_chan)


def join_chan(from_chan, blocks):
    n = len(blocks)
    rows, width = blocks[0].shape
    ch = width // 3

    def kernel(src, *refs):
        out = refs[n]
        out[:, : 2 * ch] = sum(r[:, : 2 * ch].astype(F32) for r in refs[:n]).astype(BF)
        for k in range(n):
            at = pl.multiple_of(2 * ch + src[k] * ch, LANES)
            out[:, pl.ds(at, ch)] = refs[k][:, 2 * ch :]

    return call(
        kernel,
        grid=(1,),
        prefetch=1,
        ins=[(b, None, None) for b in blocks],
        outs=[(far((rows, 2 * ch + n * ch), BF), None, None)],
        name="join_chan",
    )(from_chan)[0]


def finish_pre(place, half_rows, ch, earlier=()):
    half, width = half_rows.shape
    m = (width - LANES) // ch
    steps = 4
    block = half // steps

    def kernel(place_ref, x, *outs):
        outs = outs[len(earlier) :]
        for i in range(m):
            outs[i][...] = x[:, i * ch : (i + 1) * ch].astype(F32)
        outs[m][...] = x[:, m * ch :].astype(F32)

    return call(
        kernel,
        grid=(steps,),
        prefetch=1,
        ins=[(half_rows, (block, width), lambda i, c: (i, 0))],
        outs=[(shape((2 * half, ch), F32), (block, ch), lambda i, c: (c[0] * steps + i, 0)) for _ in range(m)]
        + [(shape((half, LANES), F32), (block, LANES), lambda i, c: (i, 0))],
        aliased=earlier,
        name="finish_pre",
    )(place)


def finish_post(place, gathered, n, earlier=()):
    groups, per, width = gathered.shape
    share = 2 * groups * per
    ch = width // (n + 2)

    def kernel(place_ref, x, *outs):
        reduce_out, expand_out, read_out = outs[len(earlier) :]
        reduce_out[...] = x[0, :, :ch].astype(F32)
        for q in range(n):
            expand_out[q] = x[0, :, ch + q * share : ch + (q + 1) * share].astype(F32)
        read_out[...] = x[0, :, 2 * ch :].astype(F32)

    at = lambda i, c: (2 * i + c[0], 0)
    return call(
        kernel,
        grid=(groups,),
        prefetch=1,
        ins=[(gathered, (1, per, width), lambda i, c: (i, 0, 0))],
        outs=[
            (shape((share, ch), F32), (per, ch), at),
            (shape((n, share, share), F32), (n, per, share), lambda i, c: (0, 2 * i + c[0], 0)),
            (shape((share, n * ch), F32), (per, n * ch), at),
        ],
        aliased=earlier,
        name="finish_post",
    )(place)


def after(values, *earlier):
    return lax.optimization_barrier((values, *earlier))[0]


def pool_matrix(part, high, wide):
    half = wide // 2
    m = np.zeros((high // 2 * half * part, part * (high // 2) * wide), np.float32)
    for u in range(part):
        for i in range(high // 2):
            for j in range(wide):
                m[(i * half + j // 2) * part + u, (u * (high // 2) + i) * wide + j] = 0.25
    return m


def spread_matrix(part, high, wide):
    half = wide // 2
    m = np.zeros((part * high * wide, high // 2 * half * part), np.float32)
    for u in range(part):
        for i in range(high):
            for j in range(wide):
                m[(u * high + i) * wide + j, ((i // 2) * half + j // 2) * part + u] = 0.25
    return m


def body(features, counts, pre_reduce, pre_conv, pre_expand, pre_gain, post_reduce, post_conv, post_expand, post_gain, readout, cotangent):
    n = lax.axis_size("chan")
    row = lax.axis_index("rows").astype(jnp.int32)
    chan = lax.axis_index("chan").astype(jnp.int32)
    core = lax.axis_index("core").astype(jnp.int32)
    ch = pre_reduce.shape[0]
    slots, high, wide = features.shape[0], features.shape[1], features.shape[2]
    part = slots // n
    cells = high * wide
    pool = wide // 2
    share = ch // n
    out_share = cotangent.shape[3]
    steps = jnp.arange(n, dtype=jnp.int32)
    order = (row + steps) % n
    source = (row - steps) % n
    pair_of = (chan + steps) % n
    rank = jnp.full((1,), chan, jnp.int32)
    core_at = jnp.full((1,), core, jnp.int32)
    pre_taps = pre_conv.astype(F32).reshape(9, ch)
    post_taps = post_conv.astype(F32).reshape(9, ch)
    pre_gain_row = pre_gain.reshape(1, ch)
    pool_m = jnp.asarray(pool_matrix(part, high, wide), BF)
    up_m = jnp.asarray(spread_matrix(part, high, wide), BF)

    ends = n - 1
    down_pairs = [(i, i + 1) for i in range(ends)]
    up_pairs = [(i + 1, i) for i in range(ends)]
    above = lax.ppermute(features[:, -1], "rows", down_pairs)
    below = lax.ppermute(features[:, 0], "rows", up_pairs)
    gain_hi = post_gain.astype(BF)
    gain_lo = (post_gain - gain_hi.astype(F32)).astype(BF)
    gain_row = jnp.concatenate([gain_hi, gain_lo, jnp.zeros((ch - 2 * share,), BF)])[None]
    square = post_expand.reshape(n, share, share)
    shards = jnp.concatenate(
        [post_reduce, jnp.concatenate([square[q] for q in range(n)], axis=1), jnp.pad(gain_row, ((0, 63), (0, 0)))], axis=0
    )
    shard = lax.dynamic_index_in_dim(shards.reshape(2, -1, ch), core, 0, keepdims=False)
    full = lax.all_gather(shard, ("chan", "core"), axis=0, tiled=True)
    full = full.reshape(n, 2 * share + 64, ch)
    flat_features = features.reshape(slots * cells, ch)
    live = (jnp.arange(SLOT)[None, :] < counts[:, None]).astype(F32).reshape(slots)
    size, each = 16 * slots, 16 * part
    at = lax.broadcasted_iota(jnp.int32, (size, size), 0)
    column = lax.broadcasted_iota(jnp.int32, (size, size), 1)
    wanted = (at % each) // part * slots + part * ((chan + at // each) % n) + at % part
    select = jnp.where(column == wanted, jnp.tile(live, 16)[None, :], 0.0).astype(BF)
    wanted = (column % each) // part * slots + part * ((row - column // each) % n) + column % part
    place = jnp.where(at == wanted, 1.0, 0.0).astype(BF)
    cot_rows = cotangent.transpose(1, 2, 0, 3).reshape(-1, out_share)
    sends = cotangent_by_image(cot_rows, select, n)
    away = after(sends, above, below)
    cots = [lax.ppermute(away[k], ("rows", "chan"), cross(n, k)) for k in range(n)]

    reduced, convolved, convolved_act, normal_pre, pre_std, *pooled = pre_forward(
        order, above, below, features, pre_reduce, pre_taps, pre_expand, pre_gain_row, pool_m
    )

    pooled = after(pooled, cots)
    moved = [pooled[0]] + [lax.ppermute(pooled[k], "rows", turn(n, k)) for k in range(1, n)]
    flat, post_reduced, post_act, post_convolved, post_cact, post_normal, post_std, low = post_forward(
        source, moved, full, post_taps, pool
    )
    lows = [low] + [lax.ppermute(low, "chan", turn(n, k)) for k in range(1, n)]
    refined_grad = readout_backward(source, low, readout, cots)
    post_expanded_grad, post_reduced_grad, post_taps_grad, post_gain_grad, *back = post_backward(
        source, refined_grad, full, post_taps, post_act, post_reduced, post_convolved, post_normal, post_std, pool
    )

    returned = [back[0]] + [lax.ppermute(back[k], "rows", turn(n, -k)) for k in range(1, n)]

    flat = after(flat, lows)
    load = post_weight_grads(flat, post_reduced_grad, post_cact, post_expanded_grad, n)

    post_sum = lax.psum_scatter(load, ("x", "core"), scatter_dimension=0, tiled=False)

    stacked = jnp.stack(after(lows, load, returned))
    lows = [lax.dynamic_index_in_dim(stacked, (chan - row - k) % n, 0, keepdims=False) for k in range(n)]
    lows = [lows[0]] + [lax.ppermute(lows[k], "rows", turn(n, k)) for k in range(1, n)]

    expanded_grad, convolved_grad, top, bottom, pre_gain_grad = pre_backward(
        order, returned, up_m, normal_pre, pre_std, pre_gain_row, convolved, pre_expand
    )
    top, bottom, lows[1], lows[3] = lax.optimization_barrier((top, bottom, lows[1], lows[3]))
    grad_above = lax.ppermute(bottom, "rows", down_pairs)
    grad_below = lax.ppermute(top, "rows", up_pairs)
    act_rows = after(convolved_act, bottom).reshape(-1, ch)
    pre_expand_grad = dot(act_rows, expanded_grad.reshape(-1, ch), TN).astype(BF)

    lows = after(lows, pre_expand_grad)
    tokens, piece = token_block(rank, source, pair_of, lows, place, readout, sends)
    read_load = readout_weight_grad(lows, after(piece, grad_above, grad_below), n)
    tokens = tokens.reshape(pool, pool, slots, out_share).transpose(2, 0, 1, 3)
    convolved_grad = after(convolved_grad, read_load)
    read_sum = lax.psum_scatter(after(read_load, post_sum), ("x", "core"), scatter_dimension=0, tiled=False)

    reduced_grad, pre_taps_grad = pre_conv_backward(convolved_grad, grad_above, grad_below, reduced, pre_taps)
    small = small_rows(pre_taps_grad, pre_gain_grad, post_taps_grad, post_gain_grad)
    pre_reduce_grad = dot(after(flat_features, small), reduced_grad.reshape(-1, ch), TN).astype(BF)

    chips = ("x", "rows", "chan")
    mine = [pre_reduce_grad, pre_expand_grad]
    theirs = [other_core(lax.dynamic_index_in_dim(g.reshape(2, ch // 2, ch), 1 - core, 0, keepdims=False)) for g in mine]
    load = join_halves(core_at, mine, theirs, small, other_core(small), 64)
    pieces = lax.all_to_all(load, chips, 0, 0, tiled=False)
    feature_grad = feature_backward(order, after(reduced_grad, load), pre_reduce, returned, up_m).reshape(features.shape)

    post_sum, read_sum = lax.optimization_barrier((post_sum, read_sum, feature_grad))[:2]
    blocks = split_rows(order, post_sum, read_sum)
    blocks = [blocks[0]] + [lax.ppermute(blocks[k], "rows", turn(n, k)) for k in range(1, n)]
    blocks = sum_rows(pair_of, blocks)
    load = sum_and_copy(after(pieces, *blocks))
    blocks = [blocks[0]] + [lax.ppermute(blocks[k], "chan", turn(n, k)) for k in range(1, n)]
    rest = join_chan((chan - steps) % n, after(blocks, load))
    ready = rest
    rest = lax.all_gather(rest, ("x", "rows"), axis=0, tiled=False).reshape(4, share // 8, -1)
    load_all = lax.all_to_all(after(load, ready), chips, 0, 0, tiled=False).reshape(ch // 2, -1)

    def finish(kernel, values, *sizes):
        theirs = other_core(values)
        own = kernel(core_at, values, *sizes)
        theirs = after(theirs, *own)
        return own, theirs

    own, theirs = finish(finish_pre, load_all, ch)
    pre_reduce_out, pre_expand_out, small_their = finish_pre(1 - core_at, theirs, ch, earlier=tuple(own[:2]))
    small_out = jnp.where(core == 0, own[2], small_their)
    own, theirs = finish(finish_post, after(rest, pre_reduce_out), n)
    post_reduce_out, post_expand_out, readout_out = finish_post(1 - core_at, theirs, n, earlier=tuple(own))
    per = ch // LANES
    cut = [0, 9 * per, 10 * per, 19 * per, 20 * per]
    pre_conv_out, pre_gain_out, post_conv_out, post_gain_out = [small_out[a:b] for a, b in zip(cut, cut[1:])]
    return (
        tokens,
        feature_grad,
        pre_reduce_out,
        pre_conv_out.reshape(3, 3, ch),
        pre_expand_out,
        pre_gain_out.reshape(ch),
        post_reduce_out,
        post_conv_out.reshape(3, 3, ch),
        post_expand_out.reshape(ch, share),
        lax.dynamic_slice_in_dim(post_gain_out.reshape(ch), chan * share, share, 0),
        readout_out,
    )


def solution(mesh):
    grid = Mesh(mesh.devices.reshape(4, 2, 4, 4), ("x", "core", "rows", "chan"))
    images = P(("x", "core", "chan"), "rows", None, None)
    grids = P(("x", "core", "rows"), None, None, "chan")
    return jax.shard_map(
        body,
        mesh=grid,
        in_specs=(
            images,
            P(("x", "core", "rows")),
            P(),
            P(),
            P(),
            P(),
            P("chan", None),
            P(),
            P(None, "chan"),
            P("chan"),
            P(),
            grids,
        ),
        out_specs=(grids, images, P(), P(), P(), P(), P("chan", None), P(), P(None, "chan"), P("chan"), P("chan", None)),
        check_vma=False,
    )
```

```python
import functools

import jax
import jax.numpy as jnp
import numpy as np
from jax import lax
from jax.experimental import pallas as pl
from jax.experimental.pallas import tpu as pltpu
from jax.sharding import Mesh, PartitionSpec as P

SLOT = 4
EPS = 1e-06
BF = jnp.bfloat16
F32 = jnp.float32
LANES = 128
VMEM_LIMIT = 20 * 1024 * 1024
NN = ((1,), (0,))
NT = ((1,), (1,))
TN = ((0,), (0,))


def dot(a, b, dims=NN):
    return lax.dot_general(a, b, (dims, ((), ())), preferred_element_type=F32)


def sigmoid(v):
    return 0.5 * jnp.tanh(0.5 * v) + 0.5


def silu(v):
    return v * sigmoid(v)


def silu_slope(v):
    s = sigmoid(v)
    return s * (1.0 + v * (1.0 - s))


def gelu_parts(v):
    c = 0.7978845608028654
    square = v * v
    t = jnp.tanh(v * (c + (c * 0.044715) * square))
    half = 0.5 * (1.0 + t)
    slope = half + 0.5 * v * (1.0 - t * t) * (c + (3.0 * c * 0.044715) * square)
    return v * half, slope


def chunks(count, body, width=LANES):
    for i in range(count):
        body(pl.ds(i * width, width))


def call(kernel, *, grid, ins, outs, scratch=(), prefetch=0, aliased=(), cost=1, name):
    def spec(shape, block, index):
        if block is None:
            block, index = shape, lambda *_: (0,) * len(shape)
        return pl.BlockSpec(block, index)

    arrays = [i[0] for i in ins] + list(aliased)
    in_specs = [spec(a.shape, b, m) for a, b, m in ins] + [pl.BlockSpec(memory_space=pl.ANY)] * len(aliased)
    out_specs = [spec(s.shape, b, m) for s, b, m in outs]

    def run(*scalars):
        return pl.pallas_call(
            kernel,
            grid_spec=pltpu.PrefetchScalarGridSpec(
                num_scalar_prefetch=prefetch,
                grid=grid,
                in_specs=in_specs,
                out_specs=out_specs,
                scratch_shapes=list(scratch),
            ),
            out_shape=[s[0] for s in outs],
            compiler_params=pltpu.CompilerParams(
                dimension_semantics=("arbitrary",) * len(grid), vmem_limit_bytes=VMEM_LIMIT
            ),
            input_output_aliases={prefetch + len(ins) + i: i for i in range(len(aliased))},
            cost_estimate=pl.CostEstimate(flops=cost, bytes_accessed=1, transcendentals=0),
            name=name,
        )(*scalars, *arrays)

    return run


def shape(dims, dtype):
    return jax.ShapeDtypeStruct(dims, dtype)


def far(values, dtype=None):
    if dtype is None:
        return pltpu.with_memory_space_constraint(values, pltpu.HBM)
    return pltpu.HBM(values, dtype)


def columns_moved(t, by, first, last):
    rows = t.shape[0]
    return pltpu.roll(t, by % rows, 0) * (first if by > 0 else last)


def edge_masks(rows, width, depth):
    at = lax.broadcasted_iota(jnp.int32, (rows, LANES), 0) % (width * depth)
    return (at >= depth).astype(F32), (at < (width - 1) * depth).astype(F32)


def pre_forward(order, above, below, features, pre_reduce, taps, pre_expand, gain, pool):
    slots, high, wide, ch = features.shape
    cells = high * wide
    n = order.shape[0]
    part = slots // n
    rows_all = part * cells

    def kernel(order_ref, up_ref, down_ref, feat, wr, tap, we, gn, pool_ref, red_out, conv_out, act_out, norm_out, std_out, *rest):
        pooled_out, (red, halo, exp, sums) = rest[:n], rest[n:]
        k = pl.program_id(0)
        for side, ref in enumerate((up_ref, down_ref)):
            halo[side] = dot(ref[...].reshape(part * wide, ch), wr[...]).reshape(part, wide, ch)
        red[...] = dot(feat[...].reshape(rows_all, ch), wr[...]).reshape(part, cells, ch)
        red_out[...] = red[...].astype(BF)
        first, last = edge_masks(wide, wide, 1)
        for u in range(part):

            def conv(lanes):
                w = [tap[pl.ds(i, 1), lanes] for i in range(9)]
                rows = [halo[0, u, :, lanes]]
                rows += [red[u, pl.ds(i * wide, wide), lanes] for i in range(high)]
                rows += [halo[1, u, :, lanes]]
                rows = [silu(r).astype(BF).astype(F32) for r in rows]
                out = []
                for i in range(high):
                    t = [sum(rows[i + a] * w[3 * a + b] for a in range(3)) for b in range(3)]
                    out.append(t[1] + columns_moved(t[0], 1, first, last) + columns_moved(t[2], -1, first, last))
                conv_out[u, :, lanes] = jnp.concatenate(out, 0).astype(BF)
                act_out[u, :, lanes] = jnp.concatenate([silu(c) for c in out], 0).astype(BF)

            chunks(ch // LANES, conv)

        exp[...] = dot(act_out[...].reshape(rows_all, ch), we[...])

        def norm(p, carry):
            u, i = p // (high // 2), p % (high // 2)
            tiles = wide // 8
            f = [feat[u, 2 * i + half].astype(F32) for half in range(2)]
            nrms, blends = [], []
            for t in range(2 * tiles):
                e = exp[pl.ds(p * 2 * wide + 8 * t, 8), :]
                mean = jnp.mean(e, -1, keepdims=True)
                square = jnp.mean(e * e, -1, keepdims=True)
                std = lax.rsqrt(square - mean * mean + EPS)
                nrm = (e - mean) * std
                std_out[u, pl.ds(i * 2 * wide + 8 * t, 8), :] = std
                nrms.append(nrm)
                at = t % tiles
                blends.append(f[t // tiles][8 * at : 8 * at + 8] + silu(nrm * gn[...]))
                if t % 2 == 1:
                    both = jnp.concatenate(nrms[-2:], 0).astype(BF)
                    norm_out[u, pl.ds(i * 2 * wide + 8 * (t - 1), 16), :] = both
            for t in range(tiles):
                sums[pl.ds(p * wide + 8 * t, 8), :] = blends[t] + blends[tiles + t]
            return carry

        for p in range(part * high // 2):
            norm(p, 0)
        s = sums[...]
        hi = s.astype(BF)
        lo = (s - hi.astype(F32)).astype(BF)
        pooled = (dot(pool_ref[...], hi) + dot(pool_ref[...], lo)).astype(BF)
        for i in range(n):

            @pl.when(k == i)
            def _():
                pooled_out[i][...] = pooled

    def by_order(rest):
        return lambda k, order: (order[k],) + (0,) * rest

    pooled_rows = pool.shape[0]
    block = (part, cells, ch)
    return call(
        kernel,
        grid=(n,),
        prefetch=1,
        ins=[
            (far(above), (part, wide, ch), by_order(2)),
            (far(below), (part, wide, ch), by_order(2)),
            (far(features), (part, high, wide, ch), by_order(3)),
            (far(pre_reduce), None, None),
            (taps, None, None),
            (far(pre_expand), None, None),
            (gain, None, None),
            (pool, None, None),
        ],
        outs=[(far((slots, cells, ch), BF), block, by_order(2))] * 4
        + [(far((slots, cells, 1), F32), (part, cells, 1), by_order(2))]
        + [(shape((pooled_rows, ch), BF), None, None)] * n,
        scratch=[
            pltpu.VMEM((part, cells, ch), F32),
            pltpu.VMEM((2, part, wide, ch), F32),
            pltpu.VMEM((rows_all, ch), F32),
            pltpu.VMEM((rows_all // 2, ch), F32),
        ],
        name="pre_forward",
    )(order)


def gain_row(w, n, share):
    at = 2 * share
    parts = [w[c, at : at + 16, :].astype(F32)[:1] for c in range(n)]
    return jnp.concatenate([p[:, :share] + p[:, share : 2 * share] for p in parts], 1)


def post_forward(source, moved, weights, taps, pool):
    n, (rows, ch) = len(moved), moved[0].shape
    total = n * rows
    depth = total // (pool * pool)
    share = ch // n

    def kernel(src, *refs):
        got, refs = refs[:n], refs[n:]
        w, tap, flat_out, red_out, act_out, conv_out, cact_out, norm_out, std_out, low_out, wide_ref, red, exp = refs
        for k in range(n):
            at = pl.multiple_of(src[k] * rows, 8)
            wide_ref[pl.ds(at, rows), :] = got[k][...].astype(F32)
        gain = gain_row(w, n, share)
        flat_out[...] = wide_ref[...].astype(BF)
        total_red = 0.0
        for c in range(n):
            total_red = total_red + dot(flat_out[:, c * share : (c + 1) * share], w[c, :share])
        red[...] = total_red
        first, last = edge_masks(total, pool, depth)
        step = pool * depth

        def conv(lanes):
            v = red[:, lanes]
            red_out[:, lanes] = v.astype(BF)
            x = silu(v).astype(BF)
            act_out[:, lanes] = x
            x = x.astype(F32)
            moves = [columns_moved(x, depth, first, last), x, columns_moved(x, -depth, first, last)]
            t = [sum(moves[b] * tap[pl.ds(3 * a + b, 1), lanes] for b in range(3)) for a in range(3)]
            none = jnp.zeros((step, LANES), F32)
            c = t[1] + jnp.concatenate([none, t[0][:-step]], 0) + jnp.concatenate([t[2][step:], none], 0)
            conv_out[:, lanes] = c.astype(BF)
            cact_out[:, lanes] = silu(c).astype(BF)

        chunks(ch // LANES, conv)
        for c in range(n):
            e = 0.0
            for q in range(n):
                cut = slice(q * share, (q + 1) * share)
                e = e + dot(cact_out[:, cut], w[c, share : 2 * share, cut])
            exp[:, c * share : (c + 1) * share] = e

        def norm(i, carry):
            for t in range(3):
                at = pl.ds(i * 48 + 16 * t, 16)
                e = exp[at, :]
                mean = jnp.mean(e, -1, keepdims=True)
                square = jnp.mean(e * e, -1, keepdims=True)
                std = lax.rsqrt(square - mean * mean + EPS)
                nrm = (e - mean) * std
                norm_out[at, :] = nrm.astype(BF)
                std_out[at, :] = std
                low_out[at, :] = (wide_ref[at, :] + silu(nrm * gain)).astype(BF)
            return carry

        for i in range(total // 48):
            norm(i, 0)

    narrow = shape((total, ch), BF)
    return call(
        kernel,
        grid=(1,),
        prefetch=1,
        ins=[(a, None, None) for a in (*moved, far(weights), taps)],
        outs=[(s, None, None) for s in (narrow, narrow, narrow, narrow, narrow, narrow, shape((total, 1), F32), narrow)],
        scratch=[pltpu.VMEM((total, ch), F32)] * 3,
        name="post_forward",
    )(source)


def readout_backward(source, low, readout, cots):
    total, ch = low.shape
    n, out_share = len(cots), cots[0].shape[1]

    def kernel(src, low_ref, ro, *rest):
        cot, grad = rest[:n], rest[n]
        k = pl.program_id(0)
        logits = dot(low_ref[...], ro[...])
        slope = gelu_parts(logits)[1]
        for i in range(n):

            @pl.when(k == i)
            def _():
                piece = (cot[i][...].astype(F32) * slope).astype(BF)
                term = dot(piece, ro[...], NT)
                grad[...] = term if i == 0 else grad[...] + term

    return call(
        kernel,
        grid=(n,),
        prefetch=1,
        ins=[(low, None, None), (far(readout), (ch, out_share), lambda k, s: (0, s[k]))] + [(c, None, None) for c in cots],
        outs=[(shape((total, ch), F32), None, None)],
        name="readout_backward",
    )(source)[0]


def post_backward(source, refined_grad, weights, taps, act, red, conv, nrm, std, pool):
    total, ch = act.shape
    n = weights.shape[0]
    share = ch // n
    rows = total // n
    depth = total // (pool * pool)

    def kernel(src, rg, w, tap, act_ref, red_ref, conv_ref, norm_ref, std_ref, exp_out, redg_out, taps_out, gain_out, *rest):
        back_out, (grad, cgrad) = rest[:n], rest[n:]
        gain = gain_row(w, n, share)

        def norm(i, total_gain):
            for t in range(3):
                at = pl.ds(i * 48 + 16 * t, 16)
                nm = norm_ref[at, :].astype(F32)
                ng = rg[at, :] * silu_slope(nm * gain)
                sc = ng * gain
                one = jnp.mean(sc, -1, keepdims=True)
                two = jnp.mean(sc * nm, -1, keepdims=True)
                exp_out[at, :] = (std_ref[at, :] * (sc - one - nm * two)).astype(BF)
                g = ng * nm
                total_gain = total_gain + g[:8] + g[8:]
            return total_gain

        gains = jnp.zeros((8, ch), F32)
        for i in range(total // 48):
            gains = norm(i, gains)
        gain_out[...] = gains
        for q in range(n):
            cut = slice(q * share, (q + 1) * share)
            cg = 0.0
            for c in range(n):
                cg = cg + dot(exp_out[:, c * share : (c + 1) * share], w[c, share : 2 * share, cut], NT)
            cgrad[:, cut] = cg
        first, last = edge_masks(total, pool, depth)
        step = pool * depth

        def back(lanes):
            g = (cgrad[:, lanes] * silu_slope(conv_ref[:, lanes].astype(F32))).astype(BF).astype(F32)
            x = act_ref[:, lanes].astype(F32)
            moves = [columns_moved(g, -depth, first, last), g, columns_moved(g, depth, first, last)]
            none = jnp.zeros((step, LANES), F32)
            xs = [
                jnp.concatenate([none, x[:-step]], 0),
                x,
                jnp.concatenate([x[step:], none], 0),
            ]
            for a in range(3):
                for b in range(3):
                    prod = xs[a] * moves[b]
                    taps_out[3 * a + b, :, lanes] = jnp.sum(prod.reshape(total // 8, 8, LANES), 0)
            t = [sum(moves[b] * tap[pl.ds(3 * a + b, 1), lanes] for b in range(3)) for a in range(3)]
            d = t[1] + jnp.concatenate([t[0][step:], none], 0) + jnp.concatenate([none, t[2][:-step]], 0)
            redg_out[:, lanes] = (d * silu_slope(red_ref[:, lanes].astype(F32))).astype(BF)

        chunks(ch // LANES, back)
        for c in range(n):
            cut = slice(c * share, (c + 1) * share)
            grad[:, cut] = rg[:, cut] + dot(redg_out[...], w[c, :share], NT)
        for r in range(n):
            at = pl.ds(pl.multiple_of(src[r] * rows, 8), rows)
            back_out[r][...] = grad[at, :].astype(BF)

    return call(
        kernel,
        grid=(1,),
        prefetch=1,
        ins=[(a, None, None) for a in (refined_grad, far(weights), taps, act, red, conv, nrm, std)],
        outs=[
            (s, None, None)
            for s in (
                shape((total, ch), BF),
                shape((total, ch), BF),
                shape((9, 8, ch), F32),
                shape((8, ch), F32),
                *[shape((rows, ch), BF)] * n,
            )
        ],
        scratch=[pltpu.VMEM((total, ch), F32), pltpu.VMEM((total, ch), F32)],
        name="post_backward",
    )(source)


def cotangent_by_image(cotangent, select, pairs):
    rows, width = cotangent.shape
    size = select.shape[0]
    each = size // pairs
    per = 3

    def kernel(x, sel, *outs):
        for q in range(per):
            y = dot(sel[...], x[pl.ds(q * size, size), :]).astype(BF)
            for s in range(pairs):
                outs[s][pl.ds(q * each, each), :] = y[s * each : (s + 1) * each]

    return call(
        kernel,
        grid=(rows // (per * size),),
        ins=[(far(cotangent), (per * size, width), lambda i: (i, 0)), (select, None, None)],
        outs=[(shape((rows // pairs, width), BF), (per * each, width), lambda i: (i, 0))] * pairs,
        name="cotangent_by_image",
    )()


def token_block(chan, source, pair_of, low, place, readout, cotangent):
    pairs, (rows, ch) = len(low), low[0].shape
    width = cotangent[0].shape[1]
    size = place.shape[0]
    each = size // pairs
    per = 3
    block = per * each

    def kernel(chan_ref, src, pair, *refs):
        lows, cots, (place_ref, ro, tok_out, piece_out, cot) = refs[:pairs], refs[pairs : 2 * pairs], refs[2 * pairs :]
        for k in range(pairs):
            cot[pair[k]] = cots[k][...]
        logits = dot(jnp.concatenate([v[...] for v in lows], 0), ro[...])
        value, slope = gelu_parts(logits)
        value = value.astype(BF)
        for k in range(pairs):
            piece_out[k] = (cot[src[k]].astype(F32) * slope[k * block : (k + 1) * block]).astype(BF)
        for q in range(per):
            x = jnp.concatenate([value[k * block + q * each : k * block + (q + 1) * each] for k in range(pairs)], 0)
            tok_out[pl.ds(q * size, size), :] = dot(place_ref[...], x).astype(BF)

    rows_at = lambda i, c, s, p: (i, 0)
    return call(
        kernel,
        grid=(rows // block,),
        prefetch=3,
        ins=[
            *[(v, (block, ch), rows_at) for v in low],
            *[(v, (block, width), rows_at) for v in cotangent],
            (place, None, None),
            (far(readout), (ch, width), lambda i, c, s, p: (0, c[0])),
        ],
        outs=[
            (shape((pairs * rows, width), BF), (pairs * block, width), rows_at),
            (shape((pairs, rows, width), BF), (pairs, block, width), lambda i, c, s, p: (0, i, 0)),
        ],
        scratch=[pltpu.VMEM((pairs, block, width), BF)],
        name="token_block",
    )(chan, source, pair_of)


def pre_backward(order, returned, spread_up, nrm, std, gain, conv, pre_expand):
    slots, cells, ch = nrm.shape
    n = order.shape[0]
    part = slots // n
    wide = 24
    rows = part * cells

    def kernel(order_ref, *refs):
        ret, refs = refs[:n], refs[n:]
        up, norm_ref, std_ref, gn, conv_ref, we, exp_out, conv_grad_out, top_out, bottom_out, gain_out, grad, cgrad = refs
        k = pl.program_id(0)
        for i in range(n):

            @pl.when(k == i)
            def _():
                grad[...] = dot(up[...], ret[i][...])

        def norm(i, total_gain):
            u, j = i // (cells // 48), i % (cells // 48)
            for t in range(3):
                at = pl.ds(j * 48 + 16 * t, 16)
                nm = norm_ref[u, at, :].astype(F32)
                ng = grad[pl.ds(i * 48 + 16 * t, 16), :] * silu_slope(nm * gn[...])
                sc = ng * gn[...]
                one = jnp.mean(sc, -1, keepdims=True)
                two = jnp.mean(sc * nm, -1, keepdims=True)
                exp_out[u, at, :] = (std_ref[u, at, :] * (sc - one - nm * two)).astype(BF)
                g = ng * nm
                total_gain = total_gain + g[:8] + g[8:]
            return total_gain

        gains = jnp.zeros((8, ch), F32)
        for i in range(rows // 48):
            gains = norm(i, gains)

        @pl.when(k == 0)
        def _():
            gain_out[...] = gains

        @pl.when(k > 0)
        def _():
            gain_out[...] += gains

        cgrad[...] = dot(exp_out[...].reshape(rows, ch), we[...], NT)
        for u in range(part):

            def slope(lanes):
                g = cgrad[pl.ds(u * cells, cells), lanes] * silu_slope(conv_ref[u, :, lanes].astype(F32))
                conv_grad_out[u, :, lanes] = g.astype(BF)
                top_out[u, :, lanes] = g[:wide].astype(BF)
                bottom_out[u, :, lanes] = g[cells - wide :].astype(BF)

            chunks(ch // LANES, slope)

    by_order = lambda k, order: (order[k], 0, 0)
    whole = (part, cells, ch)
    edge = (part, wide, ch)
    return call(
        kernel,
        grid=(n,),
        prefetch=1,
        ins=[
            *[(r, None, None) for r in returned],
            (spread_up, None, None),
            (far(nrm), whole, by_order),
            (far(std), (part, cells, 1), by_order),
            (gain, None, None),
            (far(conv), whole, by_order),
            (far(pre_expand), None, None),
        ],
        outs=[
            (shape((slots, cells, ch), BF), whole, by_order),
            (shape((slots, cells, ch), BF), whole, by_order),
            (shape((slots, wide, ch), BF), edge, by_order),
            (shape((slots, wide, ch), BF), edge, by_order),
            (shape((8, ch), F32), None, None),
        ],
        scratch=[pltpu.VMEM((rows, ch), F32), pltpu.VMEM((rows, ch), F32)],
        name="pre_backward",
    )(order)


def pre_conv_backward(conv_grad, above, below, reduced, taps):
    slots, cells, ch = reduced.shape
    wide = above.shape[1]
    high = cells // wide

    def kernel(cg, up, down, red, tap, redg_out, taps_out):
        step = pl.program_id(0)
        first, last = edge_masks(wide, wide, 1)

        @pl.when(step == 0)
        def _():
            taps_out[...] = jnp.zeros_like(taps_out)

        def back(lanes):
            w = [tap[pl.ds(i, 1), lanes] for i in range(9)]
            mid = cg[0, :, lanes].astype(F32)
            rows = [up[0, :, lanes].astype(F32)]
            rows += [mid[i * wide : (i + 1) * wide] for i in range(high)]
            rows += [down[0, :, lanes].astype(F32)]
            whole = red[0, :, lanes].astype(F32)
            v = [whole[i * wide : (i + 1) * wide] for i in range(high)]
            s = [sigmoid(t) for t in v]
            x = [(a * b).astype(BF).astype(F32) for a, b in zip(v, s)]
            d = [0.0] * high
            sums = [0.0] * 9
            for p in range(high + 2):
                g = rows[p]
                moves = [columns_moved(g, -1, first, last), g, columns_moved(g, 1, first, last)]
                for a in range(3):
                    i = p - 1 + a - 1
                    if 0 <= i < high:
                        for b in range(3):
                            d[i] = d[i] + moves[b] * w[3 * a + b]
                            prod = x[i] * moves[b]
                            sums[3 * a + b] = sums[3 * a + b] + (prod[:8] + prod[8:16] + prod[16:])
            out = [d[i] * (s[i] * (1.0 + v[i] * (1.0 - s[i]))) for i in range(high)]
            redg_out[0, :, lanes] = jnp.concatenate(out, 0).astype(BF)
            for i in range(9):
                taps_out[i, :, lanes] += sums[i]

        chunks(ch // LANES, back)

    image = lambda i: (i, 0, 0)
    return call(
        kernel,
        grid=(slots,),
        ins=[
            (conv_grad, (1, cells, ch), image),
            (above, (1, wide, ch), image),
            (below, (1, wide, ch), image),
            (far(reduced), (1, cells, ch), image),
            (taps, None, None),
        ],
        outs=[
            (shape((slots, cells, ch), BF), (1, cells, ch), image),
            (shape((9, 8, ch), F32), None, None),
        ],
        name="pre_conv_backward",
    )()


def feature_backward(order, reduced_grad, pre_reduce, returned, spread_up):
    slots, cells, ch = reduced_grad.shape
    n = order.shape[0]
    part = slots // n

    def kernel(order_ref, rg, wr, up, *refs):
        ret, out = refs[:n], refs[n]
        k = pl.program_id(0)
        for i in range(n):

            @pl.when(k == i)
            def _():
                out[...] = dot(up[...], ret[i][...]).reshape(part, cells, ch)

        out[...] += dot(rg[...].reshape(part * cells, ch), wr[...], NT).reshape(part, cells, ch)

    by_order = lambda k, order: (order[k], 0, 0)
    whole = (part, cells, ch)
    return call(
        kernel,
        grid=(n,),
        prefetch=1,
        ins=[
            (reduced_grad, whole, by_order),
            (far(pre_reduce), None, None),
            (spread_up, None, None),
            *[(r, None, None) for r in returned],
        ],
        outs=[(shape((slots, cells, ch), F32), whole, by_order)],
        name="feature_backward",
    )(order)[0]


def post_weight_grads(flat, reduced_grad, act, expanded_grad, n):
    total, ch = flat.shape
    share = ch // n
    rows = share // 8

    def kernel(x, g, a, e, out):
        for c in range(n):
            cut = slice(c * share, (c + 1) * share)
            v = dot(x[:, cut], g[...], TN).astype(BF)
            for d in range(8):
                out[d, c, :, :ch] = v[d * rows : (d + 1) * rows]
            for q in range(n):
                v = dot(a[:, q * share : (q + 1) * share], e[:, cut], TN).astype(BF)
                for d in range(8):
                    out[d, c, :, ch + q * share : ch + (q + 1) * share] = v[d * rows : (d + 1) * rows]

    return call(
        kernel,
        grid=(1,),
        ins=[(v, None, None) for v in (flat, reduced_grad, act, expanded_grad)],
        outs=[(far((8, n, rows, 2 * ch), BF), None, None)],
        name="post_weight_grads",
    )()[0]


def readout_weight_grad(low, piece, n):
    pairs, total, width = piece.shape
    ch = low[0].shape[1]
    share = ch // n
    parts = 8
    rows = share // parts

    def kernel(*refs):
        x, (g, out) = refs[:pairs], refs[pairs:]
        x = jnp.concatenate([v[...] for v in x], 0)
        v = dot(x, g[...].reshape(pairs * total, width), TN).astype(BF)
        for d in range(parts):
            out[d, 0] = v[d * rows : (d + 1) * rows]

    return call(
        kernel,
        grid=(n,),
        ins=[(v, (total, share), lambda c: (0, c)) for v in low] + [(piece, None, None)],
        outs=[(far((parts, n, rows, width), BF), (parts, 1, rows, width), lambda c: (0, c, 0, 0))],
        name="readout_weight_grad",
    )()[0]


def cross(n, k):
    return [(a * n + b, ((b + k) % n) * n + a) for a in range(n) for b in range(n)]


def turn(n, k):
    return [(i, (i + k) % n) for i in range(n)]


def other_core(values):
    return lax.ppermute(values, "core", [(0, 1), (1, 0)])


def small_rows(*grads):
    ch = grads[0].shape[-1]
    counts = [g.shape[0] if g.ndim == 3 else 1 for g in grads]
    per = ch // LANES

    def kernel(*refs):
        out = refs[-1]
        at = 0
        for ref, count in zip(refs, counts):
            for i in range(count):
                v = jnp.sum(ref[i] if len(ref.shape) == 3 else ref[...], 0, keepdims=True)
                for q in range(per):
                    out[pl.ds(at, 1), :] = v[:, q * LANES : (q + 1) * LANES]
                    at += 1

    return call(
        kernel,
        grid=(1,),
        ins=[(g, None, None) for g in grads],
        outs=[(shape((sum(counts) * per, LANES), F32), None, None)],
        name="small_rows",
    )()[0]


def join_halves(core, mine, theirs, small, their_small, parts):
    rows, ch = mine[0].shape
    half = rows // 2
    width = len(mine) * ch + LANES
    count = small.shape[0]
    m = len(mine)
    steps = 2
    block = half // steps

    def kernel(core_ref, *refs):
        own, got = refs[:m], refs[m : 2 * m]
        sm, got_sm, out = refs[2 * m :]
        for i in range(m):
            out[:, i * ch : (i + 1) * ch] = (own[i][...].astype(F32) + got[i][...].astype(F32)).astype(BF)
        first = ((core_ref[0] == 0) & (pl.program_id(0) == 0)).astype(F32)
        total = (sm[...] + got_sm[...]) * first
        pad = jnp.zeros((block - count, LANES), F32)
        out[:, m * ch :] = jnp.concatenate([total, pad], 0).astype(BF)

    return call(
        kernel,
        grid=(steps,),
        prefetch=1,
        ins=[(v, (block, ch), lambda i, c: (c[0] * steps + i, 0)) for v in mine]
        + [(v, (block, ch), lambda i, c: (i, 0)) for v in theirs]
        + [(v, None, None) for v in (small, their_small)],
        outs=[(far((half, width), BF), (block, width), lambda i, c: (i, 0))],
        name="join_halves",
    )(core)[0].reshape(parts, half // parts, width)


def sum_and_copy(blocks):
    parts, rows, width = blocks.shape

    def kernel(x, out):
        def cut(lanes):
            total = jnp.sum(x[:, :, lanes].astype(F32), 0).astype(BF)
            out[:, :, lanes] = jnp.broadcast_to(total[None], (parts, rows, LANES))

        chunks(width // LANES, cut)

    return call(
        kernel,
        grid=(1,),
        ins=[(blocks, None, None)],
        outs=[(far(blocks.shape, BF), None, None)],
        name="sum_and_copy",
    )()[0]


def split_rows(to_row, post, read):
    n, rows, width = post.shape
    ch = read.shape[2]
    each = rows // n

    def kernel(to, a, b, *outs):
        outs, wide = outs[:n], outs[n]
        wide[:, :, :width] = a[...].astype(F32)
        wide[:, :, width:] = b[...].astype(F32)
        for k in range(n):
            outs[k][...] = wide[:, pl.ds(pl.multiple_of(to[k] * each, 8), each), :].astype(BF)

    return call(
        kernel,
        grid=(1,),
        prefetch=1,
        ins=[(post, None, None), (read, None, None)],
        outs=[(shape((n, each, width + ch), BF), None, None)] * n,
        scratch=[pltpu.VMEM((n, rows, width + ch), F32)],
        name="split_rows",
    )(to_row)


def sum_rows(to_chan, blocks):
    n, rows, width = blocks[0].shape

    def kernel(to, *refs):
        outs = refs[n:]
        for k in range(n):
            outs[k][...] = sum(r[to[k]].astype(F32) for r in refs[:n]).astype(BF)

    return call(
        kernel,
        grid=(1,),
        prefetch=1,
        ins=[(b, None, None) for b in blocks],
        outs=[(shape((rows, width), BF), None, None)] * n,
        name="sum_rows",
    )(to_chan)


def join_chan(from_chan, blocks):
    n = len(blocks)
    rows, width = blocks[0].shape
    ch = width // 3

    def kernel(src, *refs):
        out = refs[n]
        out[:, : 2 * ch] = sum(r[:, : 2 * ch].astype(F32) for r in refs[:n]).astype(BF)
        for k in range(n):
            at = pl.multiple_of(2 * ch + src[k] * ch, LANES)
            out[:, pl.ds(at, ch)] = refs[k][:, 2 * ch :]

    return call(
        kernel,
        grid=(1,),
        prefetch=1,
        ins=[(b, None, None) for b in blocks],
        outs=[(far((rows, 2 * ch + n * ch), BF), None, None)],
        name="join_chan",
    )(from_chan)[0]


def finish_pre(place, half_rows, ch, earlier=()):
    half, width = half_rows.shape
    m = (width - LANES) // ch
    steps = 4
    block = half // steps

    def kernel(place_ref, x, *outs):
        outs = outs[len(earlier) :]
        for i in range(m):
            outs[i][...] = x[:, i * ch : (i + 1) * ch].astype(F32)
        outs[m][...] = x[:, m * ch :].astype(F32)

    return call(
        kernel,
        grid=(steps,),
        prefetch=1,
        ins=[(half_rows, (block, width), lambda i, c: (i, 0))],
        outs=[(shape((2 * half, ch), F32), (block, ch), lambda i, c: (c[0] * steps + i, 0)) for _ in range(m)]
        + [(shape((half, LANES), F32), (block, LANES), lambda i, c: (i, 0))],
        aliased=earlier,
        name="finish_pre",
    )(place)


def join_rows(from_row, blocks):
    n = len(blocks)
    each, width = blocks[0].shape

    def kernel(src, *refs):
        out, wide = refs[n:]
        for k in range(n):
            wide[pl.ds(pl.multiple_of(src[k] * each, 8), each), :] = refs[k][...].astype(F32)
        out[...] = wide[...].astype(BF)

    return call(
        kernel,
        grid=(1,),
        prefetch=1,
        ins=[(b, None, None) for b in blocks],
        outs=[(shape((n * each, width), BF), None, None)],
        scratch=[pltpu.VMEM((n * each, width), F32)],
        name="join_rows",
    )(from_row)[0]


def finish_post(places, blocks):
    m = len(blocks)
    per, width = blocks[0].shape
    share = m * per
    n = 4
    ch = width // (n + 2)

    def kernel(place, *refs):
        x, (reduce_out, expand_out, read_out) = refs[:m], refs[m:]
        step = pl.program_id(0)
        for i in range(m):

            @pl.when(step == i)
            def _():
                reduce_out[...] = x[i][:, :ch].astype(F32)
                for q in range(n):
                    expand_out[q] = x[i][:, ch + q * share : ch + (q + 1) * share].astype(F32)
                read_out[...] = x[i][:, 2 * ch :].astype(F32)

    at = lambda i, c: (c[i], 0)
    return call(
        kernel,
        grid=(m,),
        prefetch=1,
        ins=[(b, None, None) for b in blocks],
        outs=[
            (shape((share, ch), F32), (per, ch), at),
            (shape((n, share, share), F32), (n, per, share), lambda i, c: (0, c[i], 0)),
            (shape((share, n * ch), F32), (per, n * ch), at),
        ],
        name="finish_post",
    )(places)


def after(values, *earlier):
    return lax.optimization_barrier((values, *earlier))[0]


def pool_matrix(part, high, wide):
    half = wide // 2
    m = np.zeros((high // 2 * half * part, part * (high // 2) * wide), np.float32)
    for u in range(part):
        for i in range(high // 2):
            for j in range(wide):
                m[(i * half + j // 2) * part + u, (u * (high // 2) + i) * wide + j] = 0.25
    return m


def spread_matrix(part, high, wide):
    half = wide // 2
    m = np.zeros((part * high * wide, high // 2 * half * part), np.float32)
    for u in range(part):
        for i in range(high):
            for j in range(wide):
                m[(u * high + i) * wide + j, ((i // 2) * half + j // 2) * part + u] = 0.25
    return m


def body(features, counts, pre_reduce, pre_conv, pre_expand, pre_gain, post_reduce, post_conv, post_expand, post_gain, readout, cotangent):
    n = lax.axis_size("chan")
    row = lax.axis_index("rows").astype(jnp.int32)
    chan = lax.axis_index("chan").astype(jnp.int32)
    core = lax.axis_index("core").astype(jnp.int32)
    ch = pre_reduce.shape[0]
    slots, high, wide = features.shape[0], features.shape[1], features.shape[2]
    part = slots // n
    cells = high * wide
    pool = wide // 2
    share = ch // n
    out_share = cotangent.shape[3]
    steps = jnp.arange(n, dtype=jnp.int32)
    order = (row + steps) % n
    source = (row - steps) % n
    pair_of = (chan + steps) % n
    rank = jnp.full((1,), chan, jnp.int32)
    core_at = jnp.full((1,), core, jnp.int32)
    pre_taps = pre_conv.astype(F32).reshape(9, ch)
    post_taps = post_conv.astype(F32).reshape(9, ch)
    pre_gain_row = pre_gain.reshape(1, ch)
    pool_m = jnp.asarray(pool_matrix(part, high, wide), BF)
    up_m = jnp.asarray(spread_matrix(part, high, wide), BF)

    ends = n - 1
    down_pairs = [(i, i + 1) for i in range(ends)]
    up_pairs = [(i + 1, i) for i in range(ends)]
    above = lax.ppermute(features[:, -1], "rows", down_pairs)
    below = lax.ppermute(features[:, 0], "rows", up_pairs)
    gain_hi = post_gain.astype(BF)
    gain_lo = (post_gain - gain_hi.astype(F32)).astype(BF)
    gain_row = jnp.concatenate([gain_hi, gain_lo, jnp.zeros((ch - 2 * share,), BF)])[None]
    square = post_expand.reshape(n, share, share)
    shards = jnp.concatenate(
        [post_reduce, jnp.concatenate([square[q] for q in range(n)], axis=1), jnp.pad(gain_row, ((0, 63), (0, 0)))], axis=0
    )
    shard = lax.dynamic_index_in_dim(shards.reshape(2, -1, ch), core, 0, keepdims=False)
    full = lax.all_gather(shard, ("chan", "core"), axis=0, tiled=True)
    full = full.reshape(n, 2 * share + 64, ch)
    flat_features = features.reshape(slots * cells, ch)
    live = (jnp.arange(SLOT)[None, :] < counts[:, None]).astype(F32).reshape(slots)
    size, each = 16 * slots, 16 * part
    at = lax.broadcasted_iota(jnp.int32, (size, size), 0)
    column = lax.broadcasted_iota(jnp.int32, (size, size), 1)
    wanted = (at % each) // part * slots + part * ((chan + at // each) % n) + at % part
    select = jnp.where(column == wanted, jnp.tile(live, 16)[None, :], 0.0).astype(BF)
    wanted = (column % each) // part * slots + part * ((row - column // each) % n) + column % part
    place = jnp.where(at == wanted, 1.0, 0.0).astype(BF)
    cot_rows = cotangent.transpose(1, 2, 0, 3).reshape(-1, out_share)
    sends = cotangent_by_image(cot_rows, select, n)
    away = after(sends, above, below)
    cots = [lax.ppermute(away[k], ("rows", "chan"), cross(n, k)) for k in range(n)]

    reduced, convolved, convolved_act, normal_pre, pre_std, *pooled = pre_forward(
        order, above, below, features, pre_reduce, pre_taps, pre_expand, pre_gain_row, pool_m
    )

    pooled = after(pooled, cots)
    moved = [pooled[0]] + [lax.ppermute(pooled[k], "rows", turn(n, k)) for k in range(1, n)]
    flat, post_reduced, post_act, post_convolved, post_cact, post_normal, post_std, low = post_forward(
        source, moved, full, post_taps, pool
    )
    lows = [low] + [lax.ppermute(low, "chan", turn(n, k)) for k in range(1, n)]
    refined_grad = readout_backward(source, low, readout, cots)
    post_expanded_grad, post_reduced_grad, post_taps_grad, post_gain_grad, *back = post_backward(
        source, refined_grad, full, post_taps, post_act, post_reduced, post_convolved, post_normal, post_std, pool
    )

    returned = [back[0]] + [lax.ppermute(back[k], "rows", turn(n, -k)) for k in range(1, n)]

    flat = after(flat, lows, returned)
    load = post_weight_grads(flat, post_reduced_grad, post_cact, post_expanded_grad, n)

    post_sum = lax.psum_scatter(load, ("x", "core"), scatter_dimension=0, tiled=False)

    stacked = jnp.stack(after(lows, returned))
    lows = [lax.dynamic_index_in_dim(stacked, (chan - row - k) % n, 0, keepdims=False) for k in range(n)]
    lows = [lows[0]] + [lax.ppermute(lows[k], "rows", turn(n, k)) for k in range(1, n)]

    expanded_grad, convolved_grad, top, bottom, pre_gain_grad = pre_backward(
        order, returned, up_m, normal_pre, pre_std, pre_gain_row, convolved, pre_expand
    )
    top, bottom, lows[1], lows[3] = lax.optimization_barrier((top, bottom, lows[1], lows[3]))
    grad_above = lax.ppermute(bottom, "rows", down_pairs)
    grad_below = lax.ppermute(top, "rows", up_pairs)
    act_rows = after(convolved_act, bottom).reshape(-1, ch)
    pre_expand_grad = dot(act_rows, expanded_grad.reshape(-1, ch), TN).astype(BF)

    lows = after(lows, pre_expand_grad)
    tokens, piece = token_block(rank, source, pair_of, lows, place, readout, sends)
    read_load = readout_weight_grad(lows, after(piece, grad_above, grad_below), n)
    tokens = tokens.reshape(pool, pool, slots, out_share).transpose(2, 0, 1, 3)
    convolved_grad = after(convolved_grad, read_load)
    read_sum = lax.psum_scatter(after(read_load, post_sum), ("x", "core"), scatter_dimension=0, tiled=False)

    reduced_grad, pre_taps_grad = pre_conv_backward(convolved_grad, grad_above, grad_below, reduced, pre_taps)
    small = small_rows(pre_taps_grad, pre_gain_grad, post_taps_grad, post_gain_grad)
    pre_reduce_grad = dot(after(flat_features, small), reduced_grad.reshape(-1, ch), TN).astype(BF)

    chips = ("x", "rows", "chan")
    mine = [pre_reduce_grad, pre_expand_grad]
    theirs = [other_core(lax.dynamic_index_in_dim(g.reshape(2, ch // 2, ch), 1 - core, 0, keepdims=False)) for g in mine]
    load = join_halves(core_at, mine, theirs, small, other_core(small), 64)
    pieces = lax.all_to_all(load, chips, 0, 0, tiled=False)
    feature_grad = feature_backward(order, after(reduced_grad, load), pre_reduce, returned, up_m).reshape(features.shape)

    post_sum, read_sum = lax.optimization_barrier((post_sum, read_sum, feature_grad))[:2]
    blocks = split_rows(order, post_sum, read_sum)
    blocks = [blocks[0]] + [lax.ppermute(blocks[k], "rows", turn(n, k)) for k in range(1, n)]
    blocks = sum_rows(pair_of, blocks)
    load = sum_and_copy(after(pieces, *blocks))
    blocks = [blocks[0]] + [lax.ppermute(blocks[k], "chan", turn(n, k)) for k in range(1, n)]
    rest = join_chan((chan - steps) % n, after(blocks, load))
    ready = rest
    rest = [rest] + [lax.ppermute(rest, "rows", turn(n, k)) for k in range(1, n)]
    rest = join_rows(source, rest)
    rest = [rest] + [lax.ppermute(rest, "x", turn(4, k)) for k in range(1, 4)]
    rest += [other_core(v) for v in rest]
    x_from = (lax.axis_index("x").astype(jnp.int32) - jnp.arange(4, dtype=jnp.int32)) % 4
    places = jnp.concatenate([2 * x_from + core, 2 * x_from + 1 - core])
    load_all = lax.all_to_all(after(load, ready), chips, 0, 0, tiled=False).reshape(ch // 2, -1)
    load_all = after(load_all, *rest[:4])

    def finish(kernel, values, *sizes):
        theirs = other_core(values)
        own = kernel(core_at, values, *sizes)
        theirs = after(theirs, *own)
        return own, theirs

    own, theirs = finish(finish_pre, load_all, ch)
    pre_reduce_out, pre_expand_out, small_their = finish_pre(1 - core_at, theirs, ch, earlier=tuple(own[:2]))
    small_out = jnp.where(core == 0, own[2], small_their)
    post_reduce_out, post_expand_out, readout_out = finish_post(places, rest)
    per = ch // LANES
    cut = [0, 9 * per, 10 * per, 19 * per, 20 * per]
    pre_conv_out, pre_gain_out, post_conv_out, post_gain_out = [small_out[a:b] for a, b in zip(cut, cut[1:])]
    return (
        tokens,
        feature_grad,
        pre_reduce_out,
        pre_conv_out.reshape(3, 3, ch),
        pre_expand_out,
        pre_gain_out.reshape(ch),
        post_reduce_out,
        post_conv_out.reshape(3, 3, ch),
        post_expand_out.reshape(ch, share),
        lax.dynamic_slice_in_dim(post_gain_out.reshape(ch), chan * share, share, 0),
        readout_out,
    )


def solution(mesh):
    grid = Mesh(mesh.devices.reshape(4, 2, 4, 4), ("x", "core", "rows", "chan"))
    images = P(("x", "core", "chan"), "rows", None, None)
    grids = P(("x", "core", "rows"), None, None, "chan")
    return jax.shard_map(
        body,
        mesh=grid,
        in_specs=(
            images,
            P(("x", "core", "rows")),
            P(),
            P(),
            P(),
            P(),
            P("chan", None),
            P(),
            P(None, "chan"),
            P("chan"),
            P(),
            grids,
        ),
        out_specs=(grids, images, P(), P(), P(), P(), P("chan", None), P(), P(None, "chan"), P("chan"), P("chan", None)),
        check_vma=False,
    )
```

```python
import functools

import jax
import jax.numpy as jnp
import numpy as np
from jax import lax
from jax.experimental import pallas as pl
from jax.experimental.pallas import tpu as pltpu
from jax.sharding import Mesh, PartitionSpec as P

SLOT = 4
EPS = 1e-06
BF = jnp.bfloat16
F32 = jnp.float32
LANES = 128
VMEM_LIMIT = 20 * 1024 * 1024
NN = ((1,), (0,))
NT = ((1,), (1,))
TN = ((0,), (0,))


def dot(a, b, dims=NN):
    return lax.dot_general(a, b, (dims, ((), ())), preferred_element_type=F32)


def sigmoid(v):
    return 0.5 * jnp.tanh(0.5 * v) + 0.5


def silu(v):
    return v * sigmoid(v)


def silu_slope(v):
    s = sigmoid(v)
    return s * (1.0 + v * (1.0 - s))


def gelu_parts(v):
    c = 0.7978845608028654
    square = v * v
    t = jnp.tanh(v * (c + (c * 0.044715) * square))
    half = 0.5 * (1.0 + t)
    slope = half + 0.5 * v * (1.0 - t * t) * (c + (3.0 * c * 0.044715) * square)
    return v * half, slope


def chunks(count, body, width=LANES):
    for i in range(count):
        body(pl.ds(i * width, width))


def call(kernel, *, grid, ins, outs, scratch=(), prefetch=0, aliased=(), cost=1, name):
    def spec(shape, block, index):
        if block is None:
            block, index = shape, lambda *_: (0,) * len(shape)
        return pl.BlockSpec(block, index)

    arrays = [i[0] for i in ins] + list(aliased)
    in_specs = [spec(a.shape, b, m) for a, b, m in ins] + [pl.BlockSpec(memory_space=pl.ANY)] * len(aliased)
    out_specs = [spec(s.shape, b, m) for s, b, m in outs]

    def run(*scalars):
        return pl.pallas_call(
            kernel,
            grid_spec=pltpu.PrefetchScalarGridSpec(
                num_scalar_prefetch=prefetch,
                grid=grid,
                in_specs=in_specs,
                out_specs=out_specs,
                scratch_shapes=list(scratch),
            ),
            out_shape=[s[0] for s in outs],
            compiler_params=pltpu.CompilerParams(
                dimension_semantics=("arbitrary",) * len(grid), vmem_limit_bytes=VMEM_LIMIT
            ),
            input_output_aliases={prefetch + len(ins) + i: i for i in range(len(aliased))},
            cost_estimate=pl.CostEstimate(flops=cost, bytes_accessed=1, transcendentals=0),
            name=name,
        )(*scalars, *arrays)

    return run


def shape(dims, dtype):
    return jax.ShapeDtypeStruct(dims, dtype)


def far(values, dtype=None):
    if dtype is None:
        return pltpu.with_memory_space_constraint(values, pltpu.HBM)
    return pltpu.HBM(values, dtype)


def columns_moved(t, by, first, last):
    rows = t.shape[0]
    return pltpu.roll(t, by % rows, 0) * (first if by > 0 else last)


def edge_masks(rows, width, depth):
    at = lax.broadcasted_iota(jnp.int32, (rows, LANES), 0) % (width * depth)
    return (at >= depth).astype(F32), (at < (width - 1) * depth).astype(F32)


def pre_forward(order, above, below, features, pre_reduce, taps, pre_expand, gain, pool):
    slots, high, wide, ch = features.shape
    cells = high * wide
    n = order.shape[0]
    part = slots // n
    rows_all = part * cells

    def kernel(order_ref, up_ref, down_ref, feat, wr, tap, we, gn, pool_ref, red_out, conv_out, act_out, norm_out, std_out, *rest):
        pooled_out, (red, halo, exp, sums) = rest[:n], rest[n:]
        k = pl.program_id(0)
        for side, ref in enumerate((up_ref, down_ref)):
            halo[side] = dot(ref[...].reshape(part * wide, ch), wr[...]).reshape(part, wide, ch)
        red[...] = dot(feat[...].reshape(rows_all, ch), wr[...]).reshape(part, cells, ch)
        red_out[...] = red[...].astype(BF)
        first, last = edge_masks(wide, wide, 1)
        for u in range(part):

            def conv(lanes):
                w = [tap[pl.ds(i, 1), lanes] for i in range(9)]
                rows = [halo[0, u, :, lanes]]
                rows += [red[u, pl.ds(i * wide, wide), lanes] for i in range(high)]
                rows += [halo[1, u, :, lanes]]
                rows = [silu(r).astype(BF).astype(F32) for r in rows]
                out = []
                for i in range(high):
                    t = [sum(rows[i + a] * w[3 * a + b] for a in range(3)) for b in range(3)]
                    out.append(t[1] + columns_moved(t[0], 1, first, last) + columns_moved(t[2], -1, first, last))
                conv_out[u, :, lanes] = jnp.concatenate(out, 0).astype(BF)
                act_out[u, :, lanes] = jnp.concatenate([silu(c) for c in out], 0).astype(BF)

            chunks(ch // LANES, conv)

        exp[...] = dot(act_out[...].reshape(rows_all, ch), we[...])

        def norm(p, carry):
            u, i = p // (high // 2), p % (high // 2)
            tiles = wide // 8
            f = [feat[u, 2 * i + half].astype(F32) for half in range(2)]
            nrms, blends = [], []
            for t in range(2 * tiles):
                e = exp[pl.ds(p * 2 * wide + 8 * t, 8), :]
                mean = jnp.mean(e, -1, keepdims=True)
                square = jnp.mean(e * e, -1, keepdims=True)
                std = lax.rsqrt(square - mean * mean + EPS)
                nrm = (e - mean) * std
                std_out[u, pl.ds(i * 2 * wide + 8 * t, 8), :] = std
                nrms.append(nrm)
                at = t % tiles
                blends.append(f[t // tiles][8 * at : 8 * at + 8] + silu(nrm * gn[...]))
                if t % 2 == 1:
                    both = jnp.concatenate(nrms[-2:], 0).astype(BF)
                    norm_out[u, pl.ds(i * 2 * wide + 8 * (t - 1), 16), :] = both
            for t in range(tiles):
                sums[pl.ds(p * wide + 8 * t, 8), :] = blends[t] + blends[tiles + t]
            return carry

        for p in range(part * high // 2):
            norm(p, 0)
        s = sums[...]
        hi = s.astype(BF)
        lo = (s - hi.astype(F32)).astype(BF)
        pooled = (dot(pool_ref[...], hi) + dot(pool_ref[...], lo)).astype(BF)
        for i in range(n):

            @pl.when(k == i)
            def _():
                pooled_out[i][...] = pooled

    def by_order(rest):
        return lambda k, order: (order[k],) + (0,) * rest

    pooled_rows = pool.shape[0]
    block = (part, cells, ch)
    return call(
        kernel,
        grid=(n,),
        prefetch=1,
        ins=[
            (far(above), (part, wide, ch), by_order(2)),
            (far(below), (part, wide, ch), by_order(2)),
            (far(features), (part, high, wide, ch), by_order(3)),
            (far(pre_reduce), None, None),
            (taps, None, None),
            (far(pre_expand), None, None),
            (gain, None, None),
            (pool, None, None),
        ],
        outs=[(far((slots, cells, ch), BF), block, by_order(2))] * 4
        + [(far((slots, cells, 1), F32), (part, cells, 1), by_order(2))]
        + [(shape((pooled_rows, ch), BF), None, None)] * n,
        scratch=[
            pltpu.VMEM((part, cells, ch), F32),
            pltpu.VMEM((2, part, wide, ch), F32),
            pltpu.VMEM((rows_all, ch), F32),
            pltpu.VMEM((rows_all // 2, ch), F32),
        ],
        name="pre_forward",
    )(order)


def gain_row(w, n, share):
    at = 2 * share
    parts = [w[c, at : at + 16, :].astype(F32)[:1] for c in range(n)]
    return jnp.concatenate([p[:, :share] + p[:, share : 2 * share] for p in parts], 1)


def post_forward(source, moved, weights, taps, pool):
    n, (rows, ch) = len(moved), moved[0].shape
    total = n * rows
    depth = total // (pool * pool)
    share = ch // n

    def kernel(src, *refs):
        got, refs = refs[:n], refs[n:]
        w, tap, flat_out, red_out, act_out, conv_out, cact_out, norm_out, std_out, low_out, wide_ref, red, exp = refs
        for k in range(n):
            at = pl.multiple_of(src[k] * rows, 8)
            wide_ref[pl.ds(at, rows), :] = got[k][...].astype(F32)
        gain = gain_row(w, n, share)
        flat_out[...] = wide_ref[...].astype(BF)
        total_red = 0.0
        for c in range(n):
            total_red = total_red + dot(flat_out[:, c * share : (c + 1) * share], w[c, :share])
        red[...] = total_red
        first, last = edge_masks(total, pool, depth)
        step = pool * depth

        def conv(lanes):
            v = red[:, lanes]
            red_out[:, lanes] = v.astype(BF)
            x = silu(v).astype(BF)
            act_out[:, lanes] = x
            x = x.astype(F32)
            moves = [columns_moved(x, depth, first, last), x, columns_moved(x, -depth, first, last)]
            t = [sum(moves[b] * tap[pl.ds(3 * a + b, 1), lanes] for b in range(3)) for a in range(3)]
            none = jnp.zeros((step, LANES), F32)
            c = t[1] + jnp.concatenate([none, t[0][:-step]], 0) + jnp.concatenate([t[2][step:], none], 0)
            conv_out[:, lanes] = c.astype(BF)
            cact_out[:, lanes] = silu(c).astype(BF)

        chunks(ch // LANES, conv)
        for c in range(n):
            e = 0.0
            for q in range(n):
                cut = slice(q * share, (q + 1) * share)
                e = e + dot(cact_out[:, cut], w[c, share : 2 * share, cut])
            exp[:, c * share : (c + 1) * share] = e

        def norm(i, carry):
            for t in range(3):
                at = pl.ds(i * 48 + 16 * t, 16)
                e = exp[at, :]
                mean = jnp.mean(e, -1, keepdims=True)
                square = jnp.mean(e * e, -1, keepdims=True)
                std = lax.rsqrt(square - mean * mean + EPS)
                nrm = (e - mean) * std
                norm_out[at, :] = nrm.astype(BF)
                std_out[at, :] = std
                low_out[at, :] = (wide_ref[at, :] + silu(nrm * gain)).astype(BF)
            return carry

        for i in range(total // 48):
            norm(i, 0)

    narrow = shape((total, ch), BF)
    return call(
        kernel,
        grid=(1,),
        prefetch=1,
        ins=[(a, None, None) for a in (*moved, far(weights), taps)],
        outs=[(s, None, None) for s in (narrow, narrow, narrow, narrow, narrow, narrow, shape((total, 1), F32), narrow)],
        scratch=[pltpu.VMEM((total, ch), F32)] * 3,
        name="post_forward",
    )(source)


def readout_backward(source, low, readout, cots):
    total, ch = low.shape
    n, out_share = len(cots), cots[0].shape[1]

    def kernel(src, low_ref, ro, *rest):
        cot, grad = rest[:n], rest[n]
        k = pl.program_id(0)
        logits = dot(low_ref[...], ro[...])
        slope = gelu_parts(logits)[1]
        for i in range(n):

            @pl.when(k == i)
            def _():
                piece = (cot[i][...].astype(F32) * slope).astype(BF)
                term = dot(piece, ro[...], NT)
                grad[...] = term if i == 0 else grad[...] + term

    return call(
        kernel,
        grid=(n,),
        prefetch=1,
        ins=[(low, None, None), (far(readout), (ch, out_share), lambda k, s: (0, s[k]))] + [(c, None, None) for c in cots],
        outs=[(shape((total, ch), F32), None, None)],
        name="readout_backward",
    )(source)[0]


def post_backward(source, refined_grad, weights, taps, act, red, conv, nrm, std, pool):
    total, ch = act.shape
    n = weights.shape[0]
    share = ch // n
    rows = total // n
    depth = total // (pool * pool)

    def kernel(src, rg, w, tap, act_ref, red_ref, conv_ref, norm_ref, std_ref, exp_out, redg_out, taps_out, gain_out, *rest):
        back_out, (grad, cgrad) = rest[:n], rest[n:]
        gain = gain_row(w, n, share)

        def norm(i, total_gain):
            for t in range(3):
                at = pl.ds(i * 48 + 16 * t, 16)
                nm = norm_ref[at, :].astype(F32)
                ng = rg[at, :] * silu_slope(nm * gain)
                sc = ng * gain
                one = jnp.mean(sc, -1, keepdims=True)
                two = jnp.mean(sc * nm, -1, keepdims=True)
                exp_out[at, :] = (std_ref[at, :] * (sc - one - nm * two)).astype(BF)
                g = ng * nm
                total_gain = total_gain + g[:8] + g[8:]
            return total_gain

        gains = jnp.zeros((8, ch), F32)
        for i in range(total // 48):
            gains = norm(i, gains)
        gain_out[...] = gains
        for q in range(n):
            cut = slice(q * share, (q + 1) * share)
            cg = 0.0
            for c in range(n):
                cg = cg + dot(exp_out[:, c * share : (c + 1) * share], w[c, share : 2 * share, cut], NT)
            cgrad[:, cut] = cg
        first, last = edge_masks(total, pool, depth)
        step = pool * depth

        def back(lanes):
            g = (cgrad[:, lanes] * silu_slope(conv_ref[:, lanes].astype(F32))).astype(BF).astype(F32)
            x = act_ref[:, lanes].astype(F32)
            moves = [columns_moved(g, -depth, first, last), g, columns_moved(g, depth, first, last)]
            none = jnp.zeros((step, LANES), F32)
            xs = [
                jnp.concatenate([none, x[:-step]], 0),
                x,
                jnp.concatenate([x[step:], none], 0),
            ]
            for a in range(3):
                for b in range(3):
                    prod = xs[a] * moves[b]
                    taps_out[3 * a + b, :, lanes] = jnp.sum(prod.reshape(total // 8, 8, LANES), 0)
            t = [sum(moves[b] * tap[pl.ds(3 * a + b, 1), lanes] for b in range(3)) for a in range(3)]
            d = t[1] + jnp.concatenate([t[0][step:], none], 0) + jnp.concatenate([none, t[2][:-step]], 0)
            redg_out[:, lanes] = (d * silu_slope(red_ref[:, lanes].astype(F32))).astype(BF)

        chunks(ch // LANES, back)
        for c in range(n):
            cut = slice(c * share, (c + 1) * share)
            grad[:, cut] = rg[:, cut] + dot(redg_out[...], w[c, :share], NT)
        for r in range(n):
            at = pl.ds(pl.multiple_of(src[r] * rows, 8), rows)
            back_out[r][...] = grad[at, :].astype(BF)

    return call(
        kernel,
        grid=(1,),
        prefetch=1,
        ins=[(a, None, None) for a in (refined_grad, far(weights), taps, act, red, conv, nrm, std)],
        outs=[
            (s, None, None)
            for s in (
                shape((total, ch), BF),
                shape((total, ch), BF),
                shape((9, 8, ch), F32),
                shape((8, ch), F32),
                *[shape((rows, ch), BF)] * n,
            )
        ],
        scratch=[pltpu.VMEM((total, ch), F32), pltpu.VMEM((total, ch), F32)],
        name="post_backward",
    )(source)


def cotangent_by_image(cotangent, select, pairs):
    rows, width = cotangent.shape
    size = select.shape[0]
    each = size // pairs
    per = 3

    def kernel(x, sel, *outs):
        for q in range(per):
            y = dot(sel[...], x[pl.ds(q * size, size), :]).astype(BF)
            for s in range(pairs):
                outs[s][pl.ds(q * each, each), :] = y[s * each : (s + 1) * each]

    return call(
        kernel,
        grid=(rows // (per * size),),
        ins=[(far(cotangent), (per * size, width), lambda i: (i, 0)), (select, None, None)],
        outs=[(shape((rows // pairs, width), BF), (per * each, width), lambda i: (i, 0))] * pairs,
        name="cotangent_by_image",
    )()


def token_block(chan, source, pair_of, low, place, readout, cotangent):
    pairs, (rows, ch) = len(low), low[0].shape
    width = cotangent[0].shape[1]
    size = place.shape[0]
    each = size // pairs
    per = 3
    block = per * each

    def kernel(chan_ref, src, pair, *refs):
        lows, cots, (place_ref, ro, tok_out, piece_out, cot) = refs[:pairs], refs[pairs : 2 * pairs], refs[2 * pairs :]
        for k in range(pairs):
            cot[pair[k]] = cots[k][...]
        logits = dot(jnp.concatenate([v[...] for v in lows], 0), ro[...])
        value, slope = gelu_parts(logits)
        value = value.astype(BF)
        for k in range(pairs):
            piece_out[k] = (cot[src[k]].astype(F32) * slope[k * block : (k + 1) * block]).astype(BF)
        for q in range(per):
            x = jnp.concatenate([value[k * block + q * each : k * block + (q + 1) * each] for k in range(pairs)], 0)
            tok_out[pl.ds(q * size, size), :] = dot(place_ref[...], x).astype(BF)

    rows_at = lambda i, c, s, p: (i, 0)
    return call(
        kernel,
        grid=(rows // block,),
        prefetch=3,
        ins=[
            *[(v, (block, ch), rows_at) for v in low],
            *[(v, (block, width), rows_at) for v in cotangent],
            (place, None, None),
            (far(readout), (ch, width), lambda i, c, s, p: (0, c[0])),
        ],
        outs=[
            (shape((pairs * rows, width), BF), (pairs * block, width), rows_at),
            (shape((pairs, rows, width), BF), (pairs, block, width), lambda i, c, s, p: (0, i, 0)),
        ],
        scratch=[pltpu.VMEM((pairs, block, width), BF)],
        name="token_block",
    )(chan, source, pair_of)


def pre_backward(order, returned, spread_up, nrm, std, gain, conv, pre_expand):
    slots, cells, ch = nrm.shape
    n = order.shape[0]
    part = slots // n
    wide = 24
    rows = part * cells

    def kernel(order_ref, *refs):
        ret, refs = refs[:n], refs[n:]
        up, norm_ref, std_ref, gn, conv_ref, we, exp_out, conv_grad_out, top_out, bottom_out, gain_out, grad, cgrad = refs
        k = pl.program_id(0)
        for i in range(n):

            @pl.when(k == i)
            def _():
                grad[...] = dot(up[...], ret[i][...])

        def norm(i, total_gain):
            u, j = i // (cells // 48), i % (cells // 48)
            for t in range(3):
                at = pl.ds(j * 48 + 16 * t, 16)
                nm = norm_ref[u, at, :].astype(F32)
                ng = grad[pl.ds(i * 48 + 16 * t, 16), :] * silu_slope(nm * gn[...])
                sc = ng * gn[...]
                one = jnp.mean(sc, -1, keepdims=True)
                two = jnp.mean(sc * nm, -1, keepdims=True)
                exp_out[u, at, :] = (std_ref[u, at, :] * (sc - one - nm * two)).astype(BF)
                g = ng * nm
                total_gain = total_gain + g[:8] + g[8:]
            return total_gain

        gains = jnp.zeros((8, ch), F32)
        for i in range(rows // 48):
            gains = norm(i, gains)

        @pl.when(k == 0)
        def _():
            gain_out[...] = gains

        @pl.when(k > 0)
        def _():
            gain_out[...] += gains

        cgrad[...] = dot(exp_out[...].reshape(rows, ch), we[...], NT)
        for u in range(part):

            def slope(lanes):
                g = cgrad[pl.ds(u * cells, cells), lanes] * silu_slope(conv_ref[u, :, lanes].astype(F32))
                conv_grad_out[u, :, lanes] = g.astype(BF)
                top_out[u, :, lanes] = g[:wide].astype(BF)
                bottom_out[u, :, lanes] = g[cells - wide :].astype(BF)

            chunks(ch // LANES, slope)

    by_order = lambda k, order: (order[k], 0, 0)
    whole = (part, cells, ch)
    edge = (part, wide, ch)
    return call(
        kernel,
        grid=(n,),
        prefetch=1,
        ins=[
            *[(r, None, None) for r in returned],
            (spread_up, None, None),
            (far(nrm), whole, by_order),
            (far(std), (part, cells, 1), by_order),
            (gain, None, None),
            (far(conv), whole, by_order),
            (far(pre_expand), None, None),
        ],
        outs=[
            (shape((slots, cells, ch), BF), whole, by_order),
            (shape((slots, cells, ch), BF), whole, by_order),
            (shape((slots, wide, ch), BF), edge, by_order),
            (shape((slots, wide, ch), BF), edge, by_order),
            (shape((8, ch), F32), None, None),
        ],
        scratch=[pltpu.VMEM((rows, ch), F32), pltpu.VMEM((rows, ch), F32)],
        name="pre_backward",
    )(order)


def pre_conv_backward(conv_grad, above, below, reduced, taps):
    slots, cells, ch = reduced.shape
    wide = above.shape[1]
    high = cells // wide

    def kernel(cg, up, down, red, tap, redg_out, taps_out):
        step = pl.program_id(0)
        first, last = edge_masks(wide, wide, 1)

        @pl.when(step == 0)
        def _():
            taps_out[...] = jnp.zeros_like(taps_out)

        def back(lanes):
            w = [tap[pl.ds(i, 1), lanes] for i in range(9)]
            mid = cg[0, :, lanes].astype(F32)
            rows = [up[0, :, lanes].astype(F32)]
            rows += [mid[i * wide : (i + 1) * wide] for i in range(high)]
            rows += [down[0, :, lanes].astype(F32)]
            whole = red[0, :, lanes].astype(F32)
            v = [whole[i * wide : (i + 1) * wide] for i in range(high)]
            s = [sigmoid(t) for t in v]
            x = [(a * b).astype(BF).astype(F32) for a, b in zip(v, s)]
            d = [0.0] * high
            sums = [0.0] * 9
            for p in range(high + 2):
                g = rows[p]
                moves = [columns_moved(g, -1, first, last), g, columns_moved(g, 1, first, last)]
                for a in range(3):
                    i = p - 1 + a - 1
                    if 0 <= i < high:
                        for b in range(3):
                            d[i] = d[i] + moves[b] * w[3 * a + b]
                            prod = x[i] * moves[b]
                            sums[3 * a + b] = sums[3 * a + b] + (prod[:8] + prod[8:16] + prod[16:])
            out = [d[i] * (s[i] * (1.0 + v[i] * (1.0 - s[i]))) for i in range(high)]
            redg_out[0, :, lanes] = jnp.concatenate(out, 0).astype(BF)
            for i in range(9):
                taps_out[i, :, lanes] += sums[i]

        chunks(ch // LANES, back)

    image = lambda i: (i, 0, 0)
    return call(
        kernel,
        grid=(slots,),
        ins=[
            (conv_grad, (1, cells, ch), image),
            (above, (1, wide, ch), image),
            (below, (1, wide, ch), image),
            (far(reduced), (1, cells, ch), image),
            (taps, None, None),
        ],
        outs=[
            (shape((slots, cells, ch), BF), (1, cells, ch), image),
            (shape((9, 8, ch), F32), None, None),
        ],
        name="pre_conv_backward",
    )()


def feature_backward(order, reduced_grad, pre_reduce, returned, spread_up):
    slots, cells, ch = reduced_grad.shape
    n = order.shape[0]
    part = slots // n

    def kernel(order_ref, rg, wr, up, *refs):
        ret, out = refs[:n], refs[n]
        k = pl.program_id(0)
        for i in range(n):

            @pl.when(k == i)
            def _():
                out[...] = dot(up[...], ret[i][...]).reshape(part, cells, ch)

        out[...] += dot(rg[...].reshape(part * cells, ch), wr[...], NT).reshape(part, cells, ch)

    by_order = lambda k, order: (order[k], 0, 0)
    whole = (part, cells, ch)
    return call(
        kernel,
        grid=(n,),
        prefetch=1,
        ins=[
            (reduced_grad, whole, by_order),
            (far(pre_reduce), None, None),
            (spread_up, None, None),
            *[(r, None, None) for r in returned],
        ],
        outs=[(shape((slots, cells, ch), F32), whole, by_order)],
        name="feature_backward",
    )(order)[0]


def post_weight_grads(flat, reduced_grad, act, expanded_grad, n):
    total, ch = flat.shape
    share = ch // n
    rows = share // 8

    def kernel(x, g, a, e, out):
        for c in range(n):
            cut = slice(c * share, (c + 1) * share)
            v = dot(x[:, cut], g[...], TN).astype(BF)
            for d in range(8):
                out[d, c, :, :ch] = v[d * rows : (d + 1) * rows]
            for q in range(n):
                v = dot(a[:, q * share : (q + 1) * share], e[:, cut], TN).astype(BF)
                for d in range(8):
                    out[d, c, :, ch + q * share : ch + (q + 1) * share] = v[d * rows : (d + 1) * rows]

    return call(
        kernel,
        grid=(1,),
        ins=[(v, None, None) for v in (flat, reduced_grad, act, expanded_grad)],
        outs=[(far((8, n, rows, 2 * ch), BF), None, None)],
        name="post_weight_grads",
    )()[0]


def readout_weight_grad(low, piece, n):
    pairs, total, width = piece.shape
    ch = low[0].shape[1]
    share = ch // n
    parts = 8
    rows = share // parts

    def kernel(*refs):
        x, (g, out) = refs[:pairs], refs[pairs:]
        x = jnp.concatenate([v[...] for v in x], 0)
        v = dot(x, g[...].reshape(pairs * total, width), TN).astype(BF)
        for d in range(parts):
            out[d, 0] = v[d * rows : (d + 1) * rows]

    return call(
        kernel,
        grid=(n,),
        ins=[(v, (total, share), lambda c: (0, c)) for v in low] + [(piece, None, None)],
        outs=[(far((parts, n, rows, width), BF), (parts, 1, rows, width), lambda c: (0, c, 0, 0))],
        name="readout_weight_grad",
    )()[0]


def cross(n, k):
    return [(a * n + b, ((b + k) % n) * n + a) for a in range(n) for b in range(n)]


def turn(n, k):
    return [(i, (i + k) % n) for i in range(n)]


def other_core(values):
    return lax.ppermute(values, "core", [(0, 1), (1, 0)])


def small_rows(*grads):
    ch = grads[0].shape[-1]
    counts = [g.shape[0] if g.ndim == 3 else 1 for g in grads]
    per = ch // LANES

    def kernel(*refs):
        out = refs[-1]
        at = 0
        for ref, count in zip(refs, counts):
            for i in range(count):
                v = jnp.sum(ref[i] if len(ref.shape) == 3 else ref[...], 0, keepdims=True)
                for q in range(per):
                    out[pl.ds(at, 1), :] = v[:, q * LANES : (q + 1) * LANES]
                    at += 1

    return call(
        kernel,
        grid=(1,),
        ins=[(g, None, None) for g in grads],
        outs=[(shape((sum(counts) * per, LANES), F32), None, None)],
        name="small_rows",
    )()[0]


def join_halves(core, mine, theirs, small, their_small, parts):
    rows, ch = mine[0].shape
    half = rows // 2
    width = len(mine) * ch + LANES
    count = small.shape[0]
    m = len(mine)
    steps = 2
    block = half // steps

    def kernel(core_ref, *refs):
        own, got = refs[:m], refs[m : 2 * m]
        sm, got_sm, out = refs[2 * m :]
        for i in range(m):
            out[:, i * ch : (i + 1) * ch] = (own[i][...].astype(F32) + got[i][...].astype(F32)).astype(BF)
        first = ((core_ref[0] == 0) & (pl.program_id(0) == 0)).astype(F32)
        total = (sm[...] + got_sm[...]) * first
        pad = jnp.zeros((block - count, LANES), F32)
        out[:, m * ch :] = jnp.concatenate([total, pad], 0).astype(BF)

    return call(
        kernel,
        grid=(steps,),
        prefetch=1,
        ins=[(v, (block, ch), lambda i, c: (c[0] * steps + i, 0)) for v in mine]
        + [(v, (block, ch), lambda i, c: (i, 0)) for v in theirs]
        + [(v, None, None) for v in (small, their_small)],
        outs=[(far((half, width), BF), (block, width), lambda i, c: (i, 0))],
        name="join_halves",
    )(core)[0].reshape(parts, half // parts, width)


def sum_and_copy(blocks):
    parts, rows, width = blocks.shape

    def kernel(x, out):
        def cut(lanes):
            total = jnp.sum(x[:, :, lanes].astype(F32), 0).astype(BF)
            out[:, :, lanes] = jnp.broadcast_to(total[None], (parts, rows, LANES))

        chunks(width // LANES, cut)

    return call(
        kernel,
        grid=(1,),
        ins=[(blocks, None, None)],
        outs=[(far(blocks.shape, BF), None, None)],
        name="sum_and_copy",
    )()[0]


def split_rows(to_row, post, read):
    n, rows, width = post.shape
    ch = read.shape[2]
    each = rows // n

    def kernel(to, a, b, *outs):
        outs, wide = outs[:n], outs[n]
        wide[:, :, :width] = a[...].astype(F32)
        wide[:, :, width:] = b[...].astype(F32)
        for k in range(n):
            outs[k][...] = wide[:, pl.ds(pl.multiple_of(to[k] * each, 8), each), :].astype(BF)

    return call(
        kernel,
        grid=(1,),
        prefetch=1,
        ins=[(post, None, None), (read, None, None)],
        outs=[(shape((n, each, width + ch), BF), None, None)] * n,
        scratch=[pltpu.VMEM((n, rows, width + ch), F32)],
        name="split_rows",
    )(to_row)


def sum_rows(to_chan, blocks):
    n, rows, width = blocks[0].shape

    def kernel(to, *refs):
        outs = refs[n:]
        for k in range(n):
            outs[k][...] = sum(r[to[k]].astype(F32) for r in refs[:n]).astype(BF)

    return call(
        kernel,
        grid=(1,),
        prefetch=1,
        ins=[(b, None, None) for b in blocks],
        outs=[(shape((rows, width), BF), None, None)] * n,
        name="sum_rows",
    )(to_chan)


def join_chan(from_chan, blocks):
    n = len(blocks)
    rows, width = blocks[0].shape
    ch = width // 3

    def kernel(src, *refs):
        out = refs[n]
        out[:, : 2 * ch] = sum(r[:, : 2 * ch].astype(F32) for r in refs[:n]).astype(BF)
        for k in range(n):
            at = pl.multiple_of(2 * ch + src[k] * ch, LANES)
            out[:, pl.ds(at, ch)] = refs[k][:, 2 * ch :]

    return call(
        kernel,
        grid=(1,),
        prefetch=1,
        ins=[(b, None, None) for b in blocks],
        outs=[(far((rows, 2 * ch + n * ch), BF), None, None)],
        name="join_chan",
    )(from_chan)[0]


def finish_pre(place, half_rows, ch, earlier=()):
    half, width = half_rows.shape
    m = (width - LANES) // ch
    steps = 4
    block = half // steps

    def kernel(place_ref, x, *outs):
        outs = outs[len(earlier) :]
        for i in range(m):
            outs[i][...] = x[:, i * ch : (i + 1) * ch].astype(F32)
        outs[m][...] = x[:, m * ch :].astype(F32)

    return call(
        kernel,
        grid=(steps,),
        prefetch=1,
        ins=[(half_rows, (block, width), lambda i, c: (i, 0))],
        outs=[(shape((2 * half, ch), F32), (block, ch), lambda i, c: (c[0] * steps + i, 0)) for _ in range(m)]
        + [(shape((half, LANES), F32), (block, LANES), lambda i, c: (i, 0))],
        aliased=earlier,
        name="finish_pre",
    )(place)


def finish_post(place, gathered, n, earlier=()):
    groups, per, width = gathered.shape
    share = 2 * groups * per
    ch = width // (n + 2)

    def kernel(place_ref, x, *outs):
        reduce_out, expand_out, read_out = outs[len(earlier) :]
        reduce_out[...] = x[0, :, :ch].astype(F32)
        for q in range(n):
            expand_out[q] = x[0, :, ch + q * share : ch + (q + 1) * share].astype(F32)
        read_out[...] = x[0, :, 2 * ch :].astype(F32)

    at = lambda i, c: (2 * i + c[0], 0)
    return call(
        kernel,
        grid=(groups,),
        prefetch=1,
        ins=[(gathered, (1, per, width), lambda i, c: (i, 0, 0))],
        outs=[
            (shape((share, ch), F32), (per, ch), at),
            (shape((n, share, share), F32), (n, per, share), lambda i, c: (0, 2 * i + c[0], 0)),
            (shape((share, n * ch), F32), (per, n * ch), at),
        ],
        aliased=earlier,
        name="finish_post",
    )(place)


def after(values, *earlier):
    return lax.optimization_barrier((values, *earlier))[0]


def pool_matrix(part, high, wide):
    half = wide // 2
    m = np.zeros((high // 2 * half * part, part * (high // 2) * wide), np.float32)
    for u in range(part):
        for i in range(high // 2):
            for j in range(wide):
                m[(i * half + j // 2) * part + u, (u * (high // 2) + i) * wide + j] = 0.25
    return m


def spread_matrix(part, high, wide):
    half = wide // 2
    m = np.zeros((part * high * wide, high // 2 * half * part), np.float32)
    for u in range(part):
        for i in range(high):
            for j in range(wide):
                m[(u * high + i) * wide + j, ((i // 2) * half + j // 2) * part + u] = 0.25
    return m


def body(features, counts, pre_reduce, pre_conv, pre_expand, pre_gain, post_reduce, post_conv, post_expand, post_gain, readout, cotangent):
    n = lax.axis_size("chan")
    row = lax.axis_index("rows").astype(jnp.int32)
    chan = lax.axis_index("chan").astype(jnp.int32)
    core = lax.axis_index("core").astype(jnp.int32)
    ch = pre_reduce.shape[0]
    slots, high, wide = features.shape[0], features.shape[1], features.shape[2]
    part = slots // n
    cells = high * wide
    pool = wide // 2
    share = ch // n
    out_share = cotangent.shape[3]
    steps = jnp.arange(n, dtype=jnp.int32)
    order = (row + steps) % n
    source = (row - steps) % n
    pair_of = (chan + steps) % n
    rank = jnp.full((1,), chan, jnp.int32)
    core_at = jnp.full((1,), core, jnp.int32)
    pre_taps = pre_conv.astype(F32).reshape(9, ch)
    post_taps = post_conv.astype(F32).reshape(9, ch)
    pre_gain_row = pre_gain.reshape(1, ch)
    pool_m = jnp.asarray(pool_matrix(part, high, wide), BF)
    up_m = jnp.asarray(spread_matrix(part, high, wide), BF)

    ends = n - 1
    down_pairs = [(i, i + 1) for i in range(ends)]
    up_pairs = [(i + 1, i) for i in range(ends)]
    above = lax.ppermute(features[:, -1], "rows", down_pairs)
    below = lax.ppermute(features[:, 0], "rows", up_pairs)
    gain_hi = post_gain.astype(BF)
    gain_lo = (post_gain - gain_hi.astype(F32)).astype(BF)
    gain_row = jnp.concatenate([gain_hi, gain_lo, jnp.zeros((ch - 2 * share,), BF)])[None]
    square = post_expand.reshape(n, share, share)
    shards = jnp.concatenate(
        [post_reduce, jnp.concatenate([square[q] for q in range(n)], axis=1), jnp.pad(gain_row, ((0, 63), (0, 0)))], axis=0
    )
    shard = lax.dynamic_index_in_dim(shards.reshape(2, -1, ch), core, 0, keepdims=False)
    full = lax.all_gather(shard, ("chan", "core"), axis=0, tiled=True)
    full = full.reshape(n, 2 * share + 64, ch)
    flat_features = features.reshape(slots * cells, ch)
    live = (jnp.arange(SLOT)[None, :] < counts[:, None]).astype(F32).reshape(slots)
    size, each = 16 * slots, 16 * part
    at = lax.broadcasted_iota(jnp.int32, (size, size), 0)
    column = lax.broadcasted_iota(jnp.int32, (size, size), 1)
    wanted = (at % each) // part * slots + part * ((chan + at // each) % n) + at % part
    select = jnp.where(column == wanted, jnp.tile(live, 16)[None, :], 0.0).astype(BF)
    wanted = (column % each) // part * slots + part * ((row - column // each) % n) + column % part
    place = jnp.where(at == wanted, 1.0, 0.0).astype(BF)
    cot_rows = cotangent.transpose(1, 2, 0, 3).reshape(-1, out_share)
    sends = cotangent_by_image(cot_rows, select, n)
    away = after(sends, above, below)
    cots = [lax.ppermute(away[k], ("rows", "chan"), cross(n, k)) for k in range(n)]

    reduced, convolved, convolved_act, normal_pre, pre_std, *pooled = pre_forward(
        order, above, below, features, pre_reduce, pre_taps, pre_expand, pre_gain_row, pool_m
    )

    pooled = after(pooled, cots)
    moved = [pooled[0]] + [lax.ppermute(pooled[k], "rows", turn(n, k)) for k in range(1, n)]
    flat, post_reduced, post_act, post_convolved, post_cact, post_normal, post_std, low = post_forward(
        source, moved, full, post_taps, pool
    )
    lows = [low] + [lax.ppermute(low, "chan", turn(n, k)) for k in range(1, n)]
    refined_grad = readout_backward(source, low, readout, cots)
    post_expanded_grad, post_reduced_grad, post_taps_grad, post_gain_grad, *back = post_backward(
        source, refined_grad, full, post_taps, post_act, post_reduced, post_convolved, post_normal, post_std, pool
    )

    returned = [back[0]] + [lax.ppermute(back[k], "rows", turn(n, -k)) for k in range(1, n)]

    flat = after(flat, lows)
    load = post_weight_grads(flat, post_reduced_grad, post_cact, post_expanded_grad, n)

    post_sum = lax.psum_scatter(load, ("x", "core"), scatter_dimension=0, tiled=False)

    stacked = jnp.stack(after(lows, load, returned))
    lows = [lax.dynamic_index_in_dim(stacked, (chan - row - k) % n, 0, keepdims=False) for k in range(n)]
    lows = [lows[0]] + [lax.ppermute(lows[k], "rows", turn(n, k)) for k in range(1, n)]

    expanded_grad, convolved_grad, top, bottom, pre_gain_grad = pre_backward(
        order, returned, up_m, normal_pre, pre_std, pre_gain_row, convolved, pre_expand
    )
    top, bottom, lows[1], lows[3] = lax.optimization_barrier((top, bottom, lows[1], lows[3]))
    grad_above = lax.ppermute(bottom, "rows", down_pairs)
    grad_below = lax.ppermute(top, "rows", up_pairs)
    act_rows = after(convolved_act, bottom).reshape(-1, ch)
    pre_expand_grad = dot(act_rows, expanded_grad.reshape(-1, ch), TN).astype(BF)

    lows = after(lows, pre_expand_grad)
    tokens, piece = token_block(rank, source, pair_of, lows, place, readout, sends)
    read_load = readout_weight_grad(lows, after(piece, grad_above, grad_below), n)
    tokens = tokens.reshape(pool, pool, slots, out_share).transpose(2, 0, 1, 3)
    convolved_grad = after(convolved_grad, read_load)
    read_sum = lax.psum_scatter(after(read_load, post_sum), ("x", "core"), scatter_dimension=0, tiled=False)

    reduced_grad, pre_taps_grad = pre_conv_backward(convolved_grad, grad_above, grad_below, reduced, pre_taps)
    small = small_rows(pre_taps_grad, pre_gain_grad, post_taps_grad, post_gain_grad)
    pre_reduce_grad = dot(after(flat_features, small), reduced_grad.reshape(-1, ch), TN).astype(BF)

    chips = ("x", "rows", "chan")
    mine = [pre_reduce_grad, pre_expand_grad]
    theirs = [other_core(lax.dynamic_index_in_dim(g.reshape(2, ch // 2, ch), 1 - core, 0, keepdims=False)) for g in mine]
    load = join_halves(core_at, mine, theirs, small, other_core(small), 64)
    pieces = lax.all_to_all(load, chips, 0, 0, tiled=False)
    feature_grad = feature_backward(order, after(reduced_grad, load), pre_reduce, returned, up_m).reshape(features.shape)

    post_sum, read_sum = lax.optimization_barrier((post_sum, read_sum, feature_grad))[:2]
    blocks = split_rows(order, post_sum, read_sum)
    blocks = [blocks[0]] + [lax.ppermute(blocks[k], "rows", turn(n, k)) for k in range(1, n)]
    blocks = sum_rows(pair_of, blocks)
    blocks = [blocks[0]] + [lax.ppermute(blocks[k], "chan", turn(n, k)) for k in range(1, n)]
    rest = join_chan((chan - steps) % n, blocks)
    load = sum_and_copy(after(pieces, rest))
    rest = lax.all_gather(rest, ("x", "rows"), axis=0, tiled=False).reshape(4, share // 8, -1)
    load_all = lax.all_to_all(load, chips, 0, 0, tiled=False).reshape(ch // 2, -1)

    def finish(kernel, values, *sizes):
        theirs = other_core(values)
        own = kernel(core_at, values, *sizes)
        theirs = after(theirs, *own)
        return own, theirs

    own, theirs = finish(finish_post, rest, n)
    load_all = after(load_all, *own)
    post_reduce_out, post_expand_out, readout_out = finish_post(1 - core_at, theirs, n, earlier=tuple(own))
    own, theirs = finish(finish_pre, load_all, ch)
    pre_reduce_out, pre_expand_out, small_their = finish_pre(1 - core_at, theirs, ch, earlier=tuple(own[:2]))
    small_out = jnp.where(core == 0, own[2], small_their)
    per = ch // LANES
    cut = [0, 9 * per, 10 * per, 19 * per, 20 * per]
    pre_conv_out, pre_gain_out, post_conv_out, post_gain_out = [small_out[a:b] for a, b in zip(cut, cut[1:])]
    return (
        tokens,
        feature_grad,
        pre_reduce_out,
        pre_conv_out.reshape(3, 3, ch),
        pre_expand_out,
        pre_gain_out.reshape(ch),
        post_reduce_out,
        post_conv_out.reshape(3, 3, ch),
        post_expand_out.reshape(ch, share),
        lax.dynamic_slice_in_dim(post_gain_out.reshape(ch), chan * share, share, 0),
        readout_out,
    )


def solution(mesh):
    grid = Mesh(mesh.devices.reshape(4, 2, 4, 4), ("x", "core", "rows", "chan"))
    images = P(("x", "core", "chan"), "rows", None, None)
    grids = P(("x", "core", "rows"), None, None, "chan")
    return jax.shard_map(
        body,
        mesh=grid,
        in_specs=(
            images,
            P(("x", "core", "rows")),
            P(),
            P(),
            P(),
            P(),
            P("chan", None),
            P(),
            P(None, "chan"),
            P("chan"),
            P(),
            grids,
        ),
        out_specs=(grids, images, P(), P(), P(), P(), P("chan", None), P(), P(None, "chan"), P("chan"), P("chan", None)),
        check_vma=False,
    )
```

```python
import functools

import jax
import jax.numpy as jnp
import numpy as np
from jax import lax
from jax.experimental import pallas as pl
from jax.experimental.pallas import tpu as pltpu
from jax.sharding import Mesh, PartitionSpec as P

SLOT = 4
EPS = 1e-06
BF = jnp.bfloat16
F32 = jnp.float32
LANES = 128
VMEM_LIMIT = 20 * 1024 * 1024
NN = ((1,), (0,))
NT = ((1,), (1,))
TN = ((0,), (0,))


def dot(a, b, dims=NN):
    return lax.dot_general(a, b, (dims, ((), ())), preferred_element_type=F32)


def sigmoid(v):
    return 0.5 * jnp.tanh(0.5 * v) + 0.5


def silu(v):
    return v * sigmoid(v)


def silu_slope(v):
    s = sigmoid(v)
    return s * (1.0 + v * (1.0 - s))


def gelu_parts(v):
    c = 0.7978845608028654
    square = v * v
    t = jnp.tanh(v * (c + (c * 0.044715) * square))
    half = 0.5 * (1.0 + t)
    slope = half + 0.5 * v * (1.0 - t * t) * (c + (3.0 * c * 0.044715) * square)
    return v * half, slope


def chunks(count, body, width=LANES):
    for i in range(count):
        body(pl.ds(i * width, width))


def call(kernel, *, grid, ins, outs, scratch=(), prefetch=0, aliased=(), cost=1, name):
    def spec(shape, block, index):
        if block is None:
            block, index = shape, lambda *_: (0,) * len(shape)
        return pl.BlockSpec(block, index)

    arrays = [i[0] for i in ins] + list(aliased)
    in_specs = [spec(a.shape, b, m) for a, b, m in ins] + [pl.BlockSpec(memory_space=pl.ANY)] * len(aliased)
    out_specs = [spec(s.shape, b, m) for s, b, m in outs]

    def run(*scalars):
        return pl.pallas_call(
            kernel,
            grid_spec=pltpu.PrefetchScalarGridSpec(
                num_scalar_prefetch=prefetch,
                grid=grid,
                in_specs=in_specs,
                out_specs=out_specs,
                scratch_shapes=list(scratch),
            ),
            out_shape=[s[0] for s in outs],
            compiler_params=pltpu.CompilerParams(
                dimension_semantics=("arbitrary",) * len(grid), vmem_limit_bytes=VMEM_LIMIT
            ),
            input_output_aliases={prefetch + len(ins) + i: i for i in range(len(aliased))},
            cost_estimate=pl.CostEstimate(flops=cost, bytes_accessed=1, transcendentals=0),
            name=name,
        )(*scalars, *arrays)

    return run


def shape(dims, dtype):
    return jax.ShapeDtypeStruct(dims, dtype)


def far(values, dtype=None):
    if dtype is None:
        return pltpu.with_memory_space_constraint(values, pltpu.HBM)
    return pltpu.HBM(values, dtype)


def columns_moved(t, by, first, last):
    rows = t.shape[0]
    return pltpu.roll(t, by % rows, 0) * (first if by > 0 else last)


def edge_masks(rows, width, depth):
    at = lax.broadcasted_iota(jnp.int32, (rows, LANES), 0) % (width * depth)
    return (at >= depth).astype(F32), (at < (width - 1) * depth).astype(F32)


def pre_forward(order, above, below, features, pre_reduce, taps, pre_expand, gain, pool):
    slots, high, wide, ch = features.shape
    cells = high * wide
    n = order.shape[0]
    part = slots // n
    rows_all = part * cells

    def kernel(order_ref, up_ref, down_ref, feat, wr, tap, we, gn, pool_ref, red_out, conv_out, act_out, norm_out, std_out, *rest):
        pooled_out, (red, halo, exp, sums) = rest[:n], rest[n:]
        k = pl.program_id(0)
        for side, ref in enumerate((up_ref, down_ref)):
            halo[side] = dot(ref[...].reshape(part * wide, ch), wr[...]).reshape(part, wide, ch)
        red[...] = dot(feat[...].reshape(rows_all, ch), wr[...]).reshape(part, cells, ch)
        red_out[...] = red[...].astype(BF)
        first, last = edge_masks(wide, wide, 1)
        for u in range(part):

            def conv(lanes):
                w = [tap[pl.ds(i, 1), lanes] for i in range(9)]
                rows = [halo[0, u, :, lanes]]
                rows += [red[u, pl.ds(i * wide, wide), lanes] for i in range(high)]
                rows += [halo[1, u, :, lanes]]
                rows = [silu(r).astype(BF).astype(F32) for r in rows]
                out = []
                for i in range(high):
                    t = [sum(rows[i + a] * w[3 * a + b] for a in range(3)) for b in range(3)]
                    out.append(t[1] + columns_moved(t[0], 1, first, last) + columns_moved(t[2], -1, first, last))
                conv_out[u, :, lanes] = jnp.concatenate(out, 0).astype(BF)
                act_out[u, :, lanes] = jnp.concatenate([silu(c) for c in out], 0).astype(BF)

            chunks(ch // LANES, conv)

        exp[...] = dot(act_out[...].reshape(rows_all, ch), we[...])

        def norm(p, carry):
            u, i = p // (high // 2), p % (high // 2)
            tiles = wide // 8
            f = [feat[u, 2 * i + half].astype(F32) for half in range(2)]
            nrms, blends = [], []
            for t in range(2 * tiles):
                e = exp[pl.ds(p * 2 * wide + 8 * t, 8), :]
                mean = jnp.mean(e, -1, keepdims=True)
                square = jnp.mean(e * e, -1, keepdims=True)
                std = lax.rsqrt(square - mean * mean + EPS)
                nrm = (e - mean) * std
                std_out[u, pl.ds(i * 2 * wide + 8 * t, 8), :] = std
                nrms.append(nrm)
                at = t % tiles
                blends.append(f[t // tiles][8 * at : 8 * at + 8] + silu(nrm * gn[...]))
                if t % 2 == 1:
                    both = jnp.concatenate(nrms[-2:], 0).astype(BF)
                    norm_out[u, pl.ds(i * 2 * wide + 8 * (t - 1), 16), :] = both
            for t in range(tiles):
                sums[pl.ds(p * wide + 8 * t, 8), :] = blends[t] + blends[tiles + t]
            return carry

        for p in range(part * high // 2):
            norm(p, 0)
        s = sums[...]
        hi = s.astype(BF)
        lo = (s - hi.astype(F32)).astype(BF)
        pooled = (dot(pool_ref[...], hi) + dot(pool_ref[...], lo)).astype(BF)
        for i in range(n):

            @pl.when(k == i)
            def _():
                pooled_out[i][...] = pooled

    def by_order(rest):
        return lambda k, order: (order[k],) + (0,) * rest

    pooled_rows = pool.shape[0]
    block = (part, cells, ch)
    return call(
        kernel,
        grid=(n,),
        prefetch=1,
        ins=[
            (far(above), (part, wide, ch), by_order(2)),
            (far(below), (part, wide, ch), by_order(2)),
            (far(features), (part, high, wide, ch), by_order(3)),
            (far(pre_reduce), None, None),
            (taps, None, None),
            (far(pre_expand), None, None),
            (gain, None, None),
            (pool, None, None),
        ],
        outs=[(far((slots, cells, ch), BF), block, by_order(2))] * 4
        + [(far((slots, cells, 1), F32), (part, cells, 1), by_order(2))]
        + [(shape((pooled_rows, ch), BF), None, None)] * n,
        scratch=[
            pltpu.VMEM((part, cells, ch), F32),
            pltpu.VMEM((2, part, wide, ch), F32),
            pltpu.VMEM((rows_all, ch), F32),
            pltpu.VMEM((rows_all // 2, ch), F32),
        ],
        name="pre_forward",
    )(order)


def gain_row(w, n, share):
    at = 2 * share
    parts = [w[c, at : at + 16, :].astype(F32)[:1] for c in range(n)]
    return jnp.concatenate([p[:, :share] + p[:, share : 2 * share] for p in parts], 1)


def post_forward(source, moved, weights, taps, pool):
    n, (rows, ch) = len(moved), moved[0].shape
    total = n * rows
    depth = total // (pool * pool)
    share = ch // n

    def kernel(src, *refs):
        got, refs = refs[:n], refs[n:]
        w, tap, flat_out, red_out, act_out, conv_out, cact_out, norm_out, std_out, low_out, wide_ref, red, exp = refs
        for k in range(n):
            at = pl.multiple_of(src[k] * rows, 8)
            wide_ref[pl.ds(at, rows), :] = got[k][...].astype(F32)
        gain = gain_row(w, n, share)
        flat_out[...] = wide_ref[...].astype(BF)
        total_red = 0.0
        for c in range(n):
            total_red = total_red + dot(flat_out[:, c * share : (c + 1) * share], w[c, :share])
        red[...] = total_red
        first, last = edge_masks(total, pool, depth)
        step = pool * depth

        def conv(lanes):
            v = red[:, lanes]
            red_out[:, lanes] = v.astype(BF)
            x = silu(v).astype(BF)
            act_out[:, lanes] = x
            x = x.astype(F32)
            moves = [columns_moved(x, depth, first, last), x, columns_moved(x, -depth, first, last)]
            t = [sum(moves[b] * tap[pl.ds(3 * a + b, 1), lanes] for b in range(3)) for a in range(3)]
            none = jnp.zeros((step, LANES), F32)
            c = t[1] + jnp.concatenate([none, t[0][:-step]], 0) + jnp.concatenate([t[2][step:], none], 0)
            conv_out[:, lanes] = c.astype(BF)
            cact_out[:, lanes] = silu(c).astype(BF)

        chunks(ch // LANES, conv)
        for c in range(n):
            e = 0.0
            for q in range(n):
                cut = slice(q * share, (q + 1) * share)
                e = e + dot(cact_out[:, cut], w[c, share : 2 * share, cut])
            exp[:, c * share : (c + 1) * share] = e

        def norm(i, carry):
            for t in range(3):
                at = pl.ds(i * 48 + 16 * t, 16)
                e = exp[at, :]
                mean = jnp.mean(e, -1, keepdims=True)
                square = jnp.mean(e * e, -1, keepdims=True)
                std = lax.rsqrt(square - mean * mean + EPS)
                nrm = (e - mean) * std
                norm_out[at, :] = nrm.astype(BF)
                std_out[at, :] = std
                low_out[at, :] = (wide_ref[at, :] + silu(nrm * gain)).astype(BF)
            return carry

        for i in range(total // 48):
            norm(i, 0)

    narrow = shape((total, ch), BF)
    return call(
        kernel,
        grid=(1,),
        prefetch=1,
        ins=[(a, None, None) for a in (*map(far, moved), far(weights), taps)],
        outs=[(s, None, None) for s in (narrow, narrow, narrow, narrow, narrow, narrow, shape((total, 1), F32), narrow)],
        scratch=[pltpu.VMEM((total, ch), F32)] * 3,
        name="post_forward",
    )(source)


def readout_backward(source, low, readout, cots):
    total, ch = low.shape
    n, out_share = len(cots), cots[0].shape[1]

    def kernel(src, low_ref, ro, *rest):
        cot, grad = rest[:n], rest[n]
        k = pl.program_id(0)
        logits = dot(low_ref[...], ro[...])
        slope = gelu_parts(logits)[1]
        for i in range(n):

            @pl.when(k == i)
            def _():
                piece = (cot[i][...].astype(F32) * slope).astype(BF)
                term = dot(piece, ro[...], NT)
                grad[...] = term if i == 0 else grad[...] + term

    return call(
        kernel,
        grid=(n,),
        prefetch=1,
        ins=[(low, None, None), (far(readout), (ch, out_share), lambda k, s: (0, s[k]))] + [(c, None, None) for c in cots],
        outs=[(shape((total, ch), F32), None, None)],
        name="readout_backward",
    )(source)[0]


def post_backward(source, refined_grad, weights, taps, act, red, conv, nrm, std, pool):
    total, ch = act.shape
    n = weights.shape[0]
    share = ch // n
    rows = total // n
    depth = total // (pool * pool)

    def kernel(src, rg, w, tap, act_ref, red_ref, conv_ref, norm_ref, std_ref, exp_out, redg_out, taps_out, gain_out, *rest):
        back_out, (grad, cgrad) = rest[:n], rest[n:]
        gain = gain_row(w, n, share)

        def norm(i, total_gain):
            for t in range(3):
                at = pl.ds(i * 48 + 16 * t, 16)
                nm = norm_ref[at, :].astype(F32)
                ng = rg[at, :] * silu_slope(nm * gain)
                sc = ng * gain
                one = jnp.mean(sc, -1, keepdims=True)
                two = jnp.mean(sc * nm, -1, keepdims=True)
                exp_out[at, :] = (std_ref[at, :] * (sc - one - nm * two)).astype(BF)
                g = ng * nm
                total_gain = total_gain + g[:8] + g[8:]
            return total_gain

        gains = jnp.zeros((8, ch), F32)
        for i in range(total // 48):
            gains = norm(i, gains)
        gain_out[...] = gains
        for q in range(n):
            cut = slice(q * share, (q + 1) * share)
            cg = 0.0
            for c in range(n):
                cg = cg + dot(exp_out[:, c * share : (c + 1) * share], w[c, share : 2 * share, cut], NT)
            cgrad[:, cut] = cg
        first, last = edge_masks(total, pool, depth)
        step = pool * depth

        def back(lanes):
            g = (cgrad[:, lanes] * silu_slope(conv_ref[:, lanes].astype(F32))).astype(BF).astype(F32)
            x = act_ref[:, lanes].astype(F32)
            moves = [columns_moved(g, -depth, first, last), g, columns_moved(g, depth, first, last)]
            none = jnp.zeros((step, LANES), F32)
            xs = [
                jnp.concatenate([none, x[:-step]], 0),
                x,
                jnp.concatenate([x[step:], none], 0),
            ]
            for a in range(3):
                for b in range(3):
                    prod = xs[a] * moves[b]
                    taps_out[3 * a + b, :, lanes] = jnp.sum(prod.reshape(total // 8, 8, LANES), 0)
            t = [sum(moves[b] * tap[pl.ds(3 * a + b, 1), lanes] for b in range(3)) for a in range(3)]
            d = t[1] + jnp.concatenate([t[0][step:], none], 0) + jnp.concatenate([none, t[2][:-step]], 0)
            redg_out[:, lanes] = (d * silu_slope(red_ref[:, lanes].astype(F32))).astype(BF)

        chunks(ch // LANES, back)
        for c in range(n):
            cut = slice(c * share, (c + 1) * share)
            grad[:, cut] = rg[:, cut] + dot(redg_out[...], w[c, :share], NT)
        for r in range(n):
            at = pl.ds(pl.multiple_of(src[r] * rows, 8), rows)
            back_out[r][...] = grad[at, :].astype(BF)

    return call(
        kernel,
        grid=(1,),
        prefetch=1,
        ins=[(a, None, None) for a in (refined_grad, weights, taps, act, red, conv, nrm, std)],
        outs=[
            (s, None, None)
            for s in (
                shape((total, ch), BF),
                shape((total, ch), BF),
                shape((9, 8, ch), F32),
                shape((8, ch), F32),
                *[shape((rows, ch), BF)] * n,
            )
        ],
        scratch=[pltpu.VMEM((total, ch), F32), pltpu.VMEM((total, ch), F32)],
        name="post_backward",
    )(source)


def cotangent_by_image(cotangent, select, pairs):
    rows, width = cotangent.shape
    size = select.shape[0]
    each = size // pairs
    per = 3

    def kernel(x, sel, *outs):
        for q in range(per):
            y = dot(sel[...], x[pl.ds(q * size, size), :]).astype(BF)
            for s in range(pairs):
                outs[s][pl.ds(q * each, each), :] = y[s * each : (s + 1) * each]

    return call(
        kernel,
        grid=(rows // (per * size),),
        ins=[(far(cotangent), (per * size, width), lambda i: (i, 0)), (select, None, None)],
        outs=[(shape((rows // pairs, width), BF), (per * each, width), lambda i: (i, 0))] * pairs,
        name="cotangent_by_image",
    )()


def token_block(chan, source, pair_of, low, place, readout, cotangent):
    pairs, (rows, ch) = len(low), low[0].shape
    width = cotangent[0].shape[1]
    size = place.shape[0]
    each = size // pairs
    per = 3
    block = per * each

    def kernel(chan_ref, src, pair, *refs):
        lows, cots, (place_ref, ro, tok_out, piece_out, cot) = refs[:pairs], refs[pairs : 2 * pairs], refs[2 * pairs :]
        for k in range(pairs):
            cot[pair[k]] = cots[k][...]
        logits = dot(jnp.concatenate([v[...] for v in lows], 0), ro[...])
        value, slope = gelu_parts(logits)
        value = value.astype(BF)
        for k in range(pairs):
            piece_out[k] = (cot[src[k]].astype(F32) * slope[k * block : (k + 1) * block]).astype(BF)
        for q in range(per):
            x = jnp.concatenate([value[k * block + q * each : k * block + (q + 1) * each] for k in range(pairs)], 0)
            tok_out[pl.ds(q * size, size), :] = dot(place_ref[...], x).astype(BF)

    rows_at = lambda i, c, s, p: (i, 0)
    return call(
        kernel,
        grid=(rows // block,),
        prefetch=3,
        ins=[
            *[(v, (block, ch), rows_at) for v in low],
            *[(v, (block, width), rows_at) for v in cotangent],
            (place, None, None),
            (far(readout), (ch, width), lambda i, c, s, p: (0, c[0])),
        ],
        outs=[
            (shape((pairs * rows, width), BF), (pairs * block, width), rows_at),
            (shape((pairs, rows, width), BF), (pairs, block, width), lambda i, c, s, p: (0, i, 0)),
        ],
        scratch=[pltpu.VMEM((pairs, block, width), BF)],
        name="token_block",
    )(chan, source, pair_of)


def pre_backward(order, returned, spread_up, nrm, std, gain, conv, pre_expand):
    slots, cells, ch = nrm.shape
    n = order.shape[0]
    part = slots // n
    wide = 24
    rows = part * cells

    def kernel(order_ref, *refs):
        ret, refs = refs[:n], refs[n:]
        up, norm_ref, std_ref, gn, conv_ref, we, exp_out, conv_grad_out, top_out, bottom_out, gain_out, grad, cgrad = refs
        k = pl.program_id(0)
        for i in range(n):

            @pl.when(k == i)
            def _():
                grad[...] = dot(up[...], ret[i][...])

        def norm(i, total_gain):
            u, j = i // (cells // 48), i % (cells // 48)
            for t in range(3):
                at = pl.ds(j * 48 + 16 * t, 16)
                nm = norm_ref[u, at, :].astype(F32)
                ng = grad[pl.ds(i * 48 + 16 * t, 16), :] * silu_slope(nm * gn[...])
                sc = ng * gn[...]
                one = jnp.mean(sc, -1, keepdims=True)
                two = jnp.mean(sc * nm, -1, keepdims=True)
                exp_out[u, at, :] = (std_ref[u, at, :] * (sc - one - nm * two)).astype(BF)
                g = ng * nm
                total_gain = total_gain + g[:8] + g[8:]
            return total_gain

        gains = jnp.zeros((8, ch), F32)
        for i in range(rows // 48):
            gains = norm(i, gains)

        @pl.when(k == 0)
        def _():
            gain_out[...] = gains

        @pl.when(k > 0)
        def _():
            gain_out[...] += gains

        cgrad[...] = dot(exp_out[...].reshape(rows, ch), we[...], NT)
        for u in range(part):

            def slope(lanes):
                g = cgrad[pl.ds(u * cells, cells), lanes] * silu_slope(conv_ref[u, :, lanes].astype(F32))
                conv_grad_out[u, :, lanes] = g.astype(BF)
                top_out[u, :, lanes] = g[:wide].astype(BF)
                bottom_out[u, :, lanes] = g[cells - wide :].astype(BF)

            chunks(ch // LANES, slope)

    by_order = lambda k, order: (order[k], 0, 0)
    whole = (part, cells, ch)
    edge = (part, wide, ch)
    return call(
        kernel,
        grid=(n,),
        prefetch=1,
        ins=[
            *[(r, None, None) for r in returned],
            (spread_up, None, None),
            (far(nrm), whole, by_order),
            (far(std), (part, cells, 1), by_order),
            (gain, None, None),
            (far(conv), whole, by_order),
            (far(pre_expand), None, None),
        ],
        outs=[
            (shape((slots, cells, ch), BF), whole, by_order),
            (far((slots, cells, ch), BF), whole, by_order),
            (shape((slots, wide, ch), BF), edge, by_order),
            (shape((slots, wide, ch), BF), edge, by_order),
            (shape((8, ch), F32), None, None),
        ],
        scratch=[pltpu.VMEM((rows, ch), F32), pltpu.VMEM((rows, ch), F32)],
        name="pre_backward",
    )(order)


def pre_conv_backward(conv_grad, above, below, reduced, taps):
    slots, cells, ch = reduced.shape
    wide = above.shape[1]
    high = cells // wide

    def kernel(cg, up, down, red, tap, redg_out, taps_out):
        step = pl.program_id(0)
        first, last = edge_masks(wide, wide, 1)

        @pl.when(step == 0)
        def _():
            taps_out[...] = jnp.zeros_like(taps_out)

        def back(lanes):
            w = [tap[pl.ds(i, 1), lanes] for i in range(9)]
            mid = cg[0, :, lanes].astype(F32)
            rows = [up[0, :, lanes].astype(F32)]
            rows += [mid[i * wide : (i + 1) * wide] for i in range(high)]
            rows += [down[0, :, lanes].astype(F32)]
            whole = red[0, :, lanes].astype(F32)
            v = [whole[i * wide : (i + 1) * wide] for i in range(high)]
            s = [sigmoid(t) for t in v]
            x = [(a * b).astype(BF).astype(F32) for a, b in zip(v, s)]
            d = [0.0] * high
            sums = [0.0] * 9
            for p in range(high + 2):
                g = rows[p]
                moves = [columns_moved(g, -1, first, last), g, columns_moved(g, 1, first, last)]
                for a in range(3):
                    i = p - 1 + a - 1
                    if 0 <= i < high:
                        for b in range(3):
                            d[i] = d[i] + moves[b] * w[3 * a + b]
                            prod = x[i] * moves[b]
                            sums[3 * a + b] = sums[3 * a + b] + (prod[:8] + prod[8:16] + prod[16:])
            out = [d[i] * (s[i] * (1.0 + v[i] * (1.0 - s[i]))) for i in range(high)]
            redg_out[0, :, lanes] = jnp.concatenate(out, 0).astype(BF)
            for i in range(9):
                taps_out[i, :, lanes] += sums[i]

        chunks(ch // LANES, back)

    image = lambda i: (i, 0, 0)
    return call(
        kernel,
        grid=(slots,),
        ins=[
            (far(conv_grad), (1, cells, ch), image),
            (far(above), (1, wide, ch), image),
            (far(below), (1, wide, ch), image),
            (far(reduced), (1, cells, ch), image),
            (taps, None, None),
        ],
        outs=[
            (shape((slots, cells, ch), BF), (1, cells, ch), image),
            (shape((9, 8, ch), F32), None, None),
        ],
        name="pre_conv_backward",
    )()


def feature_backward(order, reduced_grad, pre_reduce, returned, spread_up):
    slots, cells, ch = reduced_grad.shape
    n = order.shape[0]
    part = slots // n

    def kernel(order_ref, rg, wr, up, *refs):
        ret, out = refs[:n], refs[n]
        k = pl.program_id(0)
        for i in range(n):

            @pl.when(k == i)
            def _():
                out[...] = dot(up[...], ret[i][...]).reshape(part, cells, ch)

        out[...] += dot(rg[...].reshape(part * cells, ch), wr[...], NT).reshape(part, cells, ch)

    by_order = lambda k, order: (order[k], 0, 0)
    whole = (part, cells, ch)
    return call(
        kernel,
        grid=(n,),
        prefetch=1,
        ins=[
            (reduced_grad, whole, by_order),
            (far(pre_reduce), None, None),
            (spread_up, None, None),
            *[(r, None, None) for r in returned],
        ],
        outs=[(shape((slots, cells, ch), F32), whole, by_order)],
        name="feature_backward",
    )(order)[0]


def post_weight_grads(flat, reduced_grad, act, expanded_grad, n):
    total, ch = flat.shape
    share = ch // n
    rows = share // 8

    def kernel(x, g, a, e, out):
        for c in range(n):
            cut = slice(c * share, (c + 1) * share)
            v = dot(x[:, cut], g[...], TN).astype(BF)
            for d in range(8):
                out[d, c, :, :ch] = v[d * rows : (d + 1) * rows]
            for q in range(n):
                v = dot(a[:, q * share : (q + 1) * share], e[:, cut], TN).astype(BF)
                for d in range(8):
                    out[d, c, :, ch + q * share : ch + (q + 1) * share] = v[d * rows : (d + 1) * rows]

    return call(
        kernel,
        grid=(1,),
        ins=[(v, None, None) for v in (flat, reduced_grad, act, expanded_grad)],
        outs=[(far((8, n, rows, 2 * ch), BF), None, None)],
        name="post_weight_grads",
    )()[0]


def readout_weight_grad(low, piece, n):
    pairs, total, width = piece.shape
    ch = low[0].shape[1]
    share = ch // n
    parts = 8
    rows = share // parts

    def kernel(*refs):
        x, (g, out) = refs[:pairs], refs[pairs:]
        x = jnp.concatenate([v[...] for v in x], 0)
        v = dot(x, g[...].reshape(pairs * total, width), TN).astype(BF)
        for d in range(parts):
            out[d, 0] = v[d * rows : (d + 1) * rows]

    return call(
        kernel,
        grid=(n,),
        ins=[(v, (total, share), lambda c: (0, c)) for v in low] + [(piece, None, None)],
        outs=[(far((parts, n, rows, width), BF), (parts, 1, rows, width), lambda c: (0, c, 0, 0))],
        name="readout_weight_grad",
    )()[0]


def cross(n, k):
    return [(a * n + b, ((b + k) % n) * n + a) for a in range(n) for b in range(n)]


def turn(n, k):
    return [(i, (i + k) % n) for i in range(n)]


def other_core(values):
    return lax.ppermute(values, "core", [(0, 1), (1, 0)])


def small_rows(*grads):
    ch = grads[0].shape[-1]
    counts = [g.shape[0] if g.ndim == 3 else 1 for g in grads]
    per = ch // LANES

    def kernel(*refs):
        out = refs[-1]
        at = 0
        for ref, count in zip(refs, counts):
            for i in range(count):
                v = jnp.sum(ref[i] if len(ref.shape) == 3 else ref[...], 0, keepdims=True)
                for q in range(per):
                    out[pl.ds(at, 1), :] = v[:, q * LANES : (q + 1) * LANES]
                    at += 1

    return call(
        kernel,
        grid=(1,),
        ins=[(g, None, None) for g in grads],
        outs=[(shape((sum(counts) * per, LANES), F32), None, None)],
        name="small_rows",
    )()[0]


def join_halves(core, mine, theirs, small, their_small, parts):
    rows, ch = mine[0].shape
    half = rows // 2
    width = len(mine) * ch + LANES
    count = small.shape[0]
    m = len(mine)
    steps = 2
    block = half // steps

    def kernel(core_ref, *refs):
        own, got = refs[:m], refs[m : 2 * m]
        sm, got_sm, out = refs[2 * m :]
        for i in range(m):
            out[:, i * ch : (i + 1) * ch] = (own[i][...].astype(F32) + got[i][...].astype(F32)).astype(BF)
        first = ((core_ref[0] == 0) & (pl.program_id(0) == 0)).astype(F32)
        total = (sm[...] + got_sm[...]) * first
        pad = jnp.zeros((block - count, LANES), F32)
        out[:, m * ch :] = jnp.concatenate([total, pad], 0).astype(BF)

    return call(
        kernel,
        grid=(steps,),
        prefetch=1,
        ins=[(v, (block, ch), lambda i, c: (c[0] * steps + i, 0)) for v in mine]
        + [(v, (block, ch), lambda i, c: (i, 0)) for v in theirs]
        + [(v, None, None) for v in (small, their_small)],
        outs=[(far((half, width), BF), (block, width), lambda i, c: (i, 0))],
        name="join_halves",
    )(core)[0].reshape(parts, half // parts, width)


def sum_and_copy(blocks):
    parts, rows, width = blocks.shape

    def kernel(x, out):
        def cut(lanes):
            total = jnp.sum(x[:, :, lanes].astype(F32), 0).astype(BF)
            out[:, :, lanes] = jnp.broadcast_to(total[None], (parts, rows, LANES))

        chunks(width // LANES, cut)

    return call(
        kernel,
        grid=(1,),
        ins=[(blocks, None, None)],
        outs=[(far(blocks.shape, BF), None, None)],
        name="sum_and_copy",
    )()[0]


def split_rows(to_row, post, read):
    n, rows, width = post.shape
    ch = read.shape[2]
    each = rows // n

    def kernel(to, a, b, *outs):
        outs, wide = outs[:n], outs[n]
        wide[:, :, :width] = a[...].astype(F32)
        wide[:, :, width:] = b[...].astype(F32)
        for k in range(n):
            outs[k][...] = wide[:, pl.ds(pl.multiple_of(to[k] * each, 8), each), :].astype(BF)

    return call(
        kernel,
        grid=(1,),
        prefetch=1,
        ins=[(post, None, None), (read, None, None)],
        outs=[(shape((n, each, width + ch), BF), None, None)] * n,
        scratch=[pltpu.VMEM((n, rows, width + ch), F32)],
        name="split_rows",
    )(to_row)


def sum_rows(to_chan, blocks):
    n, rows, width = blocks[0].shape

    def kernel(to, *refs):
        outs = refs[n:]
        for k in range(n):
            outs[k][...] = sum(r[to[k]].astype(F32) for r in refs[:n]).astype(BF)

    return call(
        kernel,
        grid=(1,),
        prefetch=1,
        ins=[(b, None, None) for b in blocks],
        outs=[(shape((rows, width), BF), None, None)] * n,
        name="sum_rows",
    )(to_chan)


def join_chan(from_chan, blocks):
    n = len(blocks)
    rows, width = blocks[0].shape
    ch = width // 3

    def kernel(src, *refs):
        out = refs[n]
        out[:, : 2 * ch] = sum(r[:, : 2 * ch].astype(F32) for r in refs[:n]).astype(BF)
        for k in range(n):
            at = pl.multiple_of(2 * ch + src[k] * ch, LANES)
            out[:, pl.ds(at, ch)] = refs[k][:, 2 * ch :]

    return call(
        kernel,
        grid=(1,),
        prefetch=1,
        ins=[(b, None, None) for b in blocks],
        outs=[(far((rows, 2 * ch + n * ch), BF), None, None)],
        name="join_chan",
    )(from_chan)[0]


def finish_pre(place, half_rows, ch, earlier=()):
    half, width = half_rows.shape
    m = (width - LANES) // ch
    steps = 4
    block = half // steps

    def kernel(place_ref, x, *outs):
        outs = outs[len(earlier) :]
        for i in range(m):
            outs[i][...] = x[:, i * ch : (i + 1) * ch].astype(F32)
        outs[m][...] = x[:, m * ch :].astype(F32)

    return call(
        kernel,
        grid=(steps,),
        prefetch=1,
        ins=[(half_rows, (block, width), lambda i, c: (i, 0))],
        outs=[(shape((2 * half, ch), F32), (block, ch), lambda i, c: (c[0] * steps + i, 0)) for _ in range(m)]
        + [(shape((half, LANES), F32), (block, LANES), lambda i, c: (i, 0))],
        aliased=earlier,
        name="finish_pre",
    )(place)


def finish_post(place, gathered, n, earlier=()):
    groups, per, width = gathered.shape
    share = 2 * groups * per
    ch = width // (n + 2)

    def kernel(place_ref, x, *outs):
        reduce_out, expand_out, read_out = outs[len(earlier) :]
        reduce_out[...] = x[0, :, :ch].astype(F32)
        for q in range(n):
            expand_out[q] = x[0, :, ch + q * share : ch + (q + 1) * share].astype(F32)
        read_out[...] = x[0, :, 2 * ch :].astype(F32)

    at = lambda i, c: (2 * i + c[0], 0)
    return call(
        kernel,
        grid=(groups,),
        prefetch=1,
        ins=[(gathered, (1, per, width), lambda i, c: (i, 0, 0))],
        outs=[
            (shape((share, ch), F32), (per, ch), at),
            (shape((n, share, share), F32), (n, per, share), lambda i, c: (0, 2 * i + c[0], 0)),
            (shape((share, n * ch), F32), (per, n * ch), at),
        ],
        aliased=earlier,
        name="finish_post",
    )(place)


def after(values, *earlier):
    return lax.optimization_barrier((values, *earlier))[0]


def pool_matrix(part, high, wide):
    half = wide // 2
    m = np.zeros((high // 2 * half * part, part * (high // 2) * wide), np.float32)
    for u in range(part):
        for i in range(high // 2):
            for j in range(wide):
                m[(i * half + j // 2) * part + u, (u * (high // 2) + i) * wide + j] = 0.25
    return m


def spread_matrix(part, high, wide):
    half = wide // 2
    m = np.zeros((part * high * wide, high // 2 * half * part), np.float32)
    for u in range(part):
        for i in range(high):
            for j in range(wide):
                m[(u * high + i) * wide + j, ((i // 2) * half + j // 2) * part + u] = 0.25
    return m


def body(features, counts, pre_reduce, pre_conv, pre_expand, pre_gain, post_reduce, post_conv, post_expand, post_gain, readout, cotangent):
    n = lax.axis_size("chan")
    row = lax.axis_index("rows").astype(jnp.int32)
    chan = lax.axis_index("chan").astype(jnp.int32)
    core = lax.axis_index("core").astype(jnp.int32)
    ch = pre_reduce.shape[0]
    slots, high, wide = features.shape[0], features.shape[1], features.shape[2]
    part = slots // n
    cells = high * wide
    pool = wide // 2
    share = ch // n
    out_share = cotangent.shape[3]
    steps = jnp.arange(n, dtype=jnp.int32)
    order = (row + steps) % n
    source = (row - steps) % n
    pair_of = (chan + steps) % n
    rank = jnp.full((1,), chan, jnp.int32)
    core_at = jnp.full((1,), core, jnp.int32)
    pre_taps = pre_conv.astype(F32).reshape(9, ch)
    post_taps = post_conv.astype(F32).reshape(9, ch)
    pre_gain_row = pre_gain.reshape(1, ch)
    pool_m = jnp.asarray(pool_matrix(part, high, wide), BF)
    up_m = jnp.asarray(spread_matrix(part, high, wide), BF)

    ends = n - 1
    down_pairs = [(i, i + 1) for i in range(ends)]
    up_pairs = [(i + 1, i) for i in range(ends)]
    above = lax.ppermute(features[:, -1], "rows", down_pairs)
    below = lax.ppermute(features[:, 0], "rows", up_pairs)
    gain_hi = post_gain.astype(BF)
    gain_lo = (post_gain - gain_hi.astype(F32)).astype(BF)
    gain_row = jnp.concatenate([gain_hi, gain_lo, jnp.zeros((ch - 2 * share,), BF)])[None]
    square = post_expand.reshape(n, share, share)
    shards = jnp.concatenate(
        [post_reduce, jnp.concatenate([square[q] for q in range(n)], axis=1), jnp.pad(gain_row, ((0, 63), (0, 0)))], axis=0
    )
    shard = lax.dynamic_index_in_dim(shards.reshape(2, -1, ch), core, 0, keepdims=False)
    full = lax.all_gather(shard, ("chan", "core"), axis=0, tiled=True)
    full = full.reshape(n, 2 * share + 64, ch)
    flat_features = features.reshape(slots * cells, ch)
    live = (jnp.arange(SLOT)[None, :] < counts[:, None]).astype(F32).reshape(slots)
    size, each = 16 * slots, 16 * part
    at = lax.broadcasted_iota(jnp.int32, (size, size), 0)
    column = lax.broadcasted_iota(jnp.int32, (size, size), 1)
    wanted = (at % each) // part * slots + part * ((chan + at // each) % n) + at % part
    select = jnp.where(column == wanted, jnp.tile(live, 16)[None, :], 0.0).astype(BF)
    wanted = (column % each) // part * slots + part * ((row - column // each) % n) + column % part
    place = jnp.where(at == wanted, 1.0, 0.0).astype(BF)
    cot_rows = cotangent.transpose(1, 2, 0, 3).reshape(-1, out_share)
    sends = cotangent_by_image(cot_rows, select, n)
    away = after(sends, above, below)
    cots = [lax.ppermute(away[k], ("rows", "chan"), cross(n, k)) for k in range(n)]

    reduced, convolved, convolved_act, normal_pre, pre_std, *pooled = pre_forward(
        order, above, below, features, pre_reduce, pre_taps, pre_expand, pre_gain_row, pool_m
    )

    pooled = after(pooled, cots)
    moved = [pooled[0]] + [lax.ppermute(pooled[k], "rows", turn(n, k)) for k in range(1, n)]
    flat, post_reduced, post_act, post_convolved, post_cact, post_normal, post_std, low = post_forward(
        source, moved, full, post_taps, pool
    )
    lows = [low] + [lax.ppermute(low, "chan", turn(n, k)) for k in range(1, n)]
    refined_grad = readout_backward(source, low, readout, cots)
    post_expanded_grad, post_reduced_grad, post_taps_grad, post_gain_grad, *back = post_backward(
        source, refined_grad, full, post_taps, post_act, post_reduced, post_convolved, post_normal, post_std, pool
    )

    returned = [back[0]] + [lax.ppermute(back[k], "rows", turn(n, -k)) for k in range(1, n)]

    flat = after(flat, lows)
    load = post_weight_grads(flat, post_reduced_grad, post_cact, post_expanded_grad, n)

    post_sum = lax.psum_scatter(load, ("x", "core"), scatter_dimension=0, tiled=False)

    stacked = jnp.stack(after(lows, load, returned))
    lows = [lax.dynamic_index_in_dim(stacked, (chan - row - k) % n, 0, keepdims=False) for k in range(n)]
    lows = [lows[0]] + [lax.ppermute(lows[k], "rows", turn(n, k)) for k in range(1, n)]

    expanded_grad, convolved_grad, top, bottom, pre_gain_grad = pre_backward(
        order, returned, up_m, normal_pre, pre_std, pre_gain_row, convolved, pre_expand
    )
    top, bottom, lows[1], lows[3] = lax.optimization_barrier((top, bottom, lows[1], lows[3]))
    grad_above = lax.ppermute(bottom, "rows", down_pairs)
    grad_below = lax.ppermute(top, "rows", up_pairs)
    act_rows = after(convolved_act, bottom).reshape(-1, ch)
    pre_expand_grad = dot(act_rows, expanded_grad.reshape(-1, ch), TN).astype(BF)

    lows = after(lows, pre_expand_grad)
    tokens, piece = token_block(rank, source, pair_of, lows, place, readout, sends)
    read_load = readout_weight_grad(lows, after(piece, grad_above, grad_below), n)
    tokens = tokens.reshape(pool, pool, slots, out_share).transpose(2, 0, 1, 3)
    convolved_grad = after(convolved_grad, read_load)
    read_sum = lax.psum_scatter(after(read_load, post_sum), ("x", "core"), scatter_dimension=0, tiled=False)

    reduced_grad, pre_taps_grad = pre_conv_backward(convolved_grad, grad_above, grad_below, reduced, pre_taps)
    small = small_rows(pre_taps_grad, pre_gain_grad, post_taps_grad, post_gain_grad)
    pre_reduce_grad = dot(after(flat_features, small), reduced_grad.reshape(-1, ch), TN).astype(BF)

    chips = ("x", "rows", "chan")
    mine = [pre_reduce_grad, pre_expand_grad]
    theirs = [other_core(lax.dynamic_index_in_dim(g.reshape(2, ch // 2, ch), 1 - core, 0, keepdims=False)) for g in mine]
    load = join_halves(core_at, mine, theirs, small, other_core(small), 64)
    pieces = lax.all_to_all(load, chips, 0, 0, tiled=False)
    feature_grad = feature_backward(order, after(reduced_grad, load), pre_reduce, returned, up_m).reshape(features.shape)

    post_sum, read_sum = lax.optimization_barrier((post_sum, read_sum, feature_grad))[:2]
    blocks = split_rows(order, post_sum, read_sum)
    blocks = [blocks[0]] + [lax.ppermute(blocks[k], "rows", turn(n, k)) for k in range(1, n)]
    blocks = sum_rows(pair_of, blocks)
    load = sum_and_copy(after(pieces, *blocks))
    blocks = [blocks[0]] + [lax.ppermute(blocks[k], "chan", turn(n, k)) for k in range(1, n)]
    rest = join_chan((chan - steps) % n, after(blocks, load))
    ready = rest
    rest = lax.all_gather(rest, ("x", "rows"), axis=0, tiled=False).reshape(4, share // 8, -1)
    load_all = lax.all_to_all(after(load, ready), chips, 0, 0, tiled=False).reshape(ch // 2, -1)

    def finish(kernel, values, *sizes):
        theirs = other_core(values)
        own = kernel(core_at, values, *sizes)
        theirs = after(theirs, *own)
        return own, theirs

    own, theirs = finish(finish_pre, load_all, ch)
    pre_reduce_out, pre_expand_out, small_their = finish_pre(1 - core_at, theirs, ch, earlier=tuple(own[:2]))
    small_out = jnp.where(core == 0, own[2], small_their)
    own, theirs = finish(finish_post, after(rest, pre_reduce_out), n)
    post_reduce_out, post_expand_out, readout_out = finish_post(1 - core_at, theirs, n, earlier=tuple(own))
    per = ch // LANES
    cut = [0, 9 * per, 10 * per, 19 * per, 20 * per]
    pre_conv_out, pre_gain_out, post_conv_out, post_gain_out = [small_out[a:b] for a, b in zip(cut, cut[1:])]
    return (
        tokens,
        feature_grad,
        pre_reduce_out,
        pre_conv_out.reshape(3, 3, ch),
        pre_expand_out,
        pre_gain_out.reshape(ch),
        post_reduce_out,
        post_conv_out.reshape(3, 3, ch),
        post_expand_out.reshape(ch, share),
        lax.dynamic_slice_in_dim(post_gain_out.reshape(ch), chan * share, share, 0),
        readout_out,
    )


def solution(mesh):
    grid = Mesh(mesh.devices.reshape(4, 2, 4, 4), ("x", "core", "rows", "chan"))
    images = P(("x", "core", "chan"), "rows", None, None)
    grids = P(("x", "core", "rows"), None, None, "chan")
    return jax.shard_map(
        body,
        mesh=grid,
        in_specs=(
            images,
            P(("x", "core", "rows")),
            P(),
            P(),
            P(),
            P(),
            P("chan", None),
            P(),
            P(None, "chan"),
            P("chan"),
            P(),
            grids,
        ),
        out_specs=(grids, images, P(), P(), P(), P(), P("chan", None), P(), P(None, "chan"), P("chan"), P("chan", None)),
        check_vma=False,
    )
```

```python
import functools

import jax
import jax.numpy as jnp
import numpy as np
from jax import lax
from jax.experimental import pallas as pl
from jax.experimental.pallas import tpu as pltpu
from jax.sharding import Mesh, PartitionSpec as P

SLOT = 4
EPS = 1e-06
BF = jnp.bfloat16
F32 = jnp.float32
LANES = 128
VMEM_LIMIT = 20 * 1024 * 1024
NN = ((1,), (0,))
NT = ((1,), (1,))
TN = ((0,), (0,))


def dot(a, b, dims=NN):
    return lax.dot_general(a, b, (dims, ((), ())), preferred_element_type=F32)


def sigmoid(v):
    return 0.5 * jnp.tanh(0.5 * v) + 0.5


def silu(v):
    return v * sigmoid(v)


def silu_slope(v):
    s = sigmoid(v)
    return s * (1.0 + v * (1.0 - s))


def gelu_parts(v):
    c = 0.7978845608028654
    square = v * v
    t = jnp.tanh(v * (c + (c * 0.044715) * square))
    half = 0.5 * (1.0 + t)
    slope = half + 0.5 * v * (1.0 - t * t) * (c + (3.0 * c * 0.044715) * square)
    return v * half, slope


def chunks(count, body, width=LANES):
    for i in range(count):
        body(pl.ds(i * width, width))


def call(kernel, *, grid, ins, outs, scratch=(), prefetch=0, aliased=(), cost=1, name):
    def spec(shape, block, index):
        if block is None:
            block, index = shape, lambda *_: (0,) * len(shape)
        return pl.BlockSpec(block, index)

    arrays = [i[0] for i in ins] + list(aliased)
    in_specs = [spec(a.shape, b, m) for a, b, m in ins] + [pl.BlockSpec(memory_space=pl.ANY)] * len(aliased)
    out_specs = [spec(s.shape, b, m) for s, b, m in outs]

    def run(*scalars):
        return pl.pallas_call(
            kernel,
            grid_spec=pltpu.PrefetchScalarGridSpec(
                num_scalar_prefetch=prefetch,
                grid=grid,
                in_specs=in_specs,
                out_specs=out_specs,
                scratch_shapes=list(scratch),
            ),
            out_shape=[s[0] for s in outs],
            compiler_params=pltpu.CompilerParams(
                dimension_semantics=("arbitrary",) * len(grid), vmem_limit_bytes=VMEM_LIMIT
            ),
            input_output_aliases={prefetch + len(ins) + i: i for i in range(len(aliased))},
            cost_estimate=pl.CostEstimate(flops=cost, bytes_accessed=1, transcendentals=0),
            name=name,
        )(*scalars, *arrays)

    return run


def shape(dims, dtype):
    return jax.ShapeDtypeStruct(dims, dtype)


def far(values, dtype=None):
    if dtype is None:
        return pltpu.with_memory_space_constraint(values, pltpu.HBM)
    return pltpu.HBM(values, dtype)


def columns_moved(t, by, first, last):
    rows = t.shape[0]
    return pltpu.roll(t, by % rows, 0) * (first if by > 0 else last)


def edge_masks(rows, width, depth):
    at = lax.broadcasted_iota(jnp.int32, (rows, LANES), 0) % (width * depth)
    return (at >= depth).astype(F32), (at < (width - 1) * depth).astype(F32)


def pre_forward(order, above, below, features, pre_reduce, taps, pre_expand, gain, pool):
    slots, high, wide, ch = features.shape
    cells = high * wide
    n = order.shape[0]
    part = slots // n
    rows_all = part * cells

    def kernel(order_ref, up_ref, down_ref, feat, wr, tap, we, gn, pool_ref, red_out, conv_out, act_out, norm_out, std_out, *rest):
        pooled_out, (red, halo, exp, sums) = rest[:n], rest[n:]
        k = pl.program_id(0)
        for side, ref in enumerate((up_ref, down_ref)):
            halo[side] = dot(ref[...].reshape(part * wide, ch), wr[...]).reshape(part, wide, ch)
        red[...] = dot(feat[...].reshape(rows_all, ch), wr[...]).reshape(part, cells, ch)
        red_out[...] = red[...].astype(BF)
        first, last = edge_masks(wide, wide, 1)
        for u in range(part):

            def conv(lanes):
                w = [tap[pl.ds(i, 1), lanes] for i in range(9)]
                rows = [halo[0, u, :, lanes]]
                rows += [red[u, pl.ds(i * wide, wide), lanes] for i in range(high)]
                rows += [halo[1, u, :, lanes]]
                rows = [silu(r).astype(BF).astype(F32) for r in rows]
                out = []
                for i in range(high):
                    t = [sum(rows[i + a] * w[3 * a + b] for a in range(3)) for b in range(3)]
                    out.append(t[1] + columns_moved(t[0], 1, first, last) + columns_moved(t[2], -1, first, last))
                conv_out[u, :, lanes] = jnp.concatenate(out, 0).astype(BF)
                act_out[u, :, lanes] = jnp.concatenate([silu(c) for c in out], 0).astype(BF)

            chunks(ch // LANES, conv)

        exp[...] = dot(act_out[...].reshape(rows_all, ch), we[...])

        def norm(p, carry):
            u, i = p // (high // 2), p % (high // 2)
            tiles = wide // 8
            f = [feat[u, 2 * i + half].astype(F32) for half in range(2)]
            nrms, blends = [], []
            for t in range(2 * tiles):
                e = exp[pl.ds(p * 2 * wide + 8 * t, 8), :]
                mean = jnp.mean(e, -1, keepdims=True)
                square = jnp.mean(e * e, -1, keepdims=True)
                std = lax.rsqrt(square - mean * mean + EPS)
                nrm = (e - mean) * std
                std_out[u, pl.ds(i * 2 * wide + 8 * t, 8), :] = std
                nrms.append(nrm)
                at = t % tiles
                blends.append(f[t // tiles][8 * at : 8 * at + 8] + silu(nrm * gn[...]))
                if t % 2 == 1:
                    both = jnp.concatenate(nrms[-2:], 0).astype(BF)
                    norm_out[u, pl.ds(i * 2 * wide + 8 * (t - 1), 16), :] = both
            for t in range(tiles):
                sums[pl.ds(p * wide + 8 * t, 8), :] = blends[t] + blends[tiles + t]
            return carry

        for p in range(part * high // 2):
            norm(p, 0)
        s = sums[...]
        hi = s.astype(BF)
        lo = (s - hi.astype(F32)).astype(BF)
        pooled = (dot(pool_ref[...], hi) + dot(pool_ref[...], lo)).astype(BF)
        for i in range(n):

            @pl.when(k == i)
            def _():
                pooled_out[i][...] = pooled

    def by_order(rest):
        return lambda k, order: (order[k],) + (0,) * rest

    pooled_rows = pool.shape[0]
    block = (part, cells, ch)
    return call(
        kernel,
        grid=(n,),
        prefetch=1,
        ins=[
            (far(above), (part, wide, ch), by_order(2)),
            (far(below), (part, wide, ch), by_order(2)),
            (far(features), (part, high, wide, ch), by_order(3)),
            (far(pre_reduce), None, None),
            (taps, None, None),
            (far(pre_expand), None, None),
            (gain, None, None),
            (pool, None, None),
        ],
        outs=[(far((slots, cells, ch), BF), block, by_order(2))] * 4
        + [(far((slots, cells, 1), F32), (part, cells, 1), by_order(2))]
        + [(shape((pooled_rows, ch), BF), None, None)] * n,
        scratch=[
            pltpu.VMEM((part, cells, ch), F32),
            pltpu.VMEM((2, part, wide, ch), F32),
            pltpu.VMEM((rows_all, ch), F32),
            pltpu.VMEM((rows_all // 2, ch), F32),
        ],
        name="pre_forward",
    )(order)


def gain_row(w, n, share):
    at = 2 * share
    parts = [w[c, at : at + 16, :].astype(F32)[:1] for c in range(n)]
    return jnp.concatenate([p[:, :share] + p[:, share : 2 * share] for p in parts], 1)


def post_forward(source, moved, weights, taps, pool):
    n, (rows, ch) = len(moved), moved[0].shape
    total = n * rows
    depth = total // (pool * pool)
    share = ch // n

    def kernel(src, *refs):
        got, refs = refs[:n], refs[n:]
        w, tap, flat_out, red_out, act_out, conv_out, cact_out, norm_out, std_out, low_out, wide_ref, red, exp = refs
        for k in range(n):
            at = pl.multiple_of(src[k] * rows, 8)
            wide_ref[pl.ds(at, rows), :] = got[k][...].astype(F32)
        gain = gain_row(w, n, share)
        flat_out[...] = wide_ref[...].astype(BF)
        total_red = 0.0
        for c in range(n):
            total_red = total_red + dot(flat_out[:, c * share : (c + 1) * share], w[c, :share])
        red[...] = total_red
        first, last = edge_masks(total, pool, depth)
        step = pool * depth

        def conv(lanes):
            v = red[:, lanes]
            red_out[:, lanes] = v.astype(BF)
            x = silu(v).astype(BF)
            act_out[:, lanes] = x
            x = x.astype(F32)
            moves = [columns_moved(x, depth, first, last), x, columns_moved(x, -depth, first, last)]
            t = [sum(moves[b] * tap[pl.ds(3 * a + b, 1), lanes] for b in range(3)) for a in range(3)]
            none = jnp.zeros((step, LANES), F32)
            c = t[1] + jnp.concatenate([none, t[0][:-step]], 0) + jnp.concatenate([t[2][step:], none], 0)
            conv_out[:, lanes] = c.astype(BF)
            cact_out[:, lanes] = silu(c).astype(BF)

        chunks(ch // LANES, conv)
        for c in range(n):
            e = 0.0
            for q in range(n):
                cut = slice(q * share, (q + 1) * share)
                e = e + dot(cact_out[:, cut], w[c, share : 2 * share, cut])
            exp[:, c * share : (c + 1) * share] = e

        def norm(i, carry):
            for t in range(3):
                at = pl.ds(i * 48 + 16 * t, 16)
                e = exp[at, :]
                mean = jnp.mean(e, -1, keepdims=True)
                square = jnp.mean(e * e, -1, keepdims=True)
                std = lax.rsqrt(square - mean * mean + EPS)
                nrm = (e - mean) * std
                norm_out[at, :] = nrm.astype(BF)
                std_out[at, :] = std
                low_out[at, :] = (wide_ref[at, :] + silu(nrm * gain)).astype(BF)
            return carry

        for i in range(total // 48):
            norm(i, 0)

    narrow = shape((total, ch), BF)
    return call(
        kernel,
        grid=(1,),
        prefetch=1,
        ins=[(a, None, None) for a in (*map(far, moved), far(weights), taps)],
        outs=[(s, None, None) for s in (narrow, narrow, narrow, narrow, narrow, narrow, shape((total, 1), F32), narrow)],
        scratch=[pltpu.VMEM((total, ch), F32)] * 3,
        name="post_forward",
    )(source)


def readout_backward(source, low, readout, cots):
    total, ch = low.shape
    n, out_share = len(cots), cots[0].shape[1]

    def kernel(src, low_ref, ro, *rest):
        cot, grad = rest[:n], rest[n]
        k = pl.program_id(0)
        logits = dot(low_ref[...], ro[...])
        slope = gelu_parts(logits)[1]
        for i in range(n):

            @pl.when(k == i)
            def _():
                piece = (cot[i][...].astype(F32) * slope).astype(BF)
                term = dot(piece, ro[...], NT)
                grad[...] = term if i == 0 else grad[...] + term

    return call(
        kernel,
        grid=(n,),
        prefetch=1,
        ins=[(low, None, None), (far(readout), (ch, out_share), lambda k, s: (0, s[k]))] + [(c, None, None) for c in cots],
        outs=[(shape((total, ch), F32), None, None)],
        name="readout_backward",
    )(source)[0]


def post_backward(source, refined_grad, weights, taps, act, red, conv, nrm, std, pool):
    total, ch = act.shape
    n = weights.shape[0]
    share = ch // n
    rows = total // n
    depth = total // (pool * pool)

    def kernel(src, rg, w, tap, act_ref, red_ref, conv_ref, norm_ref, std_ref, exp_out, redg_out, taps_out, gain_out, *rest):
        back_out, (grad, cgrad) = rest[:n], rest[n:]
        gain = gain_row(w, n, share)

        def norm(i, total_gain):
            for t in range(3):
                at = pl.ds(i * 48 + 16 * t, 16)
                nm = norm_ref[at, :].astype(F32)
                ng = rg[at, :] * silu_slope(nm * gain)
                sc = ng * gain
                one = jnp.mean(sc, -1, keepdims=True)
                two = jnp.mean(sc * nm, -1, keepdims=True)
                exp_out[at, :] = (std_ref[at, :] * (sc - one - nm * two)).astype(BF)
                g = ng * nm
                total_gain = total_gain + g[:8] + g[8:]
            return total_gain

        gains = jnp.zeros((8, ch), F32)
        for i in range(total // 48):
            gains = norm(i, gains)
        gain_out[...] = gains
        for q in range(n):
            cut = slice(q * share, (q + 1) * share)
            cg = 0.0
            for c in range(n):
                cg = cg + dot(exp_out[:, c * share : (c + 1) * share], w[c, share : 2 * share, cut], NT)
            cgrad[:, cut] = cg
        first, last = edge_masks(total, pool, depth)
        step = pool * depth

        def back(lanes):
            g = (cgrad[:, lanes] * silu_slope(conv_ref[:, lanes].astype(F32))).astype(BF).astype(F32)
            x = act_ref[:, lanes].astype(F32)
            moves = [columns_moved(g, -depth, first, last), g, columns_moved(g, depth, first, last)]
            none = jnp.zeros((step, LANES), F32)
            xs = [
                jnp.concatenate([none, x[:-step]], 0),
                x,
                jnp.concatenate([x[step:], none], 0),
            ]
            for a in range(3):
                for b in range(3):
                    prod = xs[a] * moves[b]
                    taps_out[3 * a + b, :, lanes] = jnp.sum(prod.reshape(total // 8, 8, LANES), 0)
            t = [sum(moves[b] * tap[pl.ds(3 * a + b, 1), lanes] for b in range(3)) for a in range(3)]
            d = t[1] + jnp.concatenate([t[0][step:], none], 0) + jnp.concatenate([none, t[2][:-step]], 0)
            redg_out[:, lanes] = (d * silu_slope(red_ref[:, lanes].astype(F32))).astype(BF)

        chunks(ch // LANES, back)
        for c in range(n):
            cut = slice(c * share, (c + 1) * share)
            grad[:, cut] = rg[:, cut] + dot(redg_out[...], w[c, :share], NT)
        for r in range(n):
            at = pl.ds(pl.multiple_of(src[r] * rows, 8), rows)
            back_out[r][...] = grad[at, :].astype(BF)

    return call(
        kernel,
        grid=(1,),
        prefetch=1,
        ins=[(a, None, None) for a in (refined_grad, weights, taps, act, red, conv, nrm, std)],
        outs=[
            (s, None, None)
            for s in (
                shape((total, ch), BF),
                shape((total, ch), BF),
                shape((9, 8, ch), F32),
                shape((8, ch), F32),
                *[shape((rows, ch), BF)] * n,
            )
        ],
        scratch=[pltpu.VMEM((total, ch), F32), pltpu.VMEM((total, ch), F32)],
        name="post_backward",
    )(source)


def cotangent_by_image(cotangent, select, pairs):
    rows, width = cotangent.shape
    size = select.shape[0]
    each = size // pairs
    per = 3

    def kernel(x, sel, *outs):
        for q in range(per):
            y = dot(sel[...], x[pl.ds(q * size, size), :]).astype(BF)
            for s in range(pairs):
                outs[s][pl.ds(q * each, each), :] = y[s * each : (s + 1) * each]

    return call(
        kernel,
        grid=(rows // (per * size),),
        ins=[(far(cotangent), (per * size, width), lambda i: (i, 0)), (select, None, None)],
        outs=[(shape((rows // pairs, width), BF), (per * each, width), lambda i: (i, 0))] * pairs,
        name="cotangent_by_image",
    )()


def token_block(chan, source, pair_of, low, place, readout, cotangent):
    pairs, (rows, ch) = len(low), low[0].shape
    width = cotangent[0].shape[1]
    size = place.shape[0]
    each = size // pairs
    per = 3
    block = per * each

    def kernel(chan_ref, src, pair, *refs):
        lows, cots, (place_ref, ro, tok_out, piece_out, cot) = refs[:pairs], refs[pairs : 2 * pairs], refs[2 * pairs :]
        for k in range(pairs):
            cot[pair[k]] = cots[k][...]
        logits = dot(jnp.concatenate([v[...] for v in lows], 0), ro[...])
        value, slope = gelu_parts(logits)
        value = value.astype(BF)
        for k in range(pairs):
            piece_out[k] = (cot[src[k]].astype(F32) * slope[k * block : (k + 1) * block]).astype(BF)
        for q in range(per):
            x = jnp.concatenate([value[k * block + q * each : k * block + (q + 1) * each] for k in range(pairs)], 0)
            tok_out[pl.ds(q * size, size), :] = dot(place_ref[...], x).astype(BF)

    rows_at = lambda i, c, s, p: (i, 0)
    return call(
        kernel,
        grid=(rows // block,),
        prefetch=3,
        ins=[
            *[(v, (block, ch), rows_at) for v in low],
            *[(v, (block, width), rows_at) for v in cotangent],
            (place, None, None),
            (far(readout), (ch, width), lambda i, c, s, p: (0, c[0])),
        ],
        outs=[
            (shape((pairs * rows, width), BF), (pairs * block, width), rows_at),
            (shape((pairs, rows, width), BF), (pairs, block, width), lambda i, c, s, p: (0, i, 0)),
        ],
        scratch=[pltpu.VMEM((pairs, block, width), BF)],
        name="token_block",
    )(chan, source, pair_of)


def pre_backward(order, returned, spread_up, nrm, std, gain, conv, pre_expand):
    slots, cells, ch = nrm.shape
    n = order.shape[0]
    part = slots // n
    wide = 24
    rows = part * cells

    def kernel(order_ref, *refs):
        ret, refs = refs[:n], refs[n:]
        up, norm_ref, std_ref, gn, conv_ref, we, exp_out, conv_grad_out, top_out, bottom_out, gain_out, grad, cgrad = refs
        k = pl.program_id(0)
        for i in range(n):

            @pl.when(k == i)
            def _():
                grad[...] = dot(up[...], ret[i][...])

        def norm(i, total_gain):
            u, j = i // (cells // 48), i % (cells // 48)
            for t in range(3):
                at = pl.ds(j * 48 + 16 * t, 16)
                nm = norm_ref[u, at, :].astype(F32)
                ng = grad[pl.ds(i * 48 + 16 * t, 16), :] * silu_slope(nm * gn[...])
                sc = ng * gn[...]
                one = jnp.mean(sc, -1, keepdims=True)
                two = jnp.mean(sc * nm, -1, keepdims=True)
                exp_out[u, at, :] = (std_ref[u, at, :] * (sc - one - nm * two)).astype(BF)
                g = ng * nm
                total_gain = total_gain + g[:8] + g[8:]
            return total_gain

        gains = jnp.zeros((8, ch), F32)
        for i in range(rows // 48):
            gains = norm(i, gains)

        @pl.when(k == 0)
        def _():
            gain_out[...] = gains

        @pl.when(k > 0)
        def _():
            gain_out[...] += gains

        cgrad[...] = dot(exp_out[...].reshape(rows, ch), we[...], NT)
        for u in range(part):

            def slope(lanes):
                g = cgrad[pl.ds(u * cells, cells), lanes] * silu_slope(conv_ref[u, :, lanes].astype(F32))
                conv_grad_out[u, :, lanes] = g.astype(BF)
                top_out[u, :, lanes] = g[:wide].astype(BF)
                bottom_out[u, :, lanes] = g[cells - wide :].astype(BF)

            chunks(ch // LANES, slope)

    by_order = lambda k, order: (order[k], 0, 0)
    whole = (part, cells, ch)
    edge = (part, wide, ch)
    return call(
        kernel,
        grid=(n,),
        prefetch=1,
        ins=[
            *[(r, None, None) for r in returned],
            (spread_up, None, None),
            (far(nrm), whole, by_order),
            (far(std), (part, cells, 1), by_order),
            (gain, None, None),
            (far(conv), whole, by_order),
            (far(pre_expand), None, None),
        ],
        outs=[
            (shape((slots, cells, ch), BF), whole, by_order),
            (far((slots, cells, ch), BF), whole, by_order),
            (shape((slots, wide, ch), BF), edge, by_order),
            (shape((slots, wide, ch), BF), edge, by_order),
            (shape((8, ch), F32), None, None),
        ],
        scratch=[pltpu.VMEM((rows, ch), F32), pltpu.VMEM((rows, ch), F32)],
        name="pre_backward",
    )(order)


def pre_conv_backward(conv_grad, above, below, reduced, taps):
    slots, cells, ch = reduced.shape
    wide = above.shape[1]
    high = cells // wide

    def kernel(cg, up, down, red, tap, redg_out, taps_out):
        step = pl.program_id(0)
        first, last = edge_masks(wide, wide, 1)

        @pl.when(step == 0)
        def _():
            taps_out[...] = jnp.zeros_like(taps_out)

        def back(lanes):
            w = [tap[pl.ds(i, 1), lanes] for i in range(9)]
            mid = cg[0, :, lanes].astype(F32)
            rows = [up[0, :, lanes].astype(F32)]
            rows += [mid[i * wide : (i + 1) * wide] for i in range(high)]
            rows += [down[0, :, lanes].astype(F32)]
            whole = red[0, :, lanes].astype(F32)
            v = [whole[i * wide : (i + 1) * wide] for i in range(high)]
            s = [sigmoid(t) for t in v]
            x = [(a * b).astype(BF).astype(F32) for a, b in zip(v, s)]
            d = [0.0] * high
            sums = [0.0] * 9
            for p in range(high + 2):
                g = rows[p]
                moves = [columns_moved(g, -1, first, last), g, columns_moved(g, 1, first, last)]
                for a in range(3):
                    i = p - 1 + a - 1
                    if 0 <= i < high:
                        for b in range(3):
                            d[i] = d[i] + moves[b] * w[3 * a + b]
                            prod = x[i] * moves[b]
                            sums[3 * a + b] = sums[3 * a + b] + (prod[:8] + prod[8:16] + prod[16:])
            out = [d[i] * (s[i] * (1.0 + v[i] * (1.0 - s[i]))) for i in range(high)]
            redg_out[0, :, lanes] = jnp.concatenate(out, 0).astype(BF)
            for i in range(9):
                taps_out[i, :, lanes] += sums[i]

        chunks(ch // LANES, back)

    image = lambda i: (i, 0, 0)
    return call(
        kernel,
        grid=(slots,),
        ins=[
            (far(conv_grad), (1, cells, ch), image),
            (far(above), (1, wide, ch), image),
            (far(below), (1, wide, ch), image),
            (far(reduced), (1, cells, ch), image),
            (taps, None, None),
        ],
        outs=[
            (shape((slots, cells, ch), BF), (1, cells, ch), image),
            (shape((9, 8, ch), F32), None, None),
        ],
        name="pre_conv_backward",
    )()


def feature_backward(order, reduced_grad, pre_reduce, returned, spread_up):
    slots, cells, ch = reduced_grad.shape
    n = order.shape[0]
    part = slots // n

    def kernel(order_ref, rg, wr, up, *refs):
        ret, out = refs[:n], refs[n]
        k = pl.program_id(0)
        for i in range(n):

            @pl.when(k == i)
            def _():
                out[...] = dot(up[...], ret[i][...]).reshape(part, cells, ch)

        out[...] += dot(rg[...].reshape(part * cells, ch), wr[...], NT).reshape(part, cells, ch)

    by_order = lambda k, order: (order[k], 0, 0)
    whole = (part, cells, ch)
    return call(
        kernel,
        grid=(n,),
        prefetch=1,
        ins=[
            (reduced_grad, whole, by_order),
            (far(pre_reduce), None, None),
            (spread_up, None, None),
            *[(r, None, None) for r in returned],
        ],
        outs=[(shape((slots, cells, ch), F32), whole, by_order)],
        name="feature_backward",
    )(order)[0]


def post_weight_grads(flat, reduced_grad, act, expanded_grad, n):
    total, ch = flat.shape
    share = ch // n
    rows = share // 8

    def kernel(x, g, a, e, out):
        for c in range(n):
            cut = slice(c * share, (c + 1) * share)
            v = dot(x[:, cut], g[...], TN).astype(BF)
            for d in range(8):
                out[d, c, :, :ch] = v[d * rows : (d + 1) * rows]
            for q in range(n):
                v = dot(a[:, q * share : (q + 1) * share], e[:, cut], TN).astype(BF)
                for d in range(8):
                    out[d, c, :, ch + q * share : ch + (q + 1) * share] = v[d * rows : (d + 1) * rows]

    return call(
        kernel,
        grid=(1,),
        ins=[(v, None, None) for v in (flat, reduced_grad, act, expanded_grad)],
        outs=[(far((8, n, rows, 2 * ch), BF), None, None)],
        name="post_weight_grads",
    )()[0]


def readout_weight_grad(low, piece, n):
    pairs, total, width = piece.shape
    ch = low[0].shape[1]
    share = ch // n
    halves, groups, eight = 2, 16, 8

    def kernel(*refs):
        x, (g, out) = refs[:pairs], refs[pairs:]
        x = jnp.concatenate([v[...] for v in x], 0)
        v = dot(x, g[...].reshape(pairs * total, width), TN)
        out[:, :, 0] = v.reshape(halves, groups, eight, width).astype(BF)

    return call(
        kernel,
        grid=(n,),
        ins=[(v, (total, share), lambda c: (0, c)) for v in low] + [(piece, None, None)],
        outs=[(shape((halves, groups, n, eight, width), BF), (halves, groups, 1, eight, width), lambda c: (0, 0, c, 0, 0))],
        name="readout_weight_grad",
    )()[0].reshape(ch, width)


def cross(n, k):
    return [(a * n + b, ((b + k) % n) * n + a) for a in range(n) for b in range(n)]


def turn(n, k):
    return [(i, (i + k) % n) for i in range(n)]


def other_core(values):
    return lax.ppermute(values, "core", [(0, 1), (1, 0)])


def small_rows(*grads):
    ch = grads[0].shape[-1]
    counts = [g.shape[0] if g.ndim == 3 else 1 for g in grads]
    per = ch // LANES

    def kernel(*refs):
        out = refs[-1]
        at = 0
        for ref, count in zip(refs, counts):
            for i in range(count):
                v = jnp.sum(ref[i] if len(ref.shape) == 3 else ref[...], 0, keepdims=True)
                for q in range(per):
                    out[pl.ds(at, 1), :] = v[:, q * LANES : (q + 1) * LANES]
                    at += 1

    return call(
        kernel,
        grid=(1,),
        ins=[(g, None, None) for g in grads],
        outs=[(shape((sum(counts) * per, LANES), F32), None, None)],
        name="small_rows",
    )()[0]


def join_halves(core, mine, theirs, small, their_small, parts):
    rows, ch = mine[0].shape
    half = rows // 2
    width = len(mine) * ch + LANES
    count = small.shape[0]
    m = len(mine)
    steps = 2
    block = half // steps

    def kernel(core_ref, *refs):
        own, got = refs[:m], refs[m : 2 * m]
        sm, got_sm, out = refs[2 * m :]
        for i in range(m):
            out[:, i * ch : (i + 1) * ch] = (own[i][...].astype(F32) + got[i][...].astype(F32)).astype(BF)
        first = ((core_ref[0] == 0) & (pl.program_id(0) == 0)).astype(F32)
        total = (sm[...] + got_sm[...]) * first
        pad = jnp.zeros((block - count, LANES), F32)
        out[:, m * ch :] = jnp.concatenate([total, pad], 0).astype(BF)

    return call(
        kernel,
        grid=(steps,),
        prefetch=1,
        ins=[(v, (block, ch), lambda i, c: (c[0] * steps + i, 0)) for v in mine]
        + [(v, (block, ch), lambda i, c: (i, 0)) for v in theirs]
        + [(v, None, None) for v in (small, their_small)],
        outs=[(far((half, width), BF), (block, width), lambda i, c: (i, 0))],
        name="join_halves",
    )(core)[0].reshape(parts, half // parts, width)


def sum_and_copy(blocks, post, n, ch):
    parts, rows, width = blocks.shape
    kept = width - ch

    def kernel(x, post_ref, out, read_out):
        read_out[:, : 2 * ch] = post_ref[...]
        for i in range(width // LANES):
            at = i * LANES
            v = x[:, :, at : at + LANES].astype(F32)
            if 2 * ch <= at < 3 * ch:
                v = jnp.sum(v.reshape(parts // n, n, rows, LANES), 0)
                for c in range(n):
                    to = c * ch + at
                    read_out[:, to : to + LANES] = v[c].astype(BF)
            else:
                to = at if at < 2 * ch else at - ch
                total = jnp.sum(v, 0).astype(BF)
                out[:, :, to : to + LANES] = jnp.broadcast_to(total[None], (parts, rows, LANES))

    return call(
        kernel,
        grid=(1,),
        ins=[(blocks, None, None), (post, None, None)],
        outs=[(far((parts, rows, kept), BF), None, None), (far((rows, (2 + n) * ch), BF), None, None)],
        name="sum_and_copy",
    )()


def finish_pre(place, half_rows, ch, earlier=()):
    half, width = half_rows.shape
    m = (width - LANES) // ch
    steps = 4
    block = half // steps

    def kernel(place_ref, x, *outs):
        outs = outs[len(earlier) :]
        for i in range(m):
            outs[i][...] = x[:, i * ch : (i + 1) * ch].astype(F32)
        outs[m][...] = x[:, m * ch :].astype(F32)

    return call(
        kernel,
        grid=(steps,),
        prefetch=1,
        ins=[(half_rows, (block, width), lambda i, c: (i, 0))],
        outs=[(shape((2 * half, ch), F32), (block, ch), lambda i, c: (c[0] * steps + i, 0)) for _ in range(m)]
        + [(shape((half, LANES), F32), (block, LANES), lambda i, c: (i, 0))],
        aliased=earlier,
        name="finish_pre",
    )(place)


def finish_post(place, gathered, n, earlier=()):
    groups, per, width = gathered.shape
    share = 2 * groups * per
    ch = width // (n + 2)

    def kernel(place_ref, x, *outs):
        reduce_out, expand_out, read_out = outs[len(earlier) :]
        reduce_out[...] = x[0, :, :ch].astype(F32)
        for q in range(n):
            expand_out[q] = x[0, :, ch + q * share : ch + (q + 1) * share].astype(F32)
        read_out[...] = x[0, :, 2 * ch :].astype(F32)

    return call(
        kernel,
        grid=(groups,),
        prefetch=1,
        ins=[(gathered, (1, per, width), lambda i, c: (i, 0, 0))],
        outs=[
            (shape((share, ch), F32), (per, ch), lambda i, c: (2 * i + c[0], 0)),
            (shape((n, share, share), F32), (n, per, share), lambda i, c: (0, 2 * i + c[0], 0)),
            (shape((share, n * ch), F32), (per, n * ch), lambda i, c: (groups * c[0] + i, 0)),
        ],
        aliased=earlier,
        name="finish_post",
    )(place)


def after(values, *earlier):
    return lax.optimization_barrier((values, *earlier))[0]


def pool_matrix(part, high, wide):
    half = wide // 2
    m = np.zeros((high // 2 * half * part, part * (high // 2) * wide), np.float32)
    for u in range(part):
        for i in range(high // 2):
            for j in range(wide):
                m[(i * half + j // 2) * part + u, (u * (high // 2) + i) * wide + j] = 0.25
    return m


def spread_matrix(part, high, wide):
    half = wide // 2
    m = np.zeros((part * high * wide, high // 2 * half * part), np.float32)
    for u in range(part):
        for i in range(high):
            for j in range(wide):
                m[(u * high + i) * wide + j, ((i // 2) * half + j // 2) * part + u] = 0.25
    return m


def body(features, counts, pre_reduce, pre_conv, pre_expand, pre_gain, post_reduce, post_conv, post_expand, post_gain, readout, cotangent):
    n = lax.axis_size("chan")
    row = lax.axis_index("rows").astype(jnp.int32)
    chan = lax.axis_index("chan").astype(jnp.int32)
    core = lax.axis_index("core").astype(jnp.int32)
    ch = pre_reduce.shape[0]
    slots, high, wide = features.shape[0], features.shape[1], features.shape[2]
    part = slots // n
    cells = high * wide
    pool = wide // 2
    share = ch // n
    out_share = cotangent.shape[3]
    steps = jnp.arange(n, dtype=jnp.int32)
    order = (row + steps) % n
    source = (row - steps) % n
    pair_of = (chan + steps) % n
    rank = jnp.full((1,), chan, jnp.int32)
    core_at = jnp.full((1,), core, jnp.int32)
    pre_taps = pre_conv.astype(F32).reshape(9, ch)
    post_taps = post_conv.astype(F32).reshape(9, ch)
    pre_gain_row = pre_gain.reshape(1, ch)
    pool_m = jnp.asarray(pool_matrix(part, high, wide), BF)
    up_m = jnp.asarray(spread_matrix(part, high, wide), BF)

    ends = n - 1
    down_pairs = [(i, i + 1) for i in range(ends)]
    up_pairs = [(i + 1, i) for i in range(ends)]
    above = lax.ppermute(features[:, -1], "rows", down_pairs)
    below = lax.ppermute(features[:, 0], "rows", up_pairs)
    gain_hi = post_gain.astype(BF)
    gain_lo = (post_gain - gain_hi.astype(F32)).astype(BF)
    gain_row = jnp.concatenate([gain_hi, gain_lo, jnp.zeros((ch - 2 * share,), BF)])[None]
    square = post_expand.reshape(n, share, share)
    shards = jnp.concatenate(
        [post_reduce, jnp.concatenate([square[q] for q in range(n)], axis=1), jnp.pad(gain_row, ((0, 63), (0, 0)))], axis=0
    )
    shard = lax.dynamic_index_in_dim(shards.reshape(2, -1, ch), core, 0, keepdims=False)
    full = lax.all_gather(shard, ("chan", "core"), axis=0, tiled=True)
    full = full.reshape(n, 2 * share + 64, ch)
    flat_features = features.reshape(slots * cells, ch)
    live = (jnp.arange(SLOT)[None, :] < counts[:, None]).astype(F32).reshape(slots)
    size, each = 16 * slots, 16 * part
    at = lax.broadcasted_iota(jnp.int32, (size, size), 0)
    column = lax.broadcasted_iota(jnp.int32, (size, size), 1)
    wanted = (at % each) // part * slots + part * ((chan + at // each) % n) + at % part
    select = jnp.where(column == wanted, jnp.tile(live, 16)[None, :], 0.0).astype(BF)
    wanted = (column % each) // part * slots + part * ((row - column // each) % n) + column % part
    place = jnp.where(at == wanted, 1.0, 0.0).astype(BF)
    cot_rows = cotangent.transpose(1, 2, 0, 3).reshape(-1, out_share)
    sends = cotangent_by_image(cot_rows, select, n)
    away = after(sends, above, below)
    cots = [lax.ppermute(away[k], ("rows", "chan"), cross(n, k)) for k in range(n)]

    reduced, convolved, convolved_act, normal_pre, pre_std, *pooled = pre_forward(
        order, above, below, features, pre_reduce, pre_taps, pre_expand, pre_gain_row, pool_m
    )

    pooled = after(pooled, cots)
    moved = [pooled[0]] + [lax.ppermute(pooled[k], "rows", turn(n, k)) for k in range(1, n)]
    flat, post_reduced, post_act, post_convolved, post_cact, post_normal, post_std, low = post_forward(
        source, moved, full, post_taps, pool
    )
    lows = [low] + [lax.ppermute(low, "chan", turn(n, k)) for k in range(1, n)]
    refined_grad = readout_backward(source, low, readout, cots)
    post_expanded_grad, post_reduced_grad, post_taps_grad, post_gain_grad, *back = post_backward(
        source, refined_grad, full, post_taps, post_act, post_reduced, post_convolved, post_normal, post_std, pool
    )

    returned = [back[0]] + [lax.ppermute(back[k], "rows", turn(n, -k)) for k in range(1, n)]

    flat = after(flat, lows)
    load = post_weight_grads(flat, post_reduced_grad, post_cact, post_expanded_grad, n)

    post_sum = lax.psum_scatter(load, ("x", "core"), scatter_dimension=0, tiled=False)

    stacked = jnp.stack(after(lows, load, returned))
    lows = [lax.dynamic_index_in_dim(stacked, (chan - row - k) % n, 0, keepdims=False) for k in range(n)]
    lows = [lows[0]] + [lax.ppermute(lows[k], "rows", turn(n, k)) for k in range(1, n)]

    expanded_grad, convolved_grad, top, bottom, pre_gain_grad = pre_backward(
        order, returned, up_m, normal_pre, pre_std, pre_gain_row, convolved, pre_expand
    )
    top, bottom, lows[1], lows[3] = lax.optimization_barrier((top, bottom, lows[1], lows[3]))
    grad_above = lax.ppermute(bottom, "rows", down_pairs)
    grad_below = lax.ppermute(top, "rows", up_pairs)
    act_rows = after(convolved_act, bottom).reshape(-1, ch)
    pre_expand_grad = dot(act_rows, expanded_grad.reshape(-1, ch), TN).astype(BF)

    eight = share // 32
    post_sum = post_sum.reshape(n, 4, eight, 2 * ch).transpose(1, 0, 2, 3)
    lows = after(lows, pre_expand_grad, post_sum)
    post_sum = lax.psum_scatter(post_sum, "rows", scatter_dimension=0, tiled=False)
    tokens, piece = token_block(rank, source, pair_of, lows, place, readout, sends)
    read_grad = readout_weight_grad(lows, after(piece, grad_above, grad_below), n)
    tokens = tokens.reshape(pool, pool, slots, out_share).transpose(2, 0, 1, 3)
    convolved_grad = after(convolved_grad, read_grad, post_sum)
    reduced_grad, pre_taps_grad = pre_conv_backward(convolved_grad, grad_above, grad_below, reduced, pre_taps)
    small = small_rows(pre_taps_grad, pre_gain_grad, post_taps_grad, post_gain_grad)
    post_sum = lax.psum_scatter(post_sum, "chan", scatter_dimension=0, tiled=False)
    pre_reduce_grad = dot(after(flat_features, small), reduced_grad.reshape(-1, ch), TN).astype(BF)

    chips = ("x", "rows", "chan")
    mine = [pre_reduce_grad, pre_expand_grad, read_grad]
    theirs = [other_core(lax.dynamic_index_in_dim(g.reshape(2, ch // 2, ch), 1 - core, 0, keepdims=False)) for g in mine]
    load = join_halves(core_at, mine, theirs, small, other_core(small), 64)
    pieces = lax.all_to_all(load, chips, 0, 0, tiled=False)
    feature_grad = feature_backward(order, after(reduced_grad, load, post_sum), pre_reduce, returned, up_m).reshape(features.shape)

    load, rest = sum_and_copy(after(pieces, feature_grad), post_sum, n, ch)
    rest = lax.all_gather(rest, ("x", "rows"), axis=0, tiled=True).reshape(4, 4 * eight, -1)
    load_all = lax.all_to_all(load, chips, 0, 0, tiled=False).reshape(ch // 2, -1)

    def finish(kernel, values, *sizes):
        theirs = other_core(values)
        own = kernel(core_at, values, *sizes)
        theirs = after(theirs, *own)
        return own, theirs

    own, theirs = finish(finish_pre, load_all, ch)
    pre_reduce_out, pre_expand_out, small_their = finish_pre(1 - core_at, theirs, ch, earlier=tuple(own[:2]))
    small_out = jnp.where(core == 0, own[2], small_their)
    own, theirs = finish(finish_post, after(rest, pre_reduce_out), n)
    post_reduce_out, post_expand_out, readout_out = finish_post(1 - core_at, theirs, n, earlier=tuple(own))
    per = ch // LANES
    cut = [0, 9 * per, 10 * per, 19 * per, 20 * per]
    pre_conv_out, pre_gain_out, post_conv_out, post_gain_out = [small_out[a:b] for a, b in zip(cut, cut[1:])]
    return (
        tokens,
        feature_grad,
        pre_reduce_out,
        pre_conv_out.reshape(3, 3, ch),
        pre_expand_out,
        pre_gain_out.reshape(ch),
        post_reduce_out,
        post_conv_out.reshape(3, 3, ch),
        post_expand_out.reshape(ch, share),
        lax.dynamic_slice_in_dim(post_gain_out.reshape(ch), chan * share, share, 0),
        readout_out,
    )


def solution(mesh):
    grid = Mesh(mesh.devices.reshape(4, 2, 4, 4), ("x", "core", "rows", "chan"))
    images = P(("x", "core", "chan"), "rows", None, None)
    grids = P(("x", "core", "rows"), None, None, "chan")
    return jax.shard_map(
        body,
        mesh=grid,
        in_specs=(
            images,
            P(("x", "core", "rows")),
            P(),
            P(),
            P(),
            P(),
            P("chan", None),
            P(),
            P(None, "chan"),
            P("chan"),
            P(),
            grids,
        ),
        out_specs=(grids, images, P(), P(), P(), P(), P("chan", None), P(), P(None, "chan"), P("chan"), P("chan", None)),
        check_vma=False,
    )
```

```python
import functools

import jax
import jax.numpy as jnp
import numpy as np
from jax import lax
from jax.experimental import pallas as pl
from jax.experimental.pallas import tpu as pltpu
from jax.sharding import Mesh, PartitionSpec as P

SLOT = 4
EPS = 1e-06
BF = jnp.bfloat16
F32 = jnp.float32
LANES = 128
VMEM_LIMIT = 20 * 1024 * 1024
NN = ((1,), (0,))
NT = ((1,), (1,))
TN = ((0,), (0,))


def dot(a, b, dims=NN):
    return lax.dot_general(a, b, (dims, ((), ())), preferred_element_type=F32)


def sigmoid(v):
    return 0.5 * jnp.tanh(0.5 * v) + 0.5


def silu(v):
    return v * sigmoid(v)


def silu_slope(v):
    s = sigmoid(v)
    return s * (1.0 + v * (1.0 - s))


def gelu_parts(v):
    c = 0.7978845608028654
    square = v * v
    t = jnp.tanh(v * (c + (c * 0.044715) * square))
    half = 0.5 * (1.0 + t)
    slope = half + 0.5 * v * (1.0 - t * t) * (c + (3.0 * c * 0.044715) * square)
    return v * half, slope


def chunks(count, body, width=LANES):
    for i in range(count):
        body(pl.ds(i * width, width))


def call(kernel, *, grid, ins, outs, scratch=(), prefetch=0, aliased=(), cost=1, name):
    def spec(shape, block, index):
        if block is None:
            block, index = shape, lambda *_: (0,) * len(shape)
        return pl.BlockSpec(block, index)

    arrays = [i[0] for i in ins] + list(aliased)
    in_specs = [spec(a.shape, b, m) for a, b, m in ins] + [pl.BlockSpec(memory_space=pl.ANY)] * len(aliased)
    out_specs = [spec(s.shape, b, m) for s, b, m in outs]

    def run(*scalars):
        return pl.pallas_call(
            kernel,
            grid_spec=pltpu.PrefetchScalarGridSpec(
                num_scalar_prefetch=prefetch,
                grid=grid,
                in_specs=in_specs,
                out_specs=out_specs,
                scratch_shapes=list(scratch),
            ),
            out_shape=[s[0] for s in outs],
            compiler_params=pltpu.CompilerParams(
                dimension_semantics=("arbitrary",) * len(grid), vmem_limit_bytes=VMEM_LIMIT
            ),
            input_output_aliases={prefetch + len(ins) + i: i for i in range(len(aliased))},
            cost_estimate=pl.CostEstimate(flops=cost, bytes_accessed=1, transcendentals=0),
            name=name,
        )(*scalars, *arrays)

    return run


def shape(dims, dtype):
    return jax.ShapeDtypeStruct(dims, dtype)


def far(values, dtype=None):
    if dtype is None:
        return pltpu.with_memory_space_constraint(values, pltpu.HBM)
    return pltpu.HBM(values, dtype)


def columns_moved(t, by, first, last):
    rows = t.shape[0]
    return pltpu.roll(t, by % rows, 0) * (first if by > 0 else last)


def edge_masks(rows, width, depth):
    at = lax.broadcasted_iota(jnp.int32, (rows, LANES), 0) % (width * depth)
    return (at >= depth).astype(F32), (at < (width - 1) * depth).astype(F32)


def pre_forward(order, above, below, features, pre_reduce, taps, pre_expand, gain, pool):
    slots, high, wide, ch = features.shape
    cells = high * wide
    n = order.shape[0]
    part = slots // n
    rows_all = part * cells

    def kernel(order_ref, up_ref, down_ref, feat, wr, tap, we, gn, pool_ref, red_out, conv_out, act_out, norm_out, std_out, *rest):
        pooled_out, (red, halo, exp, sums) = rest[:n], rest[n:]
        k = pl.program_id(0)
        for side, ref in enumerate((up_ref, down_ref)):
            halo[side] = dot(ref[...].reshape(part * wide, ch), wr[...]).reshape(part, wide, ch)
        red[...] = dot(feat[...].reshape(rows_all, ch), wr[...]).reshape(part, cells, ch)
        red_out[...] = red[...].astype(BF)
        first, last = edge_masks(wide, wide, 1)
        for u in range(part):

            def conv(lanes):
                w = [tap[pl.ds(i, 1), lanes] for i in range(9)]
                rows = [halo[0, u, :, lanes]]
                rows += [red[u, pl.ds(i * wide, wide), lanes] for i in range(high)]
                rows += [halo[1, u, :, lanes]]
                rows = [silu(r).astype(BF).astype(F32) for r in rows]
                out = []
                for i in range(high):
                    t = [sum(rows[i + a] * w[3 * a + b] for a in range(3)) for b in range(3)]
                    out.append(t[1] + columns_moved(t[0], 1, first, last) + columns_moved(t[2], -1, first, last))
                conv_out[u, :, lanes] = jnp.concatenate(out, 0).astype(BF)
                act_out[u, :, lanes] = jnp.concatenate([silu(c) for c in out], 0).astype(BF)

            chunks(ch // LANES, conv)

        exp[...] = dot(act_out[...].reshape(rows_all, ch), we[...])

        def norm(p, carry):
            u, i = p // (high // 2), p % (high // 2)
            tiles = wide // 8
            f = [feat[u, 2 * i + half].astype(F32) for half in range(2)]
            nrms, blends = [], []
            for t in range(2 * tiles):
                e = exp[pl.ds(p * 2 * wide + 8 * t, 8), :]
                mean = jnp.mean(e, -1, keepdims=True)
                square = jnp.mean(e * e, -1, keepdims=True)
                std = lax.rsqrt(square - mean * mean + EPS)
                nrm = (e - mean) * std
                std_out[u, pl.ds(i * 2 * wide + 8 * t, 8), :] = std
                nrms.append(nrm)
                at = t % tiles
                blends.append(f[t // tiles][8 * at : 8 * at + 8] + silu(nrm * gn[...]))
                if t % 2 == 1:
                    both = jnp.concatenate(nrms[-2:], 0).astype(BF)
                    norm_out[u, pl.ds(i * 2 * wide + 8 * (t - 1), 16), :] = both
            for t in range(tiles):
                sums[pl.ds(p * wide + 8 * t, 8), :] = blends[t] + blends[tiles + t]
            return carry

        for p in range(part * high // 2):
            norm(p, 0)
        s = sums[...]
        hi = s.astype(BF)
        lo = (s - hi.astype(F32)).astype(BF)
        pooled = (dot(pool_ref[...], hi) + dot(pool_ref[...], lo)).astype(BF)
        for i in range(n):

            @pl.when(k == i)
            def _():
                pooled_out[i][...] = pooled

    def by_order(rest):
        return lambda k, order: (order[k],) + (0,) * rest

    pooled_rows = pool.shape[0]
    block = (part, cells, ch)
    return call(
        kernel,
        grid=(n,),
        prefetch=1,
        ins=[
            (far(above), (part, wide, ch), by_order(2)),
            (far(below), (part, wide, ch), by_order(2)),
            (far(features), (part, high, wide, ch), by_order(3)),
            (far(pre_reduce), None, None),
            (taps, None, None),
            (far(pre_expand), None, None),
            (gain, None, None),
            (pool, None, None),
        ],
        outs=[(far((slots, cells, ch), BF), block, by_order(2))] * 4
        + [(far((slots, cells, 1), F32), (part, cells, 1), by_order(2))]
        + [(shape((pooled_rows, ch), BF), None, None)] * n,
        scratch=[
            pltpu.VMEM((part, cells, ch), F32),
            pltpu.VMEM((2, part, wide, ch), F32),
            pltpu.VMEM((rows_all, ch), F32),
            pltpu.VMEM((rows_all // 2, ch), F32),
        ],
        name="pre_forward",
    )(order)


def gain_row(w, n, share):
    at = 2 * share
    parts = [w[c, at : at + 16, :].astype(F32)[:1] for c in range(n)]
    return jnp.concatenate([p[:, :share] + p[:, share : 2 * share] for p in parts], 1)


def post_forward(source, moved, weights, taps, pool):
    n, (rows, ch) = len(moved), moved[0].shape
    total = n * rows
    depth = total // (pool * pool)
    share = ch // n

    def kernel(src, *refs):
        got, refs = refs[:n], refs[n:]
        w, tap, flat_out, red_out, act_out, conv_out, cact_out, norm_out, std_out, low_out, wide_ref, red, exp = refs
        for k in range(n):
            at = pl.multiple_of(src[k] * rows, 8)
            wide_ref[pl.ds(at, rows), :] = got[k][...].astype(F32)
        gain = gain_row(w, n, share)
        flat_out[...] = wide_ref[...].astype(BF)
        total_red = 0.0
        for c in range(n):
            total_red = total_red + dot(flat_out[:, c * share : (c + 1) * share], w[c, :share])
        red[...] = total_red
        first, last = edge_masks(total, pool, depth)
        step = pool * depth

        def conv(lanes):
            v = red[:, lanes]
            red_out[:, lanes] = v.astype(BF)
            x = silu(v).astype(BF)
            act_out[:, lanes] = x
            x = x.astype(F32)
            moves = [columns_moved(x, depth, first, last), x, columns_moved(x, -depth, first, last)]
            t = [sum(moves[b] * tap[pl.ds(3 * a + b, 1), lanes] for b in range(3)) for a in range(3)]
            none = jnp.zeros((step, LANES), F32)
            c = t[1] + jnp.concatenate([none, t[0][:-step]], 0) + jnp.concatenate([t[2][step:], none], 0)
            conv_out[:, lanes] = c.astype(BF)
            cact_out[:, lanes] = silu(c).astype(BF)

        chunks(ch // LANES, conv)
        for c in range(n):
            e = 0.0
            for q in range(n):
                cut = slice(q * share, (q + 1) * share)
                e = e + dot(cact_out[:, cut], w[c, share : 2 * share, cut])
            exp[:, c * share : (c + 1) * share] = e

        def norm(i, carry):
            for t in range(3):
                at = pl.ds(i * 48 + 16 * t, 16)
                e = exp[at, :]
                mean = jnp.mean(e, -1, keepdims=True)
                square = jnp.mean(e * e, -1, keepdims=True)
                std = lax.rsqrt(square - mean * mean + EPS)
                nrm = (e - mean) * std
                norm_out[at, :] = nrm.astype(BF)
                std_out[at, :] = std
                low_out[at, :] = (wide_ref[at, :] + silu(nrm * gain)).astype(BF)
            return carry

        for i in range(total // 48):
            norm(i, 0)

    narrow = shape((total, ch), BF)
    return call(
        kernel,
        grid=(1,),
        prefetch=1,
        ins=[(a, None, None) for a in (*map(far, moved), far(weights), taps)],
        outs=[(s, None, None) for s in (narrow, narrow, narrow, narrow, narrow, narrow, shape((total, 1), F32), narrow)],
        scratch=[pltpu.VMEM((total, ch), F32)] * 3,
        name="post_forward",
    )(source)


def readout_backward(source, low, readout, cots):
    total, ch = low.shape
    n, out_share = len(cots), cots[0].shape[1]

    def kernel(src, low_ref, ro, *rest):
        cot, grad = rest[:n], rest[n]
        k = pl.program_id(0)
        logits = dot(low_ref[...], ro[...])
        slope = gelu_parts(logits)[1]
        for i in range(n):

            @pl.when(k == i)
            def _():
                piece = (cot[i][...].astype(F32) * slope).astype(BF)
                term = dot(piece, ro[...], NT)
                grad[...] = term if i == 0 else grad[...] + term

    return call(
        kernel,
        grid=(n,),
        prefetch=1,
        ins=[(low, None, None), (far(readout), (ch, out_share), lambda k, s: (0, s[k]))] + [(c, None, None) for c in cots],
        outs=[(shape((total, ch), F32), None, None)],
        name="readout_backward",
    )(source)[0]


def post_backward(source, refined_grad, weights, taps, act, red, conv, nrm, std, pool):
    total, ch = act.shape
    n = weights.shape[0]
    share = ch // n
    rows = total // n
    depth = total // (pool * pool)

    def kernel(src, rg, w, tap, act_ref, red_ref, conv_ref, norm_ref, std_ref, exp_out, redg_out, taps_out, gain_out, *rest):
        back_out, (grad, cgrad) = rest[:n], rest[n:]
        gain = gain_row(w, n, share)

        def norm(i, total_gain):
            for t in range(3):
                at = pl.ds(i * 48 + 16 * t, 16)
                nm = norm_ref[at, :].astype(F32)
                ng = rg[at, :] * silu_slope(nm * gain)
                sc = ng * gain
                one = jnp.mean(sc, -1, keepdims=True)
                two = jnp.mean(sc * nm, -1, keepdims=True)
                exp_out[at, :] = (std_ref[at, :] * (sc - one - nm * two)).astype(BF)
                g = ng * nm
                total_gain = total_gain + g[:8] + g[8:]
            return total_gain

        gains = jnp.zeros((8, ch), F32)
        for i in range(total // 48):
            gains = norm(i, gains)
        gain_out[...] = gains
        for q in range(n):
            cut = slice(q * share, (q + 1) * share)
            cg = 0.0
            for c in range(n):
                cg = cg + dot(exp_out[:, c * share : (c + 1) * share], w[c, share : 2 * share, cut], NT)
            cgrad[:, cut] = cg
        first, last = edge_masks(total, pool, depth)
        step = pool * depth

        def back(lanes):
            g = (cgrad[:, lanes] * silu_slope(conv_ref[:, lanes].astype(F32))).astype(BF).astype(F32)
            x = act_ref[:, lanes].astype(F32)
            moves = [columns_moved(g, -depth, first, last), g, columns_moved(g, depth, first, last)]
            none = jnp.zeros((step, LANES), F32)
            xs = [
                jnp.concatenate([none, x[:-step]], 0),
                x,
                jnp.concatenate([x[step:], none], 0),
            ]
            for a in range(3):
                for b in range(3):
                    prod = xs[a] * moves[b]
                    taps_out[3 * a + b, :, lanes] = jnp.sum(prod.reshape(total // 8, 8, LANES), 0)
            t = [sum(moves[b] * tap[pl.ds(3 * a + b, 1), lanes] for b in range(3)) for a in range(3)]
            d = t[1] + jnp.concatenate([t[0][step:], none], 0) + jnp.concatenate([none, t[2][:-step]], 0)
            redg_out[:, lanes] = (d * silu_slope(red_ref[:, lanes].astype(F32))).astype(BF)

        chunks(ch // LANES, back)
        for c in range(n):
            cut = slice(c * share, (c + 1) * share)
            grad[:, cut] = rg[:, cut] + dot(redg_out[...], w[c, :share], NT)
        for r in range(n):
            at = pl.ds(pl.multiple_of(src[r] * rows, 8), rows)
            back_out[r][...] = grad[at, :].astype(BF)

    return call(
        kernel,
        grid=(1,),
        prefetch=1,
        ins=[(a, None, None) for a in (refined_grad, weights, taps, act, red, conv, nrm, std)],
        outs=[
            (s, None, None)
            for s in (
                shape((total, ch), BF),
                shape((total, ch), BF),
                shape((9, 8, ch), F32),
                shape((8, ch), F32),
                *[shape((rows, ch), BF)] * n,
            )
        ],
        scratch=[pltpu.VMEM((total, ch), F32), pltpu.VMEM((total, ch), F32)],
        name="post_backward",
    )(source)


def cotangent_by_image(cotangent, select, pairs):
    rows, width = cotangent.shape
    size = select.shape[0]
    each = size // pairs
    per = 3

    def kernel(x, sel, *outs):
        for q in range(per):
            y = dot(sel[...], x[pl.ds(q * size, size), :]).astype(BF)
            for s in range(pairs):
                outs[s][pl.ds(q * each, each), :] = y[s * each : (s + 1) * each]

    return call(
        kernel,
        grid=(rows // (per * size),),
        ins=[(far(cotangent), (per * size, width), lambda i: (i, 0)), (select, None, None)],
        outs=[(shape((rows // pairs, width), BF), (per * each, width), lambda i: (i, 0))] * pairs,
        name="cotangent_by_image",
    )()


def token_block(chan, source, pair_of, low, place, readout, cotangent):
    pairs, (rows, ch) = len(low), low[0].shape
    width = cotangent[0].shape[1]
    size = place.shape[0]
    each = size // pairs
    per = 3
    block = per * each

    def kernel(chan_ref, src, pair, *refs):
        lows, cots, (place_ref, ro, tok_out, piece_out, cot) = refs[:pairs], refs[pairs : 2 * pairs], refs[2 * pairs :]
        for k in range(pairs):
            cot[pair[k]] = cots[k][...]
        logits = dot(jnp.concatenate([v[...] for v in lows], 0), ro[...])
        value, slope = gelu_parts(logits)
        value = value.astype(BF)
        for k in range(pairs):
            piece_out[k] = (cot[src[k]].astype(F32) * slope[k * block : (k + 1) * block]).astype(BF)
        for q in range(per):
            x = jnp.concatenate([value[k * block + q * each : k * block + (q + 1) * each] for k in range(pairs)], 0)
            tok_out[pl.ds(q * size, size), :] = dot(place_ref[...], x).astype(BF)

    rows_at = lambda i, c, s, p: (i, 0)
    return call(
        kernel,
        grid=(rows // block,),
        prefetch=3,
        ins=[
            *[(v, (block, ch), rows_at) for v in low],
            *[(v, (block, width), rows_at) for v in cotangent],
            (place, None, None),
            (far(readout), (ch, width), lambda i, c, s, p: (0, c[0])),
        ],
        outs=[
            (shape((pairs * rows, width), BF), (pairs * block, width), rows_at),
            (shape((pairs, rows, width), BF), (pairs, block, width), lambda i, c, s, p: (0, i, 0)),
        ],
        scratch=[pltpu.VMEM((pairs, block, width), BF)],
        name="token_block",
    )(chan, source, pair_of)


def pre_backward(order, returned, spread_up, nrm, std, gain, conv, pre_expand):
    slots, cells, ch = nrm.shape
    n = order.shape[0]
    part = slots // n
    wide = 24
    rows = part * cells

    def kernel(order_ref, *refs):
        ret, refs = refs[:n], refs[n:]
        up, norm_ref, std_ref, gn, conv_ref, we, exp_out, conv_grad_out, top_out, bottom_out, gain_out, grad, cgrad = refs
        k = pl.program_id(0)
        for i in range(n):

            @pl.when(k == i)
            def _():
                grad[...] = dot(up[...], ret[i][...])

        def norm(i, total_gain):
            u, j = i // (cells // 48), i % (cells // 48)
            for t in range(3):
                at = pl.ds(j * 48 + 16 * t, 16)
                nm = norm_ref[u, at, :].astype(F32)
                ng = grad[pl.ds(i * 48 + 16 * t, 16), :] * silu_slope(nm * gn[...])
                sc = ng * gn[...]
                one = jnp.mean(sc, -1, keepdims=True)
                two = jnp.mean(sc * nm, -1, keepdims=True)
                exp_out[u, at, :] = (std_ref[u, at, :] * (sc - one - nm * two)).astype(BF)
                g = ng * nm
                total_gain = total_gain + g[:8] + g[8:]
            return total_gain

        gains = jnp.zeros((8, ch), F32)
        for i in range(rows // 48):
            gains = norm(i, gains)

        @pl.when(k == 0)
        def _():
            gain_out[...] = gains

        @pl.when(k > 0)
        def _():
            gain_out[...] += gains

        cgrad[...] = dot(exp_out[...].reshape(rows, ch), we[...], NT)
        for u in range(part):

            def slope(lanes):
                g = cgrad[pl.ds(u * cells, cells), lanes] * silu_slope(conv_ref[u, :, lanes].astype(F32))
                conv_grad_out[u, :, lanes] = g.astype(BF)
                top_out[u, :, lanes] = g[:wide].astype(BF)
                bottom_out[u, :, lanes] = g[cells - wide :].astype(BF)

            chunks(ch // LANES, slope)

    by_order = lambda k, order: (order[k], 0, 0)
    whole = (part, cells, ch)
    edge = (part, wide, ch)
    return call(
        kernel,
        grid=(n,),
        prefetch=1,
        ins=[
            *[(r, None, None) for r in returned],
            (spread_up, None, None),
            (far(nrm), whole, by_order),
            (far(std), (part, cells, 1), by_order),
            (gain, None, None),
            (far(conv), whole, by_order),
            (far(pre_expand), None, None),
        ],
        outs=[
            (shape((slots, cells, ch), BF), whole, by_order),
            (far((slots, cells, ch), BF), whole, by_order),
            (shape((slots, wide, ch), BF), edge, by_order),
            (shape((slots, wide, ch), BF), edge, by_order),
            (shape((8, ch), F32), None, None),
        ],
        scratch=[pltpu.VMEM((rows, ch), F32), pltpu.VMEM((rows, ch), F32)],
        name="pre_backward",
    )(order)


def pre_conv_backward(conv_grad, above, below, reduced, taps):
    slots, cells, ch = reduced.shape
    wide = above.shape[1]
    high = cells // wide

    def kernel(cg, up, down, red, tap, redg_out, taps_out):
        step = pl.program_id(0)
        first, last = edge_masks(wide, wide, 1)

        @pl.when(step == 0)
        def _():
            taps_out[...] = jnp.zeros_like(taps_out)

        def back(lanes):
            w = [tap[pl.ds(i, 1), lanes] for i in range(9)]
            mid = cg[0, :, lanes].astype(F32)
            rows = [up[0, :, lanes].astype(F32)]
            rows += [mid[i * wide : (i + 1) * wide] for i in range(high)]
            rows += [down[0, :, lanes].astype(F32)]
            whole = red[0, :, lanes].astype(F32)
            v = [whole[i * wide : (i + 1) * wide] for i in range(high)]
            s = [sigmoid(t) for t in v]
            x = [(a * b).astype(BF).astype(F32) for a, b in zip(v, s)]
            d = [0.0] * high
            sums = [0.0] * 9
            for p in range(high + 2):
                g = rows[p]
                moves = [columns_moved(g, -1, first, last), g, columns_moved(g, 1, first, last)]
                for a in range(3):
                    i = p - 1 + a - 1
                    if 0 <= i < high:
                        for b in range(3):
                            d[i] = d[i] + moves[b] * w[3 * a + b]
                            prod = x[i] * moves[b]
                            sums[3 * a + b] = sums[3 * a + b] + (prod[:8] + prod[8:16] + prod[16:])
            out = [d[i] * (s[i] * (1.0 + v[i] * (1.0 - s[i]))) for i in range(high)]
            redg_out[0, :, lanes] = jnp.concatenate(out, 0).astype(BF)
            for i in range(9):
                taps_out[i, :, lanes] += sums[i]

        chunks(ch // LANES, back)

    image = lambda i: (i, 0, 0)
    return call(
        kernel,
        grid=(slots,),
        ins=[
            (far(conv_grad), (1, cells, ch), image),
            (far(above), (1, wide, ch), image),
            (far(below), (1, wide, ch), image),
            (far(reduced), (1, cells, ch), image),
            (taps, None, None),
        ],
        outs=[
            (shape((slots, cells, ch), BF), (1, cells, ch), image),
            (shape((9, 8, ch), F32), None, None),
        ],
        name="pre_conv_backward",
    )()


def feature_backward(order, reduced_grad, pre_reduce, returned, spread_up):
    slots, cells, ch = reduced_grad.shape
    n = order.shape[0]
    part = slots // n

    def kernel(order_ref, rg, wr, up, *refs):
        ret, out = refs[:n], refs[n]
        k = pl.program_id(0)
        for i in range(n):

            @pl.when(k == i)
            def _():
                out[...] = dot(up[...], ret[i][...]).reshape(part, cells, ch)

        out[...] += dot(rg[...].reshape(part * cells, ch), wr[...], NT).reshape(part, cells, ch)

    by_order = lambda k, order: (order[k], 0, 0)
    whole = (part, cells, ch)
    return call(
        kernel,
        grid=(n,),
        prefetch=1,
        ins=[
            (reduced_grad, whole, by_order),
            (far(pre_reduce), None, None),
            (spread_up, None, None),
            *[(r, None, None) for r in returned],
        ],
        outs=[(shape((slots, cells, ch), F32), whole, by_order)],
        name="feature_backward",
    )(order)[0]


def post_weight_grads(flat, reduced_grad, act, expanded_grad, n):
    total, ch = flat.shape
    share = ch // n
    rows = share // 8

    def kernel(x, g, a, e, out):
        for c in range(n):
            cut = slice(c * share, (c + 1) * share)
            v = dot(x[:, cut], g[...], TN).astype(BF)
            for d in range(8):
                out[d, c, :, :ch] = v[d * rows : (d + 1) * rows]
            for q in range(n):
                v = dot(a[:, q * share : (q + 1) * share], e[:, cut], TN).astype(BF)
                for d in range(8):
                    out[d, c, :, ch + q * share : ch + (q + 1) * share] = v[d * rows : (d + 1) * rows]

    return call(
        kernel,
        grid=(1,),
        ins=[(v, None, None) for v in (flat, reduced_grad, act, expanded_grad)],
        outs=[(far((8, n, rows, 2 * ch), BF), None, None)],
        name="post_weight_grads",
    )()[0]


def readout_weight_grad(low, piece, n):
    pairs, total, width = piece.shape
    ch = low[0].shape[1]
    share = ch // n
    parts = 8
    rows = share // parts

    def kernel(*refs):
        x, (g, out) = refs[:pairs], refs[pairs:]
        x = jnp.concatenate([v[...] for v in x], 0)
        v = dot(x, g[...].reshape(pairs * total, width), TN).astype(BF)
        for d in range(parts):
            out[d, 0] = v[d * rows : (d + 1) * rows]

    return call(
        kernel,
        grid=(n,),
        ins=[(v, (total, share), lambda c: (0, c)) for v in low] + [(piece, None, None)],
        outs=[(far((parts, n, rows, width), BF), (parts, 1, rows, width), lambda c: (0, c, 0, 0))],
        name="readout_weight_grad",
    )()[0]


def cross(n, k):
    return [(a * n + b, ((b + k) % n) * n + a) for a in range(n) for b in range(n)]


def turn(n, k):
    return [(i, (i + k) % n) for i in range(n)]


def other_core(values):
    return lax.ppermute(values, "core", [(0, 1), (1, 0)])


def small_rows(*grads):
    ch = grads[0].shape[-1]
    counts = [g.shape[0] if g.ndim == 3 else 1 for g in grads]
    per = ch // LANES

    def kernel(*refs):
        out = refs[-1]
        at = 0
        for ref, count in zip(refs, counts):
            for i in range(count):
                v = jnp.sum(ref[i] if len(ref.shape) == 3 else ref[...], 0, keepdims=True)
                for q in range(per):
                    out[pl.ds(at, 1), :] = v[:, q * LANES : (q + 1) * LANES]
                    at += 1

    return call(
        kernel,
        grid=(1,),
        ins=[(g, None, None) for g in grads],
        outs=[(shape((sum(counts) * per, LANES), F32), None, None)],
        name="small_rows",
    )()[0]


def join_halves(core, mine, theirs, small, their_small, parts):
    rows, ch = mine[0].shape
    half = rows // 2
    width = len(mine) * ch + LANES
    count = small.shape[0]
    m = len(mine)
    steps = 2
    block = half // steps

    def kernel(core_ref, *refs):
        own, got = refs[:m], refs[m : 2 * m]
        sm, got_sm, out = refs[2 * m :]
        for i in range(m):
            out[:, i * ch : (i + 1) * ch] = (own[i][...].astype(F32) + got[i][...].astype(F32)).astype(BF)
        first = ((core_ref[0] == 0) & (pl.program_id(0) == 0)).astype(F32)
        total = (sm[...] + got_sm[...]) * first
        pad = jnp.zeros((block - count, LANES), F32)
        out[:, m * ch :] = jnp.concatenate([total, pad], 0).astype(BF)

    return call(
        kernel,
        grid=(steps,),
        prefetch=1,
        ins=[(v, (block, ch), lambda i, c: (c[0] * steps + i, 0)) for v in mine]
        + [(v, (block, ch), lambda i, c: (i, 0)) for v in theirs]
        + [(v, None, None) for v in (small, their_small)],
        outs=[(far((half, width), BF), (block, width), lambda i, c: (i, 0))],
        name="join_halves",
    )(core)[0].reshape(parts, half // parts, width)


def sum_and_copy(blocks):
    parts, rows, width = blocks.shape

    def kernel(x, out):
        def cut(lanes):
            total = jnp.sum(x[:, :, lanes].astype(F32), 0).astype(BF)
            out[:, :, lanes] = jnp.broadcast_to(total[None], (parts, rows, LANES))

        chunks(width // LANES, cut)

    return call(
        kernel,
        grid=(1,),
        ins=[(blocks, None, None)],
        outs=[(far(blocks.shape, BF), None, None)],
        name="sum_and_copy",
    )()[0]


def split_rows(to_row, post, read):
    n, rows, width = post.shape
    ch = read.shape[2]
    each = rows // n

    def kernel(to, a, b, *outs):
        outs, wide = outs[:n], outs[n]
        wide[:, :, :width] = a[...].astype(F32)
        wide[:, :, width:] = b[...].astype(F32)
        for k in range(n):
            outs[k][...] = wide[:, pl.ds(pl.multiple_of(to[k] * each, 8), each), :].astype(BF)

    return call(
        kernel,
        grid=(1,),
        prefetch=1,
        ins=[(post, None, None), (read, None, None)],
        outs=[(shape((n, each, width + ch), BF), None, None)] * n,
        scratch=[pltpu.VMEM((n, rows, width + ch), F32)],
        name="split_rows",
    )(to_row)


def sum_rows(to_chan, blocks):
    n, rows, width = blocks[0].shape

    def kernel(to, *refs):
        outs = refs[n:]
        for k in range(n):
            outs[k][...] = sum(r[to[k]].astype(F32) for r in refs[:n]).astype(BF)

    return call(
        kernel,
        grid=(1,),
        prefetch=1,
        ins=[(b, None, None) for b in blocks],
        outs=[(shape((rows, width), BF), None, None)] * n,
        name="sum_rows",
    )(to_chan)


def join_chan(from_chan, blocks):
    n = len(blocks)
    rows, width = blocks[0].shape
    ch = width // 3

    def kernel(src, *refs):
        out = refs[n]
        out[:, : 2 * ch] = sum(r[:, : 2 * ch].astype(F32) for r in refs[:n]).astype(BF)
        for k in range(n):
            at = pl.multiple_of(2 * ch + src[k] * ch, LANES)
            out[:, pl.ds(at, ch)] = refs[k][:, 2 * ch :]

    return call(
        kernel,
        grid=(1,),
        prefetch=1,
        ins=[(b, None, None) for b in blocks],
        outs=[(far((rows, 2 * ch + n * ch), BF), None, None)],
        name="join_chan",
    )(from_chan)[0]


def finish_pre(place, half_rows, ch, earlier=()):
    half, width = half_rows.shape
    m = (width - LANES) // ch
    steps = 4
    block = half // steps

    def kernel(place_ref, x, *outs):
        outs = outs[len(earlier) :]
        for i in range(m):
            outs[i][...] = x[:, i * ch : (i + 1) * ch].astype(F32)
        outs[m][...] = x[:, m * ch :].astype(F32)

    return call(
        kernel,
        grid=(steps,),
        prefetch=1,
        ins=[(half_rows, (block, width), lambda i, c: (i, 0))],
        outs=[(shape((2 * half, ch), F32), (block, ch), lambda i, c: (c[0] * steps + i, 0)) for _ in range(m)]
        + [(shape((half, LANES), F32), (block, LANES), lambda i, c: (i, 0))],
        aliased=earlier,
        name="finish_pre",
    )(place)


def finish_post(place, gathered, n, earlier=()):
    groups, per, width = gathered.shape
    share = 2 * groups * per
    ch = width // (n + 2)

    def kernel(place_ref, x, *outs):
        reduce_out, expand_out, read_out = outs[len(earlier) :]
        reduce_out[...] = x[0, :, :ch].astype(F32)
        for q in range(n):
            expand_out[q] = x[0, :, ch + q * share : ch + (q + 1) * share].astype(F32)
        read_out[...] = x[0, :, 2 * ch :].astype(F32)

    at = lambda i, c: (2 * i + c[0], 0)
    return call(
        kernel,
        grid=(groups,),
        prefetch=1,
        ins=[(gathered, (1, per, width), lambda i, c: (i, 0, 0))],
        outs=[
            (shape((share, ch), F32), (per, ch), at),
            (shape((n, share, share), F32), (n, per, share), lambda i, c: (0, 2 * i + c[0], 0)),
            (shape((share, n * ch), F32), (per, n * ch), at),
        ],
        aliased=earlier,
        name="finish_post",
    )(place)


def after(values, *earlier):
    return lax.optimization_barrier((values, *earlier))[0]


def pool_matrix(part, high, wide):
    half = wide // 2
    m = np.zeros((high // 2 * half * part, part * (high // 2) * wide), np.float32)
    for u in range(part):
        for i in range(high // 2):
            for j in range(wide):
                m[(i * half + j // 2) * part + u, (u * (high // 2) + i) * wide + j] = 0.25
    return m


def spread_matrix(part, high, wide):
    half = wide // 2
    m = np.zeros((part * high * wide, high // 2 * half * part), np.float32)
    for u in range(part):
        for i in range(high):
            for j in range(wide):
                m[(u * high + i) * wide + j, ((i // 2) * half + j // 2) * part + u] = 0.25
    return m


def body(features, counts, pre_reduce, pre_conv, pre_expand, pre_gain, post_reduce, post_conv, post_expand, post_gain, readout, cotangent):
    n = lax.axis_size("chan")
    row = lax.axis_index("rows").astype(jnp.int32)
    chan = lax.axis_index("chan").astype(jnp.int32)
    core = lax.axis_index("core").astype(jnp.int32)
    ch = pre_reduce.shape[0]
    slots, high, wide = features.shape[0], features.shape[1], features.shape[2]
    part = slots // n
    cells = high * wide
    pool = wide // 2
    share = ch // n
    out_share = cotangent.shape[3]
    steps = jnp.arange(n, dtype=jnp.int32)
    order = (row + steps) % n
    source = (row - steps) % n
    pair_of = (chan + steps) % n
    rank = jnp.full((1,), chan, jnp.int32)
    core_at = jnp.full((1,), core, jnp.int32)
    pre_taps = pre_conv.astype(F32).reshape(9, ch)
    post_taps = post_conv.astype(F32).reshape(9, ch)
    pre_gain_row = pre_gain.reshape(1, ch)
    pool_m = jnp.asarray(pool_matrix(part, high, wide), BF)
    up_m = jnp.asarray(spread_matrix(part, high, wide), BF)

    ends = n - 1
    down_pairs = [(i, i + 1) for i in range(ends)]
    up_pairs = [(i + 1, i) for i in range(ends)]
    above = lax.ppermute(features[:, -1], "rows", down_pairs)
    below = lax.ppermute(features[:, 0], "rows", up_pairs)
    gain_hi = post_gain.astype(BF)
    gain_lo = (post_gain - gain_hi.astype(F32)).astype(BF)
    gain_row = jnp.concatenate([gain_hi, gain_lo, jnp.zeros((ch - 2 * share,), BF)])[None]
    square = post_expand.reshape(n, share, share)
    shards = jnp.concatenate(
        [post_reduce, jnp.concatenate([square[q] for q in range(n)], axis=1), jnp.pad(gain_row, ((0, 63), (0, 0)))], axis=0
    )
    shard = lax.dynamic_index_in_dim(shards.reshape(2, -1, ch), core, 0, keepdims=False)
    full = lax.all_gather(shard, ("chan", "core"), axis=0, tiled=True)
    full = full.reshape(n, 2 * share + 64, ch)
    flat_features = features.reshape(slots * cells, ch)
    live = (jnp.arange(SLOT)[None, :] < counts[:, None]).astype(F32).reshape(slots)
    size, each = 16 * slots, 16 * part
    at = lax.broadcasted_iota(jnp.int32, (size, size), 0)
    column = lax.broadcasted_iota(jnp.int32, (size, size), 1)
    wanted = (at % each) // part * slots + part * ((chan + at // each) % n) + at % part
    select = jnp.where(column == wanted, jnp.tile(live, 16)[None, :], 0.0).astype(BF)
    wanted = (column % each) // part * slots + part * ((row - column // each) % n) + column % part
    place = jnp.where(at == wanted, 1.0, 0.0).astype(BF)
    cot_rows = cotangent.transpose(1, 2, 0, 3).reshape(-1, out_share)
    sends = cotangent_by_image(cot_rows, select, n)
    away = after(sends, above, below)
    cots = [lax.ppermute(away[k], ("rows", "chan"), cross(n, k)) for k in range(n)]

    reduced, convolved, convolved_act, normal_pre, pre_std, *pooled = pre_forward(
        order, above, below, features, pre_reduce, pre_taps, pre_expand, pre_gain_row, pool_m
    )

    pooled = after(pooled, cots)
    moved = [pooled[0]] + [lax.ppermute(pooled[k], "rows", turn(n, k)) for k in range(1, n)]
    flat, post_reduced, post_act, post_convolved, post_cact, post_normal, post_std, low = post_forward(
        source, moved, full, post_taps, pool
    )
    lows = [low] + [lax.ppermute(low, "chan", turn(n, k)) for k in range(1, n)]
    refined_grad = readout_backward(source, low, readout, cots)
    post_expanded_grad, post_reduced_grad, post_taps_grad, post_gain_grad, *back = post_backward(
        source, refined_grad, full, post_taps, post_act, post_reduced, post_convolved, post_normal, post_std, pool
    )

    returned = [back[0]] + [lax.ppermute(back[k], "rows", turn(n, -k)) for k in range(1, n)]

    flat = after(flat, lows)
    load = post_weight_grads(flat, post_reduced_grad, post_cact, post_expanded_grad, n)

    post_sum = lax.psum_scatter(load, ("x", "core"), scatter_dimension=0, tiled=False)

    stacked = jnp.stack(after(lows, load))
    lows = [lax.dynamic_index_in_dim(stacked, (chan - row - k) % n, 0, keepdims=False) for k in range(n)]
    lows = [lows[0]] + [lax.ppermute(lows[k], "rows", turn(n, k)) for k in range(1, n)]

    tokens, piece = token_block(rank, source, pair_of, lows, place, readout, sends)
    read_load = readout_weight_grad(lows, piece, n)
    tokens = tokens.reshape(pool, pool, slots, out_share).transpose(2, 0, 1, 3)
    returned = after(returned, read_load, post_sum)
    read_sum = lax.psum_scatter(after(read_load, post_sum), ("x", "core"), scatter_dimension=0, tiled=False)

    expanded_grad, convolved_grad, top, bottom, pre_gain_grad = pre_backward(
        order, returned, up_m, normal_pre, pre_std, pre_gain_row, convolved, pre_expand
    )
    grad_above = lax.ppermute(bottom, "rows", down_pairs)
    grad_below = lax.ppermute(top, "rows", up_pairs)
    act_rows = after(convolved_act, bottom).reshape(-1, ch)
    pre_expand_grad = dot(act_rows, expanded_grad.reshape(-1, ch), TN).astype(BF)
    convolved_grad = after(convolved_grad, pre_expand_grad)
    reduced_grad, pre_taps_grad = pre_conv_backward(convolved_grad, grad_above, grad_below, reduced, pre_taps)
    small = small_rows(pre_taps_grad, pre_gain_grad, post_taps_grad, post_gain_grad)
    pre_reduce_grad = dot(after(flat_features, small), reduced_grad.reshape(-1, ch), TN).astype(BF)

    post_sum, read_sum = lax.optimization_barrier((post_sum, read_sum, pre_reduce_grad))[:2]
    blocks = split_rows(order, post_sum, read_sum)
    blocks = [blocks[0]] + [lax.ppermute(blocks[k], "rows", turn(n, k)) for k in range(1, n)]
    blocks = sum_rows(pair_of, blocks)

    chips = ("x", "rows", "chan")
    mine = [pre_reduce_grad, pre_expand_grad]
    theirs = [other_core(lax.dynamic_index_in_dim(g.reshape(2, ch // 2, ch), 1 - core, 0, keepdims=False)) for g in mine]
    load = join_halves(core_at, mine, after(theirs, *blocks), small, other_core(small), 64)
    blocks = [blocks[0]] + [lax.ppermute(blocks[k], "chan", turn(n, k)) for k in range(1, n)]
    rest = join_chan((chan - steps) % n, blocks)
    load = after(load, rest)
    rest = lax.all_gather(rest, ("x", "rows"), axis=0, tiled=False).reshape(4, share // 8, -1)
    pieces = lax.all_to_all(load, chips, 0, 0, tiled=False)
    feature_grad = feature_backward(order, after(reduced_grad, load), pre_reduce, returned, up_m).reshape(features.shape)
    load = sum_and_copy(after(pieces, feature_grad))
    load_all = lax.all_to_all(load, chips, 0, 0, tiled=False).reshape(ch // 2, -1)

    def finish(kernel, values, *sizes):
        theirs = other_core(values)
        own = kernel(core_at, values, *sizes)
        theirs = after(theirs, *own)
        return own, theirs

    own, theirs = finish(finish_post, after(rest, load), n)
    post_out = finish_post(1 - core_at, theirs, n, earlier=tuple(own))
    post_reduce_out, post_expand_out, readout_out = post_out
    own, theirs = finish(finish_pre, after(load_all, *post_out), ch)
    pre_reduce_out, pre_expand_out, small_their = finish_pre(1 - core_at, theirs, ch, earlier=tuple(own[:2]))
    small_out = jnp.where(core == 0, own[2], small_their)
    per = ch // LANES
    cut = [0, 9 * per, 10 * per, 19 * per, 20 * per]
    pre_conv_out, pre_gain_out, post_conv_out, post_gain_out = [small_out[a:b] for a, b in zip(cut, cut[1:])]
    return (
        tokens,
        feature_grad,
        pre_reduce_out,
        pre_conv_out.reshape(3, 3, ch),
        pre_expand_out,
        pre_gain_out.reshape(ch),
        post_reduce_out,
        post_conv_out.reshape(3, 3, ch),
        post_expand_out.reshape(ch, share),
        lax.dynamic_slice_in_dim(post_gain_out.reshape(ch), chan * share, share, 0),
        readout_out,
    )


def solution(mesh):
    grid = Mesh(mesh.devices.reshape(4, 2, 4, 4), ("x", "core", "rows", "chan"))
    images = P(("x", "core", "chan"), "rows", None, None)
    grids = P(("x", "core", "rows"), None, None, "chan")
    return jax.shard_map(
        body,
        mesh=grid,
        in_specs=(
            images,
            P(("x", "core", "rows")),
            P(),
            P(),
            P(),
            P(),
            P("chan", None),
            P(),
            P(None, "chan"),
            P("chan"),
            P(),
            grids,
        ),
        out_specs=(grids, images, P(), P(), P(), P(), P("chan", None), P(), P(None, "chan"), P("chan"), P("chan", None)),
        check_vma=False,
    )
```

```python
import functools

import jax
import jax.numpy as jnp
import numpy as np
from jax import lax
from jax.experimental import pallas as pl
from jax.experimental.pallas import tpu as pltpu
from jax.sharding import Mesh, PartitionSpec as P

SLOT = 4
EPS = 1e-06
BF = jnp.bfloat16
F32 = jnp.float32
LANES = 128
VMEM_LIMIT = 20 * 1024 * 1024
NN = ((1,), (0,))
NT = ((1,), (1,))
TN = ((0,), (0,))


def dot(a, b, dims=NN):
    return lax.dot_general(a, b, (dims, ((), ())), preferred_element_type=F32)


def sigmoid(v):
    return 0.5 * jnp.tanh(0.5 * v) + 0.5


def silu(v):
    return v * sigmoid(v)


def silu_slope(v):
    s = sigmoid(v)
    return s * (1.0 + v * (1.0 - s))


def gelu_parts(v):
    c = 0.7978845608028654
    square = v * v
    t = jnp.tanh(v * (c + (c * 0.044715) * square))
    half = 0.5 * (1.0 + t)
    slope = half + 0.5 * v * (1.0 - t * t) * (c + (3.0 * c * 0.044715) * square)
    return v * half, slope


def chunks(count, body, width=LANES):
    for i in range(count):
        body(pl.ds(i * width, width))


def call(kernel, *, grid, ins, outs, scratch=(), prefetch=0, aliased=(), cost=1, name):
    def spec(shape, block, index):
        if block is None:
            block, index = shape, lambda *_: (0,) * len(shape)
        return pl.BlockSpec(block, index)

    arrays = [i[0] for i in ins] + list(aliased)
    in_specs = [spec(a.shape, b, m) for a, b, m in ins] + [pl.BlockSpec(memory_space=pl.ANY)] * len(aliased)
    out_specs = [spec(s.shape, b, m) for s, b, m in outs]

    def run(*scalars):
        return pl.pallas_call(
            kernel,
            grid_spec=pltpu.PrefetchScalarGridSpec(
                num_scalar_prefetch=prefetch,
                grid=grid,
                in_specs=in_specs,
                out_specs=out_specs,
                scratch_shapes=list(scratch),
            ),
            out_shape=[s[0] for s in outs],
            compiler_params=pltpu.CompilerParams(
                dimension_semantics=("arbitrary",) * len(grid), vmem_limit_bytes=VMEM_LIMIT
            ),
            input_output_aliases={prefetch + len(ins) + i: i for i in range(len(aliased))},
            cost_estimate=pl.CostEstimate(flops=cost, bytes_accessed=1, transcendentals=0),
            name=name,
        )(*scalars, *arrays)

    return run


def shape(dims, dtype):
    return jax.ShapeDtypeStruct(dims, dtype)


def far(values, dtype=None):
    if dtype is None:
        return pltpu.with_memory_space_constraint(values, pltpu.HBM)
    return pltpu.HBM(values, dtype)


def columns_moved(t, by, first, last):
    rows = t.shape[0]
    return pltpu.roll(t, by % rows, 0) * (first if by > 0 else last)


def edge_masks(rows, width, depth):
    at = lax.broadcasted_iota(jnp.int32, (rows, LANES), 0) % (width * depth)
    return (at >= depth).astype(F32), (at < (width - 1) * depth).astype(F32)


def pre_forward(order, above, below, features, pre_reduce, taps, pre_expand, gain, pool):
    slots, high, wide, ch = features.shape
    cells = high * wide
    n = order.shape[0]
    part = slots // n
    rows_all = part * cells

    def kernel(order_ref, up_ref, down_ref, feat, wr, tap, we, gn, pool_ref, red_out, conv_out, act_out, norm_out, std_out, *rest):
        pooled_out, (red, halo, exp, sums) = rest[:n], rest[n:]
        k = pl.program_id(0)
        for side, ref in enumerate((up_ref, down_ref)):
            halo[side] = dot(ref[...].reshape(part * wide, ch), wr[...]).reshape(part, wide, ch)
        red[...] = dot(feat[...].reshape(rows_all, ch), wr[...]).reshape(part, cells, ch)
        red_out[...] = red[...].astype(BF)
        first, last = edge_masks(wide, wide, 1)
        for u in range(part):

            def conv(lanes):
                w = [tap[pl.ds(i, 1), lanes] for i in range(9)]
                rows = [halo[0, u, :, lanes]]
                rows += [red[u, pl.ds(i * wide, wide), lanes] for i in range(high)]
                rows += [halo[1, u, :, lanes]]
                rows = [silu(r).astype(BF).astype(F32) for r in rows]
                out = []
                for i in range(high):
                    t = [sum(rows[i + a] * w[3 * a + b] for a in range(3)) for b in range(3)]
                    out.append(t[1] + columns_moved(t[0], 1, first, last) + columns_moved(t[2], -1, first, last))
                conv_out[u, :, lanes] = jnp.concatenate(out, 0).astype(BF)
                act_out[u, :, lanes] = jnp.concatenate([silu(c) for c in out], 0).astype(BF)

            chunks(ch // LANES, conv)

        exp[...] = dot(act_out[...].reshape(rows_all, ch), we[...])

        def norm(p, carry):
            u, i = p // (high // 2), p % (high // 2)
            tiles = wide // 8
            f = [feat[u, 2 * i + half].astype(F32) for half in range(2)]
            nrms, blends = [], []
            for t in range(2 * tiles):
                e = exp[pl.ds(p * 2 * wide + 8 * t, 8), :]
                mean = jnp.mean(e, -1, keepdims=True)
                square = jnp.mean(e * e, -1, keepdims=True)
                std = lax.rsqrt(square - mean * mean + EPS)
                nrm = (e - mean) * std
                std_out[u, pl.ds(i * 2 * wide + 8 * t, 8), :] = std
                nrms.append(nrm)
                at = t % tiles
                blends.append(f[t // tiles][8 * at : 8 * at + 8] + silu(nrm * gn[...]))
                if t % 2 == 1:
                    both = jnp.concatenate(nrms[-2:], 0).astype(BF)
                    norm_out[u, pl.ds(i * 2 * wide + 8 * (t - 1), 16), :] = both
            for t in range(tiles):
                sums[pl.ds(p * wide + 8 * t, 8), :] = blends[t] + blends[tiles + t]
            return carry

        for p in range(part * high // 2):
            norm(p, 0)
        s = sums[...]
        hi = s.astype(BF)
        lo = (s - hi.astype(F32)).astype(BF)
        pooled = (dot(pool_ref[...], hi) + dot(pool_ref[...], lo)).astype(BF)
        for i in range(n):

            @pl.when(k == i)
            def _():
                pooled_out[i][...] = pooled

    def by_order(rest):
        return lambda k, order: (order[k],) + (0,) * rest

    pooled_rows = pool.shape[0]
    block = (part, cells, ch)
    return call(
        kernel,
        grid=(n,),
        prefetch=1,
        ins=[
            (far(above), (part, wide, ch), by_order(2)),
            (far(below), (part, wide, ch), by_order(2)),
            (far(features), (part, high, wide, ch), by_order(3)),
            (far(pre_reduce), None, None),
            (taps, None, None),
            (far(pre_expand), None, None),
            (gain, None, None),
            (pool, None, None),
        ],
        outs=[(far((slots, cells, ch), BF), block, by_order(2))] * 4
        + [(far((slots, cells, 1), F32), (part, cells, 1), by_order(2))]
        + [(shape((pooled_rows, ch), BF), None, None)] * n,
        scratch=[
            pltpu.VMEM((part, cells, ch), F32),
            pltpu.VMEM((2, part, wide, ch), F32),
            pltpu.VMEM((rows_all, ch), F32),
            pltpu.VMEM((rows_all // 2, ch), F32),
        ],
        name="pre_forward",
    )(order)


def gain_row(w, n, share):
    at = 2 * share
    parts = [w[c, at : at + 16, :].astype(F32)[:1] for c in range(n)]
    return jnp.concatenate([p[:, :share] + p[:, share : 2 * share] for p in parts], 1)


def post_forward(source, moved, weights, taps, pool):
    n, (rows, ch) = len(moved), moved[0].shape
    total = n * rows
    depth = total // (pool * pool)
    share = ch // n

    def kernel(src, *refs):
        got, refs = refs[:n], refs[n:]
        w, tap, flat_out, red_out, act_out, conv_out, cact_out, norm_out, std_out, low_out, wide_ref, red, exp = refs
        for k in range(n):
            at = pl.multiple_of(src[k] * rows, 8)
            wide_ref[pl.ds(at, rows), :] = got[k][...].astype(F32)
        gain = gain_row(w, n, share)
        flat_out[...] = wide_ref[...].astype(BF)
        total_red = 0.0
        for c in range(n):
            total_red = total_red + dot(flat_out[:, c * share : (c + 1) * share], w[c, :share])
        red[...] = total_red
        first, last = edge_masks(total, pool, depth)
        step = pool * depth

        def conv(lanes):
            v = red[:, lanes]
            red_out[:, lanes] = v.astype(BF)
            x = silu(v).astype(BF)
            act_out[:, lanes] = x
            x = x.astype(F32)
            moves = [columns_moved(x, depth, first, last), x, columns_moved(x, -depth, first, last)]
            t = [sum(moves[b] * tap[pl.ds(3 * a + b, 1), lanes] for b in range(3)) for a in range(3)]
            none = jnp.zeros((step, LANES), F32)
            c = t[1] + jnp.concatenate([none, t[0][:-step]], 0) + jnp.concatenate([t[2][step:], none], 0)
            conv_out[:, lanes] = c.astype(BF)
            cact_out[:, lanes] = silu(c).astype(BF)

        chunks(ch // LANES, conv)
        for c in range(n):
            e = 0.0
            for q in range(n):
                cut = slice(q * share, (q + 1) * share)
                e = e + dot(cact_out[:, cut], w[c, share : 2 * share, cut])
            exp[:, c * share : (c + 1) * share] = e

        def norm(i, carry):
            for t in range(3):
                at = pl.ds(i * 48 + 16 * t, 16)
                e = exp[at, :]
                mean = jnp.mean(e, -1, keepdims=True)
                square = jnp.mean(e * e, -1, keepdims=True)
                std = lax.rsqrt(square - mean * mean + EPS)
                nrm = (e - mean) * std
                norm_out[at, :] = nrm.astype(BF)
                std_out[at, :] = std
                low_out[at, :] = (wide_ref[at, :] + silu(nrm * gain)).astype(BF)
            return carry

        for i in range(total // 48):
            norm(i, 0)

    narrow = shape((total, ch), BF)
    return call(
        kernel,
        grid=(1,),
        prefetch=1,
        ins=[(a, None, None) for a in (*map(far, moved), far(weights), taps)],
        outs=[(s, None, None) for s in (narrow, narrow, narrow, narrow, narrow, narrow, shape((total, 1), F32), narrow)],
        scratch=[pltpu.VMEM((total, ch), F32)] * 3,
        name="post_forward",
    )(source)


def readout_backward(source, low, readout, cots):
    total, ch = low.shape
    n, out_share = len(cots), cots[0].shape[1]

    def kernel(src, low_ref, ro, *rest):
        cot, grad = rest[:n], rest[n]
        k = pl.program_id(0)
        logits = dot(low_ref[...], ro[...])
        slope = gelu_parts(logits)[1]
        for i in range(n):

            @pl.when(k == i)
            def _():
                piece = (cot[i][...].astype(F32) * slope).astype(BF)
                term = dot(piece, ro[...], NT)
                grad[...] = term if i == 0 else grad[...] + term

    return call(
        kernel,
        grid=(n,),
        prefetch=1,
        ins=[(low, None, None), (far(readout), (ch, out_share), lambda k, s: (0, s[k]))] + [(c, None, None) for c in cots],
        outs=[(shape((total, ch), F32), None, None)],
        name="readout_backward",
    )(source)[0]


def post_backward(source, refined_grad, weights, taps, act, red, conv, nrm, std, pool):
    total, ch = act.shape
    n = weights.shape[0]
    share = ch // n
    rows = total // n
    depth = total // (pool * pool)

    def kernel(src, rg, w, tap, act_ref, red_ref, conv_ref, norm_ref, std_ref, exp_out, redg_out, taps_out, gain_out, *rest):
        back_out, (grad, cgrad) = rest[:n], rest[n:]
        gain = gain_row(w, n, share)

        def norm(i, total_gain):
            for t in range(3):
                at = pl.ds(i * 48 + 16 * t, 16)
                nm = norm_ref[at, :].astype(F32)
                ng = rg[at, :] * silu_slope(nm * gain)
                sc = ng * gain
                one = jnp.mean(sc, -1, keepdims=True)
                two = jnp.mean(sc * nm, -1, keepdims=True)
                exp_out[at, :] = (std_ref[at, :] * (sc - one - nm * two)).astype(BF)
                g = ng * nm
                total_gain = total_gain + g[:8] + g[8:]
            return total_gain

        gains = jnp.zeros((8, ch), F32)
        for i in range(total // 48):
            gains = norm(i, gains)
        gain_out[...] = gains
        for q in range(n):
            cut = slice(q * share, (q + 1) * share)
            cg = 0.0
            for c in range(n):
                cg = cg + dot(exp_out[:, c * share : (c + 1) * share], w[c, share : 2 * share, cut], NT)
            cgrad[:, cut] = cg
        first, last = edge_masks(total, pool, depth)
        step = pool * depth

        def back(lanes):
            g = (cgrad[:, lanes] * silu_slope(conv_ref[:, lanes].astype(F32))).astype(BF).astype(F32)
            x = act_ref[:, lanes].astype(F32)
            moves = [columns_moved(g, -depth, first, last), g, columns_moved(g, depth, first, last)]
            none = jnp.zeros((step, LANES), F32)
            xs = [
                jnp.concatenate([none, x[:-step]], 0),
                x,
                jnp.concatenate([x[step:], none], 0),
            ]
            for a in range(3):
                for b in range(3):
                    prod = xs[a] * moves[b]
                    taps_out[3 * a + b, :, lanes] = jnp.sum(prod.reshape(total // 8, 8, LANES), 0)
            t = [sum(moves[b] * tap[pl.ds(3 * a + b, 1), lanes] for b in range(3)) for a in range(3)]
            d = t[1] + jnp.concatenate([t[0][step:], none], 0) + jnp.concatenate([none, t[2][:-step]], 0)
            redg_out[:, lanes] = (d * silu_slope(red_ref[:, lanes].astype(F32))).astype(BF)

        chunks(ch // LANES, back)
        for c in range(n):
            cut = slice(c * share, (c + 1) * share)
            grad[:, cut] = rg[:, cut] + dot(redg_out[...], w[c, :share], NT)
        for r in range(n):
            at = pl.ds(pl.multiple_of(src[r] * rows, 8), rows)
            back_out[r][...] = grad[at, :].astype(BF)

    return call(
        kernel,
        grid=(1,),
        prefetch=1,
        ins=[(a, None, None) for a in (refined_grad, weights, taps, act, red, conv, nrm, std)],
        outs=[
            (s, None, None)
            for s in (
                shape((total, ch), BF),
                shape((total, ch), BF),
                shape((9, 8, ch), F32),
                shape((8, ch), F32),
                *[shape((rows, ch), BF)] * n,
            )
        ],
        scratch=[pltpu.VMEM((total, ch), F32), pltpu.VMEM((total, ch), F32)],
        name="post_backward",
    )(source)


def cotangent_by_image(cotangent, select, pairs):
    rows, width = cotangent.shape
    size = select.shape[0]
    each = size // pairs
    per = 3

    def kernel(x, sel, *outs):
        for q in range(per):
            y = dot(sel[...], x[pl.ds(q * size, size), :]).astype(BF)
            for s in range(pairs):
                outs[s][pl.ds(q * each, each), :] = y[s * each : (s + 1) * each]

    return call(
        kernel,
        grid=(rows // (per * size),),
        ins=[(far(cotangent), (per * size, width), lambda i: (i, 0)), (select, None, None)],
        outs=[(shape((rows // pairs, width), BF), (per * each, width), lambda i: (i, 0))] * pairs,
        name="cotangent_by_image",
    )()


def token_block(chan, source, pair_of, low, place, readout, cotangent):
    pairs, (rows, ch) = len(low), low[0].shape
    width = cotangent[0].shape[1]
    size = place.shape[0]
    each = size // pairs
    per = 3
    block = per * each

    def kernel(chan_ref, src, pair, *refs):
        lows, cots, (place_ref, ro, tok_out, piece_out, cot) = refs[:pairs], refs[pairs : 2 * pairs], refs[2 * pairs :]
        for k in range(pairs):
            cot[pair[k]] = cots[k][...]
        logits = dot(jnp.concatenate([v[...] for v in lows], 0), ro[...])
        value, slope = gelu_parts(logits)
        value = value.astype(BF)
        for k in range(pairs):
            piece_out[k] = (cot[src[k]].astype(F32) * slope[k * block : (k + 1) * block]).astype(BF)
        for q in range(per):
            x = jnp.concatenate([value[k * block + q * each : k * block + (q + 1) * each] for k in range(pairs)], 0)
            tok_out[pl.ds(q * size, size), :] = dot(place_ref[...], x).astype(BF)

    rows_at = lambda i, c, s, p: (i, 0)
    return call(
        kernel,
        grid=(rows // block,),
        prefetch=3,
        ins=[
            *[(v, (block, ch), rows_at) for v in low],
            *[(v, (block, width), rows_at) for v in cotangent],
            (place, None, None),
            (far(readout), (ch, width), lambda i, c, s, p: (0, c[0])),
        ],
        outs=[
            (shape((pairs * rows, width), BF), (pairs * block, width), rows_at),
            (shape((pairs, rows, width), BF), (pairs, block, width), lambda i, c, s, p: (0, i, 0)),
        ],
        scratch=[pltpu.VMEM((pairs, block, width), BF)],
        name="token_block",
    )(chan, source, pair_of)


def pre_backward(order, returned, spread_up, nrm, std, gain, conv, pre_expand):
    slots, cells, ch = nrm.shape
    n = order.shape[0]
    part = slots // n
    wide = 24
    rows = part * cells

    def kernel(order_ref, *refs):
        ret, refs = refs[:n], refs[n:]
        up, norm_ref, std_ref, gn, conv_ref, we, exp_out, conv_grad_out, top_out, bottom_out, gain_out, grad, cgrad = refs
        k = pl.program_id(0)
        for i in range(n):

            @pl.when(k == i)
            def _():
                grad[...] = dot(up[...], ret[i][...])

        def norm(i, total_gain):
            u, j = i // (cells // 48), i % (cells // 48)
            for t in range(3):
                at = pl.ds(j * 48 + 16 * t, 16)
                nm = norm_ref[u, at, :].astype(F32)
                ng = grad[pl.ds(i * 48 + 16 * t, 16), :] * silu_slope(nm * gn[...])
                sc = ng * gn[...]
                one = jnp.mean(sc, -1, keepdims=True)
                two = jnp.mean(sc * nm, -1, keepdims=True)
                exp_out[u, at, :] = (std_ref[u, at, :] * (sc - one - nm * two)).astype(BF)
                g = ng * nm
                total_gain = total_gain + g[:8] + g[8:]
            return total_gain

        gains = jnp.zeros((8, ch), F32)
        for i in range(rows // 48):
            gains = norm(i, gains)

        @pl.when(k == 0)
        def _():
            gain_out[...] = gains

        @pl.when(k > 0)
        def _():
            gain_out[...] += gains

        cgrad[...] = dot(exp_out[...].reshape(rows, ch), we[...], NT)
        for u in range(part):

            def slope(lanes):
                g = cgrad[pl.ds(u * cells, cells), lanes] * silu_slope(conv_ref[u, :, lanes].astype(F32))
                conv_grad_out[u, :, lanes] = g.astype(BF)
                top_out[u, :, lanes] = g[:wide].astype(BF)
                bottom_out[u, :, lanes] = g[cells - wide :].astype(BF)

            chunks(ch // LANES, slope)

    by_order = lambda k, order: (order[k], 0, 0)
    whole = (part, cells, ch)
    edge = (part, wide, ch)
    return call(
        kernel,
        grid=(n,),
        prefetch=1,
        ins=[
            *[(r, None, None) for r in returned],
            (spread_up, None, None),
            (far(nrm), whole, by_order),
            (far(std), (part, cells, 1), by_order),
            (gain, None, None),
            (far(conv), whole, by_order),
            (far(pre_expand), None, None),
        ],
        outs=[
            (shape((slots, cells, ch), BF), whole, by_order),
            (far((slots, cells, ch), BF), whole, by_order),
            (shape((slots, wide, ch), BF), edge, by_order),
            (shape((slots, wide, ch), BF), edge, by_order),
            (shape((8, ch), F32), None, None),
        ],
        scratch=[pltpu.VMEM((rows, ch), F32), pltpu.VMEM((rows, ch), F32)],
        name="pre_backward",
    )(order)


def pre_conv_backward(conv_grad, above, below, reduced, taps):
    slots, cells, ch = reduced.shape
    wide = above.shape[1]
    high = cells // wide

    def kernel(cg, up, down, red, tap, redg_out, taps_out):
        step = pl.program_id(0)
        first, last = edge_masks(wide, wide, 1)

        @pl.when(step == 0)
        def _():
            taps_out[...] = jnp.zeros_like(taps_out)

        def back(lanes):
            w = [tap[pl.ds(i, 1), lanes] for i in range(9)]
            mid = cg[0, :, lanes].astype(F32)
            rows = [up[0, :, lanes].astype(F32)]
            rows += [mid[i * wide : (i + 1) * wide] for i in range(high)]
            rows += [down[0, :, lanes].astype(F32)]
            whole = red[0, :, lanes].astype(F32)
            v = [whole[i * wide : (i + 1) * wide] for i in range(high)]
            s = [sigmoid(t) for t in v]
            x = [(a * b).astype(BF).astype(F32) for a, b in zip(v, s)]
            d = [0.0] * high
            sums = [0.0] * 9
            for p in range(high + 2):
                g = rows[p]
                moves = [columns_moved(g, -1, first, last), g, columns_moved(g, 1, first, last)]
                for a in range(3):
                    i = p - 1 + a - 1
                    if 0 <= i < high:
                        for b in range(3):
                            d[i] = d[i] + moves[b] * w[3 * a + b]
                            prod = x[i] * moves[b]
                            sums[3 * a + b] = sums[3 * a + b] + (prod[:8] + prod[8:16] + prod[16:])
            out = [d[i] * (s[i] * (1.0 + v[i] * (1.0 - s[i]))) for i in range(high)]
            redg_out[0, :, lanes] = jnp.concatenate(out, 0).astype(BF)
            for i in range(9):
                taps_out[i, :, lanes] += sums[i]

        chunks(ch // LANES, back)

    image = lambda i: (i, 0, 0)
    return call(
        kernel,
        grid=(slots,),
        ins=[
            (far(conv_grad), (1, cells, ch), image),
            (far(above), (1, wide, ch), image),
            (far(below), (1, wide, ch), image),
            (far(reduced), (1, cells, ch), image),
            (taps, None, None),
        ],
        outs=[
            (shape((slots, cells, ch), BF), (1, cells, ch), image),
            (shape((9, 8, ch), F32), None, None),
        ],
        name="pre_conv_backward",
    )()


def feature_backward(order, reduced_grad, pre_reduce, returned, spread_up):
    slots, cells, ch = reduced_grad.shape
    n = order.shape[0]
    part = slots // n

    def kernel(order_ref, rg, wr, up, *refs):
        ret, out = refs[:n], refs[n]
        k = pl.program_id(0)
        for i in range(n):

            @pl.when(k == i)
            def _():
                out[...] = dot(up[...], ret[i][...]).reshape(part, cells, ch)

        out[...] += dot(rg[...].reshape(part * cells, ch), wr[...], NT).reshape(part, cells, ch)

    by_order = lambda k, order: (order[k], 0, 0)
    whole = (part, cells, ch)
    return call(
        kernel,
        grid=(n,),
        prefetch=1,
        ins=[
            (reduced_grad, whole, by_order),
            (far(pre_reduce), None, None),
            (spread_up, None, None),
            *[(r, None, None) for r in returned],
        ],
        outs=[(shape((slots, cells, ch), F32), whole, by_order)],
        name="feature_backward",
    )(order)[0]


def post_weight_grads(flat, reduced_grad, act, expanded_grad, n):
    total, ch = flat.shape
    share = ch // n
    rows = share // 8

    def kernel(x, g, a, e, out):
        for c in range(n):
            cut = slice(c * share, (c + 1) * share)
            v = dot(x[:, cut], g[...], TN).astype(BF)
            for d in range(8):
                out[d, c, :, :ch] = v[d * rows : (d + 1) * rows]
            for q in range(n):
                v = dot(a[:, q * share : (q + 1) * share], e[:, cut], TN).astype(BF)
                for d in range(8):
                    out[d, c, :, ch + q * share : ch + (q + 1) * share] = v[d * rows : (d + 1) * rows]

    return call(
        kernel,
        grid=(1,),
        ins=[(v, None, None) for v in (flat, reduced_grad, act, expanded_grad)],
        outs=[(far((8, n, rows, 2 * ch), BF), None, None)],
        name="post_weight_grads",
    )()[0]


def readout_weight_grad(low, piece, n):
    pairs, total, width = piece.shape
    ch = low[0].shape[1]
    share = ch // n
    parts = 8
    rows = share // parts

    def kernel(*refs):
        x, (g, out) = refs[:pairs], refs[pairs:]
        x = jnp.concatenate([v[...] for v in x], 0)
        v = dot(x, g[...].reshape(pairs * total, width), TN).astype(BF)
        for d in range(parts):
            out[d, 0] = v[d * rows : (d + 1) * rows]

    return call(
        kernel,
        grid=(n,),
        ins=[(v, (total, share), lambda c: (0, c)) for v in low] + [(piece, None, None)],
        outs=[(far((parts, n, rows, width), BF), (parts, 1, rows, width), lambda c: (0, c, 0, 0))],
        name="readout_weight_grad",
    )()[0]


def cross(n, k):
    return [(a * n + b, ((b + k) % n) * n + a) for a in range(n) for b in range(n)]


def turn(n, k):
    return [(i, (i + k) % n) for i in range(n)]


def other_core(values):
    return lax.ppermute(values, "core", [(0, 1), (1, 0)])


def small_rows(*grads):
    ch = grads[0].shape[-1]
    counts = [g.shape[0] if g.ndim == 3 else 1 for g in grads]
    per = ch // LANES

    def kernel(*refs):
        out = refs[-1]
        at = 0
        for ref, count in zip(refs, counts):
            for i in range(count):
                v = jnp.sum(ref[i] if len(ref.shape) == 3 else ref[...], 0, keepdims=True)
                for q in range(per):
                    out[pl.ds(at, 1), :] = v[:, q * LANES : (q + 1) * LANES]
                    at += 1

    return call(
        kernel,
        grid=(1,),
        ins=[(g, None, None) for g in grads],
        outs=[(shape((sum(counts) * per, LANES), F32), None, None)],
        name="small_rows",
    )()[0]


def join_halves(core, mine, theirs, small, their_small, parts):
    rows, ch = mine[0].shape
    half = rows // 2
    width = len(mine) * ch + LANES
    count = small.shape[0]
    m = len(mine)
    steps = 2
    block = half // steps

    def kernel(core_ref, *refs):
        own, got = refs[:m], refs[m : 2 * m]
        sm, got_sm, out = refs[2 * m :]
        for i in range(m):
            out[:, i * ch : (i + 1) * ch] = (own[i][...].astype(F32) + got[i][...].astype(F32)).astype(BF)
        first = ((core_ref[0] == 0) & (pl.program_id(0) == 0)).astype(F32)
        total = (sm[...] + got_sm[...]) * first
        pad = jnp.zeros((block - count, LANES), F32)
        out[:, m * ch :] = jnp.concatenate([total, pad], 0).astype(BF)

    return call(
        kernel,
        grid=(steps,),
        prefetch=1,
        ins=[(v, (block, ch), lambda i, c: (c[0] * steps + i, 0)) for v in mine]
        + [(v, (block, ch), lambda i, c: (i, 0)) for v in theirs]
        + [(v, None, None) for v in (small, their_small)],
        outs=[(far((half, width), BF), (block, width), lambda i, c: (i, 0))],
        name="join_halves",
    )(core)[0].reshape(parts, half // parts, width)


def sum_and_copy(blocks):
    parts, rows, width = blocks.shape

    def kernel(x, out):
        def cut(lanes):
            total = jnp.sum(x[:, :, lanes].astype(F32), 0).astype(BF)
            out[:, :, lanes] = jnp.broadcast_to(total[None], (parts, rows, LANES))

        chunks(width // LANES, cut)

    return call(
        kernel,
        grid=(1,),
        ins=[(blocks, None, None)],
        outs=[(far(blocks.shape, BF), None, None)],
        name="sum_and_copy",
    )()[0]


def split_rows(to_row, post, read):
    n, rows, width = post.shape
    ch = read.shape[2]
    each = rows // n

    def kernel(to, a, b, *outs):
        outs, wide = outs[:n], outs[n]
        wide[:, :, :width] = a[...].astype(F32)
        wide[:, :, width:] = b[...].astype(F32)
        for k in range(n):
            outs[k][...] = wide[:, pl.ds(pl.multiple_of(to[k] * each, 8), each), :].astype(BF)

    return call(
        kernel,
        grid=(1,),
        prefetch=1,
        ins=[(post, None, None), (read, None, None)],
        outs=[(shape((n, each, width + ch), BF), None, None)] * n,
        scratch=[pltpu.VMEM((n, rows, width + ch), F32)],
        name="split_rows",
    )(to_row)


def sum_rows(to_chan, blocks):
    n, rows, width = blocks[0].shape

    def kernel(to, *refs):
        outs = refs[n:]
        for k in range(n):
            outs[k][...] = sum(r[to[k]].astype(F32) for r in refs[:n]).astype(BF)

    return call(
        kernel,
        grid=(1,),
        prefetch=1,
        ins=[(b, None, None) for b in blocks],
        outs=[(shape((rows, width), BF), None, None)] * n,
        name="sum_rows",
    )(to_chan)


def join_chan(from_chan, blocks):
    n = len(blocks)
    rows, width = blocks[0].shape
    ch = width // 3

    def kernel(src, *refs):
        out = refs[n]
        out[:, : 2 * ch] = sum(r[:, : 2 * ch].astype(F32) for r in refs[:n]).astype(BF)
        for k in range(n):
            at = pl.multiple_of(2 * ch + src[k] * ch, LANES)
            out[:, pl.ds(at, ch)] = refs[k][:, 2 * ch :]

    return call(
        kernel,
        grid=(1,),
        prefetch=1,
        ins=[(b, None, None) for b in blocks],
        outs=[(far((rows, 2 * ch + n * ch), BF), None, None)],
        name="join_chan",
    )(from_chan)[0]


def finish_pre(place, half_rows, ch, earlier=()):
    half, width = half_rows.shape
    m = (width - LANES) // ch
    steps = 4
    block = half // steps

    def kernel(place_ref, x, *outs):
        outs = outs[len(earlier) :]
        for i in range(m):
            outs[i][...] = x[:, i * ch : (i + 1) * ch].astype(F32)
        outs[m][...] = x[:, m * ch :].astype(F32)

    return call(
        kernel,
        grid=(steps,),
        prefetch=1,
        ins=[(half_rows, (block, width), lambda i, c: (i, 0))],
        outs=[(shape((2 * half, ch), F32), (block, ch), lambda i, c: (c[0] * steps + i, 0)) for _ in range(m)]
        + [(shape((half, LANES), F32), (block, LANES), lambda i, c: (i, 0))],
        aliased=earlier,
        name="finish_pre",
    )(place)


def finish_post(place, gathered, n, earlier=()):
    groups, per, width = gathered.shape
    share = 2 * groups * per
    ch = width // (n + 2)

    def kernel(place_ref, x, *outs):
        reduce_out, expand_out, read_out = outs[len(earlier) :]
        reduce_out[...] = x[0, :, :ch].astype(F32)
        for q in range(n):
            expand_out[q] = x[0, :, ch + q * share : ch + (q + 1) * share].astype(F32)
        read_out[...] = x[0, :, 2 * ch :].astype(F32)

    at = lambda i, c: (2 * i + c[0], 0)
    return call(
        kernel,
        grid=(groups,),
        prefetch=1,
        ins=[(gathered, (1, per, width), lambda i, c: (i, 0, 0))],
        outs=[
            (shape((share, ch), F32), (per, ch), at),
            (shape((n, share, share), F32), (n, per, share), lambda i, c: (0, 2 * i + c[0], 0)),
            (shape((share, n * ch), F32), (per, n * ch), at),
        ],
        aliased=earlier,
        name="finish_post",
    )(place)


def after(values, *earlier):
    return lax.optimization_barrier((values, *earlier))[0]


def pool_matrix(part, high, wide):
    half = wide // 2
    m = np.zeros((high // 2 * half * part, part * (high // 2) * wide), np.float32)
    for u in range(part):
        for i in range(high // 2):
            for j in range(wide):
                m[(i * half + j // 2) * part + u, (u * (high // 2) + i) * wide + j] = 0.25
    return m


def spread_matrix(part, high, wide):
    half = wide // 2
    m = np.zeros((part * high * wide, high // 2 * half * part), np.float32)
    for u in range(part):
        for i in range(high):
            for j in range(wide):
                m[(u * high + i) * wide + j, ((i // 2) * half + j // 2) * part + u] = 0.25
    return m


def body(features, counts, pre_reduce, pre_conv, pre_expand, pre_gain, post_reduce, post_conv, post_expand, post_gain, readout, cotangent):
    n = lax.axis_size("chan")
    row = lax.axis_index("rows").astype(jnp.int32)
    chan = lax.axis_index("chan").astype(jnp.int32)
    core = lax.axis_index("core").astype(jnp.int32)
    ch = pre_reduce.shape[0]
    slots, high, wide = features.shape[0], features.shape[1], features.shape[2]
    part = slots // n
    cells = high * wide
    pool = wide // 2
    share = ch // n
    out_share = cotangent.shape[3]
    steps = jnp.arange(n, dtype=jnp.int32)
    order = (row + steps) % n
    source = (row - steps) % n
    pair_of = (chan + steps) % n
    rank = jnp.full((1,), chan, jnp.int32)
    core_at = jnp.full((1,), core, jnp.int32)
    pre_taps = pre_conv.astype(F32).reshape(9, ch)
    post_taps = post_conv.astype(F32).reshape(9, ch)
    pre_gain_row = pre_gain.reshape(1, ch)
    pool_m = jnp.asarray(pool_matrix(part, high, wide), BF)
    up_m = jnp.asarray(spread_matrix(part, high, wide), BF)

    ends = n - 1
    down_pairs = [(i, i + 1) for i in range(ends)]
    up_pairs = [(i + 1, i) for i in range(ends)]
    above = lax.ppermute(features[:, -1], "rows", down_pairs)
    below = lax.ppermute(features[:, 0], "rows", up_pairs)
    gain_hi = post_gain.astype(BF)
    gain_lo = (post_gain - gain_hi.astype(F32)).astype(BF)
    gain_row = jnp.concatenate([gain_hi, gain_lo, jnp.zeros((ch - 2 * share,), BF)])[None]
    square = post_expand.reshape(n, share, share)
    shards = jnp.concatenate(
        [post_reduce, jnp.concatenate([square[q] for q in range(n)], axis=1), jnp.pad(gain_row, ((0, 63), (0, 0)))], axis=0
    )
    shard = lax.dynamic_index_in_dim(shards.reshape(2, -1, ch), core, 0, keepdims=False)
    full = lax.all_gather(shard, ("chan", "core"), axis=0, tiled=True)
    full = full.reshape(n, 2 * share + 64, ch)
    flat_features = features.reshape(slots * cells, ch)
    live = (jnp.arange(SLOT)[None, :] < counts[:, None]).astype(F32).reshape(slots)
    size, each = 16 * slots, 16 * part
    at = lax.broadcasted_iota(jnp.int32, (size, size), 0)
    column = lax.broadcasted_iota(jnp.int32, (size, size), 1)
    wanted = (at % each) // part * slots + part * ((chan + at // each) % n) + at % part
    select = jnp.where(column == wanted, jnp.tile(live, 16)[None, :], 0.0).astype(BF)
    wanted = (column % each) // part * slots + part * ((row - column // each) % n) + column % part
    place = jnp.where(at == wanted, 1.0, 0.0).astype(BF)
    cot_rows = cotangent.transpose(1, 2, 0, 3).reshape(-1, out_share)
    sends = cotangent_by_image(cot_rows, select, n)
    away = after(sends, above, below)
    cots = [lax.ppermute(away[k], ("rows", "chan"), cross(n, k)) for k in range(n)]

    reduced, convolved, convolved_act, normal_pre, pre_std, *pooled = pre_forward(
        order, above, below, features, pre_reduce, pre_taps, pre_expand, pre_gain_row, pool_m
    )

    pooled = after(pooled, cots)
    moved = [pooled[0]] + [lax.ppermute(pooled[k], "rows", turn(n, k)) for k in range(1, n)]
    flat, post_reduced, post_act, post_convolved, post_cact, post_normal, post_std, low = post_forward(
        source, moved, full, post_taps, pool
    )
    lows = [low] + [lax.ppermute(low, "chan", turn(n, k)) for k in range(1, n)]
    refined_grad = readout_backward(source, low, readout, cots)
    post_expanded_grad, post_reduced_grad, post_taps_grad, post_gain_grad, *back = post_backward(
        source, refined_grad, full, post_taps, post_act, post_reduced, post_convolved, post_normal, post_std, pool
    )

    returned = [back[0]] + [lax.ppermute(back[k], "rows", turn(n, -k)) for k in range(1, n)]

    flat = after(flat, lows)
    load = post_weight_grads(flat, post_reduced_grad, post_cact, post_expanded_grad, n)

    post_sum = lax.psum_scatter(load, ("x", "core"), scatter_dimension=0, tiled=False)

    stacked = jnp.stack(after(lows, load, returned))
    lows = [lax.dynamic_index_in_dim(stacked, (chan - row - k) % n, 0, keepdims=False) for k in range(n)]
    lows = [lows[0], lax.ppermute(lows[1], "rows", turn(n, 1)), lows[2], lax.ppermute(lows[3], "rows", turn(n, 3))]

    expanded_grad, convolved_grad, top, bottom, pre_gain_grad = pre_backward(
        order, returned, up_m, normal_pre, pre_std, pre_gain_row, convolved, pre_expand
    )
    top, bottom, lows[1], lows[3] = lax.optimization_barrier((top, bottom, lows[1], lows[3]))
    grad_above = lax.ppermute(bottom, "rows", down_pairs)
    grad_below = lax.ppermute(top, "rows", up_pairs)
    act_rows = after(convolved_act, bottom).reshape(-1, ch)
    pre_expand_grad = dot(act_rows, expanded_grad.reshape(-1, ch), TN).astype(BF)

    convolved_grad = after(convolved_grad, pre_expand_grad)
    lows[2] = lax.ppermute(after(lows[2], grad_above, grad_below), "rows", turn(n, 2))
    reduced_grad, pre_taps_grad = pre_conv_backward(convolved_grad, grad_above, grad_below, reduced, pre_taps)

    lows = after(lows, reduced_grad)
    tokens, piece = token_block(rank, source, pair_of, lows, place, readout, sends)
    read_load = readout_weight_grad(lows, piece, n)
    tokens = tokens.reshape(pool, pool, slots, out_share).transpose(2, 0, 1, 3)
    read_sum = lax.psum_scatter(after(read_load, post_sum), ("x", "core"), scatter_dimension=0, tiled=False)

    small = small_rows(pre_taps_grad, pre_gain_grad, post_taps_grad, post_gain_grad)
    pre_reduce_grad = dot(after(flat_features, small, read_load), reduced_grad.reshape(-1, ch), TN).astype(BF)

    chips = ("x", "rows", "chan")
    mine = [pre_reduce_grad, pre_expand_grad]
    theirs = [other_core(lax.dynamic_index_in_dim(g.reshape(2, ch // 2, ch), 1 - core, 0, keepdims=False)) for g in mine]
    load = join_halves(core_at, mine, theirs, small, other_core(small), 64)
    pieces = lax.all_to_all(load, chips, 0, 0, tiled=False)
    feature_grad = feature_backward(order, after(reduced_grad, load), pre_reduce, returned, up_m).reshape(features.shape)

    post_sum, read_sum = lax.optimization_barrier((post_sum, read_sum, feature_grad))[:2]
    blocks = split_rows(order, post_sum, read_sum)
    blocks = [blocks[0]] + [lax.ppermute(blocks[k], "rows", turn(n, k)) for k in range(1, n)]
    blocks = sum_rows(pair_of, blocks)
    load = sum_and_copy(after(pieces, *blocks))
    blocks = [blocks[0]] + [lax.ppermute(blocks[k], "chan", turn(n, k)) for k in range(1, n)]
    rest = join_chan((chan - steps) % n, after(blocks, load))
    ready = rest
    rest = lax.all_gather(rest, ("x", "rows"), axis=0, tiled=False).reshape(4, share // 8, -1)
    load_all = lax.all_to_all(after(load, ready), chips, 0, 0, tiled=False).reshape(ch // 2, -1)

    def finish(kernel, values, *sizes):
        theirs = other_core(values)
        own = kernel(core_at, values, *sizes)
        theirs = after(theirs, *own)
        return own, theirs

    own, theirs = finish(finish_pre, load_all, ch)
    pre_reduce_out, pre_expand_out, small_their = finish_pre(1 - core_at, theirs, ch, earlier=tuple(own[:2]))
    small_out = jnp.where(core == 0, own[2], small_their)
    own, theirs = finish(finish_post, after(rest, pre_reduce_out), n)
    post_reduce_out, post_expand_out, readout_out = finish_post(1 - core_at, theirs, n, earlier=tuple(own))
    per = ch // LANES
    cut = [0, 9 * per, 10 * per, 19 * per, 20 * per]
    pre_conv_out, pre_gain_out, post_conv_out, post_gain_out = [small_out[a:b] for a, b in zip(cut, cut[1:])]
    return (
        tokens,
        feature_grad,
        pre_reduce_out,
        pre_conv_out.reshape(3, 3, ch),
        pre_expand_out,
        pre_gain_out.reshape(ch),
        post_reduce_out,
        post_conv_out.reshape(3, 3, ch),
        post_expand_out.reshape(ch, share),
        lax.dynamic_slice_in_dim(post_gain_out.reshape(ch), chan * share, share, 0),
        readout_out,
    )


def solution(mesh):
    grid = Mesh(mesh.devices.reshape(4, 2, 4, 4), ("x", "core", "rows", "chan"))
    images = P(("x", "core", "chan"), "rows", None, None)
    grids = P(("x", "core", "rows"), None, None, "chan")
    return jax.shard_map(
        body,
        mesh=grid,
        in_specs=(
            images,
            P(("x", "core", "rows")),
            P(),
            P(),
            P(),
            P(),
            P("chan", None),
            P(),
            P(None, "chan"),
            P("chan"),
            P(),
            grids,
        ),
        out_specs=(grids, images, P(), P(), P(), P(), P("chan", None), P(), P(None, "chan"), P("chan"), P("chan", None)),
        check_vma=False,
    )
```

```python
import functools

import jax
import jax.numpy as jnp
import numpy as np
from jax import lax
from jax.experimental import pallas as pl
from jax.experimental.pallas import tpu as pltpu
from jax.sharding import Mesh, PartitionSpec as P

SLOT = 4
EPS = 1e-06
BF = jnp.bfloat16
F32 = jnp.float32
LANES = 128
VMEM_LIMIT = 20 * 1024 * 1024
NN = ((1,), (0,))
NT = ((1,), (1,))
TN = ((0,), (0,))


def dot(a, b, dims=NN):
    return lax.dot_general(a, b, (dims, ((), ())), preferred_element_type=F32)


def sigmoid(v):
    return 0.5 * jnp.tanh(0.5 * v) + 0.5


def silu(v):
    return v * sigmoid(v)


def silu_slope(v):
    s = sigmoid(v)
    return s * (1.0 + v * (1.0 - s))


def gelu_parts(v):
    c = 0.7978845608028654
    square = v * v
    t = jnp.tanh(v * (c + (c * 0.044715) * square))
    half = 0.5 * (1.0 + t)
    slope = half + 0.5 * v * (1.0 - t * t) * (c + (3.0 * c * 0.044715) * square)
    return v * half, slope


def chunks(count, body, width=LANES):
    for i in range(count):
        body(pl.ds(i * width, width))


def call(kernel, *, grid, ins, outs, scratch=(), prefetch=0, aliased=(), cost=1, name):
    def spec(shape, block, index):
        if block is None:
            block, index = shape, lambda *_: (0,) * len(shape)
        return pl.BlockSpec(block, index)

    arrays = [i[0] for i in ins] + list(aliased)
    in_specs = [spec(a.shape, b, m) for a, b, m in ins] + [pl.BlockSpec(memory_space=pl.ANY)] * len(aliased)
    out_specs = [spec(s.shape, b, m) for s, b, m in outs]

    def run(*scalars):
        return pl.pallas_call(
            kernel,
            grid_spec=pltpu.PrefetchScalarGridSpec(
                num_scalar_prefetch=prefetch,
                grid=grid,
                in_specs=in_specs,
                out_specs=out_specs,
                scratch_shapes=list(scratch),
            ),
            out_shape=[s[0] for s in outs],
            compiler_params=pltpu.CompilerParams(
                dimension_semantics=("arbitrary",) * len(grid), vmem_limit_bytes=VMEM_LIMIT
            ),
            input_output_aliases={prefetch + len(ins) + i: i for i in range(len(aliased))},
            cost_estimate=pl.CostEstimate(flops=cost, bytes_accessed=1, transcendentals=0),
            name=name,
        )(*scalars, *arrays)

    return run


def shape(dims, dtype):
    return jax.ShapeDtypeStruct(dims, dtype)


def far(values, dtype=None):
    if dtype is None:
        return pltpu.with_memory_space_constraint(values, pltpu.HBM)
    return pltpu.HBM(values, dtype)


def columns_moved(t, by, first, last):
    rows = t.shape[0]
    return pltpu.roll(t, by % rows, 0) * (first if by > 0 else last)


def edge_masks(rows, width, depth):
    at = lax.broadcasted_iota(jnp.int32, (rows, LANES), 0) % (width * depth)
    return (at >= depth).astype(F32), (at < (width - 1) * depth).astype(F32)


def pre_forward(order, above, below, features, pre_reduce, taps, pre_expand, gain, pool):
    slots, high, wide, ch = features.shape
    cells = high * wide
    n = order.shape[0]
    part = slots // n
    rows_all = part * cells

    def kernel(order_ref, up_ref, down_ref, feat, wr, tap, we, gn, pool_ref, red_out, conv_out, act_out, norm_out, std_out, *rest):
        pooled_out, (red, halo, exp, sums) = rest[:n], rest[n:]
        k = pl.program_id(0)
        for side, ref in enumerate((up_ref, down_ref)):
            halo[side] = dot(ref[...].reshape(part * wide, ch), wr[...]).reshape(part, wide, ch)
        red[...] = dot(feat[...].reshape(rows_all, ch), wr[...]).reshape(part, cells, ch)
        red_out[...] = red[...].astype(BF)
        first, last = edge_masks(wide, wide, 1)
        for u in range(part):

            def conv(lanes):
                w = [tap[pl.ds(i, 1), lanes] for i in range(9)]
                rows = [halo[0, u, :, lanes]]
                rows += [red[u, pl.ds(i * wide, wide), lanes] for i in range(high)]
                rows += [halo[1, u, :, lanes]]
                rows = [silu(r).astype(BF).astype(F32) for r in rows]
                out = []
                for i in range(high):
                    t = [sum(rows[i + a] * w[3 * a + b] for a in range(3)) for b in range(3)]
                    out.append(t[1] + columns_moved(t[0], 1, first, last) + columns_moved(t[2], -1, first, last))
                conv_out[u, :, lanes] = jnp.concatenate(out, 0).astype(BF)
                act_out[u, :, lanes] = jnp.concatenate([silu(c) for c in out], 0).astype(BF)

            chunks(ch // LANES, conv)

        exp[...] = dot(act_out[...].reshape(rows_all, ch), we[...])

        def norm(p, carry):
            u, i = p // (high // 2), p % (high // 2)
            tiles = wide // 8
            f = [feat[u, 2 * i + half].astype(F32) for half in range(2)]
            nrms, blends = [], []
            for t in range(2 * tiles):
                e = exp[pl.ds(p * 2 * wide + 8 * t, 8), :]
                mean = jnp.mean(e, -1, keepdims=True)
                square = jnp.mean(e * e, -1, keepdims=True)
                std = lax.rsqrt(square - mean * mean + EPS)
                nrm = (e - mean) * std
                std_out[u, pl.ds(i * 2 * wide + 8 * t, 8), :] = std
                nrms.append(nrm)
                at = t % tiles
                blends.append(f[t // tiles][8 * at : 8 * at + 8] + silu(nrm * gn[...]))
                if t % 2 == 1:
                    both = jnp.concatenate(nrms[-2:], 0).astype(BF)
                    norm_out[u, pl.ds(i * 2 * wide + 8 * (t - 1), 16), :] = both
            for t in range(tiles):
                sums[pl.ds(p * wide + 8 * t, 8), :] = blends[t] + blends[tiles + t]
            return carry

        for p in range(part * high // 2):
            norm(p, 0)
        s = sums[...]
        hi = s.astype(BF)
        lo = (s - hi.astype(F32)).astype(BF)
        pooled = (dot(pool_ref[...], hi) + dot(pool_ref[...], lo)).astype(BF)
        for i in range(n):

            @pl.when(k == i)
            def _():
                pooled_out[i][...] = pooled

    def by_order(rest):
        return lambda k, order: (order[k],) + (0,) * rest

    pooled_rows = pool.shape[0]
    block = (part, cells, ch)
    return call(
        kernel,
        grid=(n,),
        prefetch=1,
        ins=[
            (far(above), (part, wide, ch), by_order(2)),
            (far(below), (part, wide, ch), by_order(2)),
            (far(features), (part, high, wide, ch), by_order(3)),
            (far(pre_reduce), None, None),
            (taps, None, None),
            (far(pre_expand), None, None),
            (gain, None, None),
            (pool, None, None),
        ],
        outs=[(far((slots, cells, ch), BF), block, by_order(2))] * 4
        + [(far((slots, cells, 1), F32), (part, cells, 1), by_order(2))]
        + [(shape((pooled_rows, ch), BF), None, None)] * n,
        scratch=[
            pltpu.VMEM((part, cells, ch), F32),
            pltpu.VMEM((2, part, wide, ch), F32),
            pltpu.VMEM((rows_all, ch), F32),
            pltpu.VMEM((rows_all // 2, ch), F32),
        ],
        name="pre_forward",
    )(order)


def gain_row(w, n, share):
    at = 2 * share
    parts = [w[c, at : at + 16, :].astype(F32)[:1] for c in range(n)]
    return jnp.concatenate([p[:, :share] + p[:, share : 2 * share] for p in parts], 1)


def post_forward(source, moved, weights, taps, pool):
    n, (rows, ch) = len(moved), moved[0].shape
    total = n * rows
    depth = total // (pool * pool)
    share = ch // n

    def kernel(src, *refs):
        got, refs = refs[:n], refs[n:]
        w, tap, flat_out, red_out, act_out, conv_out, cact_out, norm_out, std_out, low_out, wide_ref, red, exp = refs
        for k in range(n):
            at = pl.multiple_of(src[k] * rows, 8)
            wide_ref[pl.ds(at, rows), :] = got[k][...].astype(F32)
        gain = gain_row(w, n, share)
        flat_out[...] = wide_ref[...].astype(BF)
        total_red = 0.0
        for c in range(n):
            total_red = total_red + dot(flat_out[:, c * share : (c + 1) * share], w[c, :share])
        red[...] = total_red
        first, last = edge_masks(total, pool, depth)
        step = pool * depth

        def conv(lanes):
            v = red[:, lanes]
            red_out[:, lanes] = v.astype(BF)
            x = silu(v).astype(BF)
            act_out[:, lanes] = x
            x = x.astype(F32)
            moves = [columns_moved(x, depth, first, last), x, columns_moved(x, -depth, first, last)]
            t = [sum(moves[b] * tap[pl.ds(3 * a + b, 1), lanes] for b in range(3)) for a in range(3)]
            none = jnp.zeros((step, LANES), F32)
            c = t[1] + jnp.concatenate([none, t[0][:-step]], 0) + jnp.concatenate([t[2][step:], none], 0)
            conv_out[:, lanes] = c.astype(BF)
            cact_out[:, lanes] = silu(c).astype(BF)

        chunks(ch // LANES, conv)
        for c in range(n):
            e = 0.0
            for q in range(n):
                cut = slice(q * share, (q + 1) * share)
                e = e + dot(cact_out[:, cut], w[c, share : 2 * share, cut])
            exp[:, c * share : (c + 1) * share] = e

        def norm(i, carry):
            for t in range(3):
                at = pl.ds(i * 48 + 16 * t, 16)
                e = exp[at, :]
                mean = jnp.mean(e, -1, keepdims=True)
                square = jnp.mean(e * e, -1, keepdims=True)
                std = lax.rsqrt(square - mean * mean + EPS)
                nrm = (e - mean) * std
                norm_out[at, :] = nrm.astype(BF)
                std_out[at, :] = std
                low_out[at, :] = (wide_ref[at, :] + silu(nrm * gain)).astype(BF)
            return carry

        for i in range(total // 48):
            norm(i, 0)

    narrow = shape((total, ch), BF)
    return call(
        kernel,
        grid=(1,),
        prefetch=1,
        ins=[(a, None, None) for a in (*map(far, moved), far(weights), taps)],
        outs=[(s, None, None) for s in (narrow, narrow, narrow, narrow, narrow, narrow, shape((total, 1), F32), narrow)],
        scratch=[pltpu.VMEM((total, ch), F32)] * 3,
        name="post_forward",
    )(source)


def readout_backward(source, low, readout, cots):
    total, ch = low.shape
    n, out_share = len(cots), cots[0].shape[1]

    def kernel(src, low_ref, ro, *rest):
        cot, grad = rest[:n], rest[n]
        k = pl.program_id(0)
        logits = dot(low_ref[...], ro[...])
        slope = gelu_parts(logits)[1]
        for i in range(n):

            @pl.when(k == i)
            def _():
                piece = (cot[i][...].astype(F32) * slope).astype(BF)
                term = dot(piece, ro[...], NT)
                grad[...] = term if i == 0 else grad[...] + term

    return call(
        kernel,
        grid=(n,),
        prefetch=1,
        ins=[(low, None, None), (far(readout), (ch, out_share), lambda k, s: (0, s[k]))] + [(c, None, None) for c in cots],
        outs=[(shape((total, ch), F32), None, None)],
        name="readout_backward",
    )(source)[0]


def post_backward(source, refined_grad, weights, taps, act, red, conv, nrm, std, pool):
    total, ch = act.shape
    n = weights.shape[0]
    share = ch // n
    rows = total // n
    depth = total // (pool * pool)

    def kernel(src, rg, w, tap, act_ref, red_ref, conv_ref, norm_ref, std_ref, exp_out, redg_out, taps_out, gain_out, *rest):
        back_out, (grad, cgrad) = rest[:n], rest[n:]
        gain = gain_row(w, n, share)

        def norm(i, total_gain):
            for t in range(3):
                at = pl.ds(i * 48 + 16 * t, 16)
                nm = norm_ref[at, :].astype(F32)
                ng = rg[at, :] * silu_slope(nm * gain)
                sc = ng * gain
                one = jnp.mean(sc, -1, keepdims=True)
                two = jnp.mean(sc * nm, -1, keepdims=True)
                exp_out[at, :] = (std_ref[at, :] * (sc - one - nm * two)).astype(BF)
                g = ng * nm
                total_gain = total_gain + g[:8] + g[8:]
            return total_gain

        gains = jnp.zeros((8, ch), F32)
        for i in range(total // 48):
            gains = norm(i, gains)
        gain_out[...] = gains
        for q in range(n):
            cut = slice(q * share, (q + 1) * share)
            cg = 0.0
            for c in range(n):
                cg = cg + dot(exp_out[:, c * share : (c + 1) * share], w[c, share : 2 * share, cut], NT)
            cgrad[:, cut] = cg
        first, last = edge_masks(total, pool, depth)
        step = pool * depth

        def back(lanes):
            g = (cgrad[:, lanes] * silu_slope(conv_ref[:, lanes].astype(F32))).astype(BF).astype(F32)
            x = act_ref[:, lanes].astype(F32)
            moves = [columns_moved(g, -depth, first, last), g, columns_moved(g, depth, first, last)]
            none = jnp.zeros((step, LANES), F32)
            xs = [
                jnp.concatenate([none, x[:-step]], 0),
                x,
                jnp.concatenate([x[step:], none], 0),
            ]
            for a in range(3):
                for b in range(3):
                    prod = xs[a] * moves[b]
                    taps_out[3 * a + b, :, lanes] = jnp.sum(prod.reshape(total // 8, 8, LANES), 0)
            t = [sum(moves[b] * tap[pl.ds(3 * a + b, 1), lanes] for b in range(3)) for a in range(3)]
            d = t[1] + jnp.concatenate([t[0][step:], none], 0) + jnp.concatenate([none, t[2][:-step]], 0)
            redg_out[:, lanes] = (d * silu_slope(red_ref[:, lanes].astype(F32))).astype(BF)

        chunks(ch // LANES, back)
        for c in range(n):
            cut = slice(c * share, (c + 1) * share)
            grad[:, cut] = rg[:, cut] + dot(redg_out[...], w[c, :share], NT)
        for r in range(n):
            at = pl.ds(pl.multiple_of(src[r] * rows, 8), rows)
            back_out[r][...] = grad[at, :].astype(BF)

    return call(
        kernel,
        grid=(1,),
        prefetch=1,
        ins=[(a, None, None) for a in (refined_grad, weights, taps, act, red, conv, nrm, std)],
        outs=[
            (s, None, None)
            for s in (
                shape((total, ch), BF),
                shape((total, ch), BF),
                shape((9, 8, ch), F32),
                shape((8, ch), F32),
                *[shape((rows, ch), BF)] * n,
            )
        ],
        scratch=[pltpu.VMEM((total, ch), F32), pltpu.VMEM((total, ch), F32)],
        name="post_backward",
    )(source)


def cotangent_by_image(cotangent, select, pairs):
    rows, width = cotangent.shape
    size = select.shape[0]
    each = size // pairs
    per = 3

    def kernel(x, sel, *outs):
        for q in range(per):
            y = dot(sel[...], x[pl.ds(q * size, size), :]).astype(BF)
            for s in range(pairs):
                outs[s][pl.ds(q * each, each), :] = y[s * each : (s + 1) * each]

    return call(
        kernel,
        grid=(rows // (per * size),),
        ins=[(far(cotangent), (per * size, width), lambda i: (i, 0)), (select, None, None)],
        outs=[(shape((rows // pairs, width), BF), (per * each, width), lambda i: (i, 0))] * pairs,
        name="cotangent_by_image",
    )()


def token_grad(chan, source, pair_of, low, readout, cotangent):
    pairs, (rows, ch) = len(low), low[0].shape
    width = cotangent[0].shape[1]
    block = rows // 3

    def kernel(chan_ref, src, pair, *refs):
        lows, cots, (ro, piece_out, cot) = refs[:pairs], refs[pairs : 2 * pairs], refs[2 * pairs :]
        for k in range(pairs):
            cot[pair[k]] = cots[k][...]
        logits = dot(jnp.concatenate([v[...] for v in lows], 0), ro[...])
        slope = gelu_parts(logits)[1]
        for k in range(pairs):
            piece_out[k] = (cot[src[k]].astype(F32) * slope[k * block : (k + 1) * block]).astype(BF)

    rows_at = lambda i, c, s, p: (i, 0)
    return call(
        kernel,
        grid=(rows // block,),
        prefetch=3,
        ins=[
            *[(v, (block, ch), rows_at) for v in low],
            *[(v, (block, width), rows_at) for v in cotangent],
            (far(readout), (ch, width), lambda i, c, s, p: (0, c[0])),
        ],
        outs=[(shape((pairs, rows, width), BF), (pairs, block, width), lambda i, c, s, p: (0, i, 0))],
        scratch=[pltpu.VMEM((pairs, block, width), BF)],
        name="token_grad",
    )(chan, source, pair_of)[0]


def token_values(chan, low, place, readout, width):
    pairs, (rows, ch) = len(low), low[0].shape
    size = place.shape[0]
    each = size // pairs
    per = 3
    block = per * each

    def kernel(chan_ref, *refs):
        lows, (place_ref, ro, tok_out) = refs[:pairs], refs[pairs:]
        logits = dot(jnp.concatenate([v[...] for v in lows], 0), ro[...])
        value = gelu_parts(logits)[0].astype(BF)
        for q in range(per):
            x = jnp.concatenate([value[k * block + q * each : k * block + (q + 1) * each] for k in range(pairs)], 0)
            tok_out[pl.ds(q * size, size), :] = dot(place_ref[...], x).astype(BF)

    return call(
        kernel,
        grid=(rows // block,),
        prefetch=1,
        ins=[
            *[(v, (block, ch), lambda i, c: (i, 0)) for v in low],
            (place, None, None),
            (far(readout), (ch, width), lambda i, c: (0, c[0])),
        ],
        outs=[(shape((pairs * rows, width), BF), (pairs * block, width), lambda i, c: (i, 0))],
        name="token_values",
    )(chan)[0]


def pre_backward(order, returned, spread_up, nrm, std, gain, conv, pre_expand):
    slots, cells, ch = nrm.shape
    n = order.shape[0]
    part = slots // n
    wide = 24
    rows = part * cells

    def kernel(order_ref, *refs):
        ret, refs = refs[:n], refs[n:]
        up, norm_ref, std_ref, gn, conv_ref, we, exp_out, conv_grad_out, top_out, bottom_out, gain_out, grad, cgrad = refs
        k = pl.program_id(0)
        for i in range(n):

            @pl.when(k == i)
            def _():
                grad[...] = dot(up[...], ret[i][...])

        def norm(i, total_gain):
            u, j = i // (cells // 48), i % (cells // 48)
            for t in range(3):
                at = pl.ds(j * 48 + 16 * t, 16)
                nm = norm_ref[u, at, :].astype(F32)
                ng = grad[pl.ds(i * 48 + 16 * t, 16), :] * silu_slope(nm * gn[...])
                sc = ng * gn[...]
                one = jnp.mean(sc, -1, keepdims=True)
                two = jnp.mean(sc * nm, -1, keepdims=True)
                exp_out[u, at, :] = (std_ref[u, at, :] * (sc - one - nm * two)).astype(BF)
                g = ng * nm
                total_gain = total_gain + g[:8] + g[8:]
            return total_gain

        gains = jnp.zeros((8, ch), F32)
        for i in range(rows // 48):
            gains = norm(i, gains)

        @pl.when(k == 0)
        def _():
            gain_out[...] = gains

        @pl.when(k > 0)
        def _():
            gain_out[...] += gains

        cgrad[...] = dot(exp_out[...].reshape(rows, ch), we[...], NT)
        for u in range(part):

            def slope(lanes):
                g = cgrad[pl.ds(u * cells, cells), lanes] * silu_slope(conv_ref[u, :, lanes].astype(F32))
                conv_grad_out[u, :, lanes] = g.astype(BF)
                top_out[u, :, lanes] = g[:wide].astype(BF)
                bottom_out[u, :, lanes] = g[cells - wide :].astype(BF)

            chunks(ch // LANES, slope)

    by_order = lambda k, order: (order[k], 0, 0)
    whole = (part, cells, ch)
    edge = (part, wide, ch)
    return call(
        kernel,
        grid=(n,),
        prefetch=1,
        ins=[
            *[(r, None, None) for r in returned],
            (spread_up, None, None),
            (far(nrm), whole, by_order),
            (far(std), (part, cells, 1), by_order),
            (gain, None, None),
            (far(conv), whole, by_order),
            (far(pre_expand), None, None),
        ],
        outs=[
            (shape((slots, cells, ch), BF), whole, by_order),
            (far((slots, cells, ch), BF), whole, by_order),
            (shape((slots, wide, ch), BF), edge, by_order),
            (shape((slots, wide, ch), BF), edge, by_order),
            (shape((8, ch), F32), None, None),
        ],
        scratch=[pltpu.VMEM((rows, ch), F32), pltpu.VMEM((rows, ch), F32)],
        name="pre_backward",
    )(order)


def pre_conv_backward(conv_grad, above, below, reduced, taps):
    slots, cells, ch = reduced.shape
    wide = above.shape[1]
    high = cells // wide

    def kernel(cg, up, down, red, tap, redg_out, taps_out):
        step = pl.program_id(0)
        first, last = edge_masks(wide, wide, 1)

        @pl.when(step == 0)
        def _():
            taps_out[...] = jnp.zeros_like(taps_out)

        def back(lanes):
            w = [tap[pl.ds(i, 1), lanes] for i in range(9)]
            mid = cg[0, :, lanes].astype(F32)
            rows = [up[0, :, lanes].astype(F32)]
            rows += [mid[i * wide : (i + 1) * wide] for i in range(high)]
            rows += [down[0, :, lanes].astype(F32)]
            whole = red[0, :, lanes].astype(F32)
            v = [whole[i * wide : (i + 1) * wide] for i in range(high)]
            s = [sigmoid(t) for t in v]
            x = [(a * b).astype(BF).astype(F32) for a, b in zip(v, s)]
            d = [0.0] * high
            sums = [0.0] * 9
            for p in range(high + 2):
                g = rows[p]
                moves = [columns_moved(g, -1, first, last), g, columns_moved(g, 1, first, last)]
                for a in range(3):
                    i = p - 1 + a - 1
                    if 0 <= i < high:
                        for b in range(3):
                            d[i] = d[i] + moves[b] * w[3 * a + b]
                            prod = x[i] * moves[b]
                            sums[3 * a + b] = sums[3 * a + b] + (prod[:8] + prod[8:16] + prod[16:])
            out = [d[i] * (s[i] * (1.0 + v[i] * (1.0 - s[i]))) for i in range(high)]
            redg_out[0, :, lanes] = jnp.concatenate(out, 0).astype(BF)
            for i in range(9):
                taps_out[i, :, lanes] += sums[i]

        chunks(ch // LANES, back)

    image = lambda i: (i, 0, 0)
    return call(
        kernel,
        grid=(slots,),
        ins=[
            (far(conv_grad), (1, cells, ch), image),
            (far(above), (1, wide, ch), image),
            (far(below), (1, wide, ch), image),
            (far(reduced), (1, cells, ch), image),
            (taps, None, None),
        ],
        outs=[
            (shape((slots, cells, ch), BF), (1, cells, ch), image),
            (shape((9, 8, ch), F32), None, None),
        ],
        name="pre_conv_backward",
    )()


def feature_backward(order, reduced_grad, pre_reduce, returned, spread_up):
    slots, cells, ch = reduced_grad.shape
    n = order.shape[0]
    part = slots // n

    def kernel(order_ref, rg, wr, up, *refs):
        ret, out = refs[:n], refs[n]
        k = pl.program_id(0)
        for i in range(n):

            @pl.when(k == i)
            def _():
                out[...] = dot(up[...], ret[i][...]).reshape(part, cells, ch)

        out[...] += dot(rg[...].reshape(part * cells, ch), wr[...], NT).reshape(part, cells, ch)

    by_order = lambda k, order: (order[k], 0, 0)
    whole = (part, cells, ch)
    return call(
        kernel,
        grid=(n,),
        prefetch=1,
        ins=[
            (reduced_grad, whole, by_order),
            (far(pre_reduce), None, None),
            (spread_up, None, None),
            *[(r, None, None) for r in returned],
        ],
        outs=[(shape((slots, cells, ch), F32), whole, by_order)],
        name="feature_backward",
    )(order)[0]


def post_weight_grads(flat, reduced_grad, act, expanded_grad, n):
    total, ch = flat.shape
    share = ch // n
    rows = share // 8

    def kernel(x, g, a, e, out):
        for c in range(n):
            cut = slice(c * share, (c + 1) * share)
            v = dot(x[:, cut], g[...], TN).astype(BF)
            for d in range(8):
                out[d, c, :, :ch] = v[d * rows : (d + 1) * rows]
            for q in range(n):
                v = dot(a[:, q * share : (q + 1) * share], e[:, cut], TN).astype(BF)
                for d in range(8):
                    out[d, c, :, ch + q * share : ch + (q + 1) * share] = v[d * rows : (d + 1) * rows]

    return call(
        kernel,
        grid=(1,),
        ins=[(v, None, None) for v in (flat, reduced_grad, act, expanded_grad)],
        outs=[(far((8, n, rows, 2 * ch), BF), None, None)],
        name="post_weight_grads",
    )()[0]


def readout_weight_grad(low, piece, n):
    pairs, total, width = piece.shape
    ch = low[0].shape[1]
    share = ch // n
    parts = 8
    rows = share // parts

    def kernel(*refs):
        x, (g, out) = refs[:pairs], refs[pairs:]
        x = jnp.concatenate([v[...] for v in x], 0)
        v = dot(x, g[...].reshape(pairs * total, width), TN).astype(BF)
        for d in range(parts):
            out[d, 0] = v[d * rows : (d + 1) * rows]

    return call(
        kernel,
        grid=(n,),
        ins=[(v, (total, share), lambda c: (0, c)) for v in low] + [(piece, None, None)],
        outs=[(far((parts, n, rows, width), BF), (parts, 1, rows, width), lambda c: (0, c, 0, 0))],
        name="readout_weight_grad",
    )()[0]


def cross(n, k):
    return [(a * n + b, ((b + k) % n) * n + a) for a in range(n) for b in range(n)]


def turn(n, k):
    return [(i, (i + k) % n) for i in range(n)]


def other_core(values):
    return lax.ppermute(values, "core", [(0, 1), (1, 0)])


def small_rows(*grads):
    ch = grads[0].shape[-1]
    counts = [g.shape[0] if g.ndim == 3 else 1 for g in grads]
    per = ch // LANES

    def kernel(*refs):
        out = refs[-1]
        at = 0
        for ref, count in zip(refs, counts):
            for i in range(count):
                v = jnp.sum(ref[i] if len(ref.shape) == 3 else ref[...], 0, keepdims=True)
                for q in range(per):
                    out[pl.ds(at, 1), :] = v[:, q * LANES : (q + 1) * LANES]
                    at += 1

    return call(
        kernel,
        grid=(1,),
        ins=[(g, None, None) for g in grads],
        outs=[(shape((sum(counts) * per, LANES), F32), None, None)],
        name="small_rows",
    )()[0]


def join_halves(core, mine, theirs, small, their_small, parts):
    rows, ch = mine[0].shape
    half = rows // 2
    width = len(mine) * ch + LANES
    count = small.shape[0]
    m = len(mine)
    steps = 2
    block = half // steps

    def kernel(core_ref, *refs):
        own, got = refs[:m], refs[m : 2 * m]
        sm, got_sm, out = refs[2 * m :]
        for i in range(m):
            out[:, i * ch : (i + 1) * ch] = (own[i][...].astype(F32) + got[i][...].astype(F32)).astype(BF)
        first = ((core_ref[0] == 0) & (pl.program_id(0) == 0)).astype(F32)
        total = (sm[...] + got_sm[...]) * first
        pad = jnp.zeros((block - count, LANES), F32)
        out[:, m * ch :] = jnp.concatenate([total, pad], 0).astype(BF)

    return call(
        kernel,
        grid=(steps,),
        prefetch=1,
        ins=[(v, (block, ch), lambda i, c: (c[0] * steps + i, 0)) for v in mine]
        + [(v, (block, ch), lambda i, c: (i, 0)) for v in theirs]
        + [(v, None, None) for v in (small, their_small)],
        outs=[(far((half, width), BF), (block, width), lambda i, c: (i, 0))],
        name="join_halves",
    )(core)[0].reshape(parts, half // parts, width)


def sum_and_copy(blocks):
    parts, rows, width = blocks.shape

    def kernel(x, out):
        def cut(lanes):
            total = jnp.sum(x[:, :, lanes].astype(F32), 0).astype(BF)
            out[:, :, lanes] = jnp.broadcast_to(total[None], (parts, rows, LANES))

        chunks(width // LANES, cut)

    return call(
        kernel,
        grid=(1,),
        ins=[(blocks, None, None)],
        outs=[(far(blocks.shape, BF), None, None)],
        name="sum_and_copy",
    )()[0]


def split_rows(to_row, post, read):
    n, rows, width = post.shape
    ch = read.shape[2]
    each = rows // n

    def kernel(to, a, b, *outs):
        outs, wide = outs[:n], outs[n]
        wide[:, :, :width] = a[...].astype(F32)
        wide[:, :, width:] = b[...].astype(F32)
        for k in range(n):
            outs[k][...] = wide[:, pl.ds(pl.multiple_of(to[k] * each, 8), each), :].astype(BF)

    return call(
        kernel,
        grid=(1,),
        prefetch=1,
        ins=[(post, None, None), (read, None, None)],
        outs=[(shape((n, each, width + ch), BF), None, None)] * n,
        scratch=[pltpu.VMEM((n, rows, width + ch), F32)],
        name="split_rows",
    )(to_row)


def sum_rows(to_chan, blocks):
    n, rows, width = blocks[0].shape

    def kernel(to, *refs):
        outs = refs[n:]
        for k in range(n):
            outs[k][...] = sum(r[to[k]].astype(F32) for r in refs[:n]).astype(BF)

    return call(
        kernel,
        grid=(1,),
        prefetch=1,
        ins=[(b, None, None) for b in blocks],
        outs=[(shape((rows, width), BF), None, None)] * n,
        name="sum_rows",
    )(to_chan)


def join_chan(from_chan, blocks):
    n = len(blocks)
    rows, width = blocks[0].shape
    ch = width // 3

    def kernel(src, *refs):
        out = refs[n]
        out[:, : 2 * ch] = sum(r[:, : 2 * ch].astype(F32) for r in refs[:n]).astype(BF)
        for k in range(n):
            at = pl.multiple_of(2 * ch + src[k] * ch, LANES)
            out[:, pl.ds(at, ch)] = refs[k][:, 2 * ch :]

    return call(
        kernel,
        grid=(1,),
        prefetch=1,
        ins=[(b, None, None) for b in blocks],
        outs=[(far((rows, 2 * ch + n * ch), BF), None, None)],
        name="join_chan",
    )(from_chan)[0]


def finish_pre(place, half_rows, ch, earlier=()):
    half, width = half_rows.shape
    m = (width - LANES) // ch
    steps = 4
    block = half // steps

    def kernel(place_ref, x, *outs):
        outs = outs[len(earlier) :]
        for i in range(m):
            outs[i][...] = x[:, i * ch : (i + 1) * ch].astype(F32)
        outs[m][...] = x[:, m * ch :].astype(F32)

    return call(
        kernel,
        grid=(steps,),
        prefetch=1,
        ins=[(half_rows, (block, width), lambda i, c: (i, 0))],
        outs=[(shape((2 * half, ch), F32), (block, ch), lambda i, c: (c[0] * steps + i, 0)) for _ in range(m)]
        + [(shape((half, LANES), F32), (block, LANES), lambda i, c: (i, 0))],
        aliased=earlier,
        name="finish_pre",
    )(place)


def finish_post(place, gathered, n, earlier=()):
    groups, per, width = gathered.shape
    share = 2 * groups * per
    ch = width // (n + 2)

    def kernel(place_ref, x, *outs):
        reduce_out, expand_out, read_out = outs[len(earlier) :]
        reduce_out[...] = x[0, :, :ch].astype(F32)
        for q in range(n):
            expand_out[q] = x[0, :, ch + q * share : ch + (q + 1) * share].astype(F32)
        read_out[...] = x[0, :, 2 * ch :].astype(F32)

    at = lambda i, c: (2 * i + c[0], 0)
    return call(
        kernel,
        grid=(groups,),
        prefetch=1,
        ins=[(gathered, (1, per, width), lambda i, c: (i, 0, 0))],
        outs=[
            (shape((share, ch), F32), (per, ch), at),
            (shape((n, share, share), F32), (n, per, share), lambda i, c: (0, 2 * i + c[0], 0)),
            (shape((share, n * ch), F32), (per, n * ch), at),
        ],
        aliased=earlier,
        name="finish_post",
    )(place)


def after(values, *earlier):
    return lax.optimization_barrier((values, *earlier))[0]


def pool_matrix(part, high, wide):
    half = wide // 2
    m = np.zeros((high // 2 * half * part, part * (high // 2) * wide), np.float32)
    for u in range(part):
        for i in range(high // 2):
            for j in range(wide):
                m[(i * half + j // 2) * part + u, (u * (high // 2) + i) * wide + j] = 0.25
    return m


def spread_matrix(part, high, wide):
    half = wide // 2
    m = np.zeros((part * high * wide, high // 2 * half * part), np.float32)
    for u in range(part):
        for i in range(high):
            for j in range(wide):
                m[(u * high + i) * wide + j, ((i // 2) * half + j // 2) * part + u] = 0.25
    return m


def body(features, counts, pre_reduce, pre_conv, pre_expand, pre_gain, post_reduce, post_conv, post_expand, post_gain, readout, cotangent):
    n = lax.axis_size("chan")
    row = lax.axis_index("rows").astype(jnp.int32)
    chan = lax.axis_index("chan").astype(jnp.int32)
    core = lax.axis_index("core").astype(jnp.int32)
    ch = pre_reduce.shape[0]
    slots, high, wide = features.shape[0], features.shape[1], features.shape[2]
    part = slots // n
    cells = high * wide
    pool = wide // 2
    share = ch // n
    out_share = cotangent.shape[3]
    steps = jnp.arange(n, dtype=jnp.int32)
    order = (row + steps) % n
    source = (row - steps) % n
    pair_of = (chan + steps) % n
    rank = jnp.full((1,), chan, jnp.int32)
    core_at = jnp.full((1,), core, jnp.int32)
    pre_taps = pre_conv.astype(F32).reshape(9, ch)
    post_taps = post_conv.astype(F32).reshape(9, ch)
    pre_gain_row = pre_gain.reshape(1, ch)
    pool_m = jnp.asarray(pool_matrix(part, high, wide), BF)
    up_m = jnp.asarray(spread_matrix(part, high, wide), BF)

    ends = n - 1
    down_pairs = [(i, i + 1) for i in range(ends)]
    up_pairs = [(i + 1, i) for i in range(ends)]
    above = lax.ppermute(features[:, -1], "rows", down_pairs)
    below = lax.ppermute(features[:, 0], "rows", up_pairs)
    gain_hi = post_gain.astype(BF)
    gain_lo = (post_gain - gain_hi.astype(F32)).astype(BF)
    gain_row = jnp.concatenate([gain_hi, gain_lo, jnp.zeros((ch - 2 * share,), BF)])[None]
    square = post_expand.reshape(n, share, share)
    shards = jnp.concatenate(
        [post_reduce, jnp.concatenate([square[q] for q in range(n)], axis=1), jnp.pad(gain_row, ((0, 63), (0, 0)))], axis=0
    )
    shard = lax.dynamic_index_in_dim(shards.reshape(2, -1, ch), core, 0, keepdims=False)
    full = lax.all_gather(shard, ("chan", "core"), axis=0, tiled=True)
    full = full.reshape(n, 2 * share + 64, ch)
    flat_features = features.reshape(slots * cells, ch)
    live = (jnp.arange(SLOT)[None, :] < counts[:, None]).astype(F32).reshape(slots)
    size, each = 16 * slots, 16 * part
    at = lax.broadcasted_iota(jnp.int32, (size, size), 0)
    column = lax.broadcasted_iota(jnp.int32, (size, size), 1)
    wanted = (at % each) // part * slots + part * ((chan + at // each) % n) + at % part
    select = jnp.where(column == wanted, jnp.tile(live, 16)[None, :], 0.0).astype(BF)
    wanted = (column % each) // part * slots + part * ((row - column // each) % n) + column % part
    place = jnp.where(at == wanted, 1.0, 0.0).astype(BF)
    cot_rows = cotangent.transpose(1, 2, 0, 3).reshape(-1, out_share)
    sends = cotangent_by_image(cot_rows, select, n)
    away = after(sends, above, below)
    cots = [lax.ppermute(away[k], ("rows", "chan"), cross(n, k)) for k in range(n)]

    reduced, convolved, convolved_act, normal_pre, pre_std, *pooled = pre_forward(
        order, above, below, features, pre_reduce, pre_taps, pre_expand, pre_gain_row, pool_m
    )

    pooled = after(pooled, cots)
    moved = [pooled[0]] + [lax.ppermute(pooled[k], "rows", turn(n, k)) for k in range(1, n)]
    flat, post_reduced, post_act, post_convolved, post_cact, post_normal, post_std, low = post_forward(
        source, moved, full, post_taps, pool
    )
    lows = [low] + [lax.ppermute(low, "chan", turn(n, k)) for k in range(1, n)]
    refined_grad = readout_backward(source, low, readout, cots)
    post_expanded_grad, post_reduced_grad, post_taps_grad, post_gain_grad, *back = post_backward(
        source, refined_grad, full, post_taps, post_act, post_reduced, post_convolved, post_normal, post_std, pool
    )

    returned = [back[0]] + [lax.ppermute(back[k], "rows", turn(n, -k)) for k in range(1, n)]

    flat = after(flat, lows)
    load = post_weight_grads(flat, post_reduced_grad, post_cact, post_expanded_grad, n)

    post_sum = lax.psum_scatter(load, ("x", "core"), scatter_dimension=0, tiled=False)

    stacked = jnp.stack(after(lows, load, returned))
    lows = [lax.dynamic_index_in_dim(stacked, (chan - row - k) % n, 0, keepdims=False) for k in range(n)]
    lows = [lows[0]] + [lax.ppermute(lows[k], "rows", turn(n, k)) for k in range(1, n)]

    expanded_grad, convolved_grad, top, bottom, pre_gain_grad = pre_backward(
        order, returned, up_m, normal_pre, pre_std, pre_gain_row, convolved, pre_expand
    )
    top, bottom, lows[1], lows[3] = lax.optimization_barrier((top, bottom, lows[1], lows[3]))
    grad_above = lax.ppermute(bottom, "rows", down_pairs)
    grad_below = lax.ppermute(top, "rows", up_pairs)
    act_rows = after(convolved_act, bottom).reshape(-1, ch)
    pre_expand_grad = dot(act_rows, expanded_grad.reshape(-1, ch), TN).astype(BF)

    lows = after(lows, pre_expand_grad)
    piece = token_grad(rank, source, pair_of, lows, readout, sends)
    read_load = readout_weight_grad(lows, after(piece, grad_above, grad_below), n)
    convolved_grad = after(convolved_grad, read_load)
    read_sum = lax.psum_scatter(after(read_load, post_sum), ("x", "core"), scatter_dimension=0, tiled=False)

    reduced_grad, pre_taps_grad = pre_conv_backward(convolved_grad, grad_above, grad_below, reduced, pre_taps)
    small = small_rows(pre_taps_grad, pre_gain_grad, post_taps_grad, post_gain_grad)
    pre_reduce_grad = dot(after(flat_features, small), reduced_grad.reshape(-1, ch), TN).astype(BF)

    chips = ("x", "rows", "chan")
    mine = [pre_reduce_grad, pre_expand_grad]
    theirs = [other_core(lax.dynamic_index_in_dim(g.reshape(2, ch // 2, ch), 1 - core, 0, keepdims=False)) for g in mine]
    load = join_halves(core_at, mine, theirs, small, other_core(small), 64)
    pieces = lax.all_to_all(load, chips, 0, 0, tiled=False)
    feature_grad = feature_backward(order, after(reduced_grad, load), pre_reduce, returned, up_m).reshape(features.shape)

    post_sum, read_sum = lax.optimization_barrier((post_sum, read_sum, feature_grad))[:2]
    blocks = split_rows(order, post_sum, read_sum)
    blocks = [blocks[0]] + [lax.ppermute(blocks[k], "rows", turn(n, k)) for k in range(1, n)]
    blocks = sum_rows(pair_of, blocks)
    load = sum_and_copy(after(pieces, *blocks))
    blocks = [blocks[0]] + [lax.ppermute(blocks[k], "chan", turn(n, k)) for k in range(1, n)]
    rest = join_chan((chan - steps) % n, after(blocks, load))
    ready = rest
    rest = lax.all_gather(rest, ("x", "rows"), axis=0, tiled=False).reshape(4, share // 8, -1)
    load_all = lax.all_to_all(after(load, ready), chips, 0, 0, tiled=False).reshape(ch // 2, -1)

    tokens = token_values(rank, after(lows, load, ready), place, readout, out_share)
    load_all = after(load_all, tokens)
    tokens = tokens.reshape(pool, pool, slots, out_share).transpose(2, 0, 1, 3)

    def finish(kernel, values, *sizes):
        theirs = other_core(values)
        own = kernel(core_at, values, *sizes)
        theirs = after(theirs, *own)
        return own, theirs

    own, theirs = finish(finish_pre, load_all, ch)
    pre_reduce_out, pre_expand_out, small_their = finish_pre(1 - core_at, theirs, ch, earlier=tuple(own[:2]))
    small_out = jnp.where(core == 0, own[2], small_their)
    own, theirs = finish(finish_post, after(rest, pre_reduce_out), n)
    post_reduce_out, post_expand_out, readout_out = finish_post(1 - core_at, theirs, n, earlier=tuple(own))
    per = ch // LANES
    cut = [0, 9 * per, 10 * per, 19 * per, 20 * per]
    pre_conv_out, pre_gain_out, post_conv_out, post_gain_out = [small_out[a:b] for a, b in zip(cut, cut[1:])]
    return (
        tokens,
        feature_grad,
        pre_reduce_out,
        pre_conv_out.reshape(3, 3, ch),
        pre_expand_out,
        pre_gain_out.reshape(ch),
        post_reduce_out,
        post_conv_out.reshape(3, 3, ch),
        post_expand_out.reshape(ch, share),
        lax.dynamic_slice_in_dim(post_gain_out.reshape(ch), chan * share, share, 0),
        readout_out,
    )


def solution(mesh):
    grid = Mesh(mesh.devices.reshape(4, 2, 4, 4), ("x", "core", "rows", "chan"))
    images = P(("x", "core", "chan"), "rows", None, None)
    grids = P(("x", "core", "rows"), None, None, "chan")
    return jax.shard_map(
        body,
        mesh=grid,
        in_specs=(
            images,
            P(("x", "core", "rows")),
            P(),
            P(),
            P(),
            P(),
            P("chan", None),
            P(),
            P(None, "chan"),
            P("chan"),
            P(),
            grids,
        ),
        out_specs=(grids, images, P(), P(), P(), P(), P("chan", None), P(), P(None, "chan"), P("chan"), P("chan", None)),
        check_vma=False,
    )
```
